32 devices in a mesh: sec: 8 (over y, x, core), rank: 4 (over z).
Axes of the slice: x: 2, y: 2, z: 4, core: 2. Of those that a mesh axis runs over, the one named last changes fastest.
Arguments:
- climate_field_table: float32 [8, 32, 240, 128], P('sec', 'rank'), may hold values from -6 to 6
- zonal_wind_speed: float32 [8, 32, 24, 128], P('sec', 'rank'), may hold values from -6 to 6
- meridional_wind: float32 [8, 32, 24, 128], P('sec', 'rank'), may hold values from -6 to 6
- sea_warmth_field: float32 [8, 32, 128], P('sec', 'rank'), may hold values from -6 to 6
- exchange_law_factor: float32 [4, 11], replicated, may hold values from -1.75 to 1.75
- regrid_matrix_stack: bfloat16 [8, 4, 3, 128, 8, 128], P('sec', 'rank'), may hold values from -0.1875 to 0.1875
- entry_sender_patch: int32 [2, 4, 3], P(None, 'rank'), may hold values from 0 to 5, as said below
- holder_live_total: int32 [2, 4], P(None, 'rank'), may hold values from 1 to 3, as said below
- marine_salinity_heat: float32 [8, 2, 8, 512], P('sec', None, None, 'rank'), may hold values from -6 to 6
- adjacent_offset_lists: int32 [8, 7, 512], P('sec', None, 'rank'), may hold values from -8 to 8, as said below
- polygon_side_total: int32 [8, 512], P('sec', 'rank'), may hold values from 5 to 7
- interface_mixing_factor: float32 [8, 7, 512], P('sec', None, 'rank'), may hold values from 0.5 to 2
- solute_forcing_factor: float32 [2, 4], replicated, may hold values from -3 to 3
Outputs:
- climate_fields_later: float32 [8, 32, 240, 128], P('sec', 'rank')
- marine_tracers_later: float32 [8, 2, 8, 512], P('sec', None, None, 'rank')
- warmth_regridded: float32 [8, 32, 128], P('sec', 'rank')
The draws below stay inside these ranges and needn't reach their ends.
Inputs may be any that keep to these rules, and one draw needn't show every extreme that they name: `entry_sender_patch`: every slot names an atmosphere section. `holder_live_total`: slots at or past an owner's count are not read. `adjacent_offset_lists`: offsets are never zero; slots at or past a cell's edge count are not read.
All inputs are finite; a program needn't handle non-finite values.
Results may differ from the reference program's by a relative error of at most 0.0038.
Values may be sent and summed in bfloat16 or wider, within the bound.
No kernel may reach another device: no remote copies, remote signals or barrier semaphores. Data moves between devices by JAX's collectives and lax.ppermute only.
A program may use at most 64 MiB of HBM per device.

```python
import math
import jax
import jax.numpy as jnp
import numpy as np
from jax import lax

NF = 10
LEV_A = 24
NFLUX = 4
K = 3
HOLDER_POLYGONS = 128
LEV_O = 8
MAXE = 7
HC = 8
CLIMATE_PATCHES = 6
MARINE_PATCHES = 2
XD = 8
LATTICE_COLUMNS = 32
LATTICE_LINES = 128
ROWS = 240
NCELL = 512
N_SEC = 8
N_RANK = 4


def draw_entry_sender_patch(key, part):
    picked_ids = jax.random.randint(key, (MARINE_PATCHES, N_RANK, K), 0, CLIMATE_PATCHES)
    picked_ids = picked_ids.at[0, 0, 0].set(0).at[0, 0, 1].set(CLIMATE_PATCHES - 1)
    return picked_ids.astype(jnp.int32)


def draw_holder_live_total(key, part):
    counts = jax.random.randint(key, (MARINE_PATCHES, N_RANK), 1, K + 1)
    counts = counts.at[0, 0].set(K).at[0, 1].set(1)
    return counts.astype(jnp.int32)


def draw_adjacent_offset_lists(key, part):
    distance = jax.random.randint(jax.random.fold_in(key, 1), (N_SEC, MAXE, NCELL), 1, HC + 1)
    direction = 2 * jax.random.randint(jax.random.fold_in(key, 2), (N_SEC, MAXE, NCELL), 0, 2) - 1
    offsets = (distance * direction).at[:, 0, 0].set(-HC).at[:, 0, 1].set(HC)
    return offsets.astype(jnp.int32)


def draw_polygon_side_total(key, part):
    counts = jax.random.randint(key, (N_SEC, NCELL), 5, MAXE + 1)
    counts = counts.at[:, 0].set(MAXE).at[:, 1].set(5)
    return counts.astype(jnp.int32)


def shard_levels(rng, dims, pieces, smallest, largest):
    gain, own = 1.0, jax.random.fold_in(rng, 6)
    for dim, parts in pieces:
        steps = jnp.exp(jax.random.uniform(jax.random.fold_in(own, dim), (parts,), jnp.float32, smallest / len(pieces), largest / len(pieces)))
        gain = gain * jnp.repeat(steps, dims[dim] // parts).reshape([-1 if axis == dim else 1 for axis in range(len(dims))])
    return gain


def gaussian(key, extent, spread, limit, pieces=(), held_as=jnp.bfloat16):
    entries = jax.random.normal(key, extent, jnp.float32) * spread
    if len(pieces) > 0:
        entries = shard_levels(key, extent, pieces, -0.22, 0.18) * entries
    return jnp.clip(entries, min=-limit, max=limit).astype(held_as)


def setup_inputs(seed: int = 0) -> dict:
    key_of = jax.random.split(jax.random.key(seed), 14)
    return {
        "climate_field_table": gaussian(key_of[0], (N_SEC, LATTICE_COLUMNS, ROWS, LATTICE_LINES), 1.0, 6.0, ((0, 8), (1, 4)), jnp.float32),
        "zonal_wind_speed": gaussian(key_of[1], (N_SEC, LATTICE_COLUMNS, LEV_A, LATTICE_LINES), 1.0, 6.0, ((0, 8), (1, 4)), jnp.float32),
        "meridional_wind": gaussian(key_of[2], (N_SEC, LATTICE_COLUMNS, LEV_A, LATTICE_LINES), 1.0, 6.0, ((0, 8), (1, 4)), jnp.float32),
        "sea_warmth_field": gaussian(key_of[3], (N_SEC, LATTICE_COLUMNS, LATTICE_LINES), 1.0, 6.0, ((0, 8), (1, 4)), jnp.float32),
        "exchange_law_factor": gaussian(key_of[4], (NFLUX, NF + 1), (NF + 1) ** -0.5, 1.75, (), jnp.float32),
        "regrid_matrix_stack": gaussian(key_of[5], (N_SEC, N_RANK, K, HOLDER_POLYGONS, XD, LATTICE_LINES), (XD * LATTICE_LINES) ** -0.5, 0.1875, ((0, 8), (1, 4))),
        "entry_sender_patch": draw_entry_sender_patch(jax.random.fold_in(key_of[13], 71), 0),
        "holder_live_total": draw_holder_live_total(jax.random.fold_in(key_of[13], 71), 0),
        "marine_salinity_heat": gaussian(key_of[8], (N_SEC, 2, LEV_O, NCELL), 1.0, 6.0, ((0, 8), (3, 4)), jnp.float32),
        "adjacent_offset_lists": draw_adjacent_offset_lists(jax.random.fold_in(key_of[13], 71), 0),
        "polygon_side_total": draw_polygon_side_total(jax.random.fold_in(key_of[13], 71), 0),
        "interface_mixing_factor": jnp.clip(jnp.exp(math.log(2.0) - 1.3862944 * jax.random.uniform(key_of[11], (N_SEC, MAXE, NCELL), jnp.float32) ** shard_levels(key_of[11], (N_SEC, MAXE, NCELL), ((0, 8), (2, 4)), -0.2, 0.2)), 0.5, 2.0),
        "solute_forcing_factor": gaussian(key_of[12], (2, NFLUX), NFLUX ** -0.5, 3.0, (), jnp.float32),
    }


step_atmos = 0.05
diffusivity = 0.05
step_ocean = 0.5

def gll_matrix():
    gll_nodes = np.array([-1.0, -1.0 / np.sqrt(5.0), 1.0 / np.sqrt(5.0), 1.0])
    legendre = (5.0 * gll_nodes ** 3 - 3.0 * gll_nodes) / 2.0
    matrix = np.zeros((4, 4))
    for row_index in range(4):
        for col_index in range(4):
            if row_index != col_index:
                matrix[row_index, col_index] = legendre[row_index] / (legendre[col_index] * (gll_nodes[row_index] - gll_nodes[col_index]))
    matrix[0, 0] = -3.0
    matrix[3, 3] = 3.0
    return jnp.asarray(matrix, jnp.float32)

def surface_flux(field_state, zonal_part, meridional, sea_field, exchange_law_factor):
    x_points, row_count, y_points = field_state.shape
    field_count = exchange_law_factor.shape[1] - 1
    bottom = field_state.reshape(x_points, field_count, row_count // field_count, y_points)[:, :, 0]
    wind_speed = jnp.sqrt(1.0 + zonal_part[:, 0] ** 2 + meridional[:, 0] ** 2)
    combined = jnp.einsum('nf,xfy->xny', exchange_law_factor[:, :field_count], bottom, precision=lax.Precision.HIGHEST)
    combined = combined + exchange_law_factor[:, field_count][None, :, None] * sea_field[:, None, :]
    return (wind_speed[:, None, :] * combined).astype(jnp.bfloat16)

def tendency(field_state, zonal_part, meridional):
    derivative = gll_matrix()
    x_points, row_count, y_points = field_state.shape
    blocks_x = field_state.reshape(x_points // 4, 4, row_count, y_points)
    along_x = jnp.einsum('ia,eary->eiry', derivative, blocks_x, precision=lax.Precision.HIGHEST).reshape(field_state.shape)
    blocks_y = field_state.reshape(x_points, row_count, y_points // 4, 4)
    along_y = jnp.einsum('jb,xreb->xrej', derivative, blocks_y, precision=lax.Precision.HIGHEST).reshape(field_state.shape)
    levels = zonal_part.shape[1]
    fields = row_count // levels
    zonal_rows = jnp.broadcast_to(zonal_part[:, None], (x_points, fields, levels, y_points)).reshape(field_state.shape)
    meridional_rows = jnp.broadcast_to(meridional[:, None], (x_points, fields, levels, y_points)).reshape(field_state.shape)
    return -(zonal_rows * along_x + meridional_rows * along_y)

def smooth_y(tendency_field):
    x_points, row_count, y_points = tendency_field.shape
    blocks = tendency_field.reshape(x_points, row_count, y_points // 4, 4)
    average = 0.5 * (blocks[:, :, :-1, 3] + blocks[:, :, 1:, 0])
    blocks = blocks.at[:, :, :-1, 3].set(average).at[:, :, 1:, 0].set(average)
    return blocks.reshape(tendency_field.shape)

def smooth_x(tendency_field):
    x_points, row_count, y_points = tendency_field.shape
    blocks = tendency_field.reshape(x_points // 4, 4, row_count, y_points)
    average = 0.5 * (blocks[:, 3] + jnp.roll(blocks[:, 0], -1, axis=0))
    blocks = blocks.at[:, 3].set(average).at[:, 0].set(jnp.roll(average, 1, axis=0))
    return blocks.reshape(tendency_field.shape)

def finish_ocean(flattened, diffusion, ocean_flux, solute_forcing_factor):
    levels = flattened.shape[0] // 2
    cell_count = flattened.shape[1]
    forcing = jnp.einsum('tn,nc->tc', solute_forcing_factor, ocean_flux, precision=lax.Precision.HIGHEST)
    profile = jnp.exp(-jnp.arange(levels, dtype=jnp.float32) / 2.0)
    tracers = flattened.reshape(2, levels, cell_count) + diffusivity * diffusion.reshape(2, levels, cell_count)
    return tracers + step_ocean * profile[None, :, None] * forcing[:, None, :]

def reference(climate_field_table, zonal_wind_speed, meridional_wind, sea_warmth_field, exchange_law_factor, regrid_matrix_stack, entry_sender_patch, holder_live_total, marine_salinity_heat, adjacent_offset_lists, polygon_side_total, interface_mixing_factor, solute_forcing_factor):

    def patch_exchange_amounts(packed):
        return surface_flux(packed[0], packed[1], packed[2], packed[3], exchange_law_factor)
    interface_exchanges = lax.map(patch_exchange_amounts, (climate_field_table[:CLIMATE_PATCHES], zonal_wind_speed[:CLIMATE_PATCHES], meridional_wind[:CLIMATE_PATCHES], sea_warmth_field[:CLIMATE_PATCHES]))

    def air_section(packed):
        smoothed = smooth_x(smooth_y(tendency(packed[0], packed[1], packed[2])))
        return packed[0] + step_atmos * smoothed
    air_part = lax.map(air_section, (climate_field_table[:CLIMATE_PATCHES], zonal_wind_speed[:CLIMATE_PATCHES], meridional_wind[:CLIMATE_PATCHES]))
    climate_fields_later = jnp.concatenate([air_part, jnp.zeros((MARINE_PATCHES, LATTICE_COLUMNS, ROWS, LATTICE_LINES), jnp.float32)], axis=0)
    ocean_weights = regrid_matrix_stack[CLIMATE_PATCHES:]

    def remap_rank(worker_position):
        weights = lax.dynamic_index_in_dim(ocean_weights, worker_position, 1, keepdims=False).astype(jnp.float32)
        blocks = lax.dynamic_slice_in_dim(interface_exchanges, (worker_position * XD).astype(jnp.int32), XD, 1)
        sources = lax.dynamic_index_in_dim(entry_sender_patch, worker_position, 1, keepdims=False)
        counts = lax.dynamic_index_in_dim(holder_live_total, worker_position, 1, keepdims=False)
        picked = jnp.take(blocks, sources.reshape(-1), axis=0).reshape(MARINE_PATCHES, K, XD, NFLUX, LATTICE_LINES).astype(jnp.float32)
        products = jnp.einsum('okcxy,okxny->oknc', weights, picked, precision=lax.Precision.HIGHEST)
        live_slots = jnp.arange(K, dtype=jnp.int32)[None, :] < counts[:, None]
        return lax.optimization_barrier(jnp.sum(jnp.where(live_slots[:, :, None, None], products, 0.0), axis=1))
    per_rank = lax.map(remap_rank, jnp.arange(N_RANK, dtype=jnp.int32))
    ocean_flux = per_rank.transpose(1, 2, 0, 3).reshape(MARINE_PATCHES, NFLUX, NCELL)

    def ocean_section(packed):
        flattened = packed[0].reshape(2 * LEV_O, NCELL)
        offsets = packed[1]
        counts = packed[2]
        coefficients = packed[3]
        diffusion = jnp.zeros_like(flattened)
        for edge_slot in range(MAXE):
            neighbour = jnp.take(flattened, (jnp.arange(NCELL, dtype=jnp.int32) + offsets[edge_slot]) % NCELL, axis=1)
            weight = jnp.where(edge_slot < counts, coefficients[edge_slot], 0.0)
            diffusion = diffusion + weight[None, :] * (neighbour - flattened)
        return finish_ocean(flattened, diffusion, packed[4], solute_forcing_factor)
    marine_share = jax.vmap(ocean_section)((marine_salinity_heat[CLIMATE_PATCHES:], adjacent_offset_lists[CLIMATE_PATCHES:], polygon_side_total[CLIMATE_PATCHES:], interface_mixing_factor[CLIMATE_PATCHES:], ocean_flux))
    marine_tracers_later = jnp.concatenate([jnp.zeros((CLIMATE_PATCHES, 2, LEV_O, NCELL), jnp.float32), marine_share], axis=0)
    topmost_warmth = marine_share[:, 0, 0, :].astype(jnp.bfloat16)

    def return_rank(worker_position):
        weights = lax.dynamic_index_in_dim(ocean_weights, worker_position, 1, keepdims=False).astype(jnp.float32)
        sources = lax.dynamic_index_in_dim(entry_sender_patch, worker_position, 1, keepdims=False)
        counts = lax.dynamic_index_in_dim(holder_live_total, worker_position, 1, keepdims=False)
        polygon_amounts = lax.dynamic_slice_in_dim(topmost_warmth, (worker_position * HOLDER_POLYGONS).astype(jnp.int32), HOLDER_POLYGONS, 1).astype(jnp.float32)
        returned = jnp.einsum('oc,okcxy->okxy', polygon_amounts, weights, precision=lax.Precision.HIGHEST)
        live_slots = jnp.arange(K, dtype=jnp.int32)[None, :] < counts[:, None]
        targets = (live_slots[:, :, None] & (sources[:, :, None] == jnp.arange(CLIMATE_PATCHES, dtype=jnp.int32)[None, None, :])).astype(jnp.float32)
        return jnp.einsum('oks,okxy->sxy', targets, returned, precision=lax.Precision.HIGHEST)
    back_rank = lax.map(return_rank, jnp.arange(N_RANK, dtype=jnp.int32))
    incoming_share = back_rank.transpose(1, 0, 2, 3).reshape(CLIMATE_PATCHES, LATTICE_COLUMNS, LATTICE_LINES)
    warmth_regridded = jnp.concatenate([incoming_share, jnp.zeros((MARINE_PATCHES, LATTICE_COLUMNS, LATTICE_LINES), jnp.float32)], axis=0)
    return (climate_fields_later, marine_tracers_later, warmth_regridded)
```

```python
import functools

import jax
import jax.numpy as jnp
import numpy as np
from jax import lax
from jax.experimental import pallas as pl
from jax.experimental.pallas import tpu as pltpu
from jax.sharding import PartitionSpec as P

STEP_ATMOS = 0.05
DIFFUSIVITY = 0.05
STEP_OCEAN = 0.5
NODES = 4

VMEM = pl.BlockSpec(memory_space=pltpu.VMEM)
ANY = pl.BlockSpec(memory_space=pl.ANY)
SMEM = pl.BlockSpec(memory_space=pltpu.SMEM)
HIGHEST = lax.Precision.HIGHEST


def gll_matrix():
    nodes = np.array([-1.0, -1.0 / np.sqrt(5.0), 1.0 / np.sqrt(5.0), 1.0])
    legendre = (5.0 * nodes**3 - 3.0 * nodes) / 2.0
    matrix = np.zeros((4, 4))
    for i in range(4):
        for j in range(4):
            if i != j:
                matrix[i, j] = legendre[i] / (legendre[j] * (nodes[i] - nodes[j]))
    matrix[0, 0] = -3.0
    matrix[3, 3] = 3.0
    return matrix.astype(np.float32)


def in_air():
    sections = lax.axis_size("sec")
    return lax.axis_index("sec") < sections - sections // 4


def ocean_of():
    sections = lax.axis_size("sec")
    return jnp.maximum(lax.axis_index("sec") - (sections - sections // 4), 0)


def flux_kernel(levels, rows, law, field, zonal, meridional, sea, sent):
    flux_count, columns = law.shape
    x_points = sea.shape[1]
    u = zonal[pl.ds(0, x_points, stride=levels), :]
    v = meridional[pl.ds(0, x_points, stride=levels), :]
    speed = jnp.sqrt(1.0 + u * u + v * v)
    surface = [
        field[pl.ds(f * levels, x_points, stride=rows), :] for f in range(columns - 1)
    ] + [sea[0]]
    parts = []
    for n in range(flux_count):
        total = law[n, 0] * surface[0]
        for f in range(1, columns):
            total = total + law[n, f] * surface[f]
        parts.append(speed * total)
    packed = jnp.concatenate(parts, axis=0).astype(jnp.bfloat16)
    for s in range(sent.shape[0]):
        sent[s] = packed


def smooth_lines(value, lane):
    width = value.shape[-1]
    right = pltpu.roll(value, width - 1, value.ndim - 1)
    left = pltpu.roll(value, 1, value.ndim - 1)
    at_end = (lane % NODES == NODES - 1) & (lane < width - 1)
    at_start = (lane % NODES == 0) & (lane > 0)
    partner = jnp.where(at_end, right, jnp.where(at_start, left, value))
    return 0.5 * (value + partner)


def edge_kernel(levels, rows, field, zonal, meridional, along, tracers, first, last, own):
    x_points = field.shape[0] // rows
    d = gll_matrix()

    @pl.when(in_air())
    def _():
        lane = lax.broadcasted_iota(jnp.int32, (levels, field.shape[1]), 1)
        for side, (x, sent) in enumerate(((0, first), (x_points - 1, last))):
            start = x - x % NODES
            along_y = jnp.dot(
                field[pl.ds(x * rows, rows), :],
                along[...],
                precision=HIGHEST,
                preferred_element_type=jnp.float32,
            )
            u = zonal[pl.ds(x * levels, levels), :]
            v = meridional[pl.ds(x * levels, levels), :]
            for f in range(rows // levels):
                at = f * levels
                along_x = sum(
                    float(d[x % NODES, a]) * field[pl.ds((start + a) * rows + at, levels), :]
                    for a in range(NODES)
                    if d[x % NODES, a] != 0
                )
                value = -(u * along_x + v * along_y[at : at + levels])
                value = smooth_lines(value, lane)
                own[side, pl.ds(at, levels), :] = value
                sent[pl.ds(at, levels), :] = value.astype(jnp.bfloat16)

    @pl.when(jnp.logical_not(in_air()))
    def _():
        value = tracers[...]
        high = value.astype(jnp.bfloat16)
        low = (value - high.astype(jnp.float32)).astype(jnp.bfloat16)
        both = jnp.concatenate([high, low], axis=0)
        for sent in (first, last):
            sent[...] = jnp.zeros(sent.shape, sent.dtype)
            sent[pl.ds(0, both.shape[0]), :] = both


def inner_kernel(
    levels, rows, field, zonal, meridional, along, offsets, sides, mixing, later, weights, scratch
):
    x_points = field.shape[0] // rows
    d = gll_matrix()

    @pl.when(in_air())
    def _():
        lane = lax.broadcasted_iota(jnp.int32, (levels, field.shape[1]), 1)
        inner = pl.ds(rows, (x_points - 2) * rows)
        scratch[inner, :] = jnp.dot(
            field[inner, :], along[...], precision=HIGHEST, preferred_element_type=jnp.float32
        )
        for f in range(rows // levels):
            at = f * levels
            values = {}
            q = [field[pl.ds(x * rows + at, levels), :] for x in range(x_points)]
            for x in range(1, x_points - 1):
                start = x - x % NODES
                along_x = sum(
                    float(d[x % NODES, a]) * q[start + a]
                    for a in range(NODES)
                    if d[x % NODES, a] != 0
                )
                u = zonal[pl.ds(x * levels, levels), :]
                v = meridional[pl.ds(x * levels, levels), :]
                value = -(u * along_x + v * scratch[pl.ds(x * rows + at, levels), :])
                values[x] = smooth_lines(value, lane)
            for x in range(NODES - 1, x_points - 1, NODES):
                values[x] = values[x + 1] = 0.5 * (values[x] + values[x + 1])
            for x in range(1, x_points - 1):
                later[pl.ds(x * rows + at, levels), :] = q[x] + STEP_ATMOS * values[x]

    @pl.when(jnp.logical_not(in_air()))
    def _():
        later[...] = jnp.zeros(later.shape, later.dtype)
        cells = sides.shape[1]
        source = lax.broadcasted_iota(jnp.int32, (cells, cells), 0)
        target = lax.broadcasted_iota(jnp.int32, (cells, cells), 1)
        inside = jnp.zeros((cells, cells), jnp.float32)
        outside = jnp.zeros((cells, cells), jnp.float32)
        total = jnp.zeros((1, cells), jnp.float32)
        for e in range(offsets.shape[0]):
            weight = jnp.where(e < sides[...], mixing[e], 0.0)
            place = target[:1] + offsets[e]
            total = total + weight
            inside = inside + jnp.where(source == place, weight, 0.0)
            hit = (source == place - cells) | (source == place + cells)
            outside = outside + jnp.where(hit, weight, 0.0)
        inside = inside - jnp.where(source == target, total, 0.0)
        weights[pl.ds(0, cells), :] = inside
        weights[pl.ds(cells, cells), :] = outside


def exchange_kernel(
    levels,
    rows,
    senders,
    live,
    forcing_factor,
    regrid,
    groups,
    arrived,
    tracers,
    weights,
    field,
    own,
    below,
    above,
    later_in,
    later,
    tracers_later,
    portions,
    edges,
    sems,
):
    x_points = field.shape[0] // rows

    @pl.when(in_air())
    def _():
        tracers_later[...] = jnp.zeros(tracers_later.shape, jnp.float32)
        for side, (x, halo) in enumerate(((0, below), (x_points - 1, above))):
            for f in range(rows // levels):
                at = pl.ds(f * levels, levels)
                value = own[side, at, :] + halo[at, :].astype(jnp.float32)
                place = pl.ds(x * rows + f * levels, levels)
                edges[side, at, :] = field[place, :] + (0.5 * STEP_ATMOS) * value
        copies = [
            pltpu.make_async_copy(
                edges.at[side], later.at[pl.ds(x * rows, rows), :], sems.at[side]
            )
            for side, x in enumerate((0, x_points - 1))
        ]
        for copy in copies:
            copy.start()
        for copy in copies:
            copy.wait()

    @pl.when(jnp.logical_not(in_air()))
    def _():
        ocean = ocean_of()
        count = live[0, ocean]
        slots = senders.shape[2]
        cells = tracers.shape[1]
        points = groups.shape[0]
        packed = arrived.shape[1]
        x_count = points // cells
        flux_count = packed // x_count

        matched = jnp.zeros((packed, points), jnp.float32)
        for k in range(slots):
            part = arrived[senders[ocean, 0, k]]
            product = lax.dot_general(
                part,
                regrid[pl.ds(k * points, points), :],
                (((1,), (1,)), ((), ())),
                preferred_element_type=jnp.float32,
            )
            matched = matched + jnp.where(k < count, product, 0.0)
        row = lax.broadcasted_iota(jnp.int32, matched.shape, 0) % x_count
        column = lax.broadcasted_iota(jnp.int32, matched.shape, 1) % x_count
        matched = jnp.where(row == column, matched, 0.0)
        summed = matched.reshape(flux_count, x_count, points).sum(axis=1)
        high = summed.astype(jnp.bfloat16)
        low = (summed - high.astype(jnp.float32)).astype(jnp.bfloat16)
        ocean_flux = jnp.dot(high, groups[...], preferred_element_type=jnp.float32) + jnp.dot(
            low, groups[...], preferred_element_type=jnp.float32
        )

        value = tracers[...]
        depth = value.shape[0] // forcing_factor.shape[0]
        cell = lax.broadcasted_iota(jnp.int32, value.shape, 1)
        both = [
            h[pl.ds(0, value.shape[0]), :].astype(jnp.float32)
            + h[pl.ds(value.shape[0], value.shape[0]), :].astype(jnp.float32)
            for h in (below, above)
        ]
        outer = jnp.where(cell < cells // 2, both[1], both[0])
        change = jnp.dot(
            value, weights[pl.ds(0, cells), :], precision=HIGHEST, preferred_element_type=jnp.float32
        ) + jnp.dot(
            outer,
            weights[pl.ds(cells, cells), :],
            precision=HIGHEST,
            preferred_element_type=jnp.float32,
        )
        level = lax.broadcasted_iota(jnp.int32, (depth, cells), 0).astype(jnp.float32)
        profile = STEP_OCEAN * jnp.exp(-0.5 * level)
        renewed = value + DIFFUSIVITY * change
        forced = []
        for t in range(forcing_factor.shape[0]):
            total = forcing_factor[t, 0] * ocean_flux[0:1]
            for n in range(1, flux_count):
                total = total + forcing_factor[t, n] * ocean_flux[n : n + 1]
            forced.append(profile * total)
        renewed = renewed + jnp.concatenate(forced, axis=0)
        tracers_later[...] = renewed

        top = jnp.broadcast_to(renewed[0:1], (x_count, cells)).astype(jnp.bfloat16)
        spread = lax.dot_general(
            top, groups[...], (((1,), (1,)), ((), ())), preferred_element_type=jnp.float32
        )
        row = lax.broadcasted_iota(jnp.int32, spread.shape, 0)
        column = lax.broadcasted_iota(jnp.int32, spread.shape, 1) % x_count
        spread = jnp.where(row == column, spread, 0.0).astype(jnp.bfloat16)
        portions[...] = jnp.zeros(portions.shape, jnp.float32)
        for k in range(slots):
            back = jnp.dot(
                spread, regrid[pl.ds(k * points, points), :], preferred_element_type=jnp.float32
            )
            place = senders[ocean, 0, k]
            portions[place] = portions[place] + jnp.where(k < count, back, 0.0)


def per_device(
    climate_field_table,
    zonal_wind_speed,
    meridional_wind,
    sea_warmth_field,
    exchange_law_factor,
    regrid_matrix_stack,
    entry_sender_patch,
    holder_live_total,
    marine_salinity_heat,
    adjacent_offset_lists,
    polygon_side_total,
    interface_mixing_factor,
    solute_forcing_factor,
):
    sections = lax.axis_size("sec")
    ranks = lax.axis_size("rank")
    oceans = sections // 4
    _, x_points, rows, y_points = climate_field_table.shape
    levels = zonal_wind_speed.shape[2]
    flux_count = exchange_law_factor.shape[0]
    _, tracer_count, depth, cells = marine_salinity_heat.shape
    slots = regrid_matrix_stack.shape[2]
    f32, bf16 = jnp.float32, jnp.bfloat16
    shape = jax.ShapeDtypeStruct

    field = climate_field_table.reshape(x_points * rows, y_points)
    zonal = zonal_wind_speed.reshape(x_points * levels, y_points)
    meridional = meridional_wind.reshape(x_points * levels, y_points)
    regrid = regrid_matrix_stack.reshape(slots * cells * x_points, y_points)
    tracers = marine_salinity_heat.reshape(tracer_count * depth, cells)
    offsets = jnp.transpose(adjacent_offset_lists, (1, 0, 2))
    mixing = jnp.transpose(interface_mixing_factor, (1, 0, 2))
    live = jnp.transpose(holder_live_total, (1, 0))

    along = np.kron(np.eye(y_points // NODES, dtype=np.float32), gll_matrix().T)
    groups = np.kron(np.eye(cells, dtype=np.float32), np.ones((x_points, 1), np.float32))
    along = jnp.asarray(along)
    groups = jnp.asarray(groups, bf16)

    fluxes = pl.pallas_call(
        functools.partial(flux_kernel, levels, rows),
        out_shape=shape((sections, flux_count * x_points, y_points), bf16),
        in_specs=[SMEM, VMEM, VMEM, VMEM, VMEM],
        out_specs=VMEM,
        name="flux",
    )(exchange_law_factor, field, zonal, meridional, sea_warmth_field)
    arrived = lax.all_to_all(fluxes, "sec", 0, 0, tiled=True)

    first, last, own = pl.pallas_call(
        functools.partial(edge_kernel, levels, rows),
        out_shape=(
            shape((rows, y_points), bf16),
            shape((rows, y_points), bf16),
            shape((2, rows, y_points), f32),
        ),
        in_specs=[VMEM] * 5,
        out_specs=(VMEM,) * 3,
        name="edges",
    )(field, zonal, meridional, along, tracers)
    up = [(i, (i + 1) % ranks) for i in range(ranks)]
    below = lax.ppermute(last, "rank", up)
    above = lax.ppermute(first, "rank", [(j, i) for i, j in up])

    later, weights = pl.pallas_call(
        functools.partial(inner_kernel, levels, rows),
        out_shape=(shape(field.shape, f32), shape((2 * cells, cells), f32)),
        in_specs=[VMEM] * 7,
        out_specs=(VMEM,) * 2,
        scratch_shapes=[pltpu.VMEM(field.shape, f32)],
        name="inner",
    )(field, zonal, meridional, along, offsets, polygon_side_total, mixing)

    later, tracers_later, portions = pl.pallas_call(
        functools.partial(exchange_kernel, levels, rows),
        out_shape=(
            shape(field.shape, f32),
            shape(tracers.shape, f32),
            shape((sections, x_points, y_points), f32),
        ),
        in_specs=[SMEM] * 3 + [VMEM] * 9 + [ANY],
        out_specs=(ANY, VMEM, VMEM),
        scratch_shapes=[
            pltpu.VMEM((2, rows, y_points), f32),
            pltpu.SemaphoreType.DMA((2,)),
        ],
        input_output_aliases={12: 0},
        name="exchange",
    )(
        entry_sender_patch,
        live,
        solute_forcing_factor,
        regrid,
        groups,
        arrived,
        tracers,
        weights,
        field,
        own,
        below,
        above,
        later,
    )
    returned = lax.all_to_all(portions, "sec", 0, 0, tiled=True)
    warmth = jnp.sum(returned[sections - oceans :], axis=0)
    return (
        later.reshape(climate_field_table.shape),
        tracers_later.reshape(marine_salinity_heat.shape),
        warmth[None],
    )


def solution(mesh):
    return jax.shard_map(
        per_device,
        mesh=mesh,
        in_specs=(
            P("sec", "rank", None, None),
            P("sec", "rank", None, None),
            P("sec", "rank", None, None),
            P("sec", "rank", None),
            P(),
            P("sec", "rank", None, None, None, None),
            P(None, "rank", None),
            P(None, "rank"),
            P("sec", None, None, "rank"),
            P("sec", None, "rank"),
            P("sec", "rank"),
            P("sec", None, "rank"),
            P(),
        ),
        out_specs=(
            P("sec", "rank", None, None),
            P("sec", None, None, "rank"),
            P("sec", "rank", None),
        ),
        check_vma=False,
    )
```

```python
import functools

import jax
import jax.numpy as jnp
import numpy as np
from jax import lax
from jax.experimental import pallas as pl
from jax.experimental.pallas import tpu as pltpu
from jax.sharding import PartitionSpec as P

STEP_ATMOS = 0.05
DIFFUSIVITY = 0.05
STEP_OCEAN = 0.5
NODES = 4

VMEM = pl.BlockSpec(memory_space=pltpu.VMEM)
SMEM = pl.BlockSpec(memory_space=pltpu.SMEM)
PARAMS = pltpu.CompilerParams(vmem_limit_bytes=8 * 2**20)
HIGHEST = lax.Precision.HIGHEST


def gll_matrix():
    nodes = np.array([-1.0, -1.0 / np.sqrt(5.0), 1.0 / np.sqrt(5.0), 1.0])
    legendre = (5.0 * nodes**3 - 3.0 * nodes) / 2.0
    matrix = np.zeros((4, 4))
    for i in range(4):
        for j in range(4):
            if i != j:
                matrix[i, j] = legendre[i] / (legendre[j] * (nodes[i] - nodes[j]))
    matrix[0, 0] = -3.0
    matrix[3, 3] = 3.0
    return matrix.astype(np.float32)


def cost(microseconds):
    return pl.CostEstimate(
        flops=0, bytes_accessed=int(microseconds * 3_000_000), transcendentals=0
    )


def in_air():
    sections = lax.axis_size("sec")
    return lax.axis_index("sec") < sections - sections // 4


def ocean_of():
    sections = lax.axis_size("sec")
    return jnp.maximum(lax.axis_index("sec") - (sections - sections // 4), 0)


def flux_kernel(levels, rows, law, field, zonal, meridional, sea, sent):
    @pl.when(in_air())
    def _():
        flux_count, columns = law.shape
        x_points = sea.shape[1]
        u = zonal[pl.ds(0, x_points, stride=levels), :]
        v = meridional[pl.ds(0, x_points, stride=levels), :]
        speed = jnp.sqrt(1.0 + u * u + v * v)
        surface = [
            field[pl.ds(f * levels, x_points, stride=rows), :] for f in range(columns - 1)
        ] + [sea[0]]
        parts = []
        for n in range(flux_count):
            total = law[n, 0] * surface[0]
            for f in range(1, columns):
                total = total + law[n, f] * surface[f]
            parts.append(speed * total)
        sent[...] = jnp.concatenate(parts, axis=0).astype(jnp.bfloat16)


def smooth_lines(value, lane):
    width = value.shape[-1]
    right = pltpu.roll(value, width - 1, value.ndim - 1)
    left = pltpu.roll(value, 1, value.ndim - 1)
    at_end = (lane % NODES == NODES - 1) & (lane < width - 1)
    at_start = (lane % NODES == 0) & (lane > 0)
    partner = jnp.where(at_end, right, jnp.where(at_start, left, value))
    return 0.5 * (value + partner)


def edge_kernel(levels, rows, field, zonal, meridional, along, first, last, own):
    x_points = field.shape[0] // rows
    d = gll_matrix()

    @pl.when(in_air())
    def _():
        lane = lax.broadcasted_iota(jnp.int32, (levels, field.shape[1]), 1)
        for side, (x, sent) in enumerate(((0, first), (x_points - 1, last))):
            start = x - x % NODES
            along_y = jnp.dot(
                field[pl.ds(x * rows, rows), :],
                along[...],
                precision=HIGHEST,
                preferred_element_type=jnp.float32,
            )
            u = zonal[pl.ds(x * levels, levels), :]
            v = meridional[pl.ds(x * levels, levels), :]
            for f in range(rows // levels):
                at = f * levels
                along_x = sum(
                    float(d[x % NODES, a]) * field[pl.ds((start + a) * rows + at, levels), :]
                    for a in range(NODES)
                    if d[x % NODES, a] != 0
                )
                value = -(u * along_x + v * along_y[at : at + levels])
                value = smooth_lines(value, lane)
                own[side, pl.ds(at, levels), :] = value
                sent[pl.ds(at, levels), :] = value.astype(jnp.bfloat16)


def weight_kernel(offsets, sides, mixing, weights):
    @pl.when(jnp.logical_not(in_air()))
    def _():
        cells = sides.shape[1]
        source = lax.broadcasted_iota(jnp.int32, (cells, cells), 0)
        target = lax.broadcasted_iota(jnp.int32, (cells, cells), 1)
        inside = jnp.zeros((cells, cells), jnp.float32)
        outside = jnp.zeros((cells, cells), jnp.float32)
        total = jnp.zeros((1, cells), jnp.float32)
        for e in range(offsets.shape[0]):
            weight = jnp.where(e < sides[...], mixing[e], 0.0)
            place = target[:1] + offsets[e]
            total = total + weight
            inside = inside + jnp.where(source == place, weight, 0.0)
            hit = (source == place - cells) | (source == place + cells)
            outside = outside + jnp.where(hit, weight, 0.0)
        inside = inside - jnp.where(source == target, total, 0.0)
        weights[pl.ds(0, cells), :] = inside
        weights[pl.ds(cells, cells), :] = outside


def exchange_kernel(
    senders,
    live,
    forcing_factor,
    regrid,
    groups,
    tracers,
    weights,
    below,
    above,
    *rest,
):
    air = lax.axis_size("sec") - lax.axis_size("sec") // 4
    arrived, (tracers_later, *returned) = rest[:air], rest[air:]

    @pl.when(in_air())
    def _():
        tracers_later[...] = jnp.zeros(tracers_later.shape, jnp.float32)

    @pl.when(jnp.logical_not(in_air()))
    def _():
        ocean = ocean_of()
        shift = ocean * (air // (lax.axis_size("sec") // 4))
        count = live[0, ocean]
        slots = senders.shape[2]
        cells = tracers.shape[1]
        points = groups.shape[0]
        packed = arrived[0].shape[0]
        x_count = points // cells
        flux_count = packed // x_count
        turns = []
        for k in range(slots):
            turn = senders[ocean, 0, k] - shift
            turn = jnp.where(turn < 0, turn + air, turn)
            turns.append(jnp.where(k < count, turn, air))

        matched = jnp.zeros((packed, points), jnp.float32)
        for k in range(slots):
            part = jnp.zeros((packed, arrived[0].shape[1]), jnp.float32)
            for j in range(air):
                part = jnp.where(turns[k] == j, arrived[j][...].astype(jnp.float32), part)
            matched = matched + lax.dot_general(
                part.astype(jnp.bfloat16),
                regrid[pl.ds(k * points, points), :],
                (((1,), (1,)), ((), ())),
                preferred_element_type=jnp.float32,
            )
        row = lax.broadcasted_iota(jnp.int32, matched.shape, 0) % x_count
        column = lax.broadcasted_iota(jnp.int32, matched.shape, 1) % x_count
        matched = jnp.where(row == column, matched, 0.0)
        summed = matched.reshape(flux_count, x_count, points).sum(axis=1)
        high = summed.astype(jnp.bfloat16)
        low = (summed - high.astype(jnp.float32)).astype(jnp.bfloat16)
        ocean_flux = jnp.dot(high, groups[...], preferred_element_type=jnp.float32) + jnp.dot(
            low, groups[...], preferred_element_type=jnp.float32
        )

        value = tracers[...]
        depth = value.shape[0] // forcing_factor.shape[0]
        cell = lax.broadcasted_iota(jnp.int32, value.shape, 1)
        outer = jnp.where(cell < cells // 2, above[...], below[...])
        change = jnp.dot(
            value, weights[pl.ds(0, cells), :], precision=HIGHEST, preferred_element_type=jnp.float32
        ) + jnp.dot(
            outer,
            weights[pl.ds(cells, cells), :],
            precision=HIGHEST,
            preferred_element_type=jnp.float32,
        )
        level = lax.broadcasted_iota(jnp.int32, (depth, cells), 0).astype(jnp.float32)
        profile = STEP_OCEAN * jnp.exp(-0.5 * level)
        renewed = value + DIFFUSIVITY * change
        forced = []
        for t in range(forcing_factor.shape[0]):
            total = forcing_factor[t, 0] * ocean_flux[0:1]
            for n in range(1, flux_count):
                total = total + forcing_factor[t, n] * ocean_flux[n : n + 1]
            forced.append(profile * total)
        renewed = renewed + jnp.concatenate(forced, axis=0)
        tracers_later[...] = renewed

        top = jnp.broadcast_to(renewed[0:1], (x_count, cells)).astype(jnp.bfloat16)
        spread = lax.dot_general(
            top, groups[...], (((1,), (1,)), ((), ())), preferred_element_type=jnp.float32
        )
        row = lax.broadcasted_iota(jnp.int32, spread.shape, 0)
        column = lax.broadcasted_iota(jnp.int32, spread.shape, 1) % x_count
        spread = jnp.where(row == column, spread, 0.0).astype(jnp.bfloat16)
        back = [
            jnp.dot(
                spread, regrid[pl.ds(k * points, points), :], preferred_element_type=jnp.float32
            )
            for k in range(slots)
        ]
        for j in range(air):
            total = jnp.where(turns[0] == j, back[0], 0.0)
            for k in range(1, slots):
                total = total + jnp.where(turns[k] == j, back[k], 0.0)
            returned[j][...] = total


def inner_kernel(
    levels, rows, field, zonal, meridional, along, own, below, above, later, scratch
):
    x_points = field.shape[0] // rows
    d = gll_matrix()

    @pl.when(in_air())
    def _():
        lane = lax.broadcasted_iota(jnp.int32, (levels, field.shape[1]), 1)
        inner = pl.ds(rows, (x_points - 2) * rows)
        scratch[inner, :] = jnp.dot(
            field[inner, :], along[...], precision=HIGHEST, preferred_element_type=jnp.float32
        )
        for f in range(rows // levels):
            at = f * levels
            here = pl.ds(at, levels)
            values = {
                0: 0.5 * (own[0, here, :] + below[here, :].astype(jnp.float32)),
                x_points - 1: 0.5 * (own[1, here, :] + above[here, :].astype(jnp.float32)),
            }
            q = [field[pl.ds(x * rows + at, levels), :] for x in range(x_points)]
            for x in range(1, x_points - 1):
                start = x - x % NODES
                along_x = sum(
                    float(d[x % NODES, a]) * q[start + a]
                    for a in range(NODES)
                    if d[x % NODES, a] != 0
                )
                u = zonal[pl.ds(x * levels, levels), :]
                v = meridional[pl.ds(x * levels, levels), :]
                value = -(u * along_x + v * scratch[pl.ds(x * rows + at, levels), :])
                values[x] = smooth_lines(value, lane)
            for x in range(NODES - 1, x_points - 1, NODES):
                values[x] = values[x + 1] = 0.5 * (values[x] + values[x + 1])
            for x in range(x_points):
                later[pl.ds(x * rows + at, levels), :] = q[x] + STEP_ATMOS * values[x]

    @pl.when(jnp.logical_not(in_air()))
    def _():
        later[...] = jnp.zeros(later.shape, later.dtype)


def per_device(
    climate_field_table,
    zonal_wind_speed,
    meridional_wind,
    sea_warmth_field,
    exchange_law_factor,
    regrid_matrix_stack,
    entry_sender_patch,
    holder_live_total,
    marine_salinity_heat,
    adjacent_offset_lists,
    polygon_side_total,
    interface_mixing_factor,
    solute_forcing_factor,
):
    sections = lax.axis_size("sec")
    ranks = lax.axis_size("rank")
    oceans = sections // 4
    air = sections - oceans
    _, x_points, rows, y_points = climate_field_table.shape
    levels = zonal_wind_speed.shape[2]
    flux_count = exchange_law_factor.shape[0]
    _, tracer_count, depth, cells = marine_salinity_heat.shape
    slots = regrid_matrix_stack.shape[2]
    f32, bf16 = jnp.float32, jnp.bfloat16
    shape = jax.ShapeDtypeStruct

    field = climate_field_table.reshape(x_points * rows, y_points)
    zonal = zonal_wind_speed.reshape(x_points * levels, y_points)
    meridional = meridional_wind.reshape(x_points * levels, y_points)
    regrid = regrid_matrix_stack.reshape(slots * cells * x_points, y_points)
    tracers = marine_salinity_heat.reshape(tracer_count * depth, cells)
    offsets = jnp.transpose(adjacent_offset_lists, (1, 0, 2))
    mixing = jnp.transpose(interface_mixing_factor, (1, 0, 2))
    live = jnp.transpose(holder_live_total, (1, 0))

    along = np.kron(np.eye(y_points // NODES, dtype=np.float32), gll_matrix().T)
    groups = np.kron(np.eye(cells, dtype=np.float32), np.ones((x_points, 1), np.float32))
    along = jnp.asarray(along)
    groups = jnp.asarray(groups, bf16)

    up = [(i, (i + 1) % ranks) for i in range(ranks)]
    down = [(j, i) for i, j in up]
    spacing = air // oceans

    def ocean_halo(turn):
        pairs = [(s * ranks + i, s * ranks + j) for s in range(air, sections) for i, j in turn]
        return lax.ppermute(tracers, ("sec", "rank"), pairs)

    tracers_below, tracers_above = ocean_halo(up), ocean_halo(down)

    fluxes = pl.pallas_call(
        functools.partial(flux_kernel, levels, rows),
        out_shape=shape((flux_count * x_points, y_points), bf16),
        in_specs=[SMEM, VMEM, VMEM, VMEM, VMEM],
        out_specs=VMEM,
        compiler_params=PARAMS,
        cost_estimate=cost(1),
        name="flux",
    )(exchange_law_factor, field, zonal, meridional, sea_warmth_field)
    routes = [
        [((turn + o * spacing) % air, air + o) for o in range(oceans)] for turn in range(air)
    ]
    arrived = [lax.ppermute(fluxes, "sec", route) for route in routes]

    first, last, own = pl.pallas_call(
        functools.partial(edge_kernel, levels, rows),
        out_shape=(
            shape((rows, y_points), bf16),
            shape((rows, y_points), bf16),
            shape((2, rows, y_points), f32),
        ),
        in_specs=[VMEM] * 4,
        out_specs=(VMEM,) * 3,
        compiler_params=PARAMS,
        cost_estimate=cost(2),
        name="edges",
    )(field, zonal, meridional, along)

    def air_halo(value, turn):
        pairs = [(s * ranks + i, s * ranks + j) for s in range(air) for i, j in turn]
        return lax.ppermute(value, ("sec", "rank"), pairs)

    below, above = air_halo(last, up), air_halo(first, down)

    weights = pl.pallas_call(
        weight_kernel,
        out_shape=shape((2 * cells, cells), f32),
        in_specs=[VMEM] * 3,
        out_specs=VMEM,
        compiler_params=PARAMS,
        cost_estimate=cost(1),
        name="weights",
    )(offsets, polygon_side_total, mixing)

    tracers_later, *returned = pl.pallas_call(
        exchange_kernel,
        out_shape=(shape(tracers.shape, f32),)
        + (shape((x_points, y_points), f32),) * air,
        in_specs=[SMEM] * 3 + [VMEM] * (6 + air),
        out_specs=(VMEM,) * (1 + air),
        compiler_params=PARAMS,
        cost_estimate=cost(3),
        name="exchange",
    )(
        entry_sender_patch,
        live,
        solute_forcing_factor,
        regrid,
        groups,
        tracers,
        weights,
        tracers_below,
        tracers_above,
        *arrived,
    )
    warmth = sum(
        lax.ppermute(part, "sec", [(j, i) for i, j in route])
        for part, route in zip(returned, routes)
    )

    later = pl.pallas_call(
        functools.partial(inner_kernel, levels, rows),
        out_shape=shape(field.shape, f32),
        in_specs=[VMEM] * 7,
        out_specs=VMEM,
        scratch_shapes=[pltpu.VMEM(field.shape, f32)],
        compiler_params=PARAMS,
        cost_estimate=cost(4),
        name="inner",
    )(field, zonal, meridional, along, own, below, above)
    return (
        later.reshape(climate_field_table.shape),
        tracers_later.reshape(marine_salinity_heat.shape),
        warmth[None],
    )


def solution(mesh):
    return jax.shard_map(
        per_device,
        mesh=mesh,
        in_specs=(
            P("sec", "rank", None, None),
            P("sec", "rank", None, None),
            P("sec", "rank", None, None),
            P("sec", "rank", None),
            P(),
            P("sec", "rank", None, None, None, None),
            P(None, "rank", None),
            P(None, "rank"),
            P("sec", None, None, "rank"),
            P("sec", None, "rank"),
            P("sec", "rank"),
            P("sec", None, "rank"),
            P(),
        ),
        out_specs=(
            P("sec", "rank", None, None),
            P("sec", None, None, "rank"),
            P("sec", "rank", None),
        ),
        check_vma=False,
    )
```

```python
import functools

import jax
import jax.numpy as jnp
import numpy as np
from jax import lax
from jax.experimental import pallas as pl
from jax.experimental.pallas import tpu as pltpu
from jax.sharding import PartitionSpec as P

STEP_ATMOS = 0.05
DIFFUSIVITY = 0.05
STEP_OCEAN = 0.5
NODES = 4

VMEM = pl.BlockSpec(memory_space=pltpu.VMEM)
ANY = pl.BlockSpec(memory_space=pl.ANY)
HBM = pl.BlockSpec(memory_space=pltpu.HBM)
SMEM = pl.BlockSpec(memory_space=pltpu.SMEM)
PARAMS = pltpu.CompilerParams(vmem_limit_bytes=8 * 2**20)
HIGHEST = lax.Precision.HIGHEST


def gll_matrix():
    nodes = np.array([-1.0, -1.0 / np.sqrt(5.0), 1.0 / np.sqrt(5.0), 1.0])
    legendre = (5.0 * nodes**3 - 3.0 * nodes) / 2.0
    matrix = np.zeros((4, 4))
    for i in range(4):
        for j in range(4):
            if i != j:
                matrix[i, j] = legendre[i] / (legendre[j] * (nodes[i] - nodes[j]))
    matrix[0, 0] = -3.0
    matrix[3, 3] = 3.0
    return matrix.astype(np.float32)


def cost(microseconds):
    return pl.CostEstimate(
        flops=0, bytes_accessed=int(microseconds * 3_000_000), transcendentals=0
    )


def in_air():
    sections = lax.axis_size("sec")
    return lax.axis_index("sec") < sections - sections // 4


def ocean_of():
    sections = lax.axis_size("sec")
    return jnp.maximum(lax.axis_index("sec") - (sections - sections // 4), 0)


def flux_kernel(
    levels, rows, law_in, field_in, zonal_in, meridional_in, sea_in, sent, law, field, u, v, sea, sems
):
    flux_count, columns = law.shape
    x_points = sea.shape[1]

    @pl.when(in_air())
    def _():
        lowest = pl.ds(0, u.shape[1])
        copies = [
            pltpu.make_async_copy(source, target, sems.at[i])
            for i, (source, target) in enumerate(
                (
                    (field_in.at[:, :, lowest, :], field),
                    (zonal_in.at[:, lowest, :], u),
                    (meridional_in.at[:, lowest, :], v),
                    (sea_in, sea),
                    (law_in, law),
                )
            )
        ]
        for copy in copies:
            copy.start()
        for copy in copies:
            copy.wait()
        ground = [field[:, f, 0, :] for f in range(columns - 1)] + [sea[0]]
        wind = u[:, 0, :] ** 2 + v[:, 0, :] ** 2
        speed = jnp.sqrt(1.0 + wind)
        parts = []
        for n in range(flux_count):
            total = law[n, 0] * ground[0]
            for f in range(1, columns):
                total = total + law[n, f] * ground[f]
            parts.append(speed * total)
        packed = jnp.concatenate(parts, axis=0).astype(jnp.bfloat16)
        for s in range(sent.shape[0]):
            sent[s] = packed


def smooth_lines(value, lane):
    width = value.shape[-1]
    right = pltpu.roll(value, width - 1, value.ndim - 1)
    left = pltpu.roll(value, 1, value.ndim - 1)
    at_end = (lane % NODES == NODES - 1) & (lane < width - 1)
    at_start = (lane % NODES == 0) & (lane > 0)
    partner = jnp.where(at_end, right, jnp.where(at_start, left, value))
    return 0.5 * (value + partner)


def edge_kernel(levels, rows, field, zonal, meridional, along, tracers, after, first, last, own):
    x_points = field.shape[0] // rows
    d = gll_matrix()

    @pl.when(in_air())
    def _():
        lane = lax.broadcasted_iota(jnp.int32, (levels, field.shape[1]), 1)
        for side, (x, sent) in enumerate(((0, first), (x_points - 1, last))):
            start = x - x % NODES
            along_y = jnp.dot(
                field[pl.ds(x * rows, rows), :],
                along[...],
                precision=HIGHEST,
                preferred_element_type=jnp.float32,
            )
            u = zonal[pl.ds(x * levels, levels), :]
            v = meridional[pl.ds(x * levels, levels), :]
            for f in range(rows // levels):
                at = f * levels
                along_x = sum(
                    float(d[x % NODES, a]) * field[pl.ds((start + a) * rows + at, levels), :]
                    for a in range(NODES)
                    if d[x % NODES, a] != 0
                )
                value = -(u * along_x + v * along_y[at : at + levels])
                value = smooth_lines(value, lane)
                own[side, pl.ds(at, levels), :] = value
                sent[pl.ds(at, levels), :] = value.astype(jnp.bfloat16)

    @pl.when(jnp.logical_not(in_air()))
    def _():
        value = tracers[...]
        high = value.astype(jnp.bfloat16)
        low = (value - high.astype(jnp.float32)).astype(jnp.bfloat16)
        both = jnp.concatenate([high, low], axis=0)
        for sent in (first, last):
            sent[pl.ds(0, both.shape[0]), :] = both


def weight_kernel(offsets, sides, mixing, weights):
    @pl.when(jnp.logical_not(in_air()))
    def _():
        cells = sides.shape[1]
        source = lax.broadcasted_iota(jnp.int32, (cells, cells), 0)
        target = lax.broadcasted_iota(jnp.int32, (cells, cells), 1)
        inside = jnp.zeros((cells, cells), jnp.float32)
        outside = jnp.zeros((cells, cells), jnp.float32)
        total = jnp.zeros((1, cells), jnp.float32)
        for e in range(offsets.shape[0]):
            weight = jnp.where(e < sides[...], mixing[e], 0.0)
            place = target[:1] + offsets[e]
            total = total + weight
            inside = inside + jnp.where(source == place, weight, 0.0)
            hit = (source == place - cells) | (source == place + cells)
            outside = outside + jnp.where(hit, weight, 0.0)
        inside = inside - jnp.where(source == target, total, 0.0)
        weights[pl.ds(0, cells), :] = inside
        weights[pl.ds(cells, cells), :] = outside


def air_step(levels, rows, field, zonal, meridional, along, own, below, above, later, slopes, held, sems):
    x_points = field.shape[0] // rows
    d = gll_matrix()
    lane = lax.broadcasted_iota(jnp.int32, (levels, field.shape[1]), 1)
    inner = pl.ds(rows, (x_points - 2) * rows)
    slopes[inner, :] = jnp.dot(
        field[inner, :], along[...], precision=HIGHEST, preferred_element_type=jnp.float32
    )
    copies = []
    for f in range(rows // levels):
        at = f * levels
        here = pl.ds(at, levels)
        values = {
            0: 0.5 * (own[0, here, :] + below[here, :].astype(jnp.float32)),
            x_points - 1: 0.5 * (own[1, here, :] + above[here, :].astype(jnp.float32)),
        }
        q = [field[pl.ds(x * rows + at, levels), :] for x in range(x_points)]
        for x in range(1, x_points - 1):
            start = x - x % NODES
            along_x = sum(
                float(d[x % NODES, a]) * q[start + a]
                for a in range(NODES)
                if d[x % NODES, a] != 0
            )
            u = zonal[pl.ds(x * levels, levels), :]
            v = meridional[pl.ds(x * levels, levels), :]
            value = -(u * along_x + v * slopes[pl.ds(x * rows + at, levels), :])
            values[x] = smooth_lines(value, lane)
        for x in range(NODES - 1, x_points - 1, NODES):
            values[x] = values[x + 1] = 0.5 * (values[x] + values[x + 1])
        for x in range(x_points):
            held[x, here, :] = q[x] + STEP_ATMOS * values[x]
        copy = pltpu.make_async_copy(held.at[:, here, :], later.at[:, here, :], sems.at[f])
        copy.start()
        copies.append(copy)
    for copy in copies:
        copy.wait()


def ocean_step(
    senders,
    live,
    forcing_factor,
    regrid,
    groups,
    arrived,
    tracers,
    weights,
    below,
    above,
    tracers_later,
    portions,
):
    ocean = ocean_of()
    count = live[0, ocean]
    slots = senders.shape[2]
    cells = tracers.shape[1]
    points = groups.shape[0]
    packed = arrived.shape[1]
    x_count = points // cells
    flux_count = packed // x_count

    value = tracers[...]
    height = value.shape[0]
    depth = height // forcing_factor.shape[0]
    cell = lax.broadcasted_iota(jnp.int32, value.shape, 1)
    beside = [
        h[pl.ds(0, height), :].astype(jnp.float32) + h[pl.ds(height, height), :].astype(jnp.float32)
        for h in (below, above)
    ]
    outer = jnp.where(cell < cells // 2, beside[1], beside[0])
    change = jnp.dot(
        value, weights[pl.ds(0, cells), :], precision=HIGHEST, preferred_element_type=jnp.float32
    ) + jnp.dot(
        outer, weights[pl.ds(cells, cells), :], precision=HIGHEST, preferred_element_type=jnp.float32
    )
    renewed = value + DIFFUSIVITY * change

    matched = jnp.zeros((packed, points), jnp.float32)
    for k in range(slots):
        product = lax.dot_general(
            arrived[senders[ocean, 0, k]],
            regrid[pl.ds(k * points, points), :],
            (((1,), (1,)), ((), ())),
            preferred_element_type=jnp.float32,
        )
        matched = matched + jnp.where(k < count, product, 0.0)
    row = lax.broadcasted_iota(jnp.int32, matched.shape, 0) % x_count
    column = lax.broadcasted_iota(jnp.int32, matched.shape, 1) % x_count
    matched = jnp.where(row == column, matched, 0.0)
    summed = matched.reshape(flux_count, x_count, points).sum(axis=1)
    high = summed.astype(jnp.bfloat16)
    low = (summed - high.astype(jnp.float32)).astype(jnp.bfloat16)
    ocean_flux = jnp.dot(high, groups[...], preferred_element_type=jnp.float32) + jnp.dot(
        low, groups[...], preferred_element_type=jnp.float32
    )

    level = lax.broadcasted_iota(jnp.int32, (depth, cells), 0).astype(jnp.float32)
    profile = STEP_OCEAN * jnp.exp(-0.5 * level)
    forced = []
    for t in range(forcing_factor.shape[0]):
        total = forcing_factor[t, 0] * ocean_flux[0:1]
        for n in range(1, flux_count):
            total = total + forcing_factor[t, n] * ocean_flux[n : n + 1]
        forced.append(profile * total)
    renewed = renewed + jnp.concatenate(forced, axis=0)
    tracers_later[...] = renewed

    top = jnp.broadcast_to(renewed[0:1], (x_count, cells)).astype(jnp.bfloat16)
    spread = lax.dot_general(
        top, groups[...], (((1,), (1,)), ((), ())), preferred_element_type=jnp.float32
    )
    row = lax.broadcasted_iota(jnp.int32, spread.shape, 0)
    column = lax.broadcasted_iota(jnp.int32, spread.shape, 1) % x_count
    spread = jnp.where(row == column, spread, 0.0).astype(jnp.bfloat16)
    portions[...] = jnp.zeros(portions.shape, jnp.float32)
    for k in range(slots):
        back = jnp.dot(
            spread, regrid[pl.ds(k * points, points), :], preferred_element_type=jnp.float32
        )
        place = senders[ocean, 0, k]
        portions[place] = portions[place] + jnp.where(k < count, back, 0.0)


def main_kernel(
    levels,
    rows,
    senders,
    live,
    forcing_factor,
    regrid,
    groups,
    arrived,
    tracers,
    weights,
    field,
    zonal,
    meridional,
    along,
    own,
    below,
    above,
    later,
    tracers_later,
    portions,
    slopes,
    held,
    sems,
):
    @pl.when(in_air())
    def _():
        tracers_later[...] = jnp.zeros(tracers_later.shape, jnp.float32)
        air_step(
            levels, rows, field, zonal, meridional, along, own, below, above, later, slopes, held, sems
        )

    @pl.when(jnp.logical_not(in_air()))
    def _():
        held[0] = jnp.zeros(held.shape[1:], jnp.float32)
        copies = [
            pltpu.make_async_copy(held.at[0], later.at[x], sems.at[x]) for x in range(later.shape[0])
        ]
        for copy in copies:
            copy.start()
        ocean_step(
            senders,
            live,
            forcing_factor,
            regrid,
            groups,
            arrived,
            tracers,
            weights,
            below,
            above,
            tracers_later,
            portions,
        )
        for copy in copies:
            copy.wait()


def per_device(
    climate_field_table,
    zonal_wind_speed,
    meridional_wind,
    sea_warmth_field,
    exchange_law_factor,
    regrid_matrix_stack,
    entry_sender_patch,
    holder_live_total,
    marine_salinity_heat,
    adjacent_offset_lists,
    polygon_side_total,
    interface_mixing_factor,
    solute_forcing_factor,
):
    sections = lax.axis_size("sec")
    ranks = lax.axis_size("rank")
    oceans = sections // 4
    air = sections - oceans
    _, x_points, rows, y_points = climate_field_table.shape
    levels = zonal_wind_speed.shape[2]
    flux_count = exchange_law_factor.shape[0]
    _, tracer_count, depth, cells = marine_salinity_heat.shape
    slots = regrid_matrix_stack.shape[2]
    f32, bf16 = jnp.float32, jnp.bfloat16
    shape = jax.ShapeDtypeStruct

    field = climate_field_table.reshape(x_points * rows, y_points)
    zonal = zonal_wind_speed.reshape(x_points * levels, y_points)
    meridional = meridional_wind.reshape(x_points * levels, y_points)
    regrid = regrid_matrix_stack.reshape(slots * cells * x_points, y_points)
    tracers = marine_salinity_heat.reshape(tracer_count * depth, cells)
    offsets = jnp.transpose(adjacent_offset_lists, (1, 0, 2))
    mixing = jnp.transpose(interface_mixing_factor, (1, 0, 2))
    live = jnp.transpose(holder_live_total, (1, 0))

    along = np.kron(np.eye(y_points // NODES, dtype=np.float32), gll_matrix().T)
    groups = np.kron(np.eye(cells, dtype=np.float32), np.ones((x_points, 1), np.float32))
    along = jnp.asarray(along)
    groups = jnp.asarray(groups, bf16)

    fields = rows // levels
    tile = min(8, levels)
    fluxes = pl.pallas_call(
        functools.partial(flux_kernel, levels, rows),
        out_shape=shape((sections, flux_count * x_points, y_points), bf16),
        in_specs=[HBM] * 5,
        out_specs=VMEM,
        scratch_shapes=[
            pltpu.SMEM(exchange_law_factor.shape, f32),
            pltpu.VMEM((x_points, fields, tile, y_points), f32),
            pltpu.VMEM((x_points, tile, y_points), f32),
            pltpu.VMEM((x_points, tile, y_points), f32),
            pltpu.VMEM((1, x_points, y_points), f32),
            pltpu.SemaphoreType.DMA((5,)),
        ],
        cost_estimate=cost(1),
        name="flux",
    )(
        exchange_law_factor,
        climate_field_table.reshape(x_points, fields, levels, y_points),
        zonal_wind_speed[0],
        meridional_wind[0],
        sea_warmth_field,
    )
    arrived = lax.all_to_all(fluxes, "sec", 0, 0, tiled=True)

    first, last, own = pl.pallas_call(
        functools.partial(edge_kernel, levels, rows),
        out_shape=(
            shape((rows, y_points), bf16),
            shape((rows, y_points), bf16),
            shape((2, rows, y_points), f32),
        ),
        in_specs=[VMEM] * 5 + [ANY],
        out_specs=(VMEM,) * 3,
        compiler_params=PARAMS,
        cost_estimate=cost(1),
        name="edges",
    )(field, zonal, meridional, along, tracers, fluxes)
    up = [(i, (i + 1) % ranks) for i in range(ranks)]
    below = lax.ppermute(last, "rank", up)
    above = lax.ppermute(first, "rank", [(j, i) for i, j in up])

    weights = pl.pallas_call(
        weight_kernel,
        out_shape=shape((2 * cells, cells), f32),
        in_specs=[VMEM] * 3,
        out_specs=VMEM,
        compiler_params=PARAMS,
        cost_estimate=cost(1),
        name="weights",
    )(offsets, polygon_side_total, mixing)

    later, tracers_later, portions = pl.pallas_call(
        functools.partial(main_kernel, levels, rows),
        out_shape=(
            shape((x_points, rows, y_points), f32),
            shape(tracers.shape, f32),
            shape((sections, x_points, y_points), f32),
        ),
        in_specs=[SMEM] * 3 + [VMEM] * 12,
        out_specs=(HBM, VMEM, VMEM),
        scratch_shapes=[
            pltpu.VMEM(field.shape, f32),
            pltpu.VMEM((x_points, rows, y_points), f32),
            pltpu.SemaphoreType.DMA((max(fields, x_points),)),
        ],
        compiler_params=PARAMS,
        cost_estimate=cost(3),
        name="main",
    )(
        entry_sender_patch,
        live,
        solute_forcing_factor,
        regrid,
        groups,
        arrived,
        tracers,
        weights,
        field,
        zonal,
        meridional,
        along,
        own,
        below,
        above,
    )
    returned = lax.all_to_all(portions, "sec", 0, 0, tiled=True)
    warmth = jnp.sum(returned[air:], axis=0)
    return (
        later.reshape(climate_field_table.shape),
        tracers_later.reshape(marine_salinity_heat.shape),
        warmth[None],
    )


def solution(mesh):
    return jax.shard_map(
        per_device,
        mesh=mesh,
        in_specs=(
            P("sec", "rank", None, None),
            P("sec", "rank", None, None),
            P("sec", "rank", None, None),
            P("sec", "rank", None),
            P(),
            P("sec", "rank", None, None, None, None),
            P(None, "rank", None),
            P(None, "rank"),
            P("sec", None, None, "rank"),
            P("sec", None, "rank"),
            P("sec", "rank"),
            P("sec", None, "rank"),
            P(),
        ),
        out_specs=(
            P("sec", "rank", None, None),
            P("sec", None, None, "rank"),
            P("sec", "rank", None),
        ),
        check_vma=False,
    )
```

```python
import functools

import jax
import jax.numpy as jnp
import numpy as np
from jax import lax
from jax.experimental import pallas as pl
from jax.experimental.pallas import tpu as pltpu
from jax.sharding import PartitionSpec as P

STEP_ATMOS = 0.05
DIFFUSIVITY = 0.05
STEP_OCEAN = 0.5
NODES = 4

VMEM = pl.BlockSpec(memory_space=pltpu.VMEM)
ANY = pl.BlockSpec(memory_space=pl.ANY)
HBM = pl.BlockSpec(memory_space=pltpu.HBM)
SMEM = pl.BlockSpec(memory_space=pltpu.SMEM)
PARAMS = pltpu.CompilerParams(vmem_limit_bytes=8 * 2**20)
HIGHEST = lax.Precision.HIGHEST


def gll_matrix():
    nodes = np.array([-1.0, -1.0 / np.sqrt(5.0), 1.0 / np.sqrt(5.0), 1.0])
    legendre = (5.0 * nodes**3 - 3.0 * nodes) / 2.0
    matrix = np.zeros((4, 4))
    for i in range(4):
        for j in range(4):
            if i != j:
                matrix[i, j] = legendre[i] / (legendre[j] * (nodes[i] - nodes[j]))
    matrix[0, 0] = -3.0
    matrix[3, 3] = 3.0
    return matrix.astype(np.float32)


def cost(microseconds):
    return pl.CostEstimate(
        flops=0, bytes_accessed=int(microseconds * 3_000_000), transcendentals=0
    )


def in_air():
    sections = lax.axis_size("sec")
    return lax.axis_index("sec") < sections - sections // 4


def smooth_lines(value, lane):
    width = value.shape[-1]
    right = pltpu.roll(value, width - 1, value.ndim - 1)
    left = pltpu.roll(value, 1, value.ndim - 1)
    at_end = (lane % NODES == NODES - 1) & (lane < width - 1)
    at_start = (lane % NODES == 0) & (lane > 0)
    partner = jnp.where(at_end, right, jnp.where(at_start, left, value))
    return 0.5 * (value + partner)


def start_all(pairs, sems):
    copies = [
        pltpu.make_async_copy(source, target, sems.at[i])
        for i, (source, target) in enumerate(pairs)
    ]
    for copy in copies:
        copy.start()
    return copies


def first_kernel(
    levels,
    rows,
    law_in,
    field_in,
    zonal_in,
    meridional_in,
    sea_in,
    along_in,
    tracers_in,
    sent,
    first,
    last,
    own,
    law,
    field,
    zonal,
    meridional,
    sea,
    along,
    tracers,
    sems,
):
    @pl.when(in_air())
    def _():
        copies = start_all(
            (
                (law_in, law),
                (field_in, field),
                (zonal_in, zonal),
                (meridional_in, meridional),
                (sea_in, sea),
                (along_in, along),
            ),
            sems,
        )
        for copy in copies:
            copy.wait()
        flux_count, columns = law.shape
        x_points = sea.shape[1]
        u = zonal[pl.ds(0, x_points, stride=levels), :]
        v = meridional[pl.ds(0, x_points, stride=levels), :]
        speed = jnp.sqrt(1.0 + u * u + v * v)
        ground = [
            field[pl.ds(f * levels, x_points, stride=rows), :] for f in range(columns - 1)
        ] + [sea[0]]
        parts = []
        for n in range(flux_count):
            total = law[n, 0] * ground[0]
            for f in range(1, columns):
                total = total + law[n, f] * ground[f]
            parts.append(speed * total)
        packed = jnp.concatenate(parts, axis=0).astype(jnp.bfloat16)
        for s in range(sent.shape[0]):
            sent[s] = packed

        d = gll_matrix()
        lane = lax.broadcasted_iota(jnp.int32, (levels, field.shape[1]), 1)
        for side, (x, target) in enumerate(((0, first), (x_points - 1, last))):
            start = x - x % NODES
            along_y = jnp.dot(
                field[pl.ds(x * rows, rows), :],
                along[...],
                precision=HIGHEST,
                preferred_element_type=jnp.float32,
            )
            u = zonal[pl.ds(x * levels, levels), :]
            v = meridional[pl.ds(x * levels, levels), :]
            for f in range(rows // levels):
                at = f * levels
                along_x = sum(
                    float(d[x % NODES, a]) * field[pl.ds((start + a) * rows + at, levels), :]
                    for a in range(NODES)
                    if d[x % NODES, a] != 0
                )
                value = -(u * along_x + v * along_y[at : at + levels])
                value = smooth_lines(value, lane)
                own[side, pl.ds(at, levels), :] = value
                target[pl.ds(at, levels), :] = value.astype(jnp.bfloat16)

    @pl.when(jnp.logical_not(in_air()))
    def _():
        copy = pltpu.make_async_copy(tracers_in, tracers, sems.at[0])
        copy.start()
        copy.wait()
        value = tracers[...]
        high = value.astype(jnp.bfloat16)
        low = (value - high.astype(jnp.float32)).astype(jnp.bfloat16)
        both = jnp.concatenate([high, low], axis=0)
        for target in (first, last):
            target[pl.ds(0, both.shape[0]), :] = both


def weight_kernel(
    senders, live, forcing_factor, offsets, sides, mixing, weights, chosen, returning, forcing
):
    @pl.when(jnp.logical_not(in_air()))
    def _():
        cells = sides.shape[1]
        source = lax.broadcasted_iota(jnp.int32, (cells, cells), 0)
        target = lax.broadcasted_iota(jnp.int32, (cells, cells), 1)
        inside = jnp.zeros((cells, cells), jnp.float32)
        outside = jnp.zeros((cells, cells), jnp.float32)
        total = jnp.zeros((1, cells), jnp.float32)
        for e in range(offsets.shape[0]):
            weight = jnp.where(e < sides[...], mixing[e], 0.0)
            place = target[:1] + offsets[e]
            total = total + weight
            inside = inside + jnp.where(source == place, weight, 0.0)
            hit = (source == place - cells) | (source == place + cells)
            outside = outside + jnp.where(hit, weight, 0.0)
        inside = inside - jnp.where(source == target, total, 0.0)
        weights[pl.ds(0, cells), :] = inside
        weights[pl.ds(cells, cells), :] = outside

        sections = lax.axis_size("sec")
        oceans = sections // 4
        air = sections - oceans
        ocean = jnp.maximum(lax.axis_index("sec") - air, 0)
        width = chosen.shape[1]
        count = live[0, ocean]
        for k in range(senders.shape[2]):
            place = jnp.where(k < count, senders[ocean, 0, k], sections)
            section = lax.broadcasted_iota(jnp.int32, (air, width), 0)
            chosen[pl.ds(k * air, air), :] = jnp.where(section == place, 1.0, 0.0)
            turn = lax.broadcasted_iota(jnp.int32, (air, width), 0)
            block = turn % (air // oceans)
            owner = (ocean + turn // (air // oceans)) % oceans
            returning[pl.ds(k * air, air), :] = jnp.where(
                block * oceans + owner == place, 1.0, 0.0
            )
        tracer_count, flux_count = forcing_factor.shape
        depth = forcing.shape[0] // (tracer_count * flux_count)
        level = lax.broadcasted_iota(jnp.int32, (depth, width), 0).astype(jnp.float32)
        profile = STEP_OCEAN * jnp.exp(-0.5 * level)
        for n in range(flux_count):
            for t in range(tracer_count):
                forcing[pl.ds((n * tracer_count + t) * depth, depth), :] = (
                    forcing_factor[t, n] * profile
                )


def middle_kernel(
    levels,
    rows,
    field,
    zonal,
    meridional,
    along,
    own,
    below,
    above,
    tracers,
    weights,
    later,
    diffused,
    slopes,
    held,
    sems,
):
    x_points = later.shape[0]

    @pl.when(in_air())
    def _():
        d = gll_matrix()
        lane = lax.broadcasted_iota(jnp.int32, (levels, field.shape[1]), 1)
        inner = pl.ds(rows, (x_points - 2) * rows)
        slopes[inner, :] = jnp.dot(
            field[inner, :], along[...], precision=HIGHEST, preferred_element_type=jnp.float32
        )
        copies = []
        for f in range(rows // levels):
            at = f * levels
            here = pl.ds(at, levels)
            values = {
                0: 0.5 * (own[0, here, :] + below[here, :].astype(jnp.float32)),
                x_points - 1: 0.5 * (own[1, here, :] + above[here, :].astype(jnp.float32)),
            }
            q = [field[pl.ds(x * rows + at, levels), :] for x in range(x_points)]
            for x in range(1, x_points - 1):
                start = x - x % NODES
                along_x = sum(
                    float(d[x % NODES, a]) * q[start + a]
                    for a in range(NODES)
                    if d[x % NODES, a] != 0
                )
                u = zonal[pl.ds(x * levels, levels), :]
                v = meridional[pl.ds(x * levels, levels), :]
                value = -(u * along_x + v * slopes[pl.ds(x * rows + at, levels), :])
                values[x] = smooth_lines(value, lane)
            for x in range(NODES - 1, x_points - 1, NODES):
                values[x] = values[x + 1] = 0.5 * (values[x] + values[x + 1])
            for x in range(x_points):
                held[x, here, :] = q[x] + STEP_ATMOS * values[x]
            copy = pltpu.make_async_copy(held.at[:, here, :], later.at[:, here, :], sems.at[f])
            copy.start()
            copies.append(copy)
        for copy in copies:
            copy.wait()

    @pl.when(jnp.logical_not(in_air()))
    def _():
        held[0] = jnp.zeros(held.shape[1:], jnp.float32)
        copies = start_all([(held.at[0], later.at[x]) for x in range(x_points)], sems)
        value = tracers[...]
        height, cells = value.shape
        cell = lax.broadcasted_iota(jnp.int32, value.shape, 1)
        beside = [
            h[pl.ds(0, height), :].astype(jnp.float32)
            + h[pl.ds(height, height), :].astype(jnp.float32)
            for h in (below, above)
        ]
        outer = jnp.where(cell < cells // 2, beside[1], beside[0])
        both = jnp.concatenate([value, outer], axis=1)
        change = jnp.dot(
            both, weights[...], precision=HIGHEST, preferred_element_type=jnp.float32
        )
        diffused[...] = value + DIFFUSIVITY * change
        for copy in copies:
            copy.wait()


def remap_kernel(
    regrid, gather, spread, arrived, chosen, returning, forcing, diffused, renewed, *shares
):
    @pl.when(jnp.logical_not(in_air()))
    def _():
        points, cells = gather.shape
        x_count = points // cells
        slots = regrid.shape[0] // points
        air = chosen.shape[0] // slots
        packed = arrived.shape[1]
        flux_count = packed // x_count
        row = lax.broadcasted_iota(jnp.int32, (x_count, cells), 0)
        column = lax.broadcasted_iota(jnp.int32, (x_count, cells), 1)
        same = jnp.where(row == column % x_count, 1.0, 0.0)

        blocks = [arrived[s].astype(jnp.float32) for s in range(air)]
        matched = None
        for k in range(slots):
            part = chosen[pl.ds(k * air, 1), :] * blocks[0]
            for s in range(1, air):
                part = part + chosen[pl.ds(k * air + s, 1), :] * blocks[s]
            product = lax.dot_general(
                part.astype(jnp.bfloat16),
                regrid[pl.ds(k * points, points), :],
                (((1,), (1,)), ((), ())),
                preferred_element_type=jnp.float32,
            )
            matched = product if matched is None else matched + product
        matched = matched * jnp.tile(same, (flux_count, x_count))
        high = matched.astype(jnp.bfloat16)
        low = (matched - high.astype(jnp.float32)).astype(jnp.bfloat16)
        summed = jnp.dot(high, gather[...], preferred_element_type=jnp.float32) + jnp.dot(
            low, gather[...], preferred_element_type=jnp.float32
        )
        ocean_flux = summed.reshape(flux_count, x_count, cells).sum(axis=1)
        height = diffused.shape[0]
        value = diffused[...]
        for n in range(flux_count):
            value = value + forcing[pl.ds(n * height, height), :] * ocean_flux[n : n + 1]
        renewed[...] = value

        top = jnp.broadcast_to(value[0:1], (x_count, cells)).astype(jnp.bfloat16)
        wide = jnp.dot(top, spread[...], preferred_element_type=jnp.float32)
        wide = (wide * jnp.tile(same, (1, x_count))).astype(jnp.bfloat16)
        back = [
            jnp.dot(wide, regrid[pl.ds(k * points, points), :], preferred_element_type=jnp.float32)
            for k in range(slots)
        ]
        count = shares[0].shape[0]
        for m, share in enumerate(shares):
            for j in range(count):
                at = m * count + j
                total = returning[pl.ds(at, 1), :] * back[0]
                for k in range(1, slots):
                    total = total + returning[pl.ds(k * air + at, 1), :] * back[k]
                share[j] = total


def add_kernel(*refs):
    count = refs[0].shape[0]
    shares, totals = refs[:-count], refs[-count:]

    @pl.when(jnp.logical_not(in_air()))
    def _():
        for j, total in enumerate(totals):
            value = shares[0][j]
            for share in shares[1:]:
                value = value + share[j]
            total[...] = value


def last_kernel(renewed, *refs):
    returned, (tracers_later, warmth) = refs[:-2], refs[-2:]
    sections = lax.axis_size("sec")
    block = lax.axis_index("sec") // (sections // 4)

    @pl.when(in_air())
    def _():
        tracers_later[...] = jnp.zeros(tracers_later.shape, jnp.float32)

    @pl.when(jnp.logical_not(in_air()))
    def _():
        tracers_later[...] = renewed[...]
        warmth[...] = jnp.zeros(warmth.shape, jnp.float32)

    for j, part in enumerate(returned):

        @pl.when(block == j)
        def _(part=part):
            warmth[...] = part[...]


def per_device(
    climate_field_table,
    zonal_wind_speed,
    meridional_wind,
    sea_warmth_field,
    exchange_law_factor,
    regrid_matrix_stack,
    entry_sender_patch,
    holder_live_total,
    marine_salinity_heat,
    adjacent_offset_lists,
    polygon_side_total,
    interface_mixing_factor,
    solute_forcing_factor,
):
    sections = lax.axis_size("sec")
    ranks = lax.axis_size("rank")
    oceans = sections // 4
    air = sections - oceans
    _, x_points, rows, y_points = climate_field_table.shape
    levels = zonal_wind_speed.shape[2]
    flux_count = exchange_law_factor.shape[0]
    _, tracer_count, depth, cells = marine_salinity_heat.shape
    slots = regrid_matrix_stack.shape[2]
    f32, bf16 = jnp.float32, jnp.bfloat16
    shape = jax.ShapeDtypeStruct

    field = climate_field_table.reshape(x_points * rows, y_points)
    zonal = zonal_wind_speed.reshape(x_points * levels, y_points)
    meridional = meridional_wind.reshape(x_points * levels, y_points)
    regrid = regrid_matrix_stack.reshape(slots * cells * x_points, y_points)
    tracers = marine_salinity_heat.reshape(tracer_count * depth, cells)
    offsets = jnp.transpose(adjacent_offset_lists, (1, 0, 2))
    mixing = jnp.transpose(interface_mixing_factor, (1, 0, 2))
    live = jnp.transpose(holder_live_total, (1, 0))

    along = np.kron(np.eye(y_points // NODES, dtype=np.float32), gll_matrix().T)
    gather = np.kron(np.eye(cells, dtype=np.float32), np.ones((x_points, 1), np.float32))
    along = jnp.asarray(along)
    spread = jnp.asarray(gather.T, bf16)
    gather = jnp.asarray(gather, bf16)

    fields = rows // levels
    in_place = (exchange_law_factor, field, zonal, meridional, sea_warmth_field, along, tracers)
    fluxes, first, last, own = pl.pallas_call(
        functools.partial(first_kernel, levels, rows),
        out_shape=(
            shape((sections, flux_count * x_points, y_points), bf16),
            shape((rows, y_points), bf16),
            shape((rows, y_points), bf16),
            shape((2, rows, y_points), f32),
        ),
        in_specs=[HBM] * len(in_place),
        out_specs=(VMEM,) * 4,
        scratch_shapes=[pltpu.SMEM(exchange_law_factor.shape, f32)]
        + [pltpu.VMEM(a.shape, f32) for a in in_place[1:]]
        + [pltpu.SemaphoreType.DMA((len(in_place),))],
        compiler_params=PARAMS,
        cost_estimate=cost(2),
        name="first",
    )(*(pltpu.with_memory_space_constraint(a, pltpu.HBM) for a in in_place))
    up = [(i, (i + 1) % ranks) for i in range(ranks)]
    below = lax.ppermute(last, "rank", up)
    above = lax.ppermute(first, "rank", [(j, i) for i, j in up])
    arrived = lax.all_to_all(fluxes, "sec", 0, 0, tiled=True)

    weights, chosen, returning, forcing = pl.pallas_call(
        weight_kernel,
        out_shape=(
            shape((2 * cells, cells), f32),
            shape((slots * air, y_points), f32),
            shape((slots * air, y_points), f32),
            shape((flux_count * tracer_count * depth, cells), f32),
        ),
        in_specs=[SMEM] * 3 + [VMEM] * 3,
        out_specs=(VMEM,) * 4,
        compiler_params=PARAMS,
        cost_estimate=cost(1),
        name="weights",
    )(entry_sender_patch, live, solute_forcing_factor, offsets, polygon_side_total, mixing)

    later, diffused = pl.pallas_call(
        functools.partial(middle_kernel, levels, rows),
        out_shape=(shape((x_points, rows, y_points), f32), shape(tracers.shape, f32)),
        in_specs=[VMEM] * 9,
        out_specs=(HBM, VMEM),
        scratch_shapes=[
            pltpu.VMEM(field.shape, f32),
            pltpu.VMEM((x_points, rows, y_points), f32),
            pltpu.SemaphoreType.DMA((max(fields, x_points),)),
        ],
        compiler_params=PARAMS,
        cost_estimate=cost(3),
        name="middle",
    )(field, zonal, meridional, along, own, below, above, tracers, weights)

    renewed, *shares = pl.pallas_call(
        remap_kernel,
        out_shape=(shape(tracers.shape, f32),)
        + (shape((air // oceans, x_points, y_points), f32),) * oceans,
        in_specs=[VMEM] * 8,
        out_specs=(VMEM,) * (1 + oceans),
        compiler_params=PARAMS,
        cost_estimate=cost(2),
        name="remap",
    )(regrid, gather, spread, arrived, chosen, returning, forcing, diffused)

    def between(blocks, shift):
        return [
            (s, blocks[s // oceans] * oceans + (s % oceans + shift) % oceans)
            for s in range(sections)
        ]

    for m in range(1, oceans):
        shares[m] = lax.ppermute(shares[m], "sec", between((0, 1, 2, 3), m))
    totals = pl.pallas_call(
        add_kernel,
        out_shape=(shape((x_points, y_points), f32),) * (air // oceans),
        in_specs=[VMEM] * oceans,
        out_specs=(VMEM,) * (air // oceans),
        compiler_params=PARAMS,
        cost_estimate=cost(0.3),
        name="add",
    )(*shares)
    returned = [
        lax.ppermute(total, "sec", between(blocks, 0))
        for total, blocks in zip(totals, ((3, 2, 1, 0), (3, 0, 2, 1), (3, 1, 0, 2)))
    ]
    tracers_later, warmth = pl.pallas_call(
        last_kernel,
        out_shape=(shape(tracers.shape, f32), shape((x_points, y_points), f32)),
        in_specs=[VMEM] * (1 + len(returned)),
        out_specs=(VMEM,) * 2,
        compiler_params=PARAMS,
        cost_estimate=cost(0.5),
        name="last",
    )(renewed, *returned)
    return (
        later.reshape(climate_field_table.shape),
        tracers_later.reshape(marine_salinity_heat.shape),
        warmth[None],
    )


def solution(mesh):
    return jax.shard_map(
        per_device,
        mesh=mesh,
        in_specs=(
            P("sec", "rank", None, None),
            P("sec", "rank", None, None),
            P("sec", "rank", None, None),
            P("sec", "rank", None),
            P(),
            P("sec", "rank", None, None, None, None),
            P(None, "rank", None),
            P(None, "rank"),
            P("sec", None, None, "rank"),
            P("sec", None, "rank"),
            P("sec", "rank"),
            P("sec", None, "rank"),
            P(),
        ),
        out_specs=(
            P("sec", "rank", None, None),
            P("sec", None, None, "rank"),
            P("sec", "rank", None),
        ),
        check_vma=False,
    )
```

```python
import functools

import jax
import jax.numpy as jnp
import numpy as np
from jax import lax
from jax.experimental import pallas as pl
from jax.experimental.pallas import tpu as pltpu
from jax.sharding import PartitionSpec as P

STEP_ATMOS = 0.05
DIFFUSIVITY = 0.05
STEP_OCEAN = 0.5
NODES = 4

VMEM = pl.BlockSpec(memory_space=pltpu.VMEM)
ANY = pl.BlockSpec(memory_space=pl.ANY)
HBM = pl.BlockSpec(memory_space=pltpu.HBM)
SMEM = pl.BlockSpec(memory_space=pltpu.SMEM)
PARAMS = pltpu.CompilerParams(vmem_limit_bytes=8 * 2**20)
HIGHEST = lax.Precision.HIGHEST


def gll_matrix():
    nodes = np.array([-1.0, -1.0 / np.sqrt(5.0), 1.0 / np.sqrt(5.0), 1.0])
    legendre = (5.0 * nodes**3 - 3.0 * nodes) / 2.0
    matrix = np.zeros((4, 4))
    for i in range(4):
        for j in range(4):
            if i != j:
                matrix[i, j] = legendre[i] / (legendre[j] * (nodes[i] - nodes[j]))
    matrix[0, 0] = -3.0
    matrix[3, 3] = 3.0
    return matrix.astype(np.float32)


def cost(microseconds):
    return pl.CostEstimate(
        flops=0, bytes_accessed=int(microseconds * 3_000_000), transcendentals=0
    )


def in_air():
    sections = lax.axis_size("sec")
    return lax.axis_index("sec") < sections - sections // 4


def smooth_lines(value, lane):
    width = value.shape[-1]
    right = pltpu.roll(value, width - 1, value.ndim - 1)
    left = pltpu.roll(value, 1, value.ndim - 1)
    at_end = (lane % NODES == NODES - 1) & (lane < width - 1)
    at_start = (lane % NODES == 0) & (lane > 0)
    partner = jnp.where(at_end, right, jnp.where(at_start, left, value))
    return 0.5 * (value + partner)


def start_all(pairs, sems):
    copies = [
        pltpu.make_async_copy(source, target, sems.at[i])
        for i, (source, target) in enumerate(pairs)
    ]
    for copy in copies:
        copy.start()
    return copies


def first_kernel(
    levels,
    rows,
    law_in,
    field_in,
    zonal_in,
    meridional_in,
    sea_in,
    along_in,
    tracers_in,
    sent,
    first,
    last,
    own,
    law,
    field,
    zonal,
    meridional,
    sea,
    along,
    tracers,
    packed,
    sems,
):
    @pl.when(in_air())
    def _():
        copies = start_all(
            (
                (law_in, law),
                (field_in, field),
                (zonal_in, zonal),
                (meridional_in, meridional),
                (sea_in, sea),
                (along_in, along),
            ),
            sems,
        )
        for copy in copies:
            copy.wait()
        flux_count, columns = law.shape
        x_points = sea.shape[1]
        u = zonal[pl.ds(0, x_points, stride=levels), :]
        v = meridional[pl.ds(0, x_points, stride=levels), :]
        speed = jnp.sqrt(1.0 + u * u + v * v)
        ground = [
            field[pl.ds(f * levels, x_points, stride=rows), :] for f in range(columns - 1)
        ] + [sea[0]]
        parts = []
        for n in range(flux_count):
            total = law[n, 0] * ground[0]
            for f in range(1, columns):
                total = total + law[n, f] * ground[f]
            parts.append(speed * total)
        block = jnp.concatenate(parts, axis=0).astype(jnp.bfloat16)
        for s in range(packed.shape[0]):
            packed[s] = block
        leaving = pltpu.make_async_copy(packed, sent, sems.at[0])
        leaving.start()

        d = gll_matrix()
        lane = lax.broadcasted_iota(jnp.int32, (levels, field.shape[1]), 1)
        for side, (x, target) in enumerate(((0, first), (x_points - 1, last))):
            start = x - x % NODES
            along_y = jnp.dot(
                field[pl.ds(x * rows, rows), :],
                along[...],
                precision=HIGHEST,
                preferred_element_type=jnp.float32,
            )
            u = zonal[pl.ds(x * levels, levels), :]
            v = meridional[pl.ds(x * levels, levels), :]
            for f in range(rows // levels):
                at = f * levels
                along_x = sum(
                    float(d[x % NODES, a]) * field[pl.ds((start + a) * rows + at, levels), :]
                    for a in range(NODES)
                    if d[x % NODES, a] != 0
                )
                value = -(u * along_x + v * along_y[at : at + levels])
                value = smooth_lines(value, lane)
                own[side, pl.ds(at, levels), :] = value
                target[pl.ds(at, levels), :] = value.astype(jnp.bfloat16)
        leaving.wait()

    @pl.when(jnp.logical_not(in_air()))
    def _():
        copy = pltpu.make_async_copy(tracers_in, tracers, sems.at[0])
        copy.start()
        copy.wait()
        value = tracers[...]
        high = value.astype(jnp.bfloat16)
        low = (value - high.astype(jnp.float32)).astype(jnp.bfloat16)
        both = jnp.concatenate([high, low], axis=0)
        for target in (first, last):
            target[pl.ds(0, both.shape[0]), :] = both


def weight_kernel(
    senders, live, forcing_factor, offsets, sides, mixing, weights, chosen, returning, forcing
):
    @pl.when(jnp.logical_not(in_air()))
    def _():
        cells = sides.shape[1]
        source = lax.broadcasted_iota(jnp.int32, (cells, cells), 0)
        target = lax.broadcasted_iota(jnp.int32, (cells, cells), 1)
        inside = jnp.zeros((cells, cells), jnp.float32)
        outside = jnp.zeros((cells, cells), jnp.float32)
        total = jnp.zeros((1, cells), jnp.float32)
        for e in range(offsets.shape[0]):
            weight = jnp.where(e < sides[...], mixing[e], 0.0)
            place = target[:1] + offsets[e]
            total = total + weight
            inside = inside + jnp.where(source == place, weight, 0.0)
            hit = (source == place - cells) | (source == place + cells)
            outside = outside + jnp.where(hit, weight, 0.0)
        inside = inside - jnp.where(source == target, total, 0.0)
        weights[pl.ds(0, cells), :] = inside
        weights[pl.ds(cells, cells), :] = outside

        sections = lax.axis_size("sec")
        oceans = sections // 4
        air = sections - oceans
        ocean = jnp.maximum(lax.axis_index("sec") - air, 0)
        width = chosen.shape[1]
        count = live[0, ocean]
        for k in range(senders.shape[2]):
            place = jnp.where(k < count, senders[ocean, 0, k], sections)
            section = lax.broadcasted_iota(jnp.int32, (air, width), 0)
            chosen[pl.ds(k * air, air), :] = jnp.where(section == place, 1.0, 0.0)
            turn = lax.broadcasted_iota(jnp.int32, (air, width), 0)
            block = turn % (air // oceans)
            owner = (ocean + turn // (air // oceans)) % oceans
            returning[pl.ds(k * air, air), :] = jnp.where(
                block * oceans + owner == place, 1.0, 0.0
            )
        tracer_count, flux_count = forcing_factor.shape
        depth = forcing.shape[0] // (tracer_count * flux_count)
        level = lax.broadcasted_iota(jnp.int32, (depth, width), 0).astype(jnp.float32)
        profile = STEP_OCEAN * jnp.exp(-0.5 * level)
        for n in range(flux_count):
            for t in range(tracer_count):
                forcing[pl.ds((n * tracer_count + t) * depth, depth), :] = (
                    forcing_factor[t, n] * profile
                )


def middle_kernel(
    levels,
    rows,
    field,
    zonal,
    meridional,
    along,
    own,
    below,
    above,
    tracers,
    weights,
    later,
    diffused,
    slopes,
    held,
    sems,
):
    x_points = later.shape[0]

    @pl.when(in_air())
    def _():
        d = gll_matrix()
        lane = lax.broadcasted_iota(jnp.int32, (levels, field.shape[1]), 1)
        inner = pl.ds(rows, (x_points - 2) * rows)
        slopes[inner, :] = jnp.dot(
            field[inner, :], along[...], precision=HIGHEST, preferred_element_type=jnp.float32
        )
        copies = []
        for f in range(rows // levels):
            at = f * levels
            here = pl.ds(at, levels)
            values = {
                0: 0.5 * (own[0, here, :] + below[here, :].astype(jnp.float32)),
                x_points - 1: 0.5 * (own[1, here, :] + above[here, :].astype(jnp.float32)),
            }
            q = [field[pl.ds(x * rows + at, levels), :] for x in range(x_points)]
            for x in range(1, x_points - 1):
                start = x - x % NODES
                along_x = sum(
                    float(d[x % NODES, a]) * q[start + a]
                    for a in range(NODES)
                    if d[x % NODES, a] != 0
                )
                u = zonal[pl.ds(x * levels, levels), :]
                v = meridional[pl.ds(x * levels, levels), :]
                value = -(u * along_x + v * slopes[pl.ds(x * rows + at, levels), :])
                values[x] = smooth_lines(value, lane)
            for x in range(NODES - 1, x_points - 1, NODES):
                values[x] = values[x + 1] = 0.5 * (values[x] + values[x + 1])
            for x in range(x_points):
                held[x, here, :] = q[x] + STEP_ATMOS * values[x]
            copy = pltpu.make_async_copy(held.at[:, here, :], later.at[:, here, :], sems.at[f])
            copy.start()
            copies.append(copy)
        for copy in copies:
            copy.wait()

    @pl.when(jnp.logical_not(in_air()))
    def _():
        held[0] = jnp.zeros(held.shape[1:], jnp.float32)
        copies = start_all([(held.at[0], later.at[x]) for x in range(x_points)], sems)
        value = tracers[...]
        height, cells = value.shape
        cell = lax.broadcasted_iota(jnp.int32, value.shape, 1)
        beside = [
            h[pl.ds(0, height), :].astype(jnp.float32)
            + h[pl.ds(height, height), :].astype(jnp.float32)
            for h in (below, above)
        ]
        outer = jnp.where(cell < cells // 2, beside[1], beside[0])
        both = jnp.concatenate([value, outer], axis=1)
        change = jnp.dot(
            both, weights[...], precision=HIGHEST, preferred_element_type=jnp.float32
        )
        diffused[...] = value + DIFFUSIVITY * change
        for copy in copies:
            copy.wait()


def remap_kernel(
    regrid, gather, spread, arrived, chosen, returning, forcing, diffused, renewed, *shares
):
    @pl.when(jnp.logical_not(in_air()))
    def _():
        points, cells = gather.shape
        x_count = points // cells
        slots = regrid.shape[0] // points
        air = chosen.shape[0] // slots
        packed = arrived.shape[1]
        flux_count = packed // x_count
        row = lax.broadcasted_iota(jnp.int32, (x_count, cells), 0)
        column = lax.broadcasted_iota(jnp.int32, (x_count, cells), 1)
        same = jnp.where(row == column % x_count, 1.0, 0.0)

        blocks = [arrived[s].astype(jnp.float32) for s in range(air)]
        matched = None
        for k in range(slots):
            part = chosen[pl.ds(k * air, 1), :] * blocks[0]
            for s in range(1, air):
                part = part + chosen[pl.ds(k * air + s, 1), :] * blocks[s]
            product = lax.dot_general(
                part.astype(jnp.bfloat16),
                regrid[pl.ds(k * points, points), :],
                (((1,), (1,)), ((), ())),
                preferred_element_type=jnp.float32,
            )
            matched = product if matched is None else matched + product
        matched = matched * jnp.tile(same, (flux_count, x_count))
        high = matched.astype(jnp.bfloat16)
        low = (matched - high.astype(jnp.float32)).astype(jnp.bfloat16)
        summed = jnp.dot(high, gather[...], preferred_element_type=jnp.float32) + jnp.dot(
            low, gather[...], preferred_element_type=jnp.float32
        )
        ocean_flux = summed.reshape(flux_count, x_count, cells).sum(axis=1)
        height = diffused.shape[0]
        value = diffused[...]
        for n in range(flux_count):
            value = value + forcing[pl.ds(n * height, height), :] * ocean_flux[n : n + 1]
        renewed[...] = value

        top = jnp.broadcast_to(value[0:1], (x_count, cells)).astype(jnp.bfloat16)
        wide = jnp.dot(top, spread[...], preferred_element_type=jnp.float32)
        wide = (wide * jnp.tile(same, (1, x_count))).astype(jnp.bfloat16)
        back = [
            jnp.dot(wide, regrid[pl.ds(k * points, points), :], preferred_element_type=jnp.float32)
            for k in range(slots)
        ]
        count = shares[0].shape[0]
        for m, share in enumerate(shares):
            for j in range(count):
                at = m * count + j
                total = returning[pl.ds(at, 1), :] * back[0]
                for k in range(1, slots):
                    total = total + returning[pl.ds(k * air + at, 1), :] * back[k]
                share[j] = total


def add_kernel(*refs):
    count = refs[0].shape[0]
    shares, totals = refs[:-count], refs[-count:]

    @pl.when(jnp.logical_not(in_air()))
    def _():
        for j, total in enumerate(totals):
            value = shares[0][j]
            for share in shares[1:]:
                value = value + share[j]
            total[...] = value


def last_kernel(renewed, *refs):
    returned, (tracers_later, warmth) = refs[:-2], refs[-2:]
    sections = lax.axis_size("sec")
    block = lax.axis_index("sec") // (sections // 4)

    @pl.when(in_air())
    def _():
        tracers_later[...] = jnp.zeros(tracers_later.shape, jnp.float32)

    @pl.when(jnp.logical_not(in_air()))
    def _():
        tracers_later[...] = renewed[...]
        warmth[...] = jnp.zeros(warmth.shape, jnp.float32)

    for j, part in enumerate(returned):

        @pl.when(block == j)
        def _(part=part):
            warmth[...] = part[...]


def per_device(
    climate_field_table,
    zonal_wind_speed,
    meridional_wind,
    sea_warmth_field,
    exchange_law_factor,
    regrid_matrix_stack,
    entry_sender_patch,
    holder_live_total,
    marine_salinity_heat,
    adjacent_offset_lists,
    polygon_side_total,
    interface_mixing_factor,
    solute_forcing_factor,
):
    sections = lax.axis_size("sec")
    ranks = lax.axis_size("rank")
    oceans = sections // 4
    air = sections - oceans
    _, x_points, rows, y_points = climate_field_table.shape
    levels = zonal_wind_speed.shape[2]
    flux_count = exchange_law_factor.shape[0]
    _, tracer_count, depth, cells = marine_salinity_heat.shape
    slots = regrid_matrix_stack.shape[2]
    f32, bf16 = jnp.float32, jnp.bfloat16
    shape = jax.ShapeDtypeStruct

    field = climate_field_table.reshape(x_points * rows, y_points)
    zonal = zonal_wind_speed.reshape(x_points * levels, y_points)
    meridional = meridional_wind.reshape(x_points * levels, y_points)
    regrid = regrid_matrix_stack.reshape(slots * cells * x_points, y_points)
    tracers = marine_salinity_heat.reshape(tracer_count * depth, cells)
    offsets = jnp.transpose(adjacent_offset_lists, (1, 0, 2))
    mixing = jnp.transpose(interface_mixing_factor, (1, 0, 2))
    live = jnp.transpose(holder_live_total, (1, 0))

    along = np.kron(np.eye(y_points // NODES, dtype=np.float32), gll_matrix().T)
    gather = np.kron(np.eye(cells, dtype=np.float32), np.ones((x_points, 1), np.float32))
    along = jnp.asarray(along)
    spread = jnp.asarray(gather.T, bf16)
    gather = jnp.asarray(gather, bf16)

    fields = rows // levels
    in_place = (exchange_law_factor, field, zonal, meridional, sea_warmth_field, along, tracers)
    fluxes, first, last, own = pl.pallas_call(
        functools.partial(first_kernel, levels, rows),
        out_shape=(
            shape((sections, flux_count * x_points, y_points), bf16),
            shape((rows, y_points), bf16),
            shape((rows, y_points), bf16),
            shape((2, rows, y_points), f32),
        ),
        in_specs=[HBM] * len(in_place),
        out_specs=(HBM, VMEM, VMEM, VMEM),
        scratch_shapes=[pltpu.SMEM(exchange_law_factor.shape, f32)]
        + [pltpu.VMEM(a.shape, f32) for a in in_place[1:]]
        + [pltpu.VMEM((sections, flux_count * x_points, y_points), bf16)]
        + [pltpu.SemaphoreType.DMA((len(in_place),))],
        compiler_params=PARAMS,
        cost_estimate=cost(2),
        name="first",
    )(*(pltpu.with_memory_space_constraint(a, pltpu.HBM) for a in in_place))
    up = [(i, (i + 1) % ranks) for i in range(ranks)]
    below = lax.ppermute(last, "rank", up)
    above = lax.ppermute(first, "rank", [(j, i) for i, j in up])
    arrived = lax.all_to_all(fluxes, "sec", 0, 0, tiled=True)

    weights, chosen, returning, forcing = pl.pallas_call(
        weight_kernel,
        out_shape=(
            shape((2 * cells, cells), f32),
            shape((slots * air, y_points), f32),
            shape((slots * air, y_points), f32),
            shape((flux_count * tracer_count * depth, cells), f32),
        ),
        in_specs=[SMEM] * 3 + [VMEM] * 3,
        out_specs=(VMEM,) * 4,
        compiler_params=PARAMS,
        cost_estimate=cost(1),
        name="weights",
    )(entry_sender_patch, live, solute_forcing_factor, offsets, polygon_side_total, mixing)

    later, diffused = pl.pallas_call(
        functools.partial(middle_kernel, levels, rows),
        out_shape=(shape((x_points, rows, y_points), f32), shape(tracers.shape, f32)),
        in_specs=[VMEM] * 9,
        out_specs=(HBM, VMEM),
        scratch_shapes=[
            pltpu.VMEM(field.shape, f32),
            pltpu.VMEM((x_points, rows, y_points), f32),
            pltpu.SemaphoreType.DMA((max(fields, x_points),)),
        ],
        compiler_params=PARAMS,
        cost_estimate=cost(1),
        name="middle",
    )(field, zonal, meridional, along, own, below, above, tracers, weights)

    renewed, *shares = pl.pallas_call(
        remap_kernel,
        out_shape=(shape(tracers.shape, f32),)
        + (shape((air // oceans, x_points, y_points), f32),) * oceans,
        in_specs=[VMEM] * 8,
        out_specs=(VMEM,) * (1 + oceans),
        compiler_params=PARAMS,
        cost_estimate=cost(2),
        name="remap",
    )(regrid, gather, spread, arrived, chosen, returning, forcing, diffused)

    def swap(blocks):
        return [(s, blocks[s // oceans] * oceans + s % oceans) for s in range(sections)]

    for m in range(1, oceans):
        pairs = [(s, s if s < air else air + (s - air + m) % oceans) for s in range(sections)]
        shares[m] = lax.ppermute(shares[m], "sec", pairs)
    totals = pl.pallas_call(
        add_kernel,
        out_shape=(shape((x_points, y_points), f32),) * (air // oceans),
        in_specs=[VMEM] * oceans,
        out_specs=(VMEM,) * (air // oceans),
        compiler_params=PARAMS,
        cost_estimate=cost(0.3),
        name="add",
    )(*shares)
    returned = [
        lax.ppermute(totals[0], "sec", swap((3, 1, 2, 0))),
        lax.ppermute(totals[1], "sec", swap((0, 3, 2, 1))),
        lax.ppermute(totals[2], "sec", swap((0, 1, 3, 2))),
    ]
    tracers_later, warmth = pl.pallas_call(
        last_kernel,
        out_shape=(shape(tracers.shape, f32), shape((x_points, y_points), f32)),
        in_specs=[VMEM] * (1 + len(returned)),
        out_specs=(VMEM,) * 2,
        compiler_params=PARAMS,
        cost_estimate=cost(0.5),
        name="last",
    )(renewed, *returned)
    return (
        later.reshape(climate_field_table.shape),
        tracers_later.reshape(marine_salinity_heat.shape),
        warmth[None],
    )


def solution(mesh):
    return jax.shard_map(
        per_device,
        mesh=mesh,
        in_specs=(
            P("sec", "rank", None, None),
            P("sec", "rank", None, None),
            P("sec", "rank", None, None),
            P("sec", "rank", None),
            P(),
            P("sec", "rank", None, None, None, None),
            P(None, "rank", None),
            P(None, "rank"),
            P("sec", None, None, "rank"),
            P("sec", None, "rank"),
            P("sec", "rank"),
            P("sec", None, "rank"),
            P(),
        ),
        out_specs=(
            P("sec", "rank", None, None),
            P("sec", None, None, "rank"),
            P("sec", "rank", None),
        ),
        check_vma=False,
    )
```

```python
import functools

import jax
import jax.numpy as jnp
import numpy as np
from jax import lax
from jax.experimental import pallas as pl
from jax.experimental.pallas import tpu as pltpu
from jax.sharding import PartitionSpec as P

STEP_ATMOS = 0.05
DIFFUSIVITY = 0.05
STEP_OCEAN = 0.5
NODES = 4

VMEM = pl.BlockSpec(memory_space=pltpu.VMEM)
ANY = pl.BlockSpec(memory_space=pl.ANY)
HBM = pl.BlockSpec(memory_space=pltpu.HBM)
SMEM = pl.BlockSpec(memory_space=pltpu.SMEM)
PARAMS = pltpu.CompilerParams(vmem_limit_bytes=8 * 2**20)
HIGHEST = lax.Precision.HIGHEST


def gll_matrix():
    nodes = np.array([-1.0, -1.0 / np.sqrt(5.0), 1.0 / np.sqrt(5.0), 1.0])
    legendre = (5.0 * nodes**3 - 3.0 * nodes) / 2.0
    matrix = np.zeros((4, 4))
    for i in range(4):
        for j in range(4):
            if i != j:
                matrix[i, j] = legendre[i] / (legendre[j] * (nodes[i] - nodes[j]))
    matrix[0, 0] = -3.0
    matrix[3, 3] = 3.0
    return matrix.astype(np.float32)


def cost(microseconds):
    return pl.CostEstimate(
        flops=0, bytes_accessed=int(microseconds * 3_000_000), transcendentals=0
    )


def in_air():
    sections = lax.axis_size("sec")
    return lax.axis_index("sec") < sections - sections // 4


def smooth_lines(value, lane):
    width = value.shape[-1]
    right = pltpu.roll(value, width - 1, value.ndim - 1)
    left = pltpu.roll(value, 1, value.ndim - 1)
    at_end = (lane % NODES == NODES - 1) & (lane < width - 1)
    at_start = (lane % NODES == 0) & (lane > 0)
    partner = jnp.where(at_end, right, jnp.where(at_start, left, value))
    return 0.5 * (value + partner)


def start_all(pairs, sems):
    copies = [
        pltpu.make_async_copy(source, target, sems.at[i])
        for i, (source, target) in enumerate(pairs)
    ]
    for copy in copies:
        copy.start()
    return copies


def first_kernel(
    levels,
    rows,
    law_in,
    field_in,
    zonal_in,
    meridional_in,
    sea_in,
    along_in,
    tracers_in,
    sent,
    first,
    last,
    own,
    law,
    field,
    zonal,
    meridional,
    sea,
    along,
    tracers,
    packed,
    sems,
):
    @pl.when(in_air())
    def _():
        copies = start_all(
            (
                (law_in, law),
                (field_in, field),
                (zonal_in, zonal),
                (meridional_in, meridional),
                (sea_in, sea),
                (along_in, along),
            ),
            sems,
        )
        for copy in copies:
            copy.wait()
        flux_count, columns = law.shape
        x_points = sea.shape[1]
        u = zonal[pl.ds(0, x_points, stride=levels), :]
        v = meridional[pl.ds(0, x_points, stride=levels), :]
        speed = jnp.sqrt(1.0 + u * u + v * v)
        ground = [
            field[pl.ds(f * levels, x_points, stride=rows), :] for f in range(columns - 1)
        ] + [sea[0]]
        parts = []
        for n in range(flux_count):
            total = law[n, 0] * ground[0]
            for f in range(1, columns):
                total = total + law[n, f] * ground[f]
            parts.append(speed * total)
        block = jnp.concatenate(parts, axis=0).astype(jnp.bfloat16)
        for s in range(packed.shape[0]):
            packed[s] = block
        leaving = pltpu.make_async_copy(packed, sent, sems.at[0])
        leaving.start()

        d = gll_matrix()
        lane = lax.broadcasted_iota(jnp.int32, (levels, field.shape[1]), 1)
        for side, (x, target) in enumerate(((0, first), (x_points - 1, last))):
            start = x - x % NODES
            along_y = jnp.dot(
                field[pl.ds(x * rows, rows), :],
                along[...],
                precision=HIGHEST,
                preferred_element_type=jnp.float32,
            )
            u = zonal[pl.ds(x * levels, levels), :]
            v = meridional[pl.ds(x * levels, levels), :]
            for f in range(rows // levels):
                at = f * levels
                along_x = sum(
                    float(d[x % NODES, a]) * field[pl.ds((start + a) * rows + at, levels), :]
                    for a in range(NODES)
                    if d[x % NODES, a] != 0
                )
                value = -(u * along_x + v * along_y[at : at + levels])
                value = smooth_lines(value, lane)
                own[side, pl.ds(at, levels), :] = value
                target[pl.ds(at, levels), :] = value.astype(jnp.bfloat16)
        leaving.wait()

    @pl.when(jnp.logical_not(in_air()))
    def _():
        copy = pltpu.make_async_copy(tracers_in, tracers, sems.at[0])
        copy.start()
        copy.wait()
        value = tracers[...]
        high = value.astype(jnp.bfloat16)
        low = (value - high.astype(jnp.float32)).astype(jnp.bfloat16)
        both = jnp.concatenate([high, low], axis=0)
        for target in (first, last):
            target[pl.ds(0, both.shape[0]), :] = both


def weight_kernel(
    senders, live, forcing_factor, offsets, sides, mixing, weights, chosen, returning, forcing, gather, spread
):
    @pl.when(jnp.logical_not(in_air()))
    def _():
        cells = sides.shape[1]
        source = lax.broadcasted_iota(jnp.int32, (cells, cells), 0)
        target = lax.broadcasted_iota(jnp.int32, (cells, cells), 1)
        inside = jnp.zeros((cells, cells), jnp.float32)
        outside = jnp.zeros((cells, cells), jnp.float32)
        total = jnp.zeros((1, cells), jnp.float32)
        for e in range(offsets.shape[0]):
            weight = jnp.where(e < sides[...], mixing[e], 0.0)
            place = target[:1] + offsets[e]
            total = total + weight
            inside = inside + jnp.where(source == place, weight, 0.0)
            hit = (source == place - cells) | (source == place + cells)
            outside = outside + jnp.where(hit, weight, 0.0)
        inside = inside - jnp.where(source == target, total, 0.0)
        weights[pl.ds(0, cells), :] = inside
        weights[pl.ds(cells, cells), :] = outside

        x_count = gather.shape[0] // cells
        point = lax.broadcasted_iota(jnp.int32, gather.shape, 0) // x_count
        cell = lax.broadcasted_iota(jnp.int32, gather.shape, 1)
        gather[...] = jnp.where(point == cell, 1.0, 0.0).astype(gather.dtype)
        cell = lax.broadcasted_iota(jnp.int32, spread.shape, 0)
        point = lax.broadcasted_iota(jnp.int32, spread.shape, 1) // x_count
        spread[...] = jnp.where(point == cell, 1.0, 0.0).astype(spread.dtype)

        sections = lax.axis_size("sec")
        oceans = sections // 4
        air = sections - oceans
        ocean = jnp.maximum(lax.axis_index("sec") - air, 0)
        width = chosen.shape[1]
        count = live[0, ocean]
        for k in range(senders.shape[2]):
            place = jnp.where(k < count, senders[ocean, 0, k], sections)
            section = lax.broadcasted_iota(jnp.int32, (air, width), 0)
            chosen[pl.ds(k * air, air), :] = jnp.where(section == place, 1.0, 0.0)
            turn = lax.broadcasted_iota(jnp.int32, (air, width), 0)
            block = turn % (air // oceans)
            owner = (ocean + turn // (air // oceans)) % oceans
            returning[pl.ds(k * air, air), :] = jnp.where(
                block * oceans + owner == place, 1.0, 0.0
            )
        tracer_count, flux_count = forcing_factor.shape
        depth = forcing.shape[0] // (tracer_count * flux_count)
        level = lax.broadcasted_iota(jnp.int32, (depth, width), 0).astype(jnp.float32)
        profile = STEP_OCEAN * jnp.exp(-0.5 * level)
        for n in range(flux_count):
            for t in range(tracer_count):
                forcing[pl.ds((n * tracer_count + t) * depth, depth), :] = (
                    forcing_factor[t, n] * profile
                )


def middle_kernel(
    levels,
    rows,
    field,
    zonal,
    meridional,
    along,
    own,
    below,
    above,
    tracers,
    weights,
    later,
    diffused,
    slopes,
    held,
    sems,
):
    x_points = later.shape[0]

    @pl.when(in_air())
    def _():
        d = gll_matrix()
        lane = lax.broadcasted_iota(jnp.int32, (levels, field.shape[1]), 1)
        inner = pl.ds(rows, (x_points - 2) * rows)
        slopes[inner, :] = jnp.dot(
            field[inner, :], along[...], precision=HIGHEST, preferred_element_type=jnp.float32
        )
        copies = []
        for f in range(rows // levels):
            at = f * levels
            here = pl.ds(at, levels)
            values = {
                0: 0.5 * (own[0, here, :] + below[here, :].astype(jnp.float32)),
                x_points - 1: 0.5 * (own[1, here, :] + above[here, :].astype(jnp.float32)),
            }
            q = [field[pl.ds(x * rows + at, levels), :] for x in range(x_points)]
            for x in range(1, x_points - 1):
                start = x - x % NODES
                along_x = sum(
                    float(d[x % NODES, a]) * q[start + a]
                    for a in range(NODES)
                    if d[x % NODES, a] != 0
                )
                u = zonal[pl.ds(x * levels, levels), :]
                v = meridional[pl.ds(x * levels, levels), :]
                value = -(u * along_x + v * slopes[pl.ds(x * rows + at, levels), :])
                values[x] = smooth_lines(value, lane)
            for x in range(NODES - 1, x_points - 1, NODES):
                values[x] = values[x + 1] = 0.5 * (values[x] + values[x + 1])
            for x in range(x_points):
                held[x, here, :] = q[x] + STEP_ATMOS * values[x]
            copy = pltpu.make_async_copy(held.at[:, here, :], later.at[:, here, :], sems.at[f])
            copy.start()
            copies.append(copy)
        for copy in copies:
            copy.wait()

    @pl.when(jnp.logical_not(in_air()))
    def _():
        held[0] = jnp.zeros(held.shape[1:], jnp.float32)
        copies = start_all([(held.at[0], later.at[x]) for x in range(x_points)], sems)
        value = tracers[...]
        height, cells = value.shape
        cell = lax.broadcasted_iota(jnp.int32, value.shape, 1)
        beside = [
            h[pl.ds(0, height), :].astype(jnp.float32)
            + h[pl.ds(height, height), :].astype(jnp.float32)
            for h in (below, above)
        ]
        outer = jnp.where(cell < cells // 2, beside[1], beside[0])
        both = jnp.concatenate([value, outer], axis=1)
        change = jnp.dot(
            both, weights[...], precision=HIGHEST, preferred_element_type=jnp.float32
        )
        diffused[...] = value + DIFFUSIVITY * change
        for copy in copies:
            copy.wait()


def remap_kernel(
    regrid, gather, spread, arrived, chosen, returning, forcing, diffused, renewed, *shares
):
    @pl.when(jnp.logical_not(in_air()))
    def _():
        points, cells = gather.shape
        x_count = points // cells
        slots = regrid.shape[0] // points
        air = chosen.shape[0] // slots
        packed = arrived.shape[1]
        flux_count = packed // x_count
        row = lax.broadcasted_iota(jnp.int32, (x_count, cells), 0)
        column = lax.broadcasted_iota(jnp.int32, (x_count, cells), 1)
        same = jnp.where(row == column % x_count, 1.0, 0.0)

        blocks = [arrived[s].astype(jnp.float32) for s in range(air)]
        matched = None
        for k in range(slots):
            part = chosen[pl.ds(k * air, 1), :] * blocks[0]
            for s in range(1, air):
                part = part + chosen[pl.ds(k * air + s, 1), :] * blocks[s]
            product = lax.dot_general(
                part.astype(jnp.bfloat16),
                regrid[pl.ds(k * points, points), :],
                (((1,), (1,)), ((), ())),
                preferred_element_type=jnp.float32,
            )
            matched = product if matched is None else matched + product
        matched = matched * jnp.tile(same, (flux_count, x_count))
        high = matched.astype(jnp.bfloat16)
        low = (matched - high.astype(jnp.float32)).astype(jnp.bfloat16)
        summed = jnp.dot(high, gather[...], preferred_element_type=jnp.float32) + jnp.dot(
            low, gather[...], preferred_element_type=jnp.float32
        )
        ocean_flux = summed.reshape(flux_count, x_count, cells).sum(axis=1)
        height = diffused.shape[0]
        value = diffused[...]
        for n in range(flux_count):
            value = value + forcing[pl.ds(n * height, height), :] * ocean_flux[n : n + 1]
        renewed[...] = value

        top = jnp.broadcast_to(value[0:1], (x_count, cells)).astype(jnp.bfloat16)
        wide = jnp.dot(top, spread[...], preferred_element_type=jnp.float32)
        wide = (wide * jnp.tile(same, (1, x_count))).astype(jnp.bfloat16)
        back = [
            jnp.dot(wide, regrid[pl.ds(k * points, points), :], preferred_element_type=jnp.float32)
            for k in range(slots)
        ]
        count = shares[0].shape[0]
        for m, share in enumerate(shares):
            for j in range(count):
                at = m * count + j
                total = returning[pl.ds(at, 1), :] * back[0]
                for k in range(1, slots):
                    total = total + returning[pl.ds(k * air + at, 1), :] * back[k]
                share[j] = total


def add_kernel(*refs):
    count = refs[0].shape[0]
    shares, totals = refs[:-count], refs[-count:]

    @pl.when(jnp.logical_not(in_air()))
    def _():
        for j, total in enumerate(totals):
            value = shares[0][j]
            for share in shares[1:]:
                value = value + share[j]
            total[...] = value


def last_kernel(renewed, *refs):
    returned, (tracers_later, warmth) = refs[:-2], refs[-2:]
    sections = lax.axis_size("sec")
    block = lax.axis_index("sec") // (sections // 4)

    @pl.when(in_air())
    def _():
        tracers_later[...] = jnp.zeros(tracers_later.shape, jnp.float32)

    @pl.when(jnp.logical_not(in_air()))
    def _():
        tracers_later[...] = renewed[...]
        warmth[...] = jnp.zeros(warmth.shape, jnp.float32)

    for j, part in enumerate(returned):

        @pl.when(block == j)
        def _(part=part):
            warmth[...] = part[...]


def per_device(
    climate_field_table,
    zonal_wind_speed,
    meridional_wind,
    sea_warmth_field,
    exchange_law_factor,
    regrid_matrix_stack,
    entry_sender_patch,
    holder_live_total,
    marine_salinity_heat,
    adjacent_offset_lists,
    polygon_side_total,
    interface_mixing_factor,
    solute_forcing_factor,
):
    sections = lax.axis_size("sec")
    ranks = lax.axis_size("rank")
    oceans = sections // 4
    air = sections - oceans
    _, x_points, rows, y_points = climate_field_table.shape
    levels = zonal_wind_speed.shape[2]
    flux_count = exchange_law_factor.shape[0]
    _, tracer_count, depth, cells = marine_salinity_heat.shape
    slots = regrid_matrix_stack.shape[2]
    f32, bf16 = jnp.float32, jnp.bfloat16
    shape = jax.ShapeDtypeStruct

    field = climate_field_table.reshape(x_points * rows, y_points)
    zonal = zonal_wind_speed.reshape(x_points * levels, y_points)
    meridional = meridional_wind.reshape(x_points * levels, y_points)
    regrid = regrid_matrix_stack.reshape(slots * cells * x_points, y_points)
    tracers = marine_salinity_heat.reshape(tracer_count * depth, cells)
    offsets = jnp.transpose(adjacent_offset_lists, (1, 0, 2))
    mixing = jnp.transpose(interface_mixing_factor, (1, 0, 2))
    live = jnp.transpose(holder_live_total, (1, 0))

    along = np.kron(np.eye(y_points // NODES, dtype=np.float32), gll_matrix().T)
    along = jnp.asarray(along)

    fields = rows // levels
    in_place = (exchange_law_factor, field, zonal, meridional, sea_warmth_field, along, tracers)
    fluxes, first, last, own = pl.pallas_call(
        functools.partial(first_kernel, levels, rows),
        out_shape=(
            shape((sections, flux_count * x_points, y_points), bf16),
            shape((rows, y_points), bf16),
            shape((rows, y_points), bf16),
            shape((2, rows, y_points), f32),
        ),
        in_specs=[HBM] * len(in_place),
        out_specs=(HBM, VMEM, VMEM, VMEM),
        scratch_shapes=[pltpu.SMEM(exchange_law_factor.shape, f32)]
        + [pltpu.VMEM(a.shape, f32) for a in in_place[1:]]
        + [pltpu.VMEM((sections, flux_count * x_points, y_points), bf16)]
        + [pltpu.SemaphoreType.DMA((len(in_place),))],
        compiler_params=PARAMS,
        cost_estimate=cost(2),
        name="first",
    )(*(pltpu.with_memory_space_constraint(a, pltpu.HBM) for a in in_place))
    up = [(i, (i + 1) % ranks) for i in range(ranks)]
    below = lax.ppermute(last, "rank", up)
    above = lax.ppermute(first, "rank", [(j, i) for i, j in up])
    arrived = lax.all_to_all(fluxes, "sec", 0, 0, tiled=True)

    weights, chosen, returning, forcing, gather, spread = pl.pallas_call(
        weight_kernel,
        out_shape=(
            shape((2 * cells, cells), f32),
            shape((slots * air, y_points), f32),
            shape((slots * air, y_points), f32),
            shape((flux_count * tracer_count * depth, cells), f32),
            shape((x_points * cells, cells), bf16),
            shape((cells, x_points * cells), bf16),
        ),
        in_specs=[SMEM] * 3 + [VMEM] * 3,
        out_specs=(VMEM,) * 6,
        compiler_params=PARAMS,
        cost_estimate=cost(0.3),
        name="weights",
    )(entry_sender_patch, live, solute_forcing_factor, offsets, polygon_side_total, mixing)

    later, diffused = pl.pallas_call(
        functools.partial(middle_kernel, levels, rows),
        out_shape=(shape((x_points, rows, y_points), f32), shape(tracers.shape, f32)),
        in_specs=[VMEM] * 9,
        out_specs=(HBM, VMEM),
        scratch_shapes=[
            pltpu.VMEM(field.shape, f32),
            pltpu.VMEM((x_points, rows, y_points), f32),
            pltpu.SemaphoreType.DMA((max(fields, x_points),)),
        ],
        compiler_params=PARAMS,
        cost_estimate=cost(0.3),
        name="middle",
    )(field, zonal, meridional, along, own, below, above, tracers, weights)

    renewed, *shares = pl.pallas_call(
        remap_kernel,
        out_shape=(shape(tracers.shape, f32),)
        + (shape((air // oceans, x_points, y_points), f32),) * oceans,
        in_specs=[VMEM] * 8,
        out_specs=(VMEM,) * (1 + oceans),
        compiler_params=PARAMS,
        cost_estimate=cost(2),
        name="remap",
    )(regrid, gather, spread, arrived, chosen, returning, forcing, diffused)

    for m in range(1, oceans):
        turn = [(s, s // oceans * oceans + (s + m) % oceans) for s in range(sections)]
        shares[m] = lax.ppermute(shares[m], "sec", turn)
    totals = pl.pallas_call(
        add_kernel,
        out_shape=(shape((x_points, y_points), f32),) * (air // oceans),
        in_specs=[VMEM] * oceans,
        out_specs=(VMEM,) * (air // oceans),
        compiler_params=PARAMS,
        cost_estimate=cost(0.3),
        name="add",
    )(*shares)
    returned = [
        lax.ppermute(
            total, "sec", [(s, (s + (block + 1) * oceans) % sections) for s in range(sections)]
        )
        for block, total in enumerate(totals)
    ]
    tracers_later, warmth = pl.pallas_call(
        last_kernel,
        out_shape=(shape(tracers.shape, f32), shape((x_points, y_points), f32)),
        in_specs=[VMEM] * (1 + len(returned)),
        out_specs=(VMEM,) * 2,
        compiler_params=PARAMS,
        cost_estimate=cost(0.5),
        name="last",
    )(renewed, *returned)
    return (
        later.reshape(climate_field_table.shape),
        tracers_later.reshape(marine_salinity_heat.shape),
        warmth[None],
    )


def solution(mesh):
    return jax.shard_map(
        per_device,
        mesh=mesh,
        in_specs=(
            P("sec", "rank", None, None),
            P("sec", "rank", None, None),
            P("sec", "rank", None, None),
            P("sec", "rank", None),
            P(),
            P("sec", "rank", None, None, None, None),
            P(None, "rank", None),
            P(None, "rank"),
            P("sec", None, None, "rank"),
            P("sec", None, "rank"),
            P("sec", "rank"),
            P("sec", None, "rank"),
            P(),
        ),
        out_specs=(
            P("sec", "rank", None, None),
            P("sec", None, None, "rank"),
            P("sec", "rank", None),
        ),
        check_vma=False,
    )
```

```python
import functools

import jax
import jax.numpy as jnp
import numpy as np
from jax import lax
from jax.experimental import pallas as pl
from jax.experimental.pallas import tpu as pltpu
from jax.sharding import PartitionSpec as P

STEP_ATMOS = 0.05
DIFFUSIVITY = 0.05
STEP_OCEAN = 0.5
NODES = 4

VMEM = pl.BlockSpec(memory_space=pltpu.VMEM)
ANY = pl.BlockSpec(memory_space=pl.ANY)
HBM = pl.BlockSpec(memory_space=pltpu.HBM)
SMEM = pl.BlockSpec(memory_space=pltpu.SMEM)
PARAMS = pltpu.CompilerParams(vmem_limit_bytes=8 * 2**20)
HIGHEST = lax.Precision.HIGHEST


def gll_matrix():
    nodes = np.array([-1.0, -1.0 / np.sqrt(5.0), 1.0 / np.sqrt(5.0), 1.0])
    legendre = (5.0 * nodes**3 - 3.0 * nodes) / 2.0
    matrix = np.zeros((4, 4))
    for i in range(4):
        for j in range(4):
            if i != j:
                matrix[i, j] = legendre[i] / (legendre[j] * (nodes[i] - nodes[j]))
    matrix[0, 0] = -3.0
    matrix[3, 3] = 3.0
    return matrix.astype(np.float32)


def cost(microseconds):
    return pl.CostEstimate(
        flops=0, bytes_accessed=int(microseconds * 3_000_000), transcendentals=0
    )


def in_air():
    sections = lax.axis_size("sec")
    return lax.axis_index("sec") < sections - sections // 4


def smooth_lines(value, lane):
    width = value.shape[-1]
    right = pltpu.roll(value, width - 1, value.ndim - 1)
    left = pltpu.roll(value, 1, value.ndim - 1)
    at_end = (lane % NODES == NODES - 1) & (lane < width - 1)
    at_start = (lane % NODES == 0) & (lane > 0)
    partner = jnp.where(at_end, right, jnp.where(at_start, left, value))
    return 0.5 * (value + partner)


def start_all(pairs, sems):
    copies = [
        pltpu.make_async_copy(source, target, sems.at[i])
        for i, (source, target) in enumerate(pairs)
    ]
    for copy in copies:
        copy.start()
    return copies


def first_kernel(
    levels,
    rows,
    law_in,
    field_in,
    zonal_in,
    meridional_in,
    sea_in,
    along_in,
    tracers_in,
    sent,
    first,
    last,
    own,
    law,
    field,
    zonal,
    meridional,
    sea,
    along,
    tracers,
    sems,
):
    @pl.when(in_air())
    def _():
        copies = start_all(
            (
                (law_in, law),
                (field_in, field),
                (zonal_in, zonal),
                (meridional_in, meridional),
                (sea_in, sea),
                (along_in, along),
            ),
            sems,
        )
        for copy in copies:
            copy.wait()
        flux_count, columns = law.shape
        x_points = sea.shape[1]
        u = zonal[pl.ds(0, x_points, stride=levels), :]
        v = meridional[pl.ds(0, x_points, stride=levels), :]
        speed = jnp.sqrt(1.0 + u * u + v * v)
        ground = [
            field[pl.ds(f * levels, x_points, stride=rows), :] for f in range(columns - 1)
        ] + [sea[0]]
        parts = []
        for n in range(flux_count):
            total = law[n, 0] * ground[0]
            for f in range(1, columns):
                total = total + law[n, f] * ground[f]
            parts.append(speed * total)
        sent[...] = jnp.concatenate(parts, axis=0).astype(jnp.bfloat16)

        d = gll_matrix()
        lane = lax.broadcasted_iota(jnp.int32, (levels, field.shape[1]), 1)
        for side, (x, target) in enumerate(((0, first), (x_points - 1, last))):
            start = x - x % NODES
            along_y = jnp.dot(
                field[pl.ds(x * rows, rows), :],
                along[...],
                precision=HIGHEST,
                preferred_element_type=jnp.float32,
            )
            u = zonal[pl.ds(x * levels, levels), :]
            v = meridional[pl.ds(x * levels, levels), :]
            for f in range(rows // levels):
                at = f * levels
                along_x = sum(
                    float(d[x % NODES, a]) * field[pl.ds((start + a) * rows + at, levels), :]
                    for a in range(NODES)
                    if d[x % NODES, a] != 0
                )
                value = -(u * along_x + v * along_y[at : at + levels])
                value = smooth_lines(value, lane)
                own[side, pl.ds(at, levels), :] = value
                target[pl.ds(at, levels), :] = value.astype(jnp.bfloat16)

    @pl.when(jnp.logical_not(in_air()))
    def _():
        copy = pltpu.make_async_copy(tracers_in, tracers, sems.at[0])
        copy.start()
        copy.wait()
        value = tracers[...]
        high = value.astype(jnp.bfloat16)
        low = (value - high.astype(jnp.float32)).astype(jnp.bfloat16)
        both = jnp.concatenate([high, low], axis=0)
        for target in (first, last):
            target[pl.ds(0, both.shape[0]), :] = both


def pack_kernel(own, *refs):
    received, packed = refs[:-1], refs[-1]
    count = len(refs)
    place = lax.axis_index("sec") % count
    packed[place] = own[...]
    for m, part in enumerate(received, 1):
        packed[(place - m + count) % count] = part[...]


def ocean_kernel(
    senders_in,
    live_in,
    factor_in,
    offsets_in,
    sides_in,
    mixing_in,
    tracers,
    below,
    above,
    diffused,
    chosen,
    returning,
    forcing,
    gather,
    spread,
    senders,
    live,
    factor,
    offsets,
    sides,
    mixing,
    sems,
):
    @pl.when(jnp.logical_not(in_air()))
    def _():
        copies = start_all(
            (
                (senders_in, senders),
                (live_in, live),
                (factor_in, factor),
                (offsets_in, offsets),
                (sides_in, sides),
                (mixing_in, mixing),
            ),
            sems,
        )
        cells = sides.shape[1]
        x_count = gather.shape[0] // cells
        point = lax.broadcasted_iota(jnp.int32, gather.shape, 0) // x_count
        cell = lax.broadcasted_iota(jnp.int32, gather.shape, 1)
        gather[...] = jnp.where(point == cell, 1.0, 0.0).astype(gather.dtype)
        cell = lax.broadcasted_iota(jnp.int32, spread.shape, 0)
        point = lax.broadcasted_iota(jnp.int32, spread.shape, 1) // x_count
        spread[...] = jnp.where(point == cell, 1.0, 0.0).astype(spread.dtype)
        for copy in copies:
            copy.wait()

        source = lax.broadcasted_iota(jnp.int32, (cells, cells), 0)
        target = lax.broadcasted_iota(jnp.int32, (cells, cells), 1)
        inside = jnp.zeros((cells, cells), jnp.float32)
        outside = jnp.zeros((cells, cells), jnp.float32)
        total = jnp.zeros((1, cells), jnp.float32)
        for e in range(offsets.shape[0]):
            weight = jnp.where(e < sides[...], mixing[e], 0.0)
            place = target[:1] + offsets[e]
            total = total + weight
            inside = inside + jnp.where(source == place, weight, 0.0)
            hit = (source == place - cells) | (source == place + cells)
            outside = outside + jnp.where(hit, weight, 0.0)
        inside = inside - jnp.where(source == target, total, 0.0)

        value = tracers[...]
        height = value.shape[0]
        cell = lax.broadcasted_iota(jnp.int32, value.shape, 1)
        beside = [
            h[pl.ds(0, height), :].astype(jnp.float32)
            + h[pl.ds(height, height), :].astype(jnp.float32)
            for h in (below, above)
        ]
        outer = jnp.where(cell < cells // 2, beside[1], beside[0])
        change = jnp.dot(
            jnp.concatenate([value, outer], axis=1),
            jnp.concatenate([inside, outside], axis=0),
            precision=HIGHEST,
            preferred_element_type=jnp.float32,
        )
        diffused[...] = value + DIFFUSIVITY * change

        sections = lax.axis_size("sec")
        oceans = sections // 4
        air = sections - oceans
        ocean = jnp.maximum(lax.axis_index("sec") - air, 0)
        width = chosen.shape[1]
        count = live[0, ocean]
        for k in range(senders.shape[2]):
            place = jnp.where(k < count, senders[ocean, 0, k], sections)
            section = lax.broadcasted_iota(jnp.int32, (air, width), 0)
            chosen[pl.ds(k * air, air), :] = jnp.where(section == place, 1.0, 0.0)
            block = section % (air // oceans)
            owner = (ocean + section // (air // oceans)) % oceans
            returning[pl.ds(k * air, air), :] = jnp.where(
                block * oceans + owner == place, 1.0, 0.0
            )
        tracer_count, flux_count = factor.shape
        depth = forcing.shape[0] // (tracer_count * flux_count)
        level = lax.broadcasted_iota(jnp.int32, (depth, width), 0).astype(jnp.float32)
        profile = STEP_OCEAN * jnp.exp(-0.5 * level)
        for n in range(flux_count):
            for t in range(tracer_count):
                forcing[pl.ds((n * tracer_count + t) * depth, depth), :] = factor[t, n] * profile


def field_kernel(
    levels,
    rows,
    field,
    zonal,
    meridional,
    along,
    own,
    below,
    above,
    after,
    later,
    slopes,
    held,
    sems,
):
    x_points = later.shape[0]

    @pl.when(in_air())
    def _():
        d = gll_matrix()
        lane = lax.broadcasted_iota(jnp.int32, (levels, field.shape[1]), 1)
        inner = pl.ds(rows, (x_points - 2) * rows)
        slopes[inner, :] = jnp.dot(
            field[inner, :], along[...], precision=HIGHEST, preferred_element_type=jnp.float32
        )
        copies = []
        for f in range(rows // levels):
            at = f * levels
            here = pl.ds(at, levels)
            values = {
                0: 0.5 * (own[0, here, :] + below[here, :].astype(jnp.float32)),
                x_points - 1: 0.5 * (own[1, here, :] + above[here, :].astype(jnp.float32)),
            }
            q = [field[pl.ds(x * rows + at, levels), :] for x in range(x_points)]
            for x in range(1, x_points - 1):
                start = x - x % NODES
                along_x = sum(
                    float(d[x % NODES, a]) * q[start + a]
                    for a in range(NODES)
                    if d[x % NODES, a] != 0
                )
                u = zonal[pl.ds(x * levels, levels), :]
                v = meridional[pl.ds(x * levels, levels), :]
                value = -(u * along_x + v * slopes[pl.ds(x * rows + at, levels), :])
                values[x] = smooth_lines(value, lane)
            for x in range(NODES - 1, x_points - 1, NODES):
                values[x] = values[x + 1] = 0.5 * (values[x] + values[x + 1])
            for x in range(x_points):
                held[x, here, :] = q[x] + STEP_ATMOS * values[x]
            copy = pltpu.make_async_copy(held.at[:, here, :], later.at[:, here, :], sems.at[f])
            copy.start()
            copies.append(copy)
        for copy in copies:
            copy.wait()

    @pl.when(jnp.logical_not(in_air()))
    def _():
        held[0] = jnp.zeros(held.shape[1:], jnp.float32)
        copies = start_all([(held.at[0], later.at[x]) for x in range(x_points)], sems)
        for copy in copies:
            copy.wait()


def remap_kernel(
    regrid, gather, spread, chosen, returning, forcing, diffused, *refs
):
    arrived, renewed, shares = refs[:3], refs[3], refs[4:]

    @pl.when(jnp.logical_not(in_air()))
    def _():
        points, cells = gather.shape
        x_count = points // cells
        slots = regrid.shape[0] // points
        air = chosen.shape[0] // slots
        packed = refs[0].shape[1]
        flux_count = packed // x_count
        row = lax.broadcasted_iota(jnp.int32, (x_count, cells), 0)
        column = lax.broadcasted_iota(jnp.int32, (x_count, cells), 1)
        same = jnp.where(row == column % x_count, 1.0, 0.0)

        blocks = [block[s].astype(jnp.float32) for block in arrived for s in range(block.shape[0])]
        matched = None
        for k in range(slots):
            part = chosen[pl.ds(k * air, 1), :] * blocks[0]
            for s in range(1, air):
                part = part + chosen[pl.ds(k * air + s, 1), :] * blocks[s]
            product = lax.dot_general(
                part.astype(jnp.bfloat16),
                regrid[pl.ds(k * points, points), :],
                (((1,), (1,)), ((), ())),
                preferred_element_type=jnp.float32,
            )
            matched = product if matched is None else matched + product
        matched = matched * jnp.tile(same, (flux_count, x_count))
        high = matched.astype(jnp.bfloat16)
        low = (matched - high.astype(jnp.float32)).astype(jnp.bfloat16)
        summed = jnp.dot(high, gather[...], preferred_element_type=jnp.float32) + jnp.dot(
            low, gather[...], preferred_element_type=jnp.float32
        )
        ocean_flux = summed.reshape(flux_count, x_count, cells).sum(axis=1)
        height = diffused.shape[0]
        value = diffused[...]
        for n in range(flux_count):
            value = value + forcing[pl.ds(n * height, height), :] * ocean_flux[n : n + 1]
        renewed[...] = value

        top = jnp.broadcast_to(value[0:1], (x_count, cells)).astype(jnp.bfloat16)
        wide = jnp.dot(top, spread[...], preferred_element_type=jnp.float32)
        wide = (wide * jnp.tile(same, (1, x_count))).astype(jnp.bfloat16)
        back = [
            jnp.dot(wide, regrid[pl.ds(k * points, points), :], preferred_element_type=jnp.float32)
            for k in range(slots)
        ]
        count = shares[0].shape[0]
        for m, share in enumerate(shares):
            for j in range(count):
                at = m * count + j
                total = returning[pl.ds(at, 1), :] * back[0]
                for k in range(1, slots):
                    total = total + returning[pl.ds(k * air + at, 1), :] * back[k]
                share[j] = total


def add_kernel(*refs):
    count = refs[0].shape[0]
    shares, totals = refs[:-count], refs[-count:]

    @pl.when(jnp.logical_not(in_air()))
    def _():
        for j, total in enumerate(totals):
            value = shares[0][j]
            for share in shares[1:]:
                value = value + share[j]
            total[...] = value


def last_kernel(renewed, *refs):
    returned, (tracers_later, warmth) = refs[:-2], refs[-2:]
    sections = lax.axis_size("sec")
    block = lax.axis_index("sec") // (sections // 4)

    @pl.when(in_air())
    def _():
        tracers_later[...] = jnp.zeros(tracers_later.shape, jnp.float32)

    @pl.when(jnp.logical_not(in_air()))
    def _():
        tracers_later[...] = renewed[...]
        warmth[...] = jnp.zeros(warmth.shape, jnp.float32)

    for j, part in enumerate(returned):

        @pl.when(block == j)
        def _(part=part):
            warmth[...] = part[...]


def per_device(
    climate_field_table,
    zonal_wind_speed,
    meridional_wind,
    sea_warmth_field,
    exchange_law_factor,
    regrid_matrix_stack,
    entry_sender_patch,
    holder_live_total,
    marine_salinity_heat,
    adjacent_offset_lists,
    polygon_side_total,
    interface_mixing_factor,
    solute_forcing_factor,
):
    sections = lax.axis_size("sec")
    ranks = lax.axis_size("rank")
    oceans = sections // 4
    air = sections - oceans
    _, x_points, rows, y_points = climate_field_table.shape
    levels = zonal_wind_speed.shape[2]
    flux_count = exchange_law_factor.shape[0]
    _, tracer_count, depth, cells = marine_salinity_heat.shape
    slots = regrid_matrix_stack.shape[2]
    f32, bf16 = jnp.float32, jnp.bfloat16
    shape = jax.ShapeDtypeStruct

    field = climate_field_table.reshape(x_points * rows, y_points)
    zonal = zonal_wind_speed.reshape(x_points * levels, y_points)
    meridional = meridional_wind.reshape(x_points * levels, y_points)
    regrid = regrid_matrix_stack.reshape(slots * cells * x_points, y_points)
    tracers = marine_salinity_heat.reshape(tracer_count * depth, cells)
    offsets = jnp.transpose(adjacent_offset_lists, (1, 0, 2))
    mixing = jnp.transpose(interface_mixing_factor, (1, 0, 2))
    live = jnp.transpose(holder_live_total, (1, 0))

    along = np.kron(np.eye(y_points // NODES, dtype=np.float32), gll_matrix().T)
    along = jnp.asarray(along)

    fields = rows // levels
    in_place = (exchange_law_factor, field, zonal, meridional, sea_warmth_field, along, tracers)
    fluxes, first, last, own = pl.pallas_call(
        functools.partial(first_kernel, levels, rows),
        out_shape=(
            shape((flux_count * x_points, y_points), bf16),
            shape((rows, y_points), bf16),
            shape((rows, y_points), bf16),
            shape((2, rows, y_points), f32),
        ),
        in_specs=[HBM] * len(in_place),
        out_specs=(VMEM,) * 4,
        scratch_shapes=[pltpu.SMEM(exchange_law_factor.shape, f32)]
        + [pltpu.VMEM(a.shape, f32) for a in in_place[1:]]
        + [pltpu.SemaphoreType.DMA((len(in_place),))],
        compiler_params=PARAMS,
        cost_estimate=cost(2),
        name="first",
    )(*(pltpu.with_memory_space_constraint(a, pltpu.HBM) for a in in_place))
    up = [(i, (i + 1) % ranks) for i in range(ranks)]
    below = lax.ppermute(last, "rank", up)
    above = lax.ppermute(first, "rank", [(j, i) for i, j in up])

    def turned(value, m):
        pairs = [(s, s // oceans * oceans + (s + m) % oceans) for s in range(sections)]
        return lax.ppermute(value, "sec", pairs)

    def shifted(value, blocks):
        pairs = [(s, (s + blocks * oceans) % sections) for s in range(sections)]
        return lax.ppermute(value, "sec", pairs)

    received = [turned(fluxes, m) for m in range(1, oceans)]
    packed = pl.pallas_call(
        pack_kernel,
        out_shape=shape((oceans, flux_count * x_points, y_points), bf16),
        in_specs=[VMEM] * oceans,
        out_specs=VMEM,
        compiler_params=PARAMS,
        cost_estimate=cost(0.2),
        name="pack",
    )(fluxes, *received)
    arrived = [shifted(packed, 3 - block) for block in range(3)]

    from_memory = (
        entry_sender_patch,
        live,
        solute_forcing_factor,
        offsets,
        polygon_side_total,
        mixing,
    )
    diffused, chosen, returning, forcing, gather, spread = pl.pallas_call(
        ocean_kernel,
        out_shape=(
            shape(tracers.shape, f32),
            shape((slots * air, y_points), f32),
            shape((slots * air, y_points), f32),
            shape((flux_count * tracer_count * depth, cells), f32),
            shape((x_points * cells, cells), bf16),
            shape((cells, x_points * cells), bf16),
        ),
        in_specs=[HBM] * 6 + [VMEM] * 3,
        out_specs=(VMEM,) * 6,
        scratch_shapes=[
            (pltpu.SMEM if i < 3 else pltpu.VMEM)(a.shape, a.dtype)
            for i, a in enumerate(from_memory)
        ]
        + [pltpu.SemaphoreType.DMA((len(from_memory),))],
        compiler_params=PARAMS,
        cost_estimate=cost(1),
        name="ocean",
    )(
        *(pltpu.with_memory_space_constraint(a, pltpu.HBM) for a in from_memory),
        tracers,
        below,
        above,
    )

    renewed, *shares = pl.pallas_call(
        remap_kernel,
        out_shape=(shape(tracers.shape, f32),)
        + (shape((air // oceans, x_points, y_points), f32),) * oceans,
        in_specs=[VMEM] * 10,
        out_specs=(VMEM,) * (1 + oceans),
        compiler_params=PARAMS,
        cost_estimate=cost(1),
        name="remap",
    )(regrid, gather, spread, chosen, returning, forcing, diffused, *arrived)
    shares = shares[:1] + [turned(share, m) for m, share in enumerate(shares[1:], 1)]
    totals = pl.pallas_call(
        add_kernel,
        out_shape=(shape((x_points, y_points), f32),) * (air // oceans),
        in_specs=[VMEM] * oceans,
        out_specs=(VMEM,) * (air // oceans),
        compiler_params=PARAMS,
        cost_estimate=cost(0.3),
        name="add",
    )(*shares)
    returned = [shifted(total, block + 1) for block, total in enumerate(totals)]
    later = pl.pallas_call(
        functools.partial(field_kernel, levels, rows),
        out_shape=shape((x_points, rows, y_points), f32),
        in_specs=[VMEM] * 7 + [ANY],
        out_specs=HBM,
        scratch_shapes=[
            pltpu.VMEM(field.shape, f32),
            pltpu.VMEM((x_points, rows, y_points), f32),
            pltpu.SemaphoreType.DMA((max(fields, x_points),)),
        ],
        compiler_params=PARAMS,
        cost_estimate=cost(3),
        name="field",
    )(field, zonal, meridional, along, own, below, above, totals[0])
    tracers_later, warmth = pl.pallas_call(
        last_kernel,
        out_shape=(shape(tracers.shape, f32), shape((x_points, y_points), f32)),
        in_specs=[VMEM] * (1 + len(returned)),
        out_specs=(VMEM,) * 2,
        compiler_params=PARAMS,
        cost_estimate=cost(0.5),
        name="last",
    )(renewed, *returned)
    return (
        later.reshape(climate_field_table.shape),
        tracers_later.reshape(marine_salinity_heat.shape),
        warmth[None],
    )


def solution(mesh):
    return jax.shard_map(
        per_device,
        mesh=mesh,
        in_specs=(
            P("sec", "rank", None, None),
            P("sec", "rank", None, None),
            P("sec", "rank", None, None),
            P("sec", "rank", None),
            P(),
            P("sec", "rank", None, None, None, None),
            P(None, "rank", None),
            P(None, "rank"),
            P("sec", None, None, "rank"),
            P("sec", None, "rank"),
            P("sec", "rank"),
            P("sec", None, "rank"),
            P(),
        ),
        out_specs=(
            P("sec", "rank", None, None),
            P("sec", None, None, "rank"),
            P("sec", "rank", None),
        ),
        check_vma=False,
    )
```

```python
import functools

import jax
import jax.numpy as jnp
import numpy as np
from jax import lax
from jax.experimental import pallas as pl
from jax.experimental.pallas import tpu as pltpu
from jax.sharding import PartitionSpec as P

STEP_ATMOS = 0.05
DIFFUSIVITY = 0.05
STEP_OCEAN = 0.5
NODES = 4

VMEM = pl.BlockSpec(memory_space=pltpu.VMEM)
ANY = pl.BlockSpec(memory_space=pl.ANY)
HBM = pl.BlockSpec(memory_space=pltpu.HBM)
SMEM = pl.BlockSpec(memory_space=pltpu.SMEM)
PARAMS = pltpu.CompilerParams(vmem_limit_bytes=8 * 2**20)
HIGHEST = lax.Precision.HIGHEST


def gll_matrix():
    nodes = np.array([-1.0, -1.0 / np.sqrt(5.0), 1.0 / np.sqrt(5.0), 1.0])
    legendre = (5.0 * nodes**3 - 3.0 * nodes) / 2.0
    matrix = np.zeros((4, 4))
    for i in range(4):
        for j in range(4):
            if i != j:
                matrix[i, j] = legendre[i] / (legendre[j] * (nodes[i] - nodes[j]))
    matrix[0, 0] = -3.0
    matrix[3, 3] = 3.0
    return matrix.astype(np.float32)


def cost(microseconds):
    return pl.CostEstimate(
        flops=0, bytes_accessed=int(microseconds * 3_000_000), transcendentals=0
    )


def in_air():
    sections = lax.axis_size("sec")
    return lax.axis_index("sec") < sections - sections // 4


def smooth_lines(value, lane):
    width = value.shape[-1]
    right = pltpu.roll(value, width - 1, value.ndim - 1)
    left = pltpu.roll(value, 1, value.ndim - 1)
    at_end = (lane % NODES == NODES - 1) & (lane < width - 1)
    at_start = (lane % NODES == 0) & (lane > 0)
    partner = jnp.where(at_end, right, jnp.where(at_start, left, value))
    return 0.5 * (value + partner)


def start_all(pairs, sems):
    copies = [
        pltpu.make_async_copy(source, target, sems.at[i])
        for i, (source, target) in enumerate(pairs)
    ]
    for copy in copies:
        copy.start()
    return copies


def flux_kernel(
    levels, law_in, field_in, zonal_in, meridional_in, sea_in, sent, law, field, zonal, meridional, sea, sems
):
    @pl.when(in_air())
    def _():
        lowest = pl.ds(0, zonal.shape[1])
        copies = start_all(
            (
                (field_in.at[:, :, lowest, :], field),
                (zonal_in.at[:, lowest, :], zonal),
                (meridional_in.at[:, lowest, :], meridional),
                (sea_in, sea),
                (law_in, law),
            ),
            sems,
        )
        for copy in copies:
            copy.wait()
        flux_count, columns = law.shape
        ground = [field[:, f, 0, :] for f in range(columns - 1)] + [sea[0]]
        speed = jnp.sqrt(1.0 + zonal[:, 0, :] ** 2 + meridional[:, 0, :] ** 2)
        parts = []
        for n in range(flux_count):
            total = law[n, 0] * ground[0]
            for f in range(1, columns):
                total = total + law[n, f] * ground[f]
            parts.append(speed * total)
        block = jnp.concatenate(parts, axis=0).astype(jnp.bfloat16)
        sent[pl.ds(0, block.shape[0]), :] = block


def edge_kernel(levels, rows, field, zonal, meridional, along, tracers, after, first, last, own):
    x_points = field.shape[0] // rows

    @pl.when(in_air())
    def _():
        d = gll_matrix()
        lane = lax.broadcasted_iota(jnp.int32, (levels, field.shape[1]), 1)
        for side, (x, target) in enumerate(((0, first), (x_points - 1, last))):
            start = x - x % NODES
            along_y = jnp.dot(
                field[pl.ds(x * rows, rows), :],
                along[...],
                precision=HIGHEST,
                preferred_element_type=jnp.float32,
            )
            u = zonal[pl.ds(x * levels, levels), :]
            v = meridional[pl.ds(x * levels, levels), :]
            for f in range(rows // levels):
                at = f * levels
                along_x = sum(
                    float(d[x % NODES, a]) * field[pl.ds((start + a) * rows + at, levels), :]
                    for a in range(NODES)
                    if d[x % NODES, a] != 0
                )
                value = -(u * along_x + v * along_y[at : at + levels])
                value = smooth_lines(value, lane)
                own[side, pl.ds(at, levels), :] = value
                target[pl.ds(at, levels), :] = value.astype(jnp.bfloat16)

    @pl.when(jnp.logical_not(in_air()))
    def _():
        value = tracers[...]
        high = value.astype(jnp.bfloat16)
        low = (value - high.astype(jnp.float32)).astype(jnp.bfloat16)
        both = jnp.concatenate([high, low], axis=0)
        for target in (first, last):
            target[pl.ds(0, both.shape[0]), :] = both


def pack_kernel(own, *refs):
    received, packed = refs[:-1], refs[-1]
    count = len(refs)
    place = lax.axis_index("sec") % count
    here = pl.ds(0, packed.shape[1])
    packed[place] = own[here, :]
    for m, part in enumerate(received, 1):
        packed[(place - m + count) % count] = part[here, :]


def ocean_kernel(
    senders_in,
    live_in,
    factor_in,
    offsets_in,
    sides_in,
    mixing_in,
    tracers,
    below,
    above,
    diffused,
    chosen,
    returning,
    forcing,
    gather,
    spread,
    senders,
    live,
    factor,
    offsets,
    sides,
    mixing,
    sems,
):
    @pl.when(jnp.logical_not(in_air()))
    def _():
        copies = start_all(
            (
                (senders_in, senders),
                (live_in, live),
                (factor_in, factor),
                (offsets_in, offsets),
                (sides_in, sides),
                (mixing_in, mixing),
            ),
            sems,
        )
        cells = sides.shape[1]
        x_count = gather.shape[0] // cells
        point = lax.broadcasted_iota(jnp.int32, gather.shape, 0) // x_count
        cell = lax.broadcasted_iota(jnp.int32, gather.shape, 1)
        gather[...] = jnp.where(point == cell, 1.0, 0.0).astype(gather.dtype)
        cell = lax.broadcasted_iota(jnp.int32, spread.shape, 0)
        point = lax.broadcasted_iota(jnp.int32, spread.shape, 1) // x_count
        spread[...] = jnp.where(point == cell, 1.0, 0.0).astype(spread.dtype)
        for copy in copies:
            copy.wait()

        source = lax.broadcasted_iota(jnp.int32, (cells, cells), 0)
        target = lax.broadcasted_iota(jnp.int32, (cells, cells), 1)
        inside = jnp.zeros((cells, cells), jnp.float32)
        outside = jnp.zeros((cells, cells), jnp.float32)
        total = jnp.zeros((1, cells), jnp.float32)
        for e in range(offsets.shape[0]):
            weight = jnp.where(e < sides[...], mixing[e], 0.0)
            place = target[:1] + offsets[e]
            total = total + weight
            inside = inside + jnp.where(source == place, weight, 0.0)
            hit = (source == place - cells) | (source == place + cells)
            outside = outside + jnp.where(hit, weight, 0.0)
        inside = inside - jnp.where(source == target, total, 0.0)

        value = tracers[...]
        height = value.shape[0]
        cell = lax.broadcasted_iota(jnp.int32, value.shape, 1)
        beside = [
            h[pl.ds(0, height), :].astype(jnp.float32)
            + h[pl.ds(height, height), :].astype(jnp.float32)
            for h in (below, above)
        ]
        outer = jnp.where(cell < cells // 2, beside[1], beside[0])
        change = jnp.dot(
            jnp.concatenate([value, outer], axis=1),
            jnp.concatenate([inside, outside], axis=0),
            precision=HIGHEST,
            preferred_element_type=jnp.float32,
        )
        diffused[...] = value + DIFFUSIVITY * change

        sections = lax.axis_size("sec")
        oceans = sections // 4
        air = sections - oceans
        ocean = jnp.maximum(lax.axis_index("sec") - air, 0)
        width = chosen.shape[1]
        count = live[0, ocean]
        for k in range(senders.shape[2]):
            place = jnp.where(k < count, senders[ocean, 0, k], sections)
            section = lax.broadcasted_iota(jnp.int32, (air, width), 0)
            chosen[pl.ds(k * air, air), :] = jnp.where(section == place, 1.0, 0.0)
            block = section % (air // oceans)
            owner = (ocean + section // (air // oceans)) % oceans
            returning[pl.ds(k * air, air), :] = jnp.where(
                block * oceans + owner == place, 1.0, 0.0
            )
        tracer_count, flux_count = factor.shape
        depth = forcing.shape[0] // (tracer_count * flux_count)
        level = lax.broadcasted_iota(jnp.int32, (depth, width), 0).astype(jnp.float32)
        profile = STEP_OCEAN * jnp.exp(-0.5 * level)
        for n in range(flux_count):
            for t in range(tracer_count):
                forcing[pl.ds((n * tracer_count + t) * depth, depth), :] = factor[t, n] * profile


def field_kernel(
    levels,
    rows,
    field,
    zonal,
    meridional,
    along,
    own,
    below,
    above,
    after,
    later,
    slopes,
    held,
    sems,
):
    x_points = later.shape[0]

    @pl.when(in_air())
    def _():
        d = gll_matrix()
        lane = lax.broadcasted_iota(jnp.int32, (levels, field.shape[1]), 1)
        inner = pl.ds(rows, (x_points - 2) * rows)
        slopes[inner, :] = jnp.dot(
            field[inner, :], along[...], precision=HIGHEST, preferred_element_type=jnp.float32
        )
        copies = []
        for f in range(rows // levels):
            at = f * levels
            here = pl.ds(at, levels)
            values = {
                0: 0.5 * (own[0, here, :] + below[here, :].astype(jnp.float32)),
                x_points - 1: 0.5 * (own[1, here, :] + above[here, :].astype(jnp.float32)),
            }
            q = [field[pl.ds(x * rows + at, levels), :] for x in range(x_points)]
            for x in range(1, x_points - 1):
                start = x - x % NODES
                along_x = sum(
                    float(d[x % NODES, a]) * q[start + a]
                    for a in range(NODES)
                    if d[x % NODES, a] != 0
                )
                u = zonal[pl.ds(x * levels, levels), :]
                v = meridional[pl.ds(x * levels, levels), :]
                value = -(u * along_x + v * slopes[pl.ds(x * rows + at, levels), :])
                values[x] = smooth_lines(value, lane)
            for x in range(NODES - 1, x_points - 1, NODES):
                values[x] = values[x + 1] = 0.5 * (values[x] + values[x + 1])
            for x in range(x_points):
                held[x, here, :] = q[x] + STEP_ATMOS * values[x]
            copy = pltpu.make_async_copy(held.at[:, here, :], later.at[:, here, :], sems.at[f])
            copy.start()
            copies.append(copy)
        for copy in copies:
            copy.wait()

    @pl.when(jnp.logical_not(in_air()))
    def _():
        held[0] = jnp.zeros(held.shape[1:], jnp.float32)
        copies = start_all([(held.at[0], later.at[x]) for x in range(x_points)], sems)
        for copy in copies:
            copy.wait()


def remap_kernel(
    regrid, gather, spread, chosen, returning, forcing, diffused, *refs
):
    arrived, renewed, shares = (refs[2], refs[0], refs[1]), refs[3], refs[4:]

    @pl.when(jnp.logical_not(in_air()))
    def _():
        points, cells = gather.shape
        x_count = points // cells
        slots = regrid.shape[0] // points
        air = chosen.shape[0] // slots
        packed = refs[0].shape[1]
        flux_count = packed // x_count
        row = lax.broadcasted_iota(jnp.int32, (x_count, cells), 0)
        column = lax.broadcasted_iota(jnp.int32, (x_count, cells), 1)
        same = jnp.where(row == column % x_count, 1.0, 0.0)

        blocks = [block[s].astype(jnp.float32) for block in arrived for s in range(block.shape[0])]
        matched = None
        for k in range(slots):
            part = chosen[pl.ds(k * air, 1), :] * blocks[0]
            for s in range(1, air):
                part = part + chosen[pl.ds(k * air + s, 1), :] * blocks[s]
            product = lax.dot_general(
                part.astype(jnp.bfloat16),
                regrid[pl.ds(k * points, points), :],
                (((1,), (1,)), ((), ())),
                preferred_element_type=jnp.float32,
            )
            matched = product if matched is None else matched + product
        matched = matched * jnp.tile(same, (flux_count, x_count))
        high = matched.astype(jnp.bfloat16)
        low = (matched - high.astype(jnp.float32)).astype(jnp.bfloat16)
        summed = jnp.dot(high, gather[...], preferred_element_type=jnp.float32) + jnp.dot(
            low, gather[...], preferred_element_type=jnp.float32
        )
        ocean_flux = summed.reshape(flux_count, x_count, cells).sum(axis=1)
        height = diffused.shape[0]
        value = diffused[...]
        for n in range(flux_count):
            value = value + forcing[pl.ds(n * height, height), :] * ocean_flux[n : n + 1]
        renewed[...] = value

        top = jnp.broadcast_to(value[0:1], (x_count, cells)).astype(jnp.bfloat16)
        wide = jnp.dot(top, spread[...], preferred_element_type=jnp.float32)
        wide = (wide * jnp.tile(same, (1, x_count))).astype(jnp.bfloat16)
        back = [
            jnp.dot(wide, regrid[pl.ds(k * points, points), :], preferred_element_type=jnp.float32)
            for k in range(slots)
        ]
        count = shares[0].shape[0]
        for m, share in enumerate(shares):
            for j in range(count):
                at = m * count + j
                total = returning[pl.ds(at, 1), :] * back[0]
                for k in range(1, slots):
                    total = total + returning[pl.ds(k * air + at, 1), :] * back[k]
                share[j] = total


def add_kernel(*refs):
    count = refs[0].shape[0]
    shares, totals = refs[:-count], refs[-count:]

    @pl.when(jnp.logical_not(in_air()))
    def _():
        for j, total in enumerate(totals):
            value = shares[0][j]
            for share in shares[1:]:
                value = value + share[j]
            total[...] = value


def last_kernel(renewed, *refs):
    returned, (tracers_later, warmth) = refs[:-2], refs[-2:]
    sections = lax.axis_size("sec")
    block = lax.axis_index("sec") // (sections // 4)

    @pl.when(in_air())
    def _():
        tracers_later[...] = jnp.zeros(tracers_later.shape, jnp.float32)

    @pl.when(jnp.logical_not(in_air()))
    def _():
        tracers_later[...] = renewed[...]
        warmth[...] = jnp.zeros(warmth.shape, jnp.float32)

    for j, part in enumerate(returned):

        @pl.when(block == j)
        def _(part=part):
            warmth[...] = part[...]


def per_device(
    climate_field_table,
    zonal_wind_speed,
    meridional_wind,
    sea_warmth_field,
    exchange_law_factor,
    regrid_matrix_stack,
    entry_sender_patch,
    holder_live_total,
    marine_salinity_heat,
    adjacent_offset_lists,
    polygon_side_total,
    interface_mixing_factor,
    solute_forcing_factor,
):
    sections = lax.axis_size("sec")
    ranks = lax.axis_size("rank")
    oceans = sections // 4
    air = sections - oceans
    _, x_points, rows, y_points = climate_field_table.shape
    levels = zonal_wind_speed.shape[2]
    flux_count = exchange_law_factor.shape[0]
    _, tracer_count, depth, cells = marine_salinity_heat.shape
    slots = regrid_matrix_stack.shape[2]
    f32, bf16 = jnp.float32, jnp.bfloat16
    shape = jax.ShapeDtypeStruct

    field = climate_field_table.reshape(x_points * rows, y_points)
    zonal = zonal_wind_speed.reshape(x_points * levels, y_points)
    meridional = meridional_wind.reshape(x_points * levels, y_points)
    regrid = regrid_matrix_stack.reshape(slots * cells * x_points, y_points)
    tracers = marine_salinity_heat.reshape(tracer_count * depth, cells)
    offsets = jnp.transpose(adjacent_offset_lists, (1, 0, 2))
    mixing = jnp.transpose(interface_mixing_factor, (1, 0, 2))
    live = jnp.transpose(holder_live_total, (1, 0))

    along = np.kron(np.eye(y_points // NODES, dtype=np.float32), gll_matrix().T)
    along = jnp.asarray(along)

    fields = rows // levels
    tile = min(8, levels)
    in_place = (
        exchange_law_factor,
        climate_field_table.reshape(x_points, fields, levels, y_points),
        zonal_wind_speed[0],
        meridional_wind[0],
        sea_warmth_field,
    )
    swap_rows = max(flux_count * x_points, rows + 16)
    fluxes = pl.pallas_call(
        functools.partial(flux_kernel, levels),
        out_shape=shape((swap_rows, y_points), bf16),
        in_specs=[HBM] * len(in_place),
        out_specs=VMEM,
        scratch_shapes=[
            pltpu.SMEM(exchange_law_factor.shape, f32),
            pltpu.VMEM((x_points, fields, tile, y_points), f32),
            pltpu.VMEM((x_points, tile, y_points), f32),
            pltpu.VMEM((x_points, tile, y_points), f32),
            pltpu.VMEM((1, x_points, y_points), f32),
            pltpu.SemaphoreType.DMA((len(in_place),)),
        ],
        compiler_params=PARAMS,
        cost_estimate=cost(1),
        name="flux",
    )(*(pltpu.with_memory_space_constraint(a, pltpu.HBM) for a in in_place))
    first, last, own = pl.pallas_call(
        functools.partial(edge_kernel, levels, rows),
        out_shape=(
            shape((rows, y_points), bf16),
            shape((rows, y_points), bf16),
            shape((2, rows, y_points), f32),
        ),
        in_specs=[VMEM] * 5 + [ANY],
        out_specs=(VMEM,) * 3,
        compiler_params=PARAMS,
        cost_estimate=cost(1),
        name="edges",
    )(field, zonal, meridional, along, tracers, fluxes)
    up = [(i, (i + 1) % ranks) for i in range(ranks)]
    below = lax.ppermute(last, "rank", up)
    above = lax.ppermute(first, "rank", [(j, i) for i, j in up])

    def turned(value, m):
        pairs = [(s, s // oceans * oceans + (s + m) % oceans) for s in range(sections)]
        return lax.ppermute(value, "sec", pairs)

    def shifted(value, blocks):
        pairs = [(s, (s + blocks * oceans) % sections) for s in range(sections)]
        return lax.ppermute(value, "sec", pairs)

    received = [turned(fluxes, m) for m in range(1, oceans)]
    packed = pl.pallas_call(
        pack_kernel,
        out_shape=shape((oceans, flux_count * x_points, y_points), bf16),
        in_specs=[VMEM] * oceans,
        out_specs=VMEM,
        compiler_params=PARAMS,
        cost_estimate=cost(0.2),
        name="pack",
    )(fluxes, *received)
    arrived = [shifted(packed, 3 - block) for block in range(3)]

    from_memory = (
        entry_sender_patch,
        live,
        solute_forcing_factor,
        offsets,
        polygon_side_total,
        mixing,
    )
    diffused, chosen, returning, forcing, gather, spread = pl.pallas_call(
        ocean_kernel,
        out_shape=(
            shape(tracers.shape, f32),
            shape((slots * air, y_points), f32),
            shape((slots * air, y_points), f32),
            shape((flux_count * tracer_count * depth, cells), f32),
            shape((x_points * cells, cells), bf16),
            shape((cells, x_points * cells), bf16),
        ),
        in_specs=[HBM] * 6 + [VMEM] * 3,
        out_specs=(VMEM,) * 6,
        scratch_shapes=[
            (pltpu.SMEM if i < 3 else pltpu.VMEM)(a.shape, a.dtype)
            for i, a in enumerate(from_memory)
        ]
        + [pltpu.SemaphoreType.DMA((len(from_memory),))],
        compiler_params=PARAMS,
        cost_estimate=cost(1),
        name="ocean",
    )(
        *(pltpu.with_memory_space_constraint(a, pltpu.HBM) for a in from_memory),
        tracers,
        below,
        above,
    )

    renewed, *shares = pl.pallas_call(
        remap_kernel,
        out_shape=(shape(tracers.shape, f32),)
        + (shape((air // oceans, x_points, y_points), f32),) * oceans,
        in_specs=[VMEM] * 10,
        out_specs=(VMEM,) * (1 + oceans),
        compiler_params=PARAMS,
        cost_estimate=cost(1),
        name="remap",
    )(regrid, gather, spread, chosen, returning, forcing, diffused, arrived[1], arrived[2], arrived[0])
    shares = shares[:1] + [turned(share, m) for m, share in enumerate(shares[1:], 1)]
    totals = pl.pallas_call(
        add_kernel,
        out_shape=(shape((x_points, y_points), f32),) * (air // oceans),
        in_specs=[VMEM] * oceans,
        out_specs=(VMEM,) * (air // oceans),
        compiler_params=PARAMS,
        cost_estimate=cost(0.3),
        name="add",
    )(*shares)
    returned = [shifted(total, block + 1) for block, total in enumerate(totals)]
    later = pl.pallas_call(
        functools.partial(field_kernel, levels, rows),
        out_shape=shape((x_points, rows, y_points), f32),
        in_specs=[VMEM] * 7 + [ANY],
        out_specs=HBM,
        scratch_shapes=[
            pltpu.VMEM(field.shape, f32),
            pltpu.VMEM((x_points, rows, y_points), f32),
            pltpu.SemaphoreType.DMA((max(fields, x_points),)),
        ],
        compiler_params=PARAMS,
        cost_estimate=cost(3),
        name="field",
    )(field, zonal, meridional, along, own, below, above, totals[1])
    tracers_later, warmth = pl.pallas_call(
        last_kernel,
        out_shape=(shape(tracers.shape, f32), shape((x_points, y_points), f32)),
        in_specs=[VMEM] * (1 + len(returned)),
        out_specs=(VMEM,) * 2,
        compiler_params=PARAMS,
        cost_estimate=cost(0.5),
        name="last",
    )(renewed, *returned)
    return (
        later.reshape(climate_field_table.shape),
        tracers_later.reshape(marine_salinity_heat.shape),
        warmth[None],
    )


def solution(mesh):
    return jax.shard_map(
        per_device,
        mesh=mesh,
        in_specs=(
            P("sec", "rank", None, None),
            P("sec", "rank", None, None),
            P("sec", "rank", None, None),
            P("sec", "rank", None),
            P(),
            P("sec", "rank", None, None, None, None),
            P(None, "rank", None),
            P(None, "rank"),
            P("sec", None, None, "rank"),
            P("sec", None, "rank"),
            P("sec", "rank"),
            P("sec", None, "rank"),
            P(),
        ),
        out_specs=(
            P("sec", "rank", None, None),
            P("sec", None, None, "rank"),
            P("sec", "rank", None),
        ),
        check_vma=False,
    )
```

```python
import functools

import jax
import jax.numpy as jnp
import numpy as np
from jax import lax
from jax.experimental import pallas as pl
from jax.experimental.pallas import tpu as pltpu
from jax.sharding import PartitionSpec as P

STEP_ATMOS = 0.05
DIFFUSIVITY = 0.05
STEP_OCEAN = 0.5
NODES = 4

VMEM = pl.BlockSpec(memory_space=pltpu.VMEM)
ANY = pl.BlockSpec(memory_space=pl.ANY)
HBM = pl.BlockSpec(memory_space=pltpu.HBM)
SMEM = pl.BlockSpec(memory_space=pltpu.SMEM)
PARAMS = pltpu.CompilerParams(vmem_limit_bytes=8 * 2**20)
HIGHEST = lax.Precision.HIGHEST


def gll_matrix():
    nodes = np.array([-1.0, -1.0 / np.sqrt(5.0), 1.0 / np.sqrt(5.0), 1.0])
    legendre = (5.0 * nodes**3 - 3.0 * nodes) / 2.0
    matrix = np.zeros((4, 4))
    for i in range(4):
        for j in range(4):
            if i != j:
                matrix[i, j] = legendre[i] / (legendre[j] * (nodes[i] - nodes[j]))
    matrix[0, 0] = -3.0
    matrix[3, 3] = 3.0
    return matrix.astype(np.float32)


def cost(microseconds):
    return pl.CostEstimate(
        flops=0, bytes_accessed=int(microseconds * 3_000_000), transcendentals=0
    )


def in_air():
    sections = lax.axis_size("sec")
    return lax.axis_index("sec") < sections - sections // 4


def smooth_lines(value, lane):
    width = value.shape[-1]
    right = pltpu.roll(value, width - 1, value.ndim - 1)
    left = pltpu.roll(value, 1, value.ndim - 1)
    at_end = (lane % NODES == NODES - 1) & (lane < width - 1)
    at_start = (lane % NODES == 0) & (lane > 0)
    partner = jnp.where(at_end, right, jnp.where(at_start, left, value))
    return 0.5 * (value + partner)


def start_all(pairs, sems):
    copies = [
        pltpu.make_async_copy(source, target, sems.at[i])
        for i, (source, target) in enumerate(pairs)
    ]
    for copy in copies:
        copy.start()
    return copies


def flux_kernel(
    levels, law_in, field_in, zonal_in, meridional_in, sea_in, sent, law, field, zonal, meridional, sea, sems
):
    @pl.when(in_air())
    def _():
        lowest = pl.ds(0, zonal.shape[1])
        copies = start_all(
            (
                (field_in.at[:, :, lowest, :], field),
                (zonal_in.at[:, lowest, :], zonal),
                (meridional_in.at[:, lowest, :], meridional),
                (sea_in, sea),
                (law_in, law),
            ),
            sems,
        )
        for copy in copies:
            copy.wait()
        flux_count, columns = law.shape
        ground = [field[:, f, 0, :] for f in range(columns - 1)] + [sea[0]]
        speed = jnp.sqrt(1.0 + zonal[:, 0, :] ** 2 + meridional[:, 0, :] ** 2)
        parts = []
        for n in range(flux_count):
            total = law[n, 0] * ground[0]
            for f in range(1, columns):
                total = total + law[n, f] * ground[f]
            parts.append(speed * total)
        block = jnp.concatenate(parts, axis=0).astype(jnp.bfloat16)
        sent[pl.ds(0, block.shape[0]), :] = block


def edge_kernel(levels, rows, field, zonal, meridional, along, tracers, after, first, last, own):
    x_points = field.shape[0] // rows

    @pl.when(in_air())
    def _():
        d = gll_matrix()
        lane = lax.broadcasted_iota(jnp.int32, (levels, field.shape[1]), 1)
        for side, (x, target) in enumerate(((0, first), (x_points - 1, last))):
            start = x - x % NODES
            along_y = jnp.dot(
                field[pl.ds(x * rows, rows), :],
                along[...],
                precision=HIGHEST,
                preferred_element_type=jnp.float32,
            )
            u = zonal[pl.ds(x * levels, levels), :]
            v = meridional[pl.ds(x * levels, levels), :]
            for f in range(rows // levels):
                at = f * levels
                along_x = sum(
                    float(d[x % NODES, a]) * field[pl.ds((start + a) * rows + at, levels), :]
                    for a in range(NODES)
                    if d[x % NODES, a] != 0
                )
                value = -(u * along_x + v * along_y[at : at + levels])
                value = smooth_lines(value, lane)
                own[side, pl.ds(at, levels), :] = value
                target[pl.ds(at, levels), :] = value.astype(jnp.bfloat16)

    @pl.when(jnp.logical_not(in_air()))
    def _():
        value = tracers[...]
        high = value.astype(jnp.bfloat16)
        low = (value - high.astype(jnp.float32)).astype(jnp.bfloat16)
        both = jnp.concatenate([high, low], axis=0)
        for target in (first, last):
            target[pl.ds(0, both.shape[0]), :] = both


def pack_kernel(own, *refs):
    received, packed = refs[:-1], refs[-1]
    count = len(refs)
    place = lax.axis_index("sec") % count
    here = pl.ds(0, packed.shape[1])
    packed[place] = own[here, :]
    for m, part in enumerate(received, 1):
        packed[(place - m + count) % count] = part[here, :]


def middle_kernel(
    levels,
    rows,
    field,
    zonal,
    meridional,
    along,
    own,
    below,
    above,
    tracers,
    senders_in,
    live_in,
    factor_in,
    offsets_in,
    sides_in,
    mixing_in,
    later,
    diffused,
    chosen,
    returning,
    forcing,
    gather,
    spread,
    slopes,
    held,
    senders,
    live,
    factor,
    offsets,
    sides,
    mixing,
    sems,
    load_sems,
):
    x_points = later.shape[0]

    @pl.when(in_air())
    def _():
        d = gll_matrix()
        lane = lax.broadcasted_iota(jnp.int32, (levels, field.shape[1]), 1)
        inner = pl.ds(rows, (x_points - 2) * rows)
        slopes[inner, :] = jnp.dot(
            field[inner, :], along[...], precision=HIGHEST, preferred_element_type=jnp.float32
        )
        copies = []
        for f in range(rows // levels):
            at = f * levels
            here = pl.ds(at, levels)
            values = {
                0: 0.5 * (own[0, here, :] + below[here, :].astype(jnp.float32)),
                x_points - 1: 0.5 * (own[1, here, :] + above[here, :].astype(jnp.float32)),
            }
            q = [field[pl.ds(x * rows + at, levels), :] for x in range(x_points)]
            for x in range(1, x_points - 1):
                start = x - x % NODES
                along_x = sum(
                    float(d[x % NODES, a]) * q[start + a]
                    for a in range(NODES)
                    if d[x % NODES, a] != 0
                )
                u = zonal[pl.ds(x * levels, levels), :]
                v = meridional[pl.ds(x * levels, levels), :]
                value = -(u * along_x + v * slopes[pl.ds(x * rows + at, levels), :])
                values[x] = smooth_lines(value, lane)
            for x in range(NODES - 1, x_points - 1, NODES):
                values[x] = values[x + 1] = 0.5 * (values[x] + values[x + 1])
            for x in range(x_points):
                held[x, here, :] = q[x] + STEP_ATMOS * values[x]
            copy = pltpu.make_async_copy(held.at[:, here, :], later.at[:, here, :], sems.at[f])
            copy.start()
            copies.append(copy)
        for copy in copies:
            copy.wait()

    @pl.when(jnp.logical_not(in_air()))
    def _():
        loads = start_all(
            (
                (senders_in, senders),
                (live_in, live),
                (factor_in, factor),
                (offsets_in, offsets),
                (sides_in, sides),
                (mixing_in, mixing),
            ),
            load_sems,
        )
        held[0] = jnp.zeros(held.shape[1:], jnp.float32)
        copies = start_all([(held.at[0], later.at[x]) for x in range(x_points)], sems)
        cells = sides.shape[1]
        x_count = gather.shape[0] // cells
        point = lax.broadcasted_iota(jnp.int32, gather.shape, 0) // x_count
        cell = lax.broadcasted_iota(jnp.int32, gather.shape, 1)
        gather[...] = jnp.where(point == cell, 1.0, 0.0).astype(gather.dtype)
        cell = lax.broadcasted_iota(jnp.int32, spread.shape, 0)
        point = lax.broadcasted_iota(jnp.int32, spread.shape, 1) // x_count
        spread[...] = jnp.where(point == cell, 1.0, 0.0).astype(spread.dtype)
        for load in loads:
            load.wait()

        source = lax.broadcasted_iota(jnp.int32, (cells, cells), 0)
        target = lax.broadcasted_iota(jnp.int32, (cells, cells), 1)
        inside = jnp.zeros((cells, cells), jnp.float32)
        outside = jnp.zeros((cells, cells), jnp.float32)
        total = jnp.zeros((1, cells), jnp.float32)
        for e in range(offsets.shape[0]):
            weight = jnp.where(e < sides[...], mixing[e], 0.0)
            place = target[:1] + offsets[e]
            total = total + weight
            inside = inside + jnp.where(source == place, weight, 0.0)
            hit = (source == place - cells) | (source == place + cells)
            outside = outside + jnp.where(hit, weight, 0.0)
        inside = inside - jnp.where(source == target, total, 0.0)

        value = tracers[...]
        height = value.shape[0]
        cell = lax.broadcasted_iota(jnp.int32, value.shape, 1)
        beside = [
            h[pl.ds(0, height), :].astype(jnp.float32)
            + h[pl.ds(height, height), :].astype(jnp.float32)
            for h in (below, above)
        ]
        outer = jnp.where(cell < cells // 2, beside[1], beside[0])
        change = jnp.dot(
            jnp.concatenate([value, outer], axis=1),
            jnp.concatenate([inside, outside], axis=0),
            precision=HIGHEST,
            preferred_element_type=jnp.float32,
        )
        diffused[...] = value + DIFFUSIVITY * change

        sections = lax.axis_size("sec")
        oceans = sections // 4
        air = sections - oceans
        ocean = jnp.maximum(lax.axis_index("sec") - air, 0)
        width = chosen.shape[1]
        count = live[0, ocean]
        for k in range(senders.shape[2]):
            place = jnp.where(k < count, senders[ocean, 0, k], sections)
            section = lax.broadcasted_iota(jnp.int32, (air, width), 0)
            chosen[pl.ds(k * air, air), :] = jnp.where(section == place, 1.0, 0.0)
            block = section % (air // oceans)
            owner = (ocean + section // (air // oceans)) % oceans
            returning[pl.ds(k * air, air), :] = jnp.where(
                block * oceans + owner == place, 1.0, 0.0
            )
        tracer_count, flux_count = factor.shape
        depth = forcing.shape[0] // (tracer_count * flux_count)
        level = lax.broadcasted_iota(jnp.int32, (depth, width), 0).astype(jnp.float32)
        profile = STEP_OCEAN * jnp.exp(-0.5 * level)
        for n in range(flux_count):
            for t in range(tracer_count):
                forcing[pl.ds((n * tracer_count + t) * depth, depth), :] = factor[t, n] * profile
        for copy in copies:
            copy.wait()


def remap_kernel(
    regrid, gather, spread, chosen, returning, forcing, diffused, *refs
):
    arrived, renewed, shares = (refs[2], refs[0], refs[1]), refs[3], refs[4:]

    @pl.when(jnp.logical_not(in_air()))
    def _():
        points, cells = gather.shape
        x_count = points // cells
        slots = regrid.shape[0] // points
        air = chosen.shape[0] // slots
        packed = refs[0].shape[1]
        flux_count = packed // x_count
        row = lax.broadcasted_iota(jnp.int32, (x_count, cells), 0)
        column = lax.broadcasted_iota(jnp.int32, (x_count, cells), 1)
        same = jnp.where(row == column % x_count, 1.0, 0.0)

        blocks = [block[s].astype(jnp.float32) for block in arrived for s in range(block.shape[0])]
        matched = None
        for k in range(slots):
            part = chosen[pl.ds(k * air, 1), :] * blocks[0]
            for s in range(1, air):
                part = part + chosen[pl.ds(k * air + s, 1), :] * blocks[s]
            product = lax.dot_general(
                part.astype(jnp.bfloat16),
                regrid[pl.ds(k * points, points), :],
                (((1,), (1,)), ((), ())),
                preferred_element_type=jnp.float32,
            )
            matched = product if matched is None else matched + product
        matched = matched * jnp.tile(same, (flux_count, x_count))
        high = matched.astype(jnp.bfloat16)
        low = (matched - high.astype(jnp.float32)).astype(jnp.bfloat16)
        summed = jnp.dot(high, gather[...], preferred_element_type=jnp.float32) + jnp.dot(
            low, gather[...], preferred_element_type=jnp.float32
        )
        ocean_flux = summed.reshape(flux_count, x_count, cells).sum(axis=1)
        height = diffused.shape[0]
        value = diffused[...]
        for n in range(flux_count):
            value = value + forcing[pl.ds(n * height, height), :] * ocean_flux[n : n + 1]
        renewed[...] = value

        top = jnp.broadcast_to(value[0:1], (x_count, cells)).astype(jnp.bfloat16)
        wide = jnp.dot(top, spread[...], preferred_element_type=jnp.float32)
        wide = (wide * jnp.tile(same, (1, x_count))).astype(jnp.bfloat16)
        back = [
            jnp.dot(wide, regrid[pl.ds(k * points, points), :], preferred_element_type=jnp.float32)
            for k in range(slots)
        ]
        count = shares[0].shape[0]
        for m, share in enumerate(shares):
            for j in range(count):
                at = m * count + j
                total = returning[pl.ds(at, 1), :] * back[0]
                for k in range(1, slots):
                    total = total + returning[pl.ds(k * air + at, 1), :] * back[k]
                share[j] = total


def add_kernel(*refs):
    count = refs[0].shape[0]
    shares, totals = refs[:-count], refs[-count:]

    @pl.when(jnp.logical_not(in_air()))
    def _():
        for j, total in enumerate(totals):
            value = shares[0][j]
            for share in shares[1:]:
                value = value + share[j]
            total[...] = value


def last_kernel(renewed, *refs):
    returned, (tracers_later, warmth) = refs[:-2], refs[-2:]
    sections = lax.axis_size("sec")
    block = lax.axis_index("sec") // (sections // 4)

    @pl.when(in_air())
    def _():
        tracers_later[...] = jnp.zeros(tracers_later.shape, jnp.float32)

    @pl.when(jnp.logical_not(in_air()))
    def _():
        tracers_later[...] = renewed[...]
        warmth[...] = jnp.zeros(warmth.shape, jnp.float32)

    for j, part in enumerate(returned):

        @pl.when(block == j)
        def _(part=part):
            warmth[...] = part[...]


def per_device(
    climate_field_table,
    zonal_wind_speed,
    meridional_wind,
    sea_warmth_field,
    exchange_law_factor,
    regrid_matrix_stack,
    entry_sender_patch,
    holder_live_total,
    marine_salinity_heat,
    adjacent_offset_lists,
    polygon_side_total,
    interface_mixing_factor,
    solute_forcing_factor,
):
    sections = lax.axis_size("sec")
    ranks = lax.axis_size("rank")
    oceans = sections // 4
    air = sections - oceans
    _, x_points, rows, y_points = climate_field_table.shape
    levels = zonal_wind_speed.shape[2]
    flux_count = exchange_law_factor.shape[0]
    _, tracer_count, depth, cells = marine_salinity_heat.shape
    slots = regrid_matrix_stack.shape[2]
    f32, bf16 = jnp.float32, jnp.bfloat16
    shape = jax.ShapeDtypeStruct

    field = climate_field_table.reshape(x_points * rows, y_points)
    zonal = zonal_wind_speed.reshape(x_points * levels, y_points)
    meridional = meridional_wind.reshape(x_points * levels, y_points)
    regrid = regrid_matrix_stack.reshape(slots * cells * x_points, y_points)
    tracers = marine_salinity_heat.reshape(tracer_count * depth, cells)
    offsets = jnp.transpose(adjacent_offset_lists, (1, 0, 2))
    mixing = jnp.transpose(interface_mixing_factor, (1, 0, 2))
    live = jnp.transpose(holder_live_total, (1, 0))

    along = np.kron(np.eye(y_points // NODES, dtype=np.float32), gll_matrix().T)
    along = jnp.asarray(along)

    fields = rows // levels
    tile = min(8, levels)
    in_place = (
        exchange_law_factor,
        climate_field_table.reshape(x_points, fields, levels, y_points),
        zonal_wind_speed[0],
        meridional_wind[0],
        sea_warmth_field,
    )
    swap_rows = max(flux_count * x_points, rows + 16)
    fluxes = pl.pallas_call(
        functools.partial(flux_kernel, levels),
        out_shape=shape((swap_rows, y_points), bf16),
        in_specs=[HBM] * len(in_place),
        out_specs=VMEM,
        scratch_shapes=[
            pltpu.SMEM(exchange_law_factor.shape, f32),
            pltpu.VMEM((x_points, fields, tile, y_points), f32),
            pltpu.VMEM((x_points, tile, y_points), f32),
            pltpu.VMEM((x_points, tile, y_points), f32),
            pltpu.VMEM((1, x_points, y_points), f32),
            pltpu.SemaphoreType.DMA((len(in_place),)),
        ],
        compiler_params=PARAMS,
        cost_estimate=cost(1),
        name="flux",
    )(*(pltpu.with_memory_space_constraint(a, pltpu.HBM) for a in in_place))
    first, last, own = pl.pallas_call(
        functools.partial(edge_kernel, levels, rows),
        out_shape=(
            shape((rows, y_points), bf16),
            shape((rows, y_points), bf16),
            shape((2, rows, y_points), f32),
        ),
        in_specs=[VMEM] * 5 + [ANY],
        out_specs=(VMEM,) * 3,
        compiler_params=PARAMS,
        cost_estimate=cost(1),
        name="edges",
    )(field, zonal, meridional, along, tracers, fluxes)
    up = [(i, (i + 1) % ranks) for i in range(ranks)]
    below = lax.ppermute(last, "rank", up)
    above = lax.ppermute(first, "rank", [(j, i) for i, j in up])

    def turned(value, m):
        pairs = [(s, s // oceans * oceans + (s + m) % oceans) for s in range(sections)]
        return lax.ppermute(value, "sec", pairs)

    def paired(value, mask):
        pairs = [
            (s, (s // oceans ^ mask) * oceans + s % oceans) for s in range(sections)
        ]
        return lax.ppermute(value, "sec", pairs)

    received = [turned(fluxes, m) for m in range(1, oceans)]
    packed = pl.pallas_call(
        pack_kernel,
        out_shape=shape((oceans, flux_count * x_points, y_points), bf16),
        in_specs=[VMEM] * oceans,
        out_specs=VMEM,
        compiler_params=PARAMS,
        cost_estimate=cost(0.2),
        name="pack",
    )(fluxes, *received)
    arrived = [paired(packed, 3 ^ block) for block in range(3)]

    from_memory = (
        entry_sender_patch,
        live,
        solute_forcing_factor,
        offsets,
        polygon_side_total,
        mixing,
    )
    later, diffused, chosen, returning, forcing, gather, spread = pl.pallas_call(
        functools.partial(middle_kernel, levels, rows),
        out_shape=(
            shape((x_points, rows, y_points), f32),
            shape(tracers.shape, f32),
            shape((slots * air, y_points), f32),
            shape((slots * air, y_points), f32),
            shape((flux_count * tracer_count * depth, cells), f32),
            shape((x_points * cells, cells), bf16),
            shape((cells, x_points * cells), bf16),
        ),
        in_specs=[VMEM] * 8 + [HBM] * 6,
        out_specs=(HBM,) + (VMEM,) * 6,
        scratch_shapes=[
            pltpu.VMEM(field.shape, f32),
            pltpu.VMEM((x_points, rows, y_points), f32),
        ]
        + [
            (pltpu.SMEM if i < 3 else pltpu.VMEM)(a.shape, a.dtype)
            for i, a in enumerate(from_memory)
        ]
        + [
            pltpu.SemaphoreType.DMA((max(fields, x_points),)),
            pltpu.SemaphoreType.DMA((len(from_memory),)),
        ],
        compiler_params=PARAMS,
        cost_estimate=cost(1),
        name="middle",
    )(
        field,
        zonal,
        meridional,
        along,
        own,
        below,
        above,
        tracers,
        *(pltpu.with_memory_space_constraint(a, pltpu.HBM) for a in from_memory),
    )

    renewed, *shares = pl.pallas_call(
        remap_kernel,
        out_shape=(shape(tracers.shape, f32),)
        + (shape((air // oceans, x_points, y_points), f32),) * oceans,
        in_specs=[VMEM] * 10,
        out_specs=(VMEM,) * (1 + oceans),
        compiler_params=PARAMS,
        cost_estimate=cost(1),
        name="remap",
    )(regrid, gather, spread, chosen, returning, forcing, diffused, arrived[1], arrived[2], arrived[0])
    shares = shares[:1] + [turned(share, m) for m, share in enumerate(shares[1:], 1)]
    totals = pl.pallas_call(
        add_kernel,
        out_shape=(shape((x_points, y_points), f32),) * (air // oceans),
        in_specs=[VMEM] * oceans,
        out_specs=(VMEM,) * (air // oceans),
        compiler_params=PARAMS,
        cost_estimate=cost(0.3),
        name="add",
    )(*shares)
    returned = [paired(total, 3 ^ block) for block, total in enumerate(totals)]
    tracers_later, warmth = pl.pallas_call(
        last_kernel,
        out_shape=(shape(tracers.shape, f32), shape((x_points, y_points), f32)),
        in_specs=[VMEM] * (1 + len(returned)),
        out_specs=(VMEM,) * 2,
        compiler_params=PARAMS,
        cost_estimate=cost(0.5),
        name="last",
    )(renewed, *returned)
    return (
        later.reshape(climate_field_table.shape),
        tracers_later.reshape(marine_salinity_heat.shape),
        warmth[None],
    )


def solution(mesh):
    return jax.shard_map(
        per_device,
        mesh=mesh,
        in_specs=(
            P("sec", "rank", None, None),
            P("sec", "rank", None, None),
            P("sec", "rank", None, None),
            P("sec", "rank", None),
            P(),
            P("sec", "rank", None, None, None, None),
            P(None, "rank", None),
            P(None, "rank"),
            P("sec", None, None, "rank"),
            P("sec", None, "rank"),
            P("sec", "rank"),
            P("sec", None, "rank"),
            P(),
        ),
        out_specs=(
            P("sec", "rank", None, None),
            P("sec", None, None, "rank"),
            P("sec", "rank", None),
        ),
        check_vma=False,
    )
```

```python
import functools

import jax
import jax.numpy as jnp
import numpy as np
from jax import lax
from jax.experimental import pallas as pl
from jax.experimental.pallas import tpu as pltpu
from jax.sharding import PartitionSpec as P

STEP_ATMOS = 0.05
DIFFUSIVITY = 0.05
STEP_OCEAN = 0.5
NODES = 4

VMEM = pl.BlockSpec(memory_space=pltpu.VMEM)
ANY = pl.BlockSpec(memory_space=pl.ANY)
HBM = pl.BlockSpec(memory_space=pltpu.HBM)
SMEM = pl.BlockSpec(memory_space=pltpu.SMEM)
PARAMS = pltpu.CompilerParams(vmem_limit_bytes=8 * 2**20)
HIGHEST = lax.Precision.HIGHEST


def gll_matrix():
    nodes = np.array([-1.0, -1.0 / np.sqrt(5.0), 1.0 / np.sqrt(5.0), 1.0])
    legendre = (5.0 * nodes**3 - 3.0 * nodes) / 2.0
    matrix = np.zeros((4, 4))
    for i in range(4):
        for j in range(4):
            if i != j:
                matrix[i, j] = legendre[i] / (legendre[j] * (nodes[i] - nodes[j]))
    matrix[0, 0] = -3.0
    matrix[3, 3] = 3.0
    return matrix.astype(np.float32)


def cost(microseconds):
    return pl.CostEstimate(
        flops=0, bytes_accessed=int(microseconds * 3_000_000), transcendentals=0
    )


def in_air():
    sections = lax.axis_size("sec")
    return lax.axis_index("sec") < sections - sections // 4


def smooth_lines(value, lane):
    width = value.shape[-1]
    right = pltpu.roll(value, width - 1, value.ndim - 1)
    left = pltpu.roll(value, 1, value.ndim - 1)
    at_end = (lane % NODES == NODES - 1) & (lane < width - 1)
    at_start = (lane % NODES == 0) & (lane > 0)
    partner = jnp.where(at_end, right, jnp.where(at_start, left, value))
    return 0.5 * (value + partner)


def start_all(pairs, sems):
    copies = [
        pltpu.make_async_copy(source, target, sems.at[i])
        for i, (source, target) in enumerate(pairs)
    ]
    for copy in copies:
        copy.start()
    return copies


def flux_kernel(
    levels, law_in, field_in, zonal_in, meridional_in, sea_in, sent, law, field, zonal, meridional, sea, sems
):
    @pl.when(in_air())
    def _():
        lowest = pl.ds(0, zonal.shape[1])
        copies = start_all(
            (
                (field_in.at[:, :, lowest, :], field),
                (zonal_in.at[:, lowest, :], zonal),
                (meridional_in.at[:, lowest, :], meridional),
                (sea_in, sea),
                (law_in, law),
            ),
            sems,
        )
        for copy in copies:
            copy.wait()
        flux_count, columns = law.shape
        ground = [field[:, f, 0, :] for f in range(columns - 1)] + [sea[0]]
        speed = jnp.sqrt(1.0 + zonal[:, 0, :] ** 2 + meridional[:, 0, :] ** 2)
        parts = []
        for n in range(flux_count):
            total = law[n, 0] * ground[0]
            for f in range(1, columns):
                total = total + law[n, f] * ground[f]
            parts.append(speed * total)
        block = jnp.concatenate(parts, axis=0).astype(jnp.bfloat16)
        sent[pl.ds(0, block.shape[0]), :] = block


def edge_kernel(levels, rows, field, zonal, meridional, along, tracers, after, first, last, own):
    x_points = field.shape[0] // rows

    @pl.when(in_air())
    def _():
        d = gll_matrix()
        lane = lax.broadcasted_iota(jnp.int32, (levels, field.shape[1]), 1)
        for side, (x, target) in enumerate(((0, first), (x_points - 1, last))):
            start = x - x % NODES
            along_y = jnp.dot(
                field[pl.ds(x * rows, rows), :],
                along[...],
                precision=HIGHEST,
                preferred_element_type=jnp.float32,
            )
            u = zonal[pl.ds(x * levels, levels), :]
            v = meridional[pl.ds(x * levels, levels), :]
            for f in range(rows // levels):
                at = f * levels
                along_x = sum(
                    float(d[x % NODES, a]) * field[pl.ds((start + a) * rows + at, levels), :]
                    for a in range(NODES)
                    if d[x % NODES, a] != 0
                )
                value = -(u * along_x + v * along_y[at : at + levels])
                value = smooth_lines(value, lane)
                own[side, pl.ds(at, levels), :] = value
                target[pl.ds(at, levels), :] = value.astype(jnp.bfloat16)

    @pl.when(jnp.logical_not(in_air()))
    def _():
        value = tracers[...]
        high = value.astype(jnp.bfloat16)
        low = (value - high.astype(jnp.float32)).astype(jnp.bfloat16)
        both = jnp.concatenate([high, low], axis=0)
        for target in (first, last):
            target[pl.ds(0, both.shape[0]), :] = both


def pack_kernel(own, *refs):
    received, packed = refs[:-1], refs[-1]
    count = len(refs)
    place = lax.axis_index("sec") % count
    here = pl.ds(0, packed.shape[1])
    packed[place] = own[here, :]
    for m, part in enumerate(received, 1):
        packed[(place - m + count) % count] = part[here, :]


def join_kernel(own, received, packed):
    count = own.shape[0]
    odd = lax.axis_index("sec") // count % 2
    packed[pl.ds(odd * count, count)] = own[...]
    packed[pl.ds((1 - odd) * count, count)] = received[...]


def middle_kernel(
    levels,
    rows,
    field,
    zonal,
    meridional,
    along,
    own,
    below,
    above,
    tracers,
    senders_in,
    live_in,
    factor_in,
    offsets_in,
    sides_in,
    mixing_in,
    later,
    diffused,
    chosen,
    returning,
    forcing,
    gather,
    spread,
    slopes,
    held,
    senders,
    live,
    factor,
    offsets,
    sides,
    mixing,
    sems,
    load_sems,
):
    x_points = later.shape[0]

    @pl.when(in_air())
    def _():
        d = gll_matrix()
        lane = lax.broadcasted_iota(jnp.int32, (levels, field.shape[1]), 1)
        inner = pl.ds(rows, (x_points - 2) * rows)
        slopes[inner, :] = jnp.dot(
            field[inner, :], along[...], precision=HIGHEST, preferred_element_type=jnp.float32
        )
        copies = []
        for f in range(rows // levels):
            at = f * levels
            here = pl.ds(at, levels)
            values = {
                0: 0.5 * (own[0, here, :] + below[here, :].astype(jnp.float32)),
                x_points - 1: 0.5 * (own[1, here, :] + above[here, :].astype(jnp.float32)),
            }
            q = [field[pl.ds(x * rows + at, levels), :] for x in range(x_points)]
            for x in range(1, x_points - 1):
                start = x - x % NODES
                along_x = sum(
                    float(d[x % NODES, a]) * q[start + a]
                    for a in range(NODES)
                    if d[x % NODES, a] != 0
                )
                u = zonal[pl.ds(x * levels, levels), :]
                v = meridional[pl.ds(x * levels, levels), :]
                value = -(u * along_x + v * slopes[pl.ds(x * rows + at, levels), :])
                values[x] = smooth_lines(value, lane)
            for x in range(NODES - 1, x_points - 1, NODES):
                values[x] = values[x + 1] = 0.5 * (values[x] + values[x + 1])
            for x in range(x_points):
                held[x, here, :] = q[x] + STEP_ATMOS * values[x]
            copy = pltpu.make_async_copy(held.at[:, here, :], later.at[:, here, :], sems.at[f])
            copy.start()
            copies.append(copy)
        for copy in copies:
            copy.wait()

    @pl.when(jnp.logical_not(in_air()))
    def _():
        loads = start_all(
            (
                (senders_in, senders),
                (live_in, live),
                (factor_in, factor),
                (offsets_in, offsets),
                (sides_in, sides),
                (mixing_in, mixing),
            ),
            load_sems,
        )
        held[0] = jnp.zeros(held.shape[1:], jnp.float32)
        copies = start_all([(held.at[0], later.at[x]) for x in range(x_points)], sems)
        cells = sides.shape[1]
        x_count = gather.shape[0] // cells
        point = lax.broadcasted_iota(jnp.int32, gather.shape, 0) // x_count
        cell = lax.broadcasted_iota(jnp.int32, gather.shape, 1)
        gather[...] = jnp.where(point == cell, 1.0, 0.0).astype(gather.dtype)
        cell = lax.broadcasted_iota(jnp.int32, spread.shape, 0)
        point = lax.broadcasted_iota(jnp.int32, spread.shape, 1) // x_count
        spread[...] = jnp.where(point == cell, 1.0, 0.0).astype(spread.dtype)
        for load in loads:
            load.wait()

        source = lax.broadcasted_iota(jnp.int32, (cells, cells), 0)
        target = lax.broadcasted_iota(jnp.int32, (cells, cells), 1)
        inside = jnp.zeros((cells, cells), jnp.float32)
        outside = jnp.zeros((cells, cells), jnp.float32)
        total = jnp.zeros((1, cells), jnp.float32)
        for e in range(offsets.shape[0]):
            weight = jnp.where(e < sides[...], mixing[e], 0.0)
            place = target[:1] + offsets[e]
            total = total + weight
            inside = inside + jnp.where(source == place, weight, 0.0)
            hit = (source == place - cells) | (source == place + cells)
            outside = outside + jnp.where(hit, weight, 0.0)
        inside = inside - jnp.where(source == target, total, 0.0)

        value = tracers[...]
        height = value.shape[0]
        cell = lax.broadcasted_iota(jnp.int32, value.shape, 1)
        beside = [
            h[pl.ds(0, height), :].astype(jnp.float32)
            + h[pl.ds(height, height), :].astype(jnp.float32)
            for h in (below, above)
        ]
        outer = jnp.where(cell < cells // 2, beside[1], beside[0])
        change = jnp.dot(
            jnp.concatenate([value, outer], axis=1),
            jnp.concatenate([inside, outside], axis=0),
            precision=HIGHEST,
            preferred_element_type=jnp.float32,
        )
        diffused[...] = value + DIFFUSIVITY * change

        sections = lax.axis_size("sec")
        oceans = sections // 4
        air = sections - oceans
        ocean = jnp.maximum(lax.axis_index("sec") - air, 0)
        width = chosen.shape[1]
        count = live[0, ocean]
        for k in range(senders.shape[2]):
            place = jnp.where(k < count, senders[ocean, 0, k], sections)
            section = lax.broadcasted_iota(jnp.int32, (air, width), 0)
            chosen[pl.ds(k * air, air), :] = jnp.where(section == place, 1.0, 0.0)
            block = section % (air // oceans)
            owner = (ocean + section // (air // oceans)) % oceans
            returning[pl.ds(k * air, air), :] = jnp.where(
                block * oceans + owner == place, 1.0, 0.0
            )
        tracer_count, flux_count = factor.shape
        depth = forcing.shape[0] // (tracer_count * flux_count)
        level = lax.broadcasted_iota(jnp.int32, (depth, width), 0).astype(jnp.float32)
        profile = STEP_OCEAN * jnp.exp(-0.5 * level)
        for n in range(flux_count):
            for t in range(tracer_count):
                forcing[pl.ds((n * tracer_count + t) * depth, depth), :] = factor[t, n] * profile
        for copy in copies:
            copy.wait()


def remap_kernel(
    regrid, gather, spread, chosen, returning, forcing, diffused, *refs
):
    arrived, renewed, shares = refs[:2], refs[2], refs[3:]

    @pl.when(jnp.logical_not(in_air()))
    def _():
        points, cells = gather.shape
        x_count = points // cells
        slots = regrid.shape[0] // points
        air = chosen.shape[0] // slots
        packed = refs[0].shape[1]
        flux_count = packed // x_count
        row = lax.broadcasted_iota(jnp.int32, (x_count, cells), 0)
        column = lax.broadcasted_iota(jnp.int32, (x_count, cells), 1)
        same = jnp.where(row == column % x_count, 1.0, 0.0)

        blocks = [block[s].astype(jnp.float32) for block in arrived for s in range(block.shape[0])]
        matched = None
        for k in range(slots):
            part = chosen[pl.ds(k * air, 1), :] * blocks[0]
            for s in range(1, air):
                part = part + chosen[pl.ds(k * air + s, 1), :] * blocks[s]
            product = lax.dot_general(
                part.astype(jnp.bfloat16),
                regrid[pl.ds(k * points, points), :],
                (((1,), (1,)), ((), ())),
                preferred_element_type=jnp.float32,
            )
            matched = product if matched is None else matched + product
        matched = matched * jnp.tile(same, (flux_count, x_count))
        high = matched.astype(jnp.bfloat16)
        low = (matched - high.astype(jnp.float32)).astype(jnp.bfloat16)
        summed = jnp.dot(high, gather[...], preferred_element_type=jnp.float32) + jnp.dot(
            low, gather[...], preferred_element_type=jnp.float32
        )
        ocean_flux = summed.reshape(flux_count, x_count, cells).sum(axis=1)
        height = diffused.shape[0]
        value = diffused[...]
        for n in range(flux_count):
            value = value + forcing[pl.ds(n * height, height), :] * ocean_flux[n : n + 1]
        renewed[...] = value

        top = jnp.broadcast_to(value[0:1], (x_count, cells)).astype(jnp.bfloat16)
        wide = jnp.dot(top, spread[...], preferred_element_type=jnp.float32)
        wide = (wide * jnp.tile(same, (1, x_count))).astype(jnp.bfloat16)
        back = [
            jnp.dot(wide, regrid[pl.ds(k * points, points), :], preferred_element_type=jnp.float32)
            for k in range(slots)
        ]
        count = shares[0].shape[0]
        for m, share in enumerate(shares):
            for j in range(count):
                at = m * count + j
                total = returning[pl.ds(at, 1), :] * back[0]
                for k in range(1, slots):
                    total = total + returning[pl.ds(k * air + at, 1), :] * back[k]
                share[j] = total


def add_kernel(*refs):
    shares, far, near = refs[:-2], refs[-2], refs[-1]

    @pl.when(jnp.logical_not(in_air()))
    def _():
        for j in range(shares[0].shape[0]):
            value = shares[0][j]
            for share in shares[1:]:
                value = value + share[j]
            if j < far.shape[0]:
                far[j] = value
            else:
                near[...] = value


def relay_kernel(near, far, onward):
    @pl.when(in_air())
    def _():
        onward[...] = far[0]

    @pl.when(jnp.logical_not(in_air()))
    def _():
        onward[...] = near[...]


def last_kernel(renewed, far, near, tracers_later, warmth):
    block = lax.axis_index("sec") // (lax.axis_size("sec") // 4)

    @pl.when(in_air())
    def _():
        tracers_later[...] = jnp.zeros(tracers_later.shape, jnp.float32)
        warmth[...] = jnp.where(block == 1, far[1], near[...])

    @pl.when(jnp.logical_not(in_air()))
    def _():
        tracers_later[...] = renewed[...]
        warmth[...] = jnp.zeros(warmth.shape, jnp.float32)


def per_device(
    climate_field_table,
    zonal_wind_speed,
    meridional_wind,
    sea_warmth_field,
    exchange_law_factor,
    regrid_matrix_stack,
    entry_sender_patch,
    holder_live_total,
    marine_salinity_heat,
    adjacent_offset_lists,
    polygon_side_total,
    interface_mixing_factor,
    solute_forcing_factor,
):
    sections = lax.axis_size("sec")
    ranks = lax.axis_size("rank")
    oceans = sections // 4
    air = sections - oceans
    _, x_points, rows, y_points = climate_field_table.shape
    levels = zonal_wind_speed.shape[2]
    flux_count = exchange_law_factor.shape[0]
    _, tracer_count, depth, cells = marine_salinity_heat.shape
    slots = regrid_matrix_stack.shape[2]
    f32, bf16 = jnp.float32, jnp.bfloat16
    shape = jax.ShapeDtypeStruct

    field = climate_field_table.reshape(x_points * rows, y_points)
    zonal = zonal_wind_speed.reshape(x_points * levels, y_points)
    meridional = meridional_wind.reshape(x_points * levels, y_points)
    regrid = regrid_matrix_stack.reshape(slots * cells * x_points, y_points)
    tracers = marine_salinity_heat.reshape(tracer_count * depth, cells)
    offsets = jnp.transpose(adjacent_offset_lists, (1, 0, 2))
    mixing = jnp.transpose(interface_mixing_factor, (1, 0, 2))
    live = jnp.transpose(holder_live_total, (1, 0))

    along = np.kron(np.eye(y_points // NODES, dtype=np.float32), gll_matrix().T)
    along = jnp.asarray(along)

    fields = rows // levels
    tile = min(8, levels)
    in_place = (
        exchange_law_factor,
        climate_field_table.reshape(x_points, fields, levels, y_points),
        zonal_wind_speed[0],
        meridional_wind[0],
        sea_warmth_field,
    )
    swap_rows = max(flux_count * x_points, rows + 16)
    fluxes = pl.pallas_call(
        functools.partial(flux_kernel, levels),
        out_shape=shape((swap_rows, y_points), bf16),
        in_specs=[HBM] * len(in_place),
        out_specs=VMEM,
        scratch_shapes=[
            pltpu.SMEM(exchange_law_factor.shape, f32),
            pltpu.VMEM((x_points, fields, tile, y_points), f32),
            pltpu.VMEM((x_points, tile, y_points), f32),
            pltpu.VMEM((x_points, tile, y_points), f32),
            pltpu.VMEM((1, x_points, y_points), f32),
            pltpu.SemaphoreType.DMA((len(in_place),)),
        ],
        compiler_params=PARAMS,
        cost_estimate=cost(1),
        name="flux",
    )(*(pltpu.with_memory_space_constraint(a, pltpu.HBM) for a in in_place))
    first, last, own = pl.pallas_call(
        functools.partial(edge_kernel, levels, rows),
        out_shape=(
            shape((rows, y_points), bf16),
            shape((rows, y_points), bf16),
            shape((2, rows, y_points), f32),
        ),
        in_specs=[VMEM] * 5 + [ANY],
        out_specs=(VMEM,) * 3,
        compiler_params=PARAMS,
        cost_estimate=cost(1),
        name="edges",
    )(field, zonal, meridional, along, tracers, fluxes)
    up = [(i, (i + 1) % ranks) for i in range(ranks)]
    below = lax.ppermute(last, "rank", up)
    above = lax.ppermute(first, "rank", [(j, i) for i, j in up])

    def turned(value, m):
        pairs = [(s, s // oceans * oceans + (s + m) % oceans) for s in range(sections)]
        return lax.ppermute(value, "sec", pairs)

    def paired(value, mask):
        pairs = [
            (s, (s // oceans ^ mask) * oceans + s % oceans) for s in range(sections)
        ]
        return lax.ppermute(value, "sec", pairs)

    received = [turned(fluxes, m) for m in range(1, oceans)]
    packed = pl.pallas_call(
        pack_kernel,
        out_shape=shape((oceans, flux_count * x_points, y_points), bf16),
        in_specs=[VMEM] * oceans,
        out_specs=VMEM,
        compiler_params=PARAMS,
        cost_estimate=cost(0.2),
        name="pack",
    )(fluxes, *received)
    neighbour = paired(packed, 1)
    joined = pl.pallas_call(
        join_kernel,
        out_shape=shape((2 * oceans, flux_count * x_points, y_points), bf16),
        in_specs=[VMEM] * 2,
        out_specs=VMEM,
        compiler_params=PARAMS,
        cost_estimate=cost(0.2),
        name="join",
    )(packed, neighbour)
    pair = paired(joined, 2)

    from_memory = (
        entry_sender_patch,
        live,
        solute_forcing_factor,
        offsets,
        polygon_side_total,
        mixing,
    )
    later, diffused, chosen, returning, forcing, gather, spread = pl.pallas_call(
        functools.partial(middle_kernel, levels, rows),
        out_shape=(
            shape((x_points, rows, y_points), f32),
            shape(tracers.shape, f32),
            shape((slots * air, y_points), f32),
            shape((slots * air, y_points), f32),
            shape((flux_count * tracer_count * depth, cells), f32),
            shape((x_points * cells, cells), bf16),
            shape((cells, x_points * cells), bf16),
        ),
        in_specs=[VMEM] * 8 + [HBM] * 6,
        out_specs=(HBM,) + (VMEM,) * 6,
        scratch_shapes=[
            pltpu.VMEM(field.shape, f32),
            pltpu.VMEM((x_points, rows, y_points), f32),
        ]
        + [
            (pltpu.SMEM if i < 3 else pltpu.VMEM)(a.shape, a.dtype)
            for i, a in enumerate(from_memory)
        ]
        + [
            pltpu.SemaphoreType.DMA((max(fields, x_points),)),
            pltpu.SemaphoreType.DMA((len(from_memory),)),
        ],
        compiler_params=PARAMS,
        cost_estimate=cost(1),
        name="middle",
    )(
        field,
        zonal,
        meridional,
        along,
        own,
        below,
        above,
        tracers,
        *(pltpu.with_memory_space_constraint(a, pltpu.HBM) for a in from_memory),
    )

    renewed, *shares = pl.pallas_call(
        remap_kernel,
        out_shape=(shape(tracers.shape, f32),)
        + (shape((air // oceans, x_points, y_points), f32),) * oceans,
        in_specs=[VMEM] * 9,
        out_specs=(VMEM,) * (1 + oceans),
        compiler_params=PARAMS,
        cost_estimate=cost(1),
        name="remap",
    )(regrid, gather, spread, chosen, returning, forcing, diffused, pair, neighbour)
    shares = shares[:1] + [turned(share, m) for m, share in enumerate(shares[1:], 1)]
    far, near = pl.pallas_call(
        add_kernel,
        out_shape=(shape((2, x_points, y_points), f32), shape((x_points, y_points), f32)),
        in_specs=[VMEM] * oceans,
        out_specs=(VMEM,) * 2,
        compiler_params=PARAMS,
        cost_estimate=cost(0.2),
        name="add",
    )(*shares)
    far = paired(far, 2)
    onward = pl.pallas_call(
        relay_kernel,
        out_shape=shape((x_points, y_points), f32),
        in_specs=[VMEM] * 2,
        out_specs=VMEM,
        compiler_params=PARAMS,
        cost_estimate=cost(0.2),
        name="relay",
    )(near, far)
    near = paired(onward, 1)
    tracers_later, warmth = pl.pallas_call(
        last_kernel,
        out_shape=(shape(tracers.shape, f32), shape((x_points, y_points), f32)),
        in_specs=[VMEM] * 3,
        out_specs=(VMEM,) * 2,
        compiler_params=PARAMS,
        cost_estimate=cost(0.5),
        name="last",
    )(renewed, far, near)
    return (
        later.reshape(climate_field_table.shape),
        tracers_later.reshape(marine_salinity_heat.shape),
        warmth[None],
    )


def solution(mesh):
    return jax.shard_map(
        per_device,
        mesh=mesh,
        in_specs=(
            P("sec", "rank", None, None),
            P("sec", "rank", None, None),
            P("sec", "rank", None, None),
            P("sec", "rank", None),
            P(),
            P("sec", "rank", None, None, None, None),
            P(None, "rank", None),
            P(None, "rank"),
            P("sec", None, None, "rank"),
            P("sec", None, "rank"),
            P("sec", "rank"),
            P("sec", None, "rank"),
            P(),
        ),
        out_specs=(
            P("sec", "rank", None, None),
            P("sec", None, None, "rank"),
            P("sec", "rank", None),
        ),
        check_vma=False,
    )
```

```python
import functools

import jax
import jax.numpy as jnp
import numpy as np
from jax import lax
from jax.experimental import pallas as pl
from jax.experimental.pallas import tpu as pltpu
from jax.sharding import PartitionSpec as P

STEP_ATMOS = 0.05
DIFFUSIVITY = 0.05
STEP_OCEAN = 0.5
NODES = 4

VMEM = pl.BlockSpec(memory_space=pltpu.VMEM)
ANY = pl.BlockSpec(memory_space=pl.ANY)
HBM = pl.BlockSpec(memory_space=pltpu.HBM)
SMEM = pl.BlockSpec(memory_space=pltpu.SMEM)
PARAMS = pltpu.CompilerParams(vmem_limit_bytes=8 * 2**20)
HIGHEST = lax.Precision.HIGHEST


def gll_matrix():
    nodes = np.array([-1.0, -1.0 / np.sqrt(5.0), 1.0 / np.sqrt(5.0), 1.0])
    legendre = (5.0 * nodes**3 - 3.0 * nodes) / 2.0
    matrix = np.zeros((4, 4))
    for i in range(4):
        for j in range(4):
            if i != j:
                matrix[i, j] = legendre[i] / (legendre[j] * (nodes[i] - nodes[j]))
    matrix[0, 0] = -3.0
    matrix[3, 3] = 3.0
    return matrix.astype(np.float32)


def cost(microseconds):
    return pl.CostEstimate(
        flops=0, bytes_accessed=int(microseconds * 3_000_000), transcendentals=0
    )


def in_air():
    sections = lax.axis_size("sec")
    return lax.axis_index("sec") < sections - sections // 4


def smooth_lines(value, lane):
    width = value.shape[-1]
    right = pltpu.roll(value, width - 1, value.ndim - 1)
    left = pltpu.roll(value, 1, value.ndim - 1)
    at_end = (lane % NODES == NODES - 1) & (lane < width - 1)
    at_start = (lane % NODES == 0) & (lane > 0)
    partner = jnp.where(at_end, right, jnp.where(at_start, left, value))
    return 0.5 * (value + partner)


def start_all(pairs, sems):
    copies = [
        pltpu.make_async_copy(source, target, sems.at[i])
        for i, (source, target) in enumerate(pairs)
    ]
    for copy in copies:
        copy.start()
    return copies


def flux_kernel(
    levels, law_in, field_in, zonal_in, meridional_in, sea_in, sent, law, field, zonal, meridional, sea, sems
):
    @pl.when(in_air())
    def _():
        lowest = pl.ds(0, zonal.shape[1])
        copies = start_all(
            (
                (field_in.at[:, :, lowest, :], field),
                (zonal_in.at[:, lowest, :], zonal),
                (meridional_in.at[:, lowest, :], meridional),
                (sea_in, sea),
                (law_in, law),
            ),
            sems,
        )
        for copy in copies:
            copy.wait()
        flux_count, columns = law.shape
        ground = [field[:, f, 0, :] for f in range(columns - 1)] + [sea[0]]
        speed = jnp.sqrt(1.0 + zonal[:, 0, :] ** 2 + meridional[:, 0, :] ** 2)
        parts = []
        for n in range(flux_count):
            total = law[n, 0] * ground[0]
            for f in range(1, columns):
                total = total + law[n, f] * ground[f]
            parts.append(speed * total)
        block = jnp.concatenate(parts, axis=0).astype(jnp.bfloat16)
        sent[pl.ds(0, block.shape[0]), :] = block


def edge_kernel(levels, rows, field, zonal, meridional, along, tracers, after, first, last, own):
    x_points = field.shape[0] // rows

    @pl.when(in_air())
    def _():
        d = gll_matrix()
        lane = lax.broadcasted_iota(jnp.int32, (levels, field.shape[1]), 1)
        for side, (x, target) in enumerate(((0, first), (x_points - 1, last))):
            start = x - x % NODES
            along_y = jnp.dot(
                field[pl.ds(x * rows, rows), :],
                along[...],
                precision=HIGHEST,
                preferred_element_type=jnp.float32,
            )
            u = zonal[pl.ds(x * levels, levels), :]
            v = meridional[pl.ds(x * levels, levels), :]
            for f in range(rows // levels):
                at = f * levels
                along_x = sum(
                    float(d[x % NODES, a]) * field[pl.ds((start + a) * rows + at, levels), :]
                    for a in range(NODES)
                    if d[x % NODES, a] != 0
                )
                value = -(u * along_x + v * along_y[at : at + levels])
                value = smooth_lines(value, lane)
                own[side, pl.ds(at, levels), :] = value
                target[pl.ds(at, levels), :] = value.astype(jnp.bfloat16)

    @pl.when(jnp.logical_not(in_air()))
    def _():
        value = tracers[...]
        high = value.astype(jnp.bfloat16)
        low = (value - high.astype(jnp.float32)).astype(jnp.bfloat16)
        both = jnp.concatenate([high, low], axis=0)
        for target in (first, last):
            target[pl.ds(0, both.shape[0]), :] = both


def pack_kernel(own, *refs):
    received, packed = refs[:-1], refs[-1]
    count = len(refs)
    place = lax.axis_index("sec") % count
    here = pl.ds(0, packed.shape[1])
    packed[place] = own[here, :]
    for m, part in enumerate(received, 1):
        packed[(place - m + count) % count] = part[here, :]


def ocean_kernel(
    senders_in,
    live_in,
    factor_in,
    offsets_in,
    sides_in,
    mixing_in,
    tracers,
    below,
    above,
    diffused,
    chosen,
    returning,
    forcing,
    gather,
    spread,
    senders,
    live,
    factor,
    offsets,
    sides,
    mixing,
    sems,
):
    @pl.when(jnp.logical_not(in_air()))
    def _():
        copies = start_all(
            (
                (senders_in, senders),
                (live_in, live),
                (factor_in, factor),
                (offsets_in, offsets),
                (sides_in, sides),
                (mixing_in, mixing),
            ),
            sems,
        )
        cells = sides.shape[1]
        x_count = gather.shape[0] // cells
        point = lax.broadcasted_iota(jnp.int32, gather.shape, 0) // x_count
        cell = lax.broadcasted_iota(jnp.int32, gather.shape, 1)
        gather[...] = jnp.where(point == cell, 1.0, 0.0).astype(gather.dtype)
        cell = lax.broadcasted_iota(jnp.int32, spread.shape, 0)
        point = lax.broadcasted_iota(jnp.int32, spread.shape, 1) // x_count
        spread[...] = jnp.where(point == cell, 1.0, 0.0).astype(spread.dtype)
        for copy in copies:
            copy.wait()

        source = lax.broadcasted_iota(jnp.int32, (cells, cells), 0)
        target = lax.broadcasted_iota(jnp.int32, (cells, cells), 1)
        inside = jnp.zeros((cells, cells), jnp.float32)
        outside = jnp.zeros((cells, cells), jnp.float32)
        total = jnp.zeros((1, cells), jnp.float32)
        for e in range(offsets.shape[0]):
            weight = jnp.where(e < sides[...], mixing[e], 0.0)
            place = target[:1] + offsets[e]
            total = total + weight
            inside = inside + jnp.where(source == place, weight, 0.0)
            hit = (source == place - cells) | (source == place + cells)
            outside = outside + jnp.where(hit, weight, 0.0)
        inside = inside - jnp.where(source == target, total, 0.0)

        value = tracers[...]
        height = value.shape[0]
        cell = lax.broadcasted_iota(jnp.int32, value.shape, 1)
        beside = [
            h[pl.ds(0, height), :].astype(jnp.float32)
            + h[pl.ds(height, height), :].astype(jnp.float32)
            for h in (below, above)
        ]
        outer = jnp.where(cell < cells // 2, beside[1], beside[0])
        change = jnp.dot(
            jnp.concatenate([value, outer], axis=1),
            jnp.concatenate([inside, outside], axis=0),
            precision=HIGHEST,
            preferred_element_type=jnp.float32,
        )
        diffused[...] = value + DIFFUSIVITY * change

        sections = lax.axis_size("sec")
        oceans = sections // 4
        air = sections - oceans
        ocean = jnp.maximum(lax.axis_index("sec") - air, 0)
        width = chosen.shape[1]
        count = live[0, ocean]
        for k in range(senders.shape[2]):
            place = jnp.where(k < count, senders[ocean, 0, k], sections)
            section = lax.broadcasted_iota(jnp.int32, (air, width), 0)
            chosen[pl.ds(k * air, air), :] = jnp.where(section == place, 1.0, 0.0)
            block = section % (air // oceans)
            owner = (ocean + section // (air // oceans)) % oceans
            returning[pl.ds(k * air, air), :] = jnp.where(
                block * oceans + owner == place, 1.0, 0.0
            )
        tracer_count, flux_count = factor.shape
        depth = forcing.shape[0] // (tracer_count * flux_count)
        level = lax.broadcasted_iota(jnp.int32, (depth, width), 0).astype(jnp.float32)
        profile = STEP_OCEAN * jnp.exp(-0.5 * level)
        for n in range(flux_count):
            for t in range(tracer_count):
                forcing[pl.ds((n * tracer_count + t) * depth, depth), :] = factor[t, n] * profile


def field_kernel(
    levels,
    rows,
    field,
    zonal,
    meridional,
    along,
    own,
    below,
    above,
    after,
    later,
    slopes,
    held,
    sems,
):
    x_points = later.shape[0]

    @pl.when(in_air())
    def _():
        d = gll_matrix()
        lane = lax.broadcasted_iota(jnp.int32, (levels, field.shape[1]), 1)
        inner = pl.ds(rows, (x_points - 2) * rows)
        slopes[inner, :] = jnp.dot(
            field[inner, :], along[...], precision=HIGHEST, preferred_element_type=jnp.float32
        )
        copies = []
        for f in range(rows // levels):
            at = f * levels
            here = pl.ds(at, levels)
            values = {
                0: 0.5 * (own[0, here, :] + below[here, :].astype(jnp.float32)),
                x_points - 1: 0.5 * (own[1, here, :] + above[here, :].astype(jnp.float32)),
            }
            q = [field[pl.ds(x * rows + at, levels), :] for x in range(x_points)]
            for x in range(1, x_points - 1):
                start = x - x % NODES
                along_x = sum(
                    float(d[x % NODES, a]) * q[start + a]
                    for a in range(NODES)
                    if d[x % NODES, a] != 0
                )
                u = zonal[pl.ds(x * levels, levels), :]
                v = meridional[pl.ds(x * levels, levels), :]
                value = -(u * along_x + v * slopes[pl.ds(x * rows + at, levels), :])
                values[x] = smooth_lines(value, lane)
            for x in range(NODES - 1, x_points - 1, NODES):
                values[x] = values[x + 1] = 0.5 * (values[x] + values[x + 1])
            for x in range(x_points):
                held[x, here, :] = q[x] + STEP_ATMOS * values[x]
            copy = pltpu.make_async_copy(held.at[:, here, :], later.at[:, here, :], sems.at[f])
            copy.start()
            copies.append(copy)
        for copy in copies:
            copy.wait()

    @pl.when(jnp.logical_not(in_air()))
    def _():
        held[0] = jnp.zeros(held.shape[1:], jnp.float32)
        copies = start_all([(held.at[0], later.at[x]) for x in range(x_points)], sems)
        for copy in copies:
            copy.wait()


def remap_kernel(
    regrid, gather, spread, chosen, returning, forcing, diffused, *refs
):
    arrived, renewed, shares = (refs[2], refs[0], refs[1]), refs[3], refs[4:]

    @pl.when(jnp.logical_not(in_air()))
    def _():
        points, cells = gather.shape
        x_count = points // cells
        slots = regrid.shape[0] // points
        air = chosen.shape[0] // slots
        packed = refs[0].shape[1]
        flux_count = packed // x_count
        row = lax.broadcasted_iota(jnp.int32, (x_count, cells), 0)
        column = lax.broadcasted_iota(jnp.int32, (x_count, cells), 1)
        same = jnp.where(row == column % x_count, 1.0, 0.0)

        blocks = [block[s].astype(jnp.float32) for block in arrived for s in range(block.shape[0])]
        matched = None
        for k in range(slots):
            part = chosen[pl.ds(k * air, 1), :] * blocks[0]
            for s in range(1, air):
                part = part + chosen[pl.ds(k * air + s, 1), :] * blocks[s]
            product = lax.dot_general(
                part.astype(jnp.bfloat16),
                regrid[pl.ds(k * points, points), :],
                (((1,), (1,)), ((), ())),
                preferred_element_type=jnp.float32,
            )
            matched = product if matched is None else matched + product
        matched = matched * jnp.tile(same, (flux_count, x_count))
        high = matched.astype(jnp.bfloat16)
        low = (matched - high.astype(jnp.float32)).astype(jnp.bfloat16)
        summed = jnp.dot(high, gather[...], preferred_element_type=jnp.float32) + jnp.dot(
            low, gather[...], preferred_element_type=jnp.float32
        )
        ocean_flux = summed.reshape(flux_count, x_count, cells).sum(axis=1)
        height = diffused.shape[0]
        value = diffused[...]
        for n in range(flux_count):
            value = value + forcing[pl.ds(n * height, height), :] * ocean_flux[n : n + 1]
        renewed[...] = value

        top = jnp.broadcast_to(value[0:1], (x_count, cells)).astype(jnp.bfloat16)
        wide = jnp.dot(top, spread[...], preferred_element_type=jnp.float32)
        wide = (wide * jnp.tile(same, (1, x_count))).astype(jnp.bfloat16)
        back = [
            jnp.dot(wide, regrid[pl.ds(k * points, points), :], preferred_element_type=jnp.float32)
            for k in range(slots)
        ]
        count = shares[0].shape[0]
        for m, share in enumerate(shares):
            for j in range(count):
                at = m * count + j
                total = returning[pl.ds(at, 1), :] * back[0]
                for k in range(1, slots):
                    total = total + returning[pl.ds(k * air + at, 1), :] * back[k]
                share[j] = total


def add_kernel(*refs):
    count = refs[0].shape[0]
    shares, totals = refs[:-count], refs[-count:]

    @pl.when(jnp.logical_not(in_air()))
    def _():
        for j, total in enumerate(totals):
            value = shares[0][j]
            for share in shares[1:]:
                value = value + share[j]
            total[...] = value


def last_kernel(renewed, *refs):
    returned, (tracers_later, warmth) = refs[:-2], refs[-2:]
    sections = lax.axis_size("sec")
    block = lax.axis_index("sec") // (sections // 4)

    @pl.when(in_air())
    def _():
        tracers_later[...] = jnp.zeros(tracers_later.shape, jnp.float32)

    @pl.when(jnp.logical_not(in_air()))
    def _():
        tracers_later[...] = renewed[...]
        warmth[...] = jnp.zeros(warmth.shape, jnp.float32)

    for j, part in enumerate(returned):

        @pl.when(block == j)
        def _(part=part):
            warmth[...] = part[...]


def per_device(
    climate_field_table,
    zonal_wind_speed,
    meridional_wind,
    sea_warmth_field,
    exchange_law_factor,
    regrid_matrix_stack,
    entry_sender_patch,
    holder_live_total,
    marine_salinity_heat,
    adjacent_offset_lists,
    polygon_side_total,
    interface_mixing_factor,
    solute_forcing_factor,
):
    sections = lax.axis_size("sec")
    ranks = lax.axis_size("rank")
    oceans = sections // 4
    air = sections - oceans
    _, x_points, rows, y_points = climate_field_table.shape
    levels = zonal_wind_speed.shape[2]
    flux_count = exchange_law_factor.shape[0]
    _, tracer_count, depth, cells = marine_salinity_heat.shape
    slots = regrid_matrix_stack.shape[2]
    f32, bf16 = jnp.float32, jnp.bfloat16
    shape = jax.ShapeDtypeStruct

    field = climate_field_table.reshape(x_points * rows, y_points)
    zonal = zonal_wind_speed.reshape(x_points * levels, y_points)
    meridional = meridional_wind.reshape(x_points * levels, y_points)
    regrid = regrid_matrix_stack.reshape(slots * cells * x_points, y_points)
    tracers = marine_salinity_heat.reshape(tracer_count * depth, cells)
    offsets = jnp.transpose(adjacent_offset_lists, (1, 0, 2))
    mixing = jnp.transpose(interface_mixing_factor, (1, 0, 2))
    live = jnp.transpose(holder_live_total, (1, 0))

    along = np.kron(np.eye(y_points // NODES, dtype=np.float32), gll_matrix().T)
    along = jnp.asarray(along)

    fields = rows // levels
    tile = min(8, levels)
    in_place = (
        exchange_law_factor,
        climate_field_table.reshape(x_points, fields, levels, y_points),
        zonal_wind_speed[0],
        meridional_wind[0],
        sea_warmth_field,
    )
    swap_rows = max(flux_count * x_points, rows + 16)
    fluxes = pl.pallas_call(
        functools.partial(flux_kernel, levels),
        out_shape=shape((swap_rows, y_points), bf16),
        in_specs=[HBM] * len(in_place),
        out_specs=VMEM,
        scratch_shapes=[
            pltpu.SMEM(exchange_law_factor.shape, f32),
            pltpu.VMEM((x_points, fields, tile, y_points), f32),
            pltpu.VMEM((x_points, tile, y_points), f32),
            pltpu.VMEM((x_points, tile, y_points), f32),
            pltpu.VMEM((1, x_points, y_points), f32),
            pltpu.SemaphoreType.DMA((len(in_place),)),
        ],
        compiler_params=PARAMS,
        cost_estimate=cost(1),
        name="flux",
    )(*(pltpu.with_memory_space_constraint(a, pltpu.HBM) for a in in_place))
    first, last, own = pl.pallas_call(
        functools.partial(edge_kernel, levels, rows),
        out_shape=(
            shape((rows, y_points), bf16),
            shape((rows, y_points), bf16),
            shape((2, rows, y_points), f32),
        ),
        in_specs=[VMEM] * 5 + [ANY],
        out_specs=(VMEM,) * 3,
        compiler_params=PARAMS,
        cost_estimate=cost(1),
        name="edges",
    )(field, zonal, meridional, along, tracers, fluxes)
    up = [(i, (i + 1) % ranks) for i in range(ranks)]
    below = lax.ppermute(last, "rank", up)
    above = lax.ppermute(first, "rank", [(j, i) for i, j in up])

    def turned(value, m):
        pairs = [(s, s // oceans * oceans + (s + m) % oceans) for s in range(sections)]
        return lax.ppermute(value, "sec", pairs)

    def paired(value, mask):
        pairs = [
            (s, (s // oceans ^ mask) * oceans + s % oceans) for s in range(sections)
        ]
        return lax.ppermute(value, "sec", pairs)

    received = [turned(fluxes, m) for m in range(1, oceans)]
    packed = pl.pallas_call(
        pack_kernel,
        out_shape=shape((oceans, flux_count * x_points, y_points), bf16),
        in_specs=[VMEM] * oceans,
        out_specs=VMEM,
        compiler_params=PARAMS,
        cost_estimate=cost(0.2),
        name="pack",
    )(fluxes, *received)
    arrived = [paired(packed, 3 ^ block) for block in range(3)]

    from_memory = (
        entry_sender_patch,
        live,
        solute_forcing_factor,
        offsets,
        polygon_side_total,
        mixing,
    )
    diffused, chosen, returning, forcing, gather, spread = pl.pallas_call(
        ocean_kernel,
        out_shape=(
            shape(tracers.shape, f32),
            shape((slots * air, y_points), f32),
            shape((slots * air, y_points), f32),
            shape((flux_count * tracer_count * depth, cells), f32),
            shape((x_points * cells, cells), bf16),
            shape((cells, x_points * cells), bf16),
        ),
        in_specs=[HBM] * 6 + [VMEM] * 3,
        out_specs=(VMEM,) * 6,
        scratch_shapes=[
            (pltpu.SMEM if i < 3 else pltpu.VMEM)(a.shape, a.dtype)
            for i, a in enumerate(from_memory)
        ]
        + [pltpu.SemaphoreType.DMA((len(from_memory),))],
        compiler_params=PARAMS,
        cost_estimate=cost(1),
        name="ocean",
    )(
        *(pltpu.with_memory_space_constraint(a, pltpu.HBM) for a in from_memory),
        tracers,
        below,
        above,
    )

    renewed, *shares = pl.pallas_call(
        remap_kernel,
        out_shape=(shape(tracers.shape, f32),)
        + (shape((air // oceans, x_points, y_points), f32),) * oceans,
        in_specs=[VMEM] * 10,
        out_specs=(VMEM,) * (1 + oceans),
        compiler_params=PARAMS,
        cost_estimate=cost(1),
        name="remap",
    )(regrid, gather, spread, chosen, returning, forcing, diffused, arrived[1], arrived[2], arrived[0])
    shares = shares[:1] + [turned(share, m) for m, share in enumerate(shares[1:], 1)]
    totals = pl.pallas_call(
        add_kernel,
        out_shape=(shape((x_points, y_points), f32),) * (air // oceans),
        in_specs=[VMEM] * oceans,
        out_specs=(VMEM,) * (air // oceans),
        compiler_params=PARAMS,
        cost_estimate=cost(0.3),
        name="add",
    )(*shares)
    returned = [paired(total, 3 ^ block) for block, total in enumerate(totals)]
    later = pl.pallas_call(
        functools.partial(field_kernel, levels, rows),
        out_shape=shape((x_points, rows, y_points), f32),
        in_specs=[VMEM] * 7 + [ANY],
        out_specs=HBM,
        scratch_shapes=[
            pltpu.VMEM(field.shape, f32),
            pltpu.VMEM((x_points, rows, y_points), f32),
            pltpu.SemaphoreType.DMA((max(fields, x_points),)),
        ],
        compiler_params=PARAMS,
        cost_estimate=cost(3),
        name="field",
    )(field, zonal, meridional, along, own, below, above, totals[2])
    tracers_later, warmth = pl.pallas_call(
        last_kernel,
        out_shape=(shape(tracers.shape, f32), shape((x_points, y_points), f32)),
        in_specs=[VMEM] * (1 + len(returned)),
        out_specs=(VMEM,) * 2,
        compiler_params=PARAMS,
        cost_estimate=cost(0.5),
        name="last",
    )(renewed, *returned)
    return (
        later.reshape(climate_field_table.shape),
        tracers_later.reshape(marine_salinity_heat.shape),
        warmth[None],
    )


def solution(mesh):
    return jax.shard_map(
        per_device,
        mesh=mesh,
        in_specs=(
            P("sec", "rank", None, None),
            P("sec", "rank", None, None),
            P("sec", "rank", None, None),
            P("sec", "rank", None),
            P(),
            P("sec", "rank", None, None, None, None),
            P(None, "rank", None),
            P(None, "rank"),
            P("sec", None, None, "rank"),
            P("sec", None, "rank"),
            P("sec", "rank"),
            P("sec", None, "rank"),
            P(),
        ),
        out_specs=(
            P("sec", "rank", None, None),
            P("sec", None, None, "rank"),
            P("sec", "rank", None),
        ),
        check_vma=False,
    )
```

```python
import functools

import jax
import jax.numpy as jnp
import numpy as np
from jax import lax
from jax.experimental import pallas as pl
from jax.experimental.pallas import tpu as pltpu
from jax.sharding import PartitionSpec as P

STEP_ATMOS = 0.05
DIFFUSIVITY = 0.05
STEP_OCEAN = 0.5
NODES = 4

VMEM = pl.BlockSpec(memory_space=pltpu.VMEM)
ANY = pl.BlockSpec(memory_space=pl.ANY)
HBM = pl.BlockSpec(memory_space=pltpu.HBM)
SMEM = pl.BlockSpec(memory_space=pltpu.SMEM)
PARAMS = pltpu.CompilerParams(vmem_limit_bytes=8 * 2**20)
HIGHEST = lax.Precision.HIGHEST


def gll_matrix():
    nodes = np.array([-1.0, -1.0 / np.sqrt(5.0), 1.0 / np.sqrt(5.0), 1.0])
    legendre = (5.0 * nodes**3 - 3.0 * nodes) / 2.0
    matrix = np.zeros((4, 4))
    for i in range(4):
        for j in range(4):
            if i != j:
                matrix[i, j] = legendre[i] / (legendre[j] * (nodes[i] - nodes[j]))
    matrix[0, 0] = -3.0
    matrix[3, 3] = 3.0
    return matrix.astype(np.float32)


def cost(microseconds):
    return pl.CostEstimate(
        flops=0, bytes_accessed=int(microseconds * 3_000_000), transcendentals=0
    )


def in_air():
    sections = lax.axis_size("sec")
    return lax.axis_index("sec") < sections - sections // 4


def smooth_lines(value, lane):
    width = value.shape[-1]
    right = pltpu.roll(value, width - 1, value.ndim - 1)
    left = pltpu.roll(value, 1, value.ndim - 1)
    at_end = (lane % NODES == NODES - 1) & (lane < width - 1)
    at_start = (lane % NODES == 0) & (lane > 0)
    partner = jnp.where(at_end, right, jnp.where(at_start, left, value))
    return 0.5 * (value + partner)


def start_all(pairs, sems):
    copies = [
        pltpu.make_async_copy(source, target, sems.at[i])
        for i, (source, target) in enumerate(pairs)
    ]
    for copy in copies:
        copy.start()
    return copies


def flux_kernel(
    levels, law_in, field_in, zonal_in, meridional_in, sea_in, sent, law, field, zonal, meridional, sea, sems
):
    @pl.when(in_air())
    def _():
        lowest = pl.ds(0, zonal.shape[1])
        copies = start_all(
            (
                (field_in.at[:, :, lowest, :], field),
                (zonal_in.at[:, lowest, :], zonal),
                (meridional_in.at[:, lowest, :], meridional),
                (sea_in, sea),
                (law_in, law),
            ),
            sems,
        )
        for copy in copies:
            copy.wait()
        flux_count, columns = law.shape
        ground = [field[:, f, 0, :] for f in range(columns - 1)] + [sea[0]]
        speed = jnp.sqrt(1.0 + zonal[:, 0, :] ** 2 + meridional[:, 0, :] ** 2)
        parts = []
        for n in range(flux_count):
            total = law[n, 0] * ground[0]
            for f in range(1, columns):
                total = total + law[n, f] * ground[f]
            parts.append(speed * total)
        block = jnp.concatenate(parts, axis=0).astype(jnp.bfloat16)
        sent[pl.ds(0, block.shape[0]), :] = block


def edge_kernel(levels, rows, field, zonal, meridional, along, tracers, after, first, last, own):
    x_points = field.shape[0] // rows

    @pl.when(in_air())
    def _():
        d = gll_matrix()
        lane = lax.broadcasted_iota(jnp.int32, (levels, field.shape[1]), 1)
        for side, (x, target) in enumerate(((0, first), (x_points - 1, last))):
            start = x - x % NODES
            along_y = jnp.dot(
                field[pl.ds(x * rows, rows), :],
                along[...],
                precision=HIGHEST,
                preferred_element_type=jnp.float32,
            )
            u = zonal[pl.ds(x * levels, levels), :]
            v = meridional[pl.ds(x * levels, levels), :]
            for f in range(rows // levels):
                at = f * levels
                along_x = sum(
                    float(d[x % NODES, a]) * field[pl.ds((start + a) * rows + at, levels), :]
                    for a in range(NODES)
                    if d[x % NODES, a] != 0
                )
                value = -(u * along_x + v * along_y[at : at + levels])
                value = smooth_lines(value, lane)
                own[side, pl.ds(at, levels), :] = value
                target[pl.ds(at, levels), :] = value.astype(jnp.bfloat16)

    @pl.when(jnp.logical_not(in_air()))
    def _():
        value = tracers[...]
        high = value.astype(jnp.bfloat16)
        low = (value - high.astype(jnp.float32)).astype(jnp.bfloat16)
        both = jnp.concatenate([high, low], axis=0)
        for target in (first, last):
            target[pl.ds(0, both.shape[0]), :] = both


def pack_kernel(own, *refs):
    received, packed = refs[:-1], refs[-1]
    count = len(refs)
    place = lax.axis_index("sec") % count
    here = pl.ds(0, packed.shape[1])
    packed[place] = own[here, :]
    for m, part in enumerate(received, 1):
        packed[(place - m + count) % count] = part[here, :]


def middle_kernel(
    levels,
    rows,
    field,
    zonal,
    meridional,
    along,
    own,
    below,
    above,
    tracers,
    senders_in,
    live_in,
    factor_in,
    offsets_in,
    sides_in,
    mixing_in,
    later,
    diffused,
    chosen,
    returning,
    forcing,
    gather,
    spread,
    slopes,
    held,
    senders,
    live,
    factor,
    offsets,
    sides,
    mixing,
    sems,
    load_sems,
):
    x_points = later.shape[0]

    @pl.when(in_air())
    def _():
        d = gll_matrix()
        lane = lax.broadcasted_iota(jnp.int32, (levels, field.shape[1]), 1)
        inner = pl.ds(rows, (x_points - 2) * rows)
        slopes[inner, :] = jnp.dot(
            field[inner, :], along[...], precision=HIGHEST, preferred_element_type=jnp.float32
        )
        copies = []
        for f in range(rows // levels):
            at = f * levels
            here = pl.ds(at, levels)
            values = {
                0: 0.5 * (own[0, here, :] + below[here, :].astype(jnp.float32)),
                x_points - 1: 0.5 * (own[1, here, :] + above[here, :].astype(jnp.float32)),
            }
            q = [field[pl.ds(x * rows + at, levels), :] for x in range(x_points)]
            for x in range(1, x_points - 1):
                start = x - x % NODES
                along_x = sum(
                    float(d[x % NODES, a]) * q[start + a]
                    for a in range(NODES)
                    if d[x % NODES, a] != 0
                )
                u = zonal[pl.ds(x * levels, levels), :]
                v = meridional[pl.ds(x * levels, levels), :]
                value = -(u * along_x + v * slopes[pl.ds(x * rows + at, levels), :])
                values[x] = smooth_lines(value, lane)
            for x in range(NODES - 1, x_points - 1, NODES):
                values[x] = values[x + 1] = 0.5 * (values[x] + values[x + 1])
            for x in range(x_points):
                held[x, here, :] = q[x] + STEP_ATMOS * values[x]
            copy = pltpu.make_async_copy(held.at[:, here, :], later.at[:, here, :], sems.at[f])
            copy.start()
            copies.append(copy)
        for copy in copies:
            copy.wait()

    @pl.when(jnp.logical_not(in_air()))
    def _():
        loads = start_all(
            (
                (senders_in, senders),
                (live_in, live),
                (factor_in, factor),
                (offsets_in, offsets),
                (sides_in, sides),
                (mixing_in, mixing),
            ),
            load_sems,
        )
        held[0] = jnp.zeros(held.shape[1:], jnp.float32)
        copies = start_all([(held.at[0], later.at[x]) for x in range(x_points)], sems)
        cells = sides.shape[1]
        x_count = gather.shape[0] // cells
        point = lax.broadcasted_iota(jnp.int32, gather.shape, 0) // x_count
        cell = lax.broadcasted_iota(jnp.int32, gather.shape, 1)
        gather[...] = jnp.where(point == cell, 1.0, 0.0).astype(gather.dtype)
        cell = lax.broadcasted_iota(jnp.int32, spread.shape, 0)
        point = lax.broadcasted_iota(jnp.int32, spread.shape, 1) // x_count
        spread[...] = jnp.where(point == cell, 1.0, 0.0).astype(spread.dtype)
        for load in loads:
            load.wait()

        source = lax.broadcasted_iota(jnp.int32, (cells, cells), 0)
        target = lax.broadcasted_iota(jnp.int32, (cells, cells), 1)
        inside = jnp.zeros((cells, cells), jnp.float32)
        outside = jnp.zeros((cells, cells), jnp.float32)
        total = jnp.zeros((1, cells), jnp.float32)
        for e in range(offsets.shape[0]):
            weight = jnp.where(e < sides[...], mixing[e], 0.0)
            place = target[:1] + offsets[e]
            total = total + weight
            inside = inside + jnp.where(source == place, weight, 0.0)
            hit = (source == place - cells) | (source == place + cells)
            outside = outside + jnp.where(hit, weight, 0.0)
        inside = inside - jnp.where(source == target, total, 0.0)

        value = tracers[...]
        height = value.shape[0]
        cell = lax.broadcasted_iota(jnp.int32, value.shape, 1)
        beside = [
            h[pl.ds(0, height), :].astype(jnp.float32)
            + h[pl.ds(height, height), :].astype(jnp.float32)
            for h in (below, above)
        ]
        outer = jnp.where(cell < cells // 2, beside[1], beside[0])
        change = jnp.dot(
            jnp.concatenate([value, outer], axis=1),
            jnp.concatenate([inside, outside], axis=0),
            precision=HIGHEST,
            preferred_element_type=jnp.float32,
        )
        diffused[...] = value + DIFFUSIVITY * change

        sections = lax.axis_size("sec")
        oceans = sections // 4
        air = sections - oceans
        ocean = jnp.maximum(lax.axis_index("sec") - air, 0)
        width = chosen.shape[1]
        count = live[0, ocean]
        for k in range(senders.shape[2]):
            place = jnp.where(k < count, senders[ocean, 0, k], sections)
            section = lax.broadcasted_iota(jnp.int32, (air, width), 0)
            chosen[pl.ds(k * air, air), :] = jnp.where(section == place, 1.0, 0.0)
            block = section % (air // oceans)
            owner = ((ocean + section // (air // oceans)) % oceans) ^ 1
            returning[pl.ds(k * air, air), :] = jnp.where(
                block * oceans + owner == place, 1.0, 0.0
            )
        tracer_count, flux_count = factor.shape
        depth = forcing.shape[0] // (tracer_count * flux_count)
        level = lax.broadcasted_iota(jnp.int32, (depth, width), 0).astype(jnp.float32)
        profile = STEP_OCEAN * jnp.exp(-0.5 * level)
        for n in range(flux_count):
            for t in range(tracer_count):
                forcing[pl.ds((n * tracer_count + t) * depth, depth), :] = factor[t, n] * profile
        for copy in copies:
            copy.wait()


def remap_kernel(
    regrid, gather, spread, chosen, returning, forcing, diffused, *refs
):
    arrived, renewed, shares = (refs[2], refs[0], refs[1]), refs[3], refs[4:]

    @pl.when(jnp.logical_not(in_air()))
    def _():
        points, cells = gather.shape
        x_count = points // cells
        slots = regrid.shape[0] // points
        air = chosen.shape[0] // slots
        packed = refs[0].shape[1]
        flux_count = packed // x_count
        row = lax.broadcasted_iota(jnp.int32, (x_count, cells), 0)
        column = lax.broadcasted_iota(jnp.int32, (x_count, cells), 1)
        same = jnp.where(row == column % x_count, 1.0, 0.0)

        blocks = [block[s].astype(jnp.float32) for block in arrived for s in range(block.shape[0])]
        matched = None
        for k in range(slots):
            part = chosen[pl.ds(k * air, 1), :] * blocks[0]
            for s in range(1, air):
                part = part + chosen[pl.ds(k * air + s, 1), :] * blocks[s]
            product = lax.dot_general(
                part.astype(jnp.bfloat16),
                regrid[pl.ds(k * points, points), :],
                (((1,), (1,)), ((), ())),
                preferred_element_type=jnp.float32,
            )
            matched = product if matched is None else matched + product
        matched = matched * jnp.tile(same, (flux_count, x_count))
        high = matched.astype(jnp.bfloat16)
        low = (matched - high.astype(jnp.float32)).astype(jnp.bfloat16)
        summed = jnp.dot(high, gather[...], preferred_element_type=jnp.float32) + jnp.dot(
            low, gather[...], preferred_element_type=jnp.float32
        )
        ocean_flux = summed.reshape(flux_count, x_count, cells).sum(axis=1)
        height = diffused.shape[0]
        value = diffused[...]
        for n in range(flux_count):
            value = value + forcing[pl.ds(n * height, height), :] * ocean_flux[n : n + 1]
        renewed[...] = value

        top = jnp.broadcast_to(value[0:1], (x_count, cells)).astype(jnp.bfloat16)
        wide = jnp.dot(top, spread[...], preferred_element_type=jnp.float32)
        wide = (wide * jnp.tile(same, (1, x_count))).astype(jnp.bfloat16)
        back = [
            jnp.dot(wide, regrid[pl.ds(k * points, points), :], preferred_element_type=jnp.float32)
            for k in range(slots)
        ]
        count = shares[0].shape[0]
        for m, share in enumerate(shares):
            for j in range(count):
                at = m * count + j
                total = returning[pl.ds(at, 1), :] * back[0]
                for k in range(1, slots):
                    total = total + returning[pl.ds(k * air + at, 1), :] * back[k]
                share[j] = total


def add_kernel(*refs):
    count = refs[0].shape[0]
    shares, totals = refs[:-count], refs[-count:]

    @pl.when(jnp.logical_not(in_air()))
    def _():
        for j, total in enumerate(totals):
            value = shares[0][j]
            for share in shares[1:]:
                value = value + share[j]
            total[...] = value


def last_kernel(renewed, *refs):
    returned, (tracers_later, warmth) = refs[:-2], refs[-2:]
    sections = lax.axis_size("sec")
    block = lax.axis_index("sec") // (sections // 4)

    @pl.when(in_air())
    def _():
        tracers_later[...] = jnp.zeros(tracers_later.shape, jnp.float32)

    @pl.when(jnp.logical_not(in_air()))
    def _():
        tracers_later[...] = renewed[...]
        warmth[...] = jnp.zeros(warmth.shape, jnp.float32)

    for j, part in enumerate(returned):

        @pl.when(block == j)
        def _(part=part):
            warmth[...] = part[...]


def per_device(
    climate_field_table,
    zonal_wind_speed,
    meridional_wind,
    sea_warmth_field,
    exchange_law_factor,
    regrid_matrix_stack,
    entry_sender_patch,
    holder_live_total,
    marine_salinity_heat,
    adjacent_offset_lists,
    polygon_side_total,
    interface_mixing_factor,
    solute_forcing_factor,
):
    sections = lax.axis_size("sec")
    ranks = lax.axis_size("rank")
    oceans = sections // 4
    air = sections - oceans
    _, x_points, rows, y_points = climate_field_table.shape
    levels = zonal_wind_speed.shape[2]
    flux_count = exchange_law_factor.shape[0]
    _, tracer_count, depth, cells = marine_salinity_heat.shape
    slots = regrid_matrix_stack.shape[2]
    f32, bf16 = jnp.float32, jnp.bfloat16
    shape = jax.ShapeDtypeStruct

    field = climate_field_table.reshape(x_points * rows, y_points)
    zonal = zonal_wind_speed.reshape(x_points * levels, y_points)
    meridional = meridional_wind.reshape(x_points * levels, y_points)
    regrid = regrid_matrix_stack.reshape(slots * cells * x_points, y_points)
    tracers = marine_salinity_heat.reshape(tracer_count * depth, cells)
    offsets = jnp.transpose(adjacent_offset_lists, (1, 0, 2))
    mixing = jnp.transpose(interface_mixing_factor, (1, 0, 2))
    live = jnp.transpose(holder_live_total, (1, 0))

    along = np.kron(np.eye(y_points // NODES, dtype=np.float32), gll_matrix().T)
    along = jnp.asarray(along)

    fields = rows // levels
    tile = min(8, levels)
    in_place = (
        exchange_law_factor,
        climate_field_table.reshape(x_points, fields, levels, y_points),
        zonal_wind_speed[0],
        meridional_wind[0],
        sea_warmth_field,
    )
    swap_rows = max(flux_count * x_points, rows + 16)
    fluxes = pl.pallas_call(
        functools.partial(flux_kernel, levels),
        out_shape=shape((swap_rows, y_points), bf16),
        in_specs=[HBM] * len(in_place),
        out_specs=VMEM,
        scratch_shapes=[
            pltpu.SMEM(exchange_law_factor.shape, f32),
            pltpu.VMEM((x_points, fields, tile, y_points), f32),
            pltpu.VMEM((x_points, tile, y_points), f32),
            pltpu.VMEM((x_points, tile, y_points), f32),
            pltpu.VMEM((1, x_points, y_points), f32),
            pltpu.SemaphoreType.DMA((len(in_place),)),
        ],
        compiler_params=PARAMS,
        cost_estimate=cost(1),
        name="flux",
    )(*(pltpu.with_memory_space_constraint(a, pltpu.HBM) for a in in_place))
    first, last, own = pl.pallas_call(
        functools.partial(edge_kernel, levels, rows),
        out_shape=(
            shape((rows, y_points), bf16),
            shape((rows, y_points), bf16),
            shape((2, rows, y_points), f32),
        ),
        in_specs=[VMEM] * 5 + [ANY],
        out_specs=(VMEM,) * 3,
        compiler_params=PARAMS,
        cost_estimate=cost(1),
        name="edges",
    )(field, zonal, meridional, along, tracers, fluxes)
    up = [(i, (i + 1) % ranks) for i in range(ranks)]
    below = lax.ppermute(last, "rank", up)
    above = lax.ppermute(first, "rank", [(j, i) for i, j in up])

    def turned(value, m):
        pairs = [(s, s // oceans * oceans + (s + m) % oceans) for s in range(sections)]
        return lax.ppermute(value, "sec", pairs)

    def paired(value, mask):
        pairs = [
            (s, (s // oceans ^ mask) * oceans + (s % oceans ^ 1)) for s in range(sections)
        ]
        return lax.ppermute(value, "sec", pairs)

    received = [turned(fluxes, m) for m in range(1, oceans)]
    packed = pl.pallas_call(
        pack_kernel,
        out_shape=shape((oceans, flux_count * x_points, y_points), bf16),
        in_specs=[VMEM] * oceans,
        out_specs=VMEM,
        compiler_params=PARAMS,
        cost_estimate=cost(0.2),
        name="pack",
    )(fluxes, *received)
    arrived = [paired(packed, 3 ^ block) for block in range(3)]

    from_memory = (
        entry_sender_patch,
        live,
        solute_forcing_factor,
        offsets,
        polygon_side_total,
        mixing,
    )
    later, diffused, chosen, returning, forcing, gather, spread = pl.pallas_call(
        functools.partial(middle_kernel, levels, rows),
        out_shape=(
            shape((x_points, rows, y_points), f32),
            shape(tracers.shape, f32),
            shape((slots * air, y_points), f32),
            shape((slots * air, y_points), f32),
            shape((flux_count * tracer_count * depth, cells), f32),
            shape((x_points * cells, cells), bf16),
            shape((cells, x_points * cells), bf16),
        ),
        in_specs=[VMEM] * 8 + [HBM] * 6,
        out_specs=(HBM,) + (VMEM,) * 6,
        scratch_shapes=[
            pltpu.VMEM(field.shape, f32),
            pltpu.VMEM((x_points, rows, y_points), f32),
        ]
        + [
            (pltpu.SMEM if i < 3 else pltpu.VMEM)(a.shape, a.dtype)
            for i, a in enumerate(from_memory)
        ]
        + [
            pltpu.SemaphoreType.DMA((max(fields, x_points),)),
            pltpu.SemaphoreType.DMA((len(from_memory),)),
        ],
        compiler_params=PARAMS,
        cost_estimate=cost(1),
        name="middle",
    )(
        field,
        zonal,
        meridional,
        along,
        own,
        below,
        above,
        tracers,
        *(pltpu.with_memory_space_constraint(a, pltpu.HBM) for a in from_memory),
    )

    renewed, *shares = pl.pallas_call(
        remap_kernel,
        out_shape=(shape(tracers.shape, f32),)
        + (shape((air // oceans, x_points, y_points), f32),) * oceans,
        in_specs=[VMEM] * 10,
        out_specs=(VMEM,) * (1 + oceans),
        compiler_params=PARAMS,
        cost_estimate=cost(1),
        name="remap",
    )(regrid, gather, spread, chosen, returning, forcing, diffused, arrived[1], arrived[2], arrived[0])
    shares = shares[:1] + [turned(share, m) for m, share in enumerate(shares[1:], 1)]
    totals = pl.pallas_call(
        add_kernel,
        out_shape=(shape((x_points, y_points), f32),) * (air // oceans),
        in_specs=[VMEM] * oceans,
        out_specs=(VMEM,) * (air // oceans),
        compiler_params=PARAMS,
        cost_estimate=cost(0.3),
        name="add",
    )(*shares)
    returned = [paired(total, 3 ^ block) for block, total in enumerate(totals)]
    tracers_later, warmth = pl.pallas_call(
        last_kernel,
        out_shape=(shape(tracers.shape, f32), shape((x_points, y_points), f32)),
        in_specs=[VMEM] * (1 + len(returned)),
        out_specs=(VMEM,) * 2,
        compiler_params=PARAMS,
        cost_estimate=cost(0.5),
        name="last",
    )(renewed, *returned)
    return (
        later.reshape(climate_field_table.shape),
        tracers_later.reshape(marine_salinity_heat.shape),
        warmth[None],
    )


def solution(mesh):
    return jax.shard_map(
        per_device,
        mesh=mesh,
        in_specs=(
            P("sec", "rank", None, None),
            P("sec", "rank", None, None),
            P("sec", "rank", None, None),
            P("sec", "rank", None),
            P(),
            P("sec", "rank", None, None, None, None),
            P(None, "rank", None),
            P(None, "rank"),
            P("sec", None, None, "rank"),
            P("sec", None, "rank"),
            P("sec", "rank"),
            P("sec", None, "rank"),
            P(),
        ),
        out_specs=(
            P("sec", "rank", None, None),
            P("sec", None, None, "rank"),
            P("sec", "rank", None),
        ),
        check_vma=False,
    )
```

```python
import functools

import jax
import jax.numpy as jnp
import numpy as np
from jax import lax
from jax.experimental import pallas as pl
from jax.experimental.pallas import tpu as pltpu
from jax.sharding import PartitionSpec as P

STEP_ATMOS = 0.05
DIFFUSIVITY = 0.05
STEP_OCEAN = 0.5
NODES = 4

VMEM = pl.BlockSpec(memory_space=pltpu.VMEM)
ANY = pl.BlockSpec(memory_space=pl.ANY)
HBM = pl.BlockSpec(memory_space=pltpu.HBM)
SMEM = pl.BlockSpec(memory_space=pltpu.SMEM)
PARAMS = pltpu.CompilerParams(vmem_limit_bytes=8 * 2**20)
HIGHEST = lax.Precision.HIGHEST


def gll_matrix():
    nodes = np.array([-1.0, -1.0 / np.sqrt(5.0), 1.0 / np.sqrt(5.0), 1.0])
    legendre = (5.0 * nodes**3 - 3.0 * nodes) / 2.0
    matrix = np.zeros((4, 4))
    for i in range(4):
        for j in range(4):
            if i != j:
                matrix[i, j] = legendre[i] / (legendre[j] * (nodes[i] - nodes[j]))
    matrix[0, 0] = -3.0
    matrix[3, 3] = 3.0
    return matrix.astype(np.float32)


def cost(microseconds):
    return pl.CostEstimate(
        flops=0, bytes_accessed=int(microseconds * 3_000_000), transcendentals=0
    )


def in_air():
    sections = lax.axis_size("sec")
    return lax.axis_index("sec") < sections - sections // 4


def smooth_lines(value, lane):
    width = value.shape[-1]
    right = pltpu.roll(value, width - 1, value.ndim - 1)
    left = pltpu.roll(value, 1, value.ndim - 1)
    at_end = (lane % NODES == NODES - 1) & (lane < width - 1)
    at_start = (lane % NODES == 0) & (lane > 0)
    partner = jnp.where(at_end, right, jnp.where(at_start, left, value))
    return 0.5 * (value + partner)


def start_all(pairs, sems):
    copies = [
        pltpu.make_async_copy(source, target, sems.at[i])
        for i, (source, target) in enumerate(pairs)
    ]
    for copy in copies:
        copy.start()
    return copies


def first_kernel(
    levels,
    rows,
    law_in,
    field_in,
    zonal_in,
    meridional_in,
    sea_in,
    along_in,
    tracers_in,
    sent,
    first,
    last,
    own,
    law,
    field,
    zonal,
    meridional,
    sea,
    along,
    tracers,
    sems,
    field_sems,
):
    @pl.when(in_air())
    def _():
        x_points = sea.shape[1]
        others = start_all(
            (
                (along_in, along),
                (zonal_in, zonal),
                (meridional_in, meridional),
                (law_in, law),
                (sea_in, sea),
            ),
            sems,
        )
        places = [pl.ds(x * rows, rows) for x in range(x_points)]
        parts = start_all([(field_in.at[p, :], field.at[p, :]) for p in places], field_sems)
        for copy in others[:3]:
            copy.wait()
        d = gll_matrix()
        lane = lax.broadcasted_iota(jnp.int32, (levels, field.shape[1]), 1)
        arrived = 0
        for side, (x, target) in enumerate(((0, first), (x_points - 1, last))):
            start = x - x % NODES
            while arrived < start + NODES:
                parts[arrived].wait()
                arrived += 1
            along_y = jnp.dot(
                field[places[x], :],
                along[...],
                precision=HIGHEST,
                preferred_element_type=jnp.float32,
            )
            u = zonal[pl.ds(x * levels, levels), :]
            v = meridional[pl.ds(x * levels, levels), :]
            for f in range(rows // levels):
                at = f * levels
                along_x = sum(
                    float(d[x % NODES, a]) * field[pl.ds((start + a) * rows + at, levels), :]
                    for a in range(NODES)
                    if d[x % NODES, a] != 0
                )
                value = -(u * along_x + v * along_y[at : at + levels])
                value = smooth_lines(value, lane)
                own[side, pl.ds(at, levels), :] = value
                target[pl.ds(at, levels), :] = value.astype(jnp.bfloat16)

        for copy in parts[arrived:] + others[3:]:
            copy.wait()
        flux_count, columns = law.shape
        u = zonal[pl.ds(0, x_points, stride=levels), :]
        v = meridional[pl.ds(0, x_points, stride=levels), :]
        speed = jnp.sqrt(1.0 + u * u + v * v)
        ground = [
            field[pl.ds(f * levels, x_points, stride=rows), :] for f in range(columns - 1)
        ] + [sea[0]]
        blocks = []
        for n in range(flux_count):
            total = law[n, 0] * ground[0]
            for f in range(1, columns):
                total = total + law[n, f] * ground[f]
            blocks.append(speed * total)
        block = jnp.concatenate(blocks, axis=0).astype(jnp.bfloat16)
        sent[pl.ds(0, block.shape[0]), :] = block

    @pl.when(jnp.logical_not(in_air()))
    def _():
        copy = pltpu.make_async_copy(tracers_in, tracers, sems.at[0])
        copy.start()
        copy.wait()
        value = tracers[...]
        high = value.astype(jnp.bfloat16)
        low = (value - high.astype(jnp.float32)).astype(jnp.bfloat16)
        both = jnp.concatenate([high, low], axis=0)
        for target in (first, last):
            target[pl.ds(0, both.shape[0]), :] = both


def pack_kernel(own, *refs):
    received, packed = refs[:-1], refs[-1]
    count = len(refs)
    place = lax.axis_index("sec") % count
    here = pl.ds(0, packed.shape[1])
    packed[place] = own[here, :]
    for m, part in enumerate(received, 1):
        packed[(place - m + count) % count] = part[here, :]


def middle_kernel(
    levels,
    rows,
    field,
    zonal,
    meridional,
    along,
    own,
    below,
    above,
    tracers,
    senders_in,
    live_in,
    factor_in,
    offsets_in,
    sides_in,
    mixing_in,
    later,
    diffused,
    chosen,
    returning,
    forcing,
    gather,
    spread,
    slopes,
    held,
    senders,
    live,
    factor,
    offsets,
    sides,
    mixing,
    sems,
    load_sems,
):
    x_points = later.shape[0]

    @pl.when(in_air())
    def _():
        d = gll_matrix()
        lane = lax.broadcasted_iota(jnp.int32, (levels, field.shape[1]), 1)
        inner = pl.ds(rows, (x_points - 2) * rows)
        slopes[inner, :] = jnp.dot(
            field[inner, :], along[...], precision=HIGHEST, preferred_element_type=jnp.float32
        )
        copies = []
        for f in range(rows // levels):
            at = f * levels
            here = pl.ds(at, levels)
            values = {
                0: 0.5 * (own[0, here, :] + below[here, :].astype(jnp.float32)),
                x_points - 1: 0.5 * (own[1, here, :] + above[here, :].astype(jnp.float32)),
            }
            q = [field[pl.ds(x * rows + at, levels), :] for x in range(x_points)]
            for x in range(1, x_points - 1):
                start = x - x % NODES
                along_x = sum(
                    float(d[x % NODES, a]) * q[start + a]
                    for a in range(NODES)
                    if d[x % NODES, a] != 0
                )
                u = zonal[pl.ds(x * levels, levels), :]
                v = meridional[pl.ds(x * levels, levels), :]
                value = -(u * along_x + v * slopes[pl.ds(x * rows + at, levels), :])
                values[x] = smooth_lines(value, lane)
            for x in range(NODES - 1, x_points - 1, NODES):
                values[x] = values[x + 1] = 0.5 * (values[x] + values[x + 1])
            for x in range(x_points):
                held[x, here, :] = q[x] + STEP_ATMOS * values[x]
            copy = pltpu.make_async_copy(held.at[:, here, :], later.at[:, here, :], sems.at[f])
            copy.start()
            copies.append(copy)
        for copy in copies:
            copy.wait()

    @pl.when(jnp.logical_not(in_air()))
    def _():
        loads = start_all(
            (
                (senders_in, senders),
                (live_in, live),
                (factor_in, factor),
                (offsets_in, offsets),
                (sides_in, sides),
                (mixing_in, mixing),
            ),
            load_sems,
        )
        held[0] = jnp.zeros(held.shape[1:], jnp.float32)
        copies = start_all([(held.at[0], later.at[x]) for x in range(x_points)], sems)
        cells = sides.shape[1]
        x_count = gather.shape[0] // cells
        point = lax.broadcasted_iota(jnp.int32, gather.shape, 0) // x_count
        cell = lax.broadcasted_iota(jnp.int32, gather.shape, 1)
        gather[...] = jnp.where(point == cell, 1.0, 0.0).astype(gather.dtype)
        cell = lax.broadcasted_iota(jnp.int32, spread.shape, 0)
        point = lax.broadcasted_iota(jnp.int32, spread.shape, 1) // x_count
        spread[...] = jnp.where(point == cell, 1.0, 0.0).astype(spread.dtype)
        for load in loads:
            load.wait()

        source = lax.broadcasted_iota(jnp.int32, (cells, cells), 0)
        target = lax.broadcasted_iota(jnp.int32, (cells, cells), 1)
        inside = jnp.zeros((cells, cells), jnp.float32)
        outside = jnp.zeros((cells, cells), jnp.float32)
        total = jnp.zeros((1, cells), jnp.float32)
        for e in range(offsets.shape[0]):
            weight = jnp.where(e < sides[...], mixing[e], 0.0)
            place = target[:1] + offsets[e]
            total = total + weight
            inside = inside + jnp.where(source == place, weight, 0.0)
            hit = (source == place - cells) | (source == place + cells)
            outside = outside + jnp.where(hit, weight, 0.0)
        inside = inside - jnp.where(source == target, total, 0.0)

        value = tracers[...]
        height = value.shape[0]
        cell = lax.broadcasted_iota(jnp.int32, value.shape, 1)
        beside = [
            h[pl.ds(0, height), :].astype(jnp.float32)
            + h[pl.ds(height, height), :].astype(jnp.float32)
            for h in (below, above)
        ]
        outer = jnp.where(cell < cells // 2, beside[1], beside[0])
        change = jnp.dot(
            jnp.concatenate([value, outer], axis=1),
            jnp.concatenate([inside, outside], axis=0),
            precision=HIGHEST,
            preferred_element_type=jnp.float32,
        )
        diffused[...] = value + DIFFUSIVITY * change

        sections = lax.axis_size("sec")
        oceans = sections // 4
        air = sections - oceans
        ocean = jnp.maximum(lax.axis_index("sec") - air, 0)
        width = chosen.shape[1]
        count = live[0, ocean]
        for k in range(senders.shape[2]):
            place = jnp.where(k < count, senders[ocean, 0, k], sections)
            section = lax.broadcasted_iota(jnp.int32, (air, width), 0)
            chosen[pl.ds(k * air, air), :] = jnp.where(section == place, 1.0, 0.0)
            block = section % (air // oceans)
            owner = ((ocean + section // (air // oceans)) % oceans) ^ 1
            returning[pl.ds(k * air, air), :] = jnp.where(
                block * oceans + owner == place, 1.0, 0.0
            )
        tracer_count, flux_count = factor.shape
        depth = forcing.shape[0] // (tracer_count * flux_count)
        level = lax.broadcasted_iota(jnp.int32, (depth, width), 0).astype(jnp.float32)
        profile = STEP_OCEAN * jnp.exp(-0.5 * level)
        for n in range(flux_count):
            for t in range(tracer_count):
                forcing[pl.ds((n * tracer_count + t) * depth, depth), :] = factor[t, n] * profile
        for copy in copies:
            copy.wait()


def remap_kernel(
    regrid, gather, spread, chosen, returning, forcing, diffused, *refs
):
    arrived, renewed, shares = (refs[2], refs[0], refs[1]), refs[3], refs[4:]

    @pl.when(jnp.logical_not(in_air()))
    def _():
        points, cells = gather.shape
        x_count = points // cells
        slots = regrid.shape[0] // points
        air = chosen.shape[0] // slots
        packed = refs[0].shape[1]
        flux_count = packed // x_count
        row = lax.broadcasted_iota(jnp.int32, (x_count, cells), 0)
        column = lax.broadcasted_iota(jnp.int32, (x_count, cells), 1)
        same = jnp.where(row == column % x_count, 1.0, 0.0)

        blocks = [block[s].astype(jnp.float32) for block in arrived for s in range(block.shape[0])]
        matched = None
        for k in range(slots):
            part = chosen[pl.ds(k * air, 1), :] * blocks[0]
            for s in range(1, air):
                part = part + chosen[pl.ds(k * air + s, 1), :] * blocks[s]
            product = lax.dot_general(
                part.astype(jnp.bfloat16),
                regrid[pl.ds(k * points, points), :],
                (((1,), (1,)), ((), ())),
                preferred_element_type=jnp.float32,
            )
            matched = product if matched is None else matched + product
        matched = matched * jnp.tile(same, (flux_count, x_count))
        high = matched.astype(jnp.bfloat16)
        low = (matched - high.astype(jnp.float32)).astype(jnp.bfloat16)
        summed = jnp.dot(
            jnp.concatenate([high, low], axis=0), gather[...], preferred_element_type=jnp.float32
        )
        ocean_flux = (summed[:packed] + summed[packed:]).reshape(flux_count, x_count, cells).sum(axis=1)
        height = diffused.shape[0]
        value = diffused[...]
        for n in range(flux_count):
            value = value + forcing[pl.ds(n * height, height), :] * ocean_flux[n : n + 1]
        renewed[...] = value

        top = jnp.broadcast_to(value[0:1], (x_count, cells)).astype(jnp.bfloat16)
        wide = jnp.dot(top, spread[...], preferred_element_type=jnp.float32)
        wide = (wide * jnp.tile(same, (1, x_count))).astype(jnp.bfloat16)
        back = [
            jnp.dot(wide, regrid[pl.ds(k * points, points), :], preferred_element_type=jnp.float32)
            for k in range(slots)
        ]
        count = shares[0].shape[0]
        for m, share in enumerate(shares):
            for j in range(count):
                at = m * count + j
                total = returning[pl.ds(at, 1), :] * back[0]
                for k in range(1, slots):
                    total = total + returning[pl.ds(k * air + at, 1), :] * back[k]
                share[j] = total


def add_kernel(*refs):
    count = refs[0].shape[0]
    shares, totals = refs[:-count], refs[-count:]

    @pl.when(jnp.logical_not(in_air()))
    def _():
        for j, total in enumerate(totals):
            value = shares[0][j]
            for share in shares[1:]:
                value = value + share[j]
            total[...] = value


def last_kernel(renewed, *refs):
    returned, (tracers_later, warmth) = refs[:-2], refs[-2:]
    sections = lax.axis_size("sec")
    block = lax.axis_index("sec") // (sections // 4)

    @pl.when(in_air())
    def _():
        tracers_later[...] = jnp.zeros(tracers_later.shape, jnp.float32)

    @pl.when(jnp.logical_not(in_air()))
    def _():
        tracers_later[...] = renewed[...]
        warmth[...] = jnp.zeros(warmth.shape, jnp.float32)

    for j, part in enumerate(returned):

        @pl.when(block == j)
        def _(part=part):
            warmth[...] = part[...]


def per_device(
    climate_field_table,
    zonal_wind_speed,
    meridional_wind,
    sea_warmth_field,
    exchange_law_factor,
    regrid_matrix_stack,
    entry_sender_patch,
    holder_live_total,
    marine_salinity_heat,
    adjacent_offset_lists,
    polygon_side_total,
    interface_mixing_factor,
    solute_forcing_factor,
):
    sections = lax.axis_size("sec")
    ranks = lax.axis_size("rank")
    oceans = sections // 4
    air = sections - oceans
    _, x_points, rows, y_points = climate_field_table.shape
    levels = zonal_wind_speed.shape[2]
    flux_count = exchange_law_factor.shape[0]
    _, tracer_count, depth, cells = marine_salinity_heat.shape
    slots = regrid_matrix_stack.shape[2]
    f32, bf16 = jnp.float32, jnp.bfloat16
    shape = jax.ShapeDtypeStruct

    field = climate_field_table.reshape(x_points * rows, y_points)
    zonal = zonal_wind_speed.reshape(x_points * levels, y_points)
    meridional = meridional_wind.reshape(x_points * levels, y_points)
    regrid = regrid_matrix_stack.reshape(slots * cells * x_points, y_points)
    tracers = marine_salinity_heat.reshape(tracer_count * depth, cells)
    offsets = jnp.transpose(adjacent_offset_lists, (1, 0, 2))
    mixing = jnp.transpose(interface_mixing_factor, (1, 0, 2))
    live = jnp.transpose(holder_live_total, (1, 0))

    along = np.kron(np.eye(y_points // NODES, dtype=np.float32), gll_matrix().T)
    along = jnp.asarray(along)

    fields = rows // levels
    in_place = (exchange_law_factor, field, zonal, meridional, sea_warmth_field, along, tracers)
    swap_rows = max(flux_count * x_points, rows + 16)
    fluxes, first, last, own = pl.pallas_call(
        functools.partial(first_kernel, levels, rows),
        out_shape=(
            shape((swap_rows, y_points), bf16),
            shape((rows, y_points), bf16),
            shape((rows, y_points), bf16),
            shape((2, rows, y_points), f32),
        ),
        in_specs=[HBM] * len(in_place),
        out_specs=(VMEM,) * 4,
        scratch_shapes=[pltpu.SMEM(exchange_law_factor.shape, f32)]
        + [pltpu.VMEM(a.shape, f32) for a in in_place[1:]]
        + [pltpu.SemaphoreType.DMA((5,)), pltpu.SemaphoreType.DMA((x_points,))],
        compiler_params=PARAMS,
        cost_estimate=cost(2),
        name="first",
    )(*(pltpu.with_memory_space_constraint(a, pltpu.HBM) for a in in_place))
    up = [(i, (i + 1) % ranks) for i in range(ranks)]
    below = lax.ppermute(last, "rank", up)
    above = lax.ppermute(first, "rank", [(j, i) for i, j in up])

    def turned(value, m):
        pairs = [(s, s // oceans * oceans + (s + m) % oceans) for s in range(sections)]
        return lax.ppermute(value, "sec", pairs)

    def paired(value, mask):
        pairs = [
            (s, (s // oceans ^ mask) * oceans + (s % oceans ^ 1)) for s in range(sections)
        ]
        return lax.ppermute(value, "sec", pairs)

    received = [turned(fluxes, m) for m in range(1, oceans)]
    packed = pl.pallas_call(
        pack_kernel,
        out_shape=shape((oceans, flux_count * x_points, y_points), bf16),
        in_specs=[VMEM] * oceans,
        out_specs=VMEM,
        compiler_params=PARAMS,
        cost_estimate=cost(0.2),
        name="pack",
    )(fluxes, *received)
    arrived = [paired(packed, 3 ^ block) for block in range(3)]

    from_memory = (
        entry_sender_patch,
        live,
        solute_forcing_factor,
        offsets,
        polygon_side_total,
        mixing,
    )
    later, diffused, chosen, returning, forcing, gather, spread = pl.pallas_call(
        functools.partial(middle_kernel, levels, rows),
        out_shape=(
            shape((x_points, rows, y_points), f32),
            shape(tracers.shape, f32),
            shape((slots * air, y_points), f32),
            shape((slots * air, y_points), f32),
            shape((flux_count * tracer_count * depth, cells), f32),
            shape((x_points * cells, cells), bf16),
            shape((cells, x_points * cells), bf16),
        ),
        in_specs=[VMEM] * 8 + [HBM] * 6,
        out_specs=(HBM,) + (VMEM,) * 6,
        scratch_shapes=[
            pltpu.VMEM(field.shape, f32),
            pltpu.VMEM((x_points, rows, y_points), f32),
        ]
        + [
            (pltpu.SMEM if i < 3 else pltpu.VMEM)(a.shape, a.dtype)
            for i, a in enumerate(from_memory)
        ]
        + [
            pltpu.SemaphoreType.DMA((max(fields, x_points),)),
            pltpu.SemaphoreType.DMA((len(from_memory),)),
        ],
        compiler_params=PARAMS,
        cost_estimate=cost(1),
        name="middle",
    )(
        field,
        zonal,
        meridional,
        along,
        own,
        below,
        above,
        tracers,
        *(pltpu.with_memory_space_constraint(a, pltpu.HBM) for a in from_memory),
    )

    renewed, *shares = pl.pallas_call(
        remap_kernel,
        out_shape=(shape(tracers.shape, f32),)
        + (shape((air // oceans, x_points, y_points), f32),) * oceans,
        in_specs=[VMEM] * 10,
        out_specs=(VMEM,) * (1 + oceans),
        compiler_params=PARAMS,
        cost_estimate=cost(1),
        name="remap",
    )(regrid, gather, spread, chosen, returning, forcing, diffused, arrived[1], arrived[2], arrived[0])
    shares = shares[:1] + [turned(share, m) for m, share in enumerate(shares[1:], 1)]
    totals = pl.pallas_call(
        add_kernel,
        out_shape=(shape((x_points, y_points), f32),) * (air // oceans),
        in_specs=[VMEM] * oceans,
        out_specs=(VMEM,) * (air // oceans),
        compiler_params=PARAMS,
        cost_estimate=cost(0.3),
        name="add",
    )(*shares)
    returned = [paired(total, 3 ^ block) for block, total in enumerate(totals)]
    tracers_later, warmth = pl.pallas_call(
        last_kernel,
        out_shape=(shape(tracers.shape, f32), shape((x_points, y_points), f32)),
        in_specs=[VMEM] * (1 + len(returned)),
        out_specs=(VMEM,) * 2,
        compiler_params=PARAMS,
        cost_estimate=cost(0.5),
        name="last",
    )(renewed, *returned)
    return (
        later.reshape(climate_field_table.shape),
        tracers_later.reshape(marine_salinity_heat.shape),
        warmth[None],
    )


def solution(mesh):
    return jax.shard_map(
        per_device,
        mesh=mesh,
        in_specs=(
            P("sec", "rank", None, None),
            P("sec", "rank", None, None),
            P("sec", "rank", None, None),
            P("sec", "rank", None),
            P(),
            P("sec", "rank", None, None, None, None),
            P(None, "rank", None),
            P(None, "rank"),
            P("sec", None, None, "rank"),
            P("sec", None, "rank"),
            P("sec", "rank"),
            P("sec", None, "rank"),
            P(),
        ),
        out_specs=(
            P("sec", "rank", None, None),
            P("sec", None, None, "rank"),
            P("sec", "rank", None),
        ),
        check_vma=False,
    )
```

```python
import functools

import jax
import jax.numpy as jnp
import numpy as np
from jax import lax
from jax.experimental import pallas as pl
from jax.experimental.pallas import tpu as pltpu
from jax.sharding import PartitionSpec as P

STEP_ATMOS = 0.05
DIFFUSIVITY = 0.05
STEP_OCEAN = 0.5
NODES = 4

VMEM = pl.BlockSpec(memory_space=pltpu.VMEM)
ANY = pl.BlockSpec(memory_space=pl.ANY)
HBM = pl.BlockSpec(memory_space=pltpu.HBM)
SMEM = pl.BlockSpec(memory_space=pltpu.SMEM)
PARAMS = pltpu.CompilerParams(vmem_limit_bytes=8 * 2**20)
HIGHEST = lax.Precision.HIGHEST


def gll_matrix():
    nodes = np.array([-1.0, -1.0 / np.sqrt(5.0), 1.0 / np.sqrt(5.0), 1.0])
    legendre = (5.0 * nodes**3 - 3.0 * nodes) / 2.0
    matrix = np.zeros((4, 4))
    for i in range(4):
        for j in range(4):
            if i != j:
                matrix[i, j] = legendre[i] / (legendre[j] * (nodes[i] - nodes[j]))
    matrix[0, 0] = -3.0
    matrix[3, 3] = 3.0
    return matrix.astype(np.float32)


def cost(microseconds):
    return pl.CostEstimate(
        flops=0, bytes_accessed=int(microseconds * 3_000_000), transcendentals=0
    )


def in_air():
    sections = lax.axis_size("sec")
    return lax.axis_index("sec") < sections - sections // 4


def smooth_lines(value, lane):
    width = value.shape[-1]
    right = pltpu.roll(value, width - 1, value.ndim - 1)
    left = pltpu.roll(value, 1, value.ndim - 1)
    at_end = (lane % NODES == NODES - 1) & (lane < width - 1)
    at_start = (lane % NODES == 0) & (lane > 0)
    partner = jnp.where(at_end, right, jnp.where(at_start, left, value))
    return 0.5 * (value + partner)


def start_all(pairs, sems):
    copies = [
        pltpu.make_async_copy(source, target, sems.at[i])
        for i, (source, target) in enumerate(pairs)
    ]
    for copy in copies:
        copy.start()
    return copies


def flux_kernel(
    levels, law_in, field_in, zonal_in, meridional_in, sea_in, sent, law, field, zonal, meridional, sea, sems
):
    @pl.when(in_air())
    def _():
        x_points, fields, tile, y_points = field.shape
        lowest = pl.ds(0, tile)
        copies = start_all(
            [(law_in, law)]
            + [(field_in.at[x, :, lowest, :], field.at[x]) for x in range(x_points)]
            + [
                (zonal_in.at[:, lowest, :], zonal),
                (meridional_in.at[:, lowest, :], meridional),
                (sea_in, sea),
            ],
            sems,
        )
        for copy in copies:
            copy.wait()
        flux_count, columns = law.shape
        flat = field.reshape(x_points * fields * tile, y_points)
        ground = [
            flat[pl.ds(f * tile, x_points, stride=fields * tile), :] for f in range(fields)
        ] + [sea[0]]
        u = zonal.reshape(x_points * tile, y_points)[pl.ds(0, x_points, stride=tile), :]
        v = meridional.reshape(x_points * tile, y_points)[pl.ds(0, x_points, stride=tile), :]
        speed = jnp.sqrt(1.0 + u * u + v * v)
        parts = []
        for n in range(flux_count):
            total = law[n, 0] * ground[0]
            for f in range(1, columns):
                total = total + law[n, f] * ground[f]
            parts.append(speed * total)
        block = jnp.concatenate(parts, axis=0).astype(jnp.bfloat16)
        sent[pl.ds(0, block.shape[0]), :] = block


def edge_kernel(levels, rows, field, zonal, meridional, along, tracers, after, first, last, own):
    x_points = field.shape[0] // rows

    @pl.when(in_air())
    def _():
        d = gll_matrix()
        lane = lax.broadcasted_iota(jnp.int32, (levels, field.shape[1]), 1)
        for side, (x, target) in enumerate(((0, first), (x_points - 1, last))):
            start = x - x % NODES
            along_y = jnp.dot(
                field[pl.ds(x * rows, rows), :],
                along[...],
                precision=HIGHEST,
                preferred_element_type=jnp.float32,
            )
            u = zonal[pl.ds(x * levels, levels), :]
            v = meridional[pl.ds(x * levels, levels), :]
            for f in range(rows // levels):
                at = f * levels
                along_x = sum(
                    float(d[x % NODES, a]) * field[pl.ds((start + a) * rows + at, levels), :]
                    for a in range(NODES)
                    if d[x % NODES, a] != 0
                )
                value = -(u * along_x + v * along_y[at : at + levels])
                value = smooth_lines(value, lane)
                own[side, pl.ds(at, levels), :] = value
                target[pl.ds(at, levels), :] = value.astype(jnp.bfloat16)

    @pl.when(jnp.logical_not(in_air()))
    def _():
        value = tracers[...]
        high = value.astype(jnp.bfloat16)
        low = (value - high.astype(jnp.float32)).astype(jnp.bfloat16)
        both = jnp.concatenate([high, low], axis=0)
        for target in (first, last):
            target[pl.ds(0, both.shape[0]), :] = both


def pack_kernel(own, *refs):
    received, packed = refs[:-1], refs[-1]
    count = len(refs)
    place = lax.axis_index("sec") % count
    here = pl.ds(0, packed.shape[1])
    packed[place] = own[here, :]
    for m, part in enumerate(received, 1):
        packed[(place - m + count) % count] = part[here, :]


def middle_kernel(
    levels,
    rows,
    field,
    zonal,
    meridional,
    along,
    own,
    below,
    above,
    tracers,
    senders_in,
    live_in,
    factor_in,
    offsets_in,
    sides_in,
    mixing_in,
    later,
    diffused,
    chosen,
    returning,
    forcing,
    gather,
    spread,
    slopes,
    held,
    senders,
    live,
    factor,
    offsets,
    sides,
    mixing,
    sems,
    load_sems,
):
    x_points = later.shape[0]

    @pl.when(in_air())
    def _():
        d = gll_matrix()
        lane = lax.broadcasted_iota(jnp.int32, (levels, field.shape[1]), 1)
        inner = pl.ds(rows, (x_points - 2) * rows)
        slopes[inner, :] = jnp.dot(
            field[inner, :], along[...], precision=HIGHEST, preferred_element_type=jnp.float32
        )
        copies = []
        for f in range(rows // levels):
            at = f * levels
            here = pl.ds(at, levels)
            values = {
                0: 0.5 * (own[0, here, :] + below[here, :].astype(jnp.float32)),
                x_points - 1: 0.5 * (own[1, here, :] + above[here, :].astype(jnp.float32)),
            }
            q = [field[pl.ds(x * rows + at, levels), :] for x in range(x_points)]
            for x in range(1, x_points - 1):
                start = x - x % NODES
                along_x = sum(
                    float(d[x % NODES, a]) * q[start + a]
                    for a in range(NODES)
                    if d[x % NODES, a] != 0
                )
                u = zonal[pl.ds(x * levels, levels), :]
                v = meridional[pl.ds(x * levels, levels), :]
                value = -(u * along_x + v * slopes[pl.ds(x * rows + at, levels), :])
                values[x] = smooth_lines(value, lane)
            for x in range(NODES - 1, x_points - 1, NODES):
                values[x] = values[x + 1] = 0.5 * (values[x] + values[x + 1])
            for x in range(x_points):
                held[x, here, :] = q[x] + STEP_ATMOS * values[x]
            copy = pltpu.make_async_copy(held.at[:, here, :], later.at[:, here, :], sems.at[f])
            copy.start()
            copies.append(copy)
        for copy in copies:
            copy.wait()

    @pl.when(jnp.logical_not(in_air()))
    def _():
        loads = start_all(
            (
                (senders_in, senders),
                (live_in, live),
                (factor_in, factor),
                (offsets_in, offsets),
                (sides_in, sides),
                (mixing_in, mixing),
            ),
            load_sems,
        )
        held[0] = jnp.zeros(held.shape[1:], jnp.float32)
        copies = start_all([(held.at[0], later.at[x]) for x in range(x_points)], sems)
        cells = sides.shape[1]
        x_count = gather.shape[0] // cells
        point = lax.broadcasted_iota(jnp.int32, gather.shape, 0) // x_count
        cell = lax.broadcasted_iota(jnp.int32, gather.shape, 1)
        gather[...] = jnp.where(point == cell, 1.0, 0.0).astype(gather.dtype)
        cell = lax.broadcasted_iota(jnp.int32, spread.shape, 0)
        point = lax.broadcasted_iota(jnp.int32, spread.shape, 1) // x_count
        spread[...] = jnp.where(point == cell, 1.0, 0.0).astype(spread.dtype)
        for load in loads:
            load.wait()

        source = lax.broadcasted_iota(jnp.int32, (cells, cells), 0)
        target = lax.broadcasted_iota(jnp.int32, (cells, cells), 1)
        inside = jnp.zeros((cells, cells), jnp.float32)
        outside = jnp.zeros((cells, cells), jnp.float32)
        total = jnp.zeros((1, cells), jnp.float32)
        for e in range(offsets.shape[0]):
            weight = jnp.where(e < sides[...], mixing[e], 0.0)
            place = target[:1] + offsets[e]
            total = total + weight
            inside = inside + jnp.where(source == place, weight, 0.0)
            hit = (source == place - cells) | (source == place + cells)
            outside = outside + jnp.where(hit, weight, 0.0)
        inside = inside - jnp.where(source == target, total, 0.0)

        value = tracers[...]
        height = value.shape[0]
        cell = lax.broadcasted_iota(jnp.int32, value.shape, 1)
        beside = [
            h[pl.ds(0, height), :].astype(jnp.float32)
            + h[pl.ds(height, height), :].astype(jnp.float32)
            for h in (below, above)
        ]
        outer = jnp.where(cell < cells // 2, beside[1], beside[0])
        change = jnp.dot(
            jnp.concatenate([value, outer], axis=1),
            jnp.concatenate([inside, outside], axis=0),
            precision=HIGHEST,
            preferred_element_type=jnp.float32,
        )
        diffused[...] = value + DIFFUSIVITY * change

        sections = lax.axis_size("sec")
        oceans = sections // 4
        air = sections - oceans
        ocean = jnp.maximum(lax.axis_index("sec") - air, 0)
        width = chosen.shape[1]
        count = live[0, ocean]
        for k in range(senders.shape[2]):
            place = jnp.where(k < count, senders[ocean, 0, k], sections)
            section = lax.broadcasted_iota(jnp.int32, (air, width), 0)
            chosen[pl.ds(k * air, air), :] = jnp.where(section == place, 1.0, 0.0)
            block = section % (air // oceans)
            owner = ((ocean + section // (air // oceans)) % oceans) ^ 1
            returning[pl.ds(k * air, air), :] = jnp.where(
                block * oceans + owner == place, 1.0, 0.0
            )
        tracer_count, flux_count = factor.shape
        depth = forcing.shape[0] // (tracer_count * flux_count)
        level = lax.broadcasted_iota(jnp.int32, (depth, width), 0).astype(jnp.float32)
        profile = STEP_OCEAN * jnp.exp(-0.5 * level)
        for n in range(flux_count):
            for t in range(tracer_count):
                forcing[pl.ds((n * tracer_count + t) * depth, depth), :] = factor[t, n] * profile
        for copy in copies:
            copy.wait()


def remap_kernel(
    regrid, gather, spread, chosen, returning, forcing, diffused, *refs
):
    arrived, renewed, shares = (refs[2], refs[0], refs[1]), refs[3], refs[4:]

    @pl.when(jnp.logical_not(in_air()))
    def _():
        points, cells = gather.shape
        x_count = points // cells
        slots = regrid.shape[0] // points
        air = chosen.shape[0] // slots
        packed = refs[0].shape[1]
        flux_count = packed // x_count
        row = lax.broadcasted_iota(jnp.int32, (x_count, cells), 0)
        column = lax.broadcasted_iota(jnp.int32, (x_count, cells), 1)
        same = jnp.where(row == column % x_count, 1.0, 0.0)

        blocks = [block[s].astype(jnp.float32) for block in arrived for s in range(block.shape[0])]
        matched = None
        for k in range(slots):
            part = chosen[pl.ds(k * air, 1), :] * blocks[0]
            for s in range(1, air):
                part = part + chosen[pl.ds(k * air + s, 1), :] * blocks[s]
            product = lax.dot_general(
                part.astype(jnp.bfloat16),
                regrid[pl.ds(k * points, points), :],
                (((1,), (1,)), ((), ())),
                preferred_element_type=jnp.float32,
            )
            matched = product if matched is None else matched + product
        matched = matched * jnp.tile(same, (flux_count, x_count))
        high = matched.astype(jnp.bfloat16)
        low = (matched - high.astype(jnp.float32)).astype(jnp.bfloat16)
        summed = jnp.dot(
            jnp.concatenate([high, low], axis=0), gather[...], preferred_element_type=jnp.float32
        )
        ocean_flux = (summed[:packed] + summed[packed:]).reshape(flux_count, x_count, cells).sum(axis=1)
        height = diffused.shape[0]
        value = diffused[...]
        for n in range(flux_count):
            value = value + forcing[pl.ds(n * height, height), :] * ocean_flux[n : n + 1]
        renewed[...] = value

        top = jnp.broadcast_to(value[0:1], (x_count, cells)).astype(jnp.bfloat16)
        wide = jnp.dot(top, spread[...], preferred_element_type=jnp.float32)
        wide = (wide * jnp.tile(same, (1, x_count))).astype(jnp.bfloat16)
        back = [
            jnp.dot(wide, regrid[pl.ds(k * points, points), :], preferred_element_type=jnp.float32)
            for k in range(slots)
        ]
        count = shares[0].shape[0]
        for m, share in enumerate(shares):
            for j in range(count):
                at = m * count + j
                total = returning[pl.ds(at, 1), :] * back[0]
                for k in range(1, slots):
                    total = total + returning[pl.ds(k * air + at, 1), :] * back[k]
                share[j] = total


def add_kernel(*refs):
    count = refs[0].shape[0]
    shares, totals = refs[:-count], refs[-count:]

    @pl.when(jnp.logical_not(in_air()))
    def _():
        for j, total in enumerate(totals):
            value = shares[0][j]
            for share in shares[1:]:
                value = value + share[j]
            total[...] = value


def last_kernel(renewed, *refs):
    returned, (tracers_later, warmth) = refs[:-2], refs[-2:]
    sections = lax.axis_size("sec")
    block = lax.axis_index("sec") // (sections // 4)

    @pl.when(in_air())
    def _():
        tracers_later[...] = jnp.zeros(tracers_later.shape, jnp.float32)

    @pl.when(jnp.logical_not(in_air()))
    def _():
        tracers_later[...] = renewed[...]
        warmth[...] = jnp.zeros(warmth.shape, jnp.float32)

    for j, part in enumerate(reversed(returned)):

        @pl.when(block == j)
        def _(part=part):
            warmth[...] = part[...]


def per_device(
    climate_field_table,
    zonal_wind_speed,
    meridional_wind,
    sea_warmth_field,
    exchange_law_factor,
    regrid_matrix_stack,
    entry_sender_patch,
    holder_live_total,
    marine_salinity_heat,
    adjacent_offset_lists,
    polygon_side_total,
    interface_mixing_factor,
    solute_forcing_factor,
):
    sections = lax.axis_size("sec")
    ranks = lax.axis_size("rank")
    oceans = sections // 4
    air = sections - oceans
    _, x_points, rows, y_points = climate_field_table.shape
    levels = zonal_wind_speed.shape[2]
    flux_count = exchange_law_factor.shape[0]
    _, tracer_count, depth, cells = marine_salinity_heat.shape
    slots = regrid_matrix_stack.shape[2]
    f32, bf16 = jnp.float32, jnp.bfloat16
    shape = jax.ShapeDtypeStruct

    field = climate_field_table.reshape(x_points * rows, y_points)
    zonal = zonal_wind_speed.reshape(x_points * levels, y_points)
    meridional = meridional_wind.reshape(x_points * levels, y_points)
    regrid = regrid_matrix_stack.reshape(slots * cells * x_points, y_points)
    tracers = marine_salinity_heat.reshape(tracer_count * depth, cells)
    offsets = jnp.transpose(adjacent_offset_lists, (1, 0, 2))
    mixing = jnp.transpose(interface_mixing_factor, (1, 0, 2))
    live = jnp.transpose(holder_live_total, (1, 0))

    along = np.kron(np.eye(y_points // NODES, dtype=np.float32), gll_matrix().T)
    along = jnp.asarray(along)

    fields = rows // levels
    tile = min(8, levels)
    in_place = (
        exchange_law_factor,
        climate_field_table.reshape(x_points, fields, levels, y_points),
        zonal_wind_speed[0],
        meridional_wind[0],
        sea_warmth_field,
    )
    swap_rows = max(flux_count * x_points, rows + 16)
    fluxes = pl.pallas_call(
        functools.partial(flux_kernel, levels),
        out_shape=shape((swap_rows, y_points), bf16),
        in_specs=[HBM] * len(in_place),
        out_specs=VMEM,
        scratch_shapes=[
            pltpu.SMEM(exchange_law_factor.shape, f32),
            pltpu.VMEM((x_points, fields, tile, y_points), f32),
            pltpu.VMEM((x_points, tile, y_points), f32),
            pltpu.VMEM((x_points, tile, y_points), f32),
            pltpu.VMEM((1, x_points, y_points), f32),
            pltpu.SemaphoreType.DMA((len(in_place) + x_points - 1,)),
        ],
        compiler_params=PARAMS,
        cost_estimate=cost(1),
        name="flux",
    )(*(pltpu.with_memory_space_constraint(a, pltpu.HBM) for a in in_place))
    first, last, own = pl.pallas_call(
        functools.partial(edge_kernel, levels, rows),
        out_shape=(
            shape((rows, y_points), bf16),
            shape((rows, y_points), bf16),
            shape((2, rows, y_points), f32),
        ),
        in_specs=[VMEM] * 5 + [ANY],
        out_specs=(VMEM,) * 3,
        compiler_params=PARAMS,
        cost_estimate=cost(1),
        name="edges",
    )(field, zonal, meridional, along, tracers, fluxes)
    up = [(i, (i + 1) % ranks) for i in range(ranks)]
    below = lax.ppermute(last, "rank", up)
    above = lax.ppermute(first, "rank", [(j, i) for i, j in up])

    def turned(value, m):
        pairs = [(s, s // oceans * oceans + (s + m) % oceans) for s in range(sections)]
        return lax.ppermute(value, "sec", pairs)

    def paired(value, mask):
        pairs = [
            (s, (s // oceans ^ mask) * oceans + (s % oceans ^ 1)) for s in range(sections)
        ]
        return lax.ppermute(value, "sec", pairs)

    received = [turned(fluxes, m) for m in range(1, oceans)]
    packed = pl.pallas_call(
        pack_kernel,
        out_shape=shape((oceans, flux_count * x_points, y_points), bf16),
        in_specs=[VMEM] * oceans,
        out_specs=VMEM,
        compiler_params=PARAMS,
        cost_estimate=cost(0.2),
        name="pack",
    )(fluxes, *received)
    arrived = [paired(packed, 3 ^ block) for block in range(3)]

    from_memory = (
        entry_sender_patch,
        live,
        solute_forcing_factor,
        offsets,
        polygon_side_total,
        mixing,
    )
    later, diffused, chosen, returning, forcing, gather, spread = pl.pallas_call(
        functools.partial(middle_kernel, levels, rows),
        out_shape=(
            shape((x_points, rows, y_points), f32),
            shape(tracers.shape, f32),
            shape((slots * air, y_points), f32),
            shape((slots * air, y_points), f32),
            shape((flux_count * tracer_count * depth, cells), f32),
            shape((x_points * cells, cells), bf16),
            shape((cells, x_points * cells), bf16),
        ),
        in_specs=[VMEM] * 8 + [HBM] * 6,
        out_specs=(HBM,) + (VMEM,) * 6,
        scratch_shapes=[
            pltpu.VMEM(field.shape, f32),
            pltpu.VMEM((x_points, rows, y_points), f32),
        ]
        + [
            (pltpu.SMEM if i < 3 else pltpu.VMEM)(a.shape, a.dtype)
            for i, a in enumerate(from_memory)
        ]
        + [
            pltpu.SemaphoreType.DMA((max(fields, x_points),)),
            pltpu.SemaphoreType.DMA((len(from_memory),)),
        ],
        compiler_params=PARAMS,
        cost_estimate=cost(1),
        name="middle",
    )(
        field,
        zonal,
        meridional,
        along,
        own,
        below,
        above,
        tracers,
        *(pltpu.with_memory_space_constraint(a, pltpu.HBM) for a in from_memory),
    )

    renewed, *shares = pl.pallas_call(
        remap_kernel,
        out_shape=(shape(tracers.shape, f32),)
        + (shape((air // oceans, x_points, y_points), f32),) * oceans,
        in_specs=[VMEM] * 10,
        out_specs=(VMEM,) * (1 + oceans),
        compiler_params=PARAMS,
        cost_estimate=cost(1),
        name="remap",
    )(regrid, gather, spread, chosen, returning, forcing, diffused, arrived[1], arrived[2], arrived[0])
    shares = shares[:1] + [turned(share, m) for m, share in enumerate(shares[1:], 1)]
    totals = pl.pallas_call(
        add_kernel,
        out_shape=(shape((x_points, y_points), f32),) * (air // oceans),
        in_specs=[VMEM] * oceans,
        out_specs=(VMEM,) * (air // oceans),
        compiler_params=PARAMS,
        cost_estimate=cost(0.3),
        name="add",
    )(*shares)
    returned = [paired(total, 3 ^ block) for block, total in enumerate(totals)]
    tracers_later, warmth = pl.pallas_call(
        last_kernel,
        out_shape=(shape(tracers.shape, f32), shape((x_points, y_points), f32)),
        in_specs=[VMEM] * (1 + len(returned)),
        out_specs=(VMEM,) * 2,
        compiler_params=PARAMS,
        cost_estimate=cost(0.5),
        name="last",
    )(renewed, *reversed(returned))
    return (
        later.reshape(climate_field_table.shape),
        tracers_later.reshape(marine_salinity_heat.shape),
        warmth[None],
    )


def solution(mesh):
    return jax.shard_map(
        per_device,
        mesh=mesh,
        in_specs=(
            P("sec", "rank", None, None),
            P("sec", "rank", None, None),
            P("sec", "rank", None, None),
            P("sec", "rank", None),
            P(),
            P("sec", "rank", None, None, None, None),
            P(None, "rank", None),
            P(None, "rank"),
            P("sec", None, None, "rank"),
            P("sec", None, "rank"),
            P("sec", "rank"),
            P("sec", None, "rank"),
            P(),
        ),
        out_specs=(
            P("sec", "rank", None, None),
            P("sec", None, None, "rank"),
            P("sec", "rank", None),
        ),
        check_vma=False,
    )
```

```python
import functools

import jax
import jax.numpy as jnp
import numpy as np
from jax import lax
from jax.experimental import pallas as pl
from jax.experimental.pallas import tpu as pltpu
from jax.sharding import PartitionSpec as P

STEP_ATMOS = 0.05
DIFFUSIVITY = 0.05
STEP_OCEAN = 0.5
NODES = 4

VMEM = pl.BlockSpec(memory_space=pltpu.VMEM)
ANY = pl.BlockSpec(memory_space=pl.ANY)
HBM = pl.BlockSpec(memory_space=pltpu.HBM)
SMEM = pl.BlockSpec(memory_space=pltpu.SMEM)
PARAMS = pltpu.CompilerParams(vmem_limit_bytes=8 * 2**20)
HIGHEST = lax.Precision.HIGHEST


def gll_matrix():
    nodes = np.array([-1.0, -1.0 / np.sqrt(5.0), 1.0 / np.sqrt(5.0), 1.0])
    legendre = (5.0 * nodes**3 - 3.0 * nodes) / 2.0
    matrix = np.zeros((4, 4))
    for i in range(4):
        for j in range(4):
            if i != j:
                matrix[i, j] = legendre[i] / (legendre[j] * (nodes[i] - nodes[j]))
    matrix[0, 0] = -3.0
    matrix[3, 3] = 3.0
    return matrix.astype(np.float32)


def cost(microseconds):
    return pl.CostEstimate(
        flops=0, bytes_accessed=int(microseconds * 3_000_000), transcendentals=0
    )


def in_air():
    sections = lax.axis_size("sec")
    return lax.axis_index("sec") < sections - sections // 4


def smooth_lines(value, lane):
    width = value.shape[-1]
    right = pltpu.roll(value, width - 1, value.ndim - 1)
    left = pltpu.roll(value, 1, value.ndim - 1)
    at_end = (lane % NODES == NODES - 1) & (lane < width - 1)
    at_start = (lane % NODES == 0) & (lane > 0)
    partner = jnp.where(at_end, right, jnp.where(at_start, left, value))
    return 0.5 * (value + partner)


def halves(value):
    high = value.astype(jnp.bfloat16)
    return high, (value - high.astype(jnp.float32)).astype(jnp.bfloat16)


def split_product(left, right):
    (high, low), (right_high, right_low) = halves(left), halves(right)
    return (
        jnp.dot(high, right_high, preferred_element_type=jnp.float32)
        + jnp.dot(low, right_high, preferred_element_type=jnp.float32)
        + jnp.dot(high, right_low, preferred_element_type=jnp.float32)
    )


def start_all(pairs, sems):
    copies = [
        pltpu.make_async_copy(source, target, sems.at[i])
        for i, (source, target) in enumerate(pairs)
    ]
    for copy in copies:
        copy.start()
    return copies


def flux_kernel(
    levels, law_in, field_in, zonal_in, meridional_in, sea_in, sent, law, field, zonal, meridional, sea, sems
):
    @pl.when(in_air())
    def _():
        x_points, fields, tile, y_points = field.shape
        lowest = pl.ds(0, tile)
        copies = start_all(
            [(law_in, law)]
            + [(field_in.at[x, :, lowest, :], field.at[x]) for x in range(x_points)]
            + [
                (zonal_in.at[:, lowest, :], zonal),
                (meridional_in.at[:, lowest, :], meridional),
                (sea_in, sea),
            ],
            sems,
        )
        for copy in copies:
            copy.wait()
        flux_count, columns = law.shape
        factors = law[...]
        flat = field.reshape(x_points * fields * tile, y_points)
        ground = [
            flat[pl.ds(f * tile, x_points, stride=fields * tile), :] for f in range(fields)
        ] + [sea[0]]
        u = zonal.reshape(x_points * tile, y_points)[pl.ds(0, x_points, stride=tile), :]
        v = meridional.reshape(x_points * tile, y_points)[pl.ds(0, x_points, stride=tile), :]
        speed = jnp.sqrt(1.0 + u * u + v * v)
        parts = []
        for n in range(flux_count):
            total = factors[n : n + 1, 0:1] * ground[0]
            for f in range(1, columns):
                total = total + factors[n : n + 1, f : f + 1] * ground[f]
            parts.append(speed * total)
        block = jnp.concatenate(parts, axis=0).astype(jnp.bfloat16)
        sent[pl.ds(0, block.shape[0]), :] = block


def edge_kernel(levels, rows, field, zonal, meridional, along, tracers, after, first, last, own):
    x_points = field.shape[0] // rows

    @pl.when(in_air())
    def _():
        d = gll_matrix()
        lane = lax.broadcasted_iota(jnp.int32, (levels, field.shape[1]), 1)
        for side, (x, target) in enumerate(((0, first), (x_points - 1, last))):
            start = x - x % NODES
            along_y = split_product(field[pl.ds(x * rows, rows), :], along[...])
            u = zonal[pl.ds(x * levels, levels), :]
            v = meridional[pl.ds(x * levels, levels), :]
            for f in range(rows // levels):
                at = f * levels
                along_x = sum(
                    float(d[x % NODES, a]) * field[pl.ds((start + a) * rows + at, levels), :]
                    for a in range(NODES)
                    if d[x % NODES, a] != 0
                )
                value = -(u * along_x + v * along_y[at : at + levels])
                value = smooth_lines(value, lane)
                own[side, pl.ds(at, levels), :] = value
                target[pl.ds(at, levels), :] = value.astype(jnp.bfloat16)

    @pl.when(jnp.logical_not(in_air()))
    def _():
        value = tracers[...]
        high = value.astype(jnp.bfloat16)
        low = (value - high.astype(jnp.float32)).astype(jnp.bfloat16)
        both = jnp.concatenate([high, low], axis=0)
        for target in (first, last):
            target[pl.ds(0, both.shape[0]), :] = both


def pack_kernel(own, *refs):
    received, packed = refs[:-1], refs[-1]
    count = len(refs)
    place = lax.axis_index("sec") % count
    here = pl.ds(0, packed.shape[1])
    packed[place] = own[here, :]
    for m, part in enumerate(received, 1):
        packed[(place - m + count) % count] = part[here, :]


def middle_kernel(
    levels,
    rows,
    field,
    zonal,
    meridional,
    along,
    own,
    below,
    above,
    tracers,
    senders_in,
    live_in,
    factor_in,
    offsets_in,
    sides_in,
    mixing_in,
    later,
    diffused,
    chosen,
    returning,
    forcing,
    gather,
    spread,
    slopes,
    held,
    senders,
    live,
    factor,
    offsets,
    sides,
    mixing,
    sems,
    load_sems,
):
    x_points = later.shape[0]

    @pl.when(in_air())
    def _():
        d = gll_matrix()
        lane = lax.broadcasted_iota(jnp.int32, (levels, field.shape[1]), 1)
        inner = pl.ds(rows, (x_points - 2) * rows)
        slopes[inner, :] = jnp.dot(
            field[inner, :], along[...], precision=HIGHEST, preferred_element_type=jnp.float32
        )
        copies = []
        for f in range(rows // levels):
            at = f * levels
            here = pl.ds(at, levels)
            values = {
                0: 0.5 * (own[0, here, :] + below[here, :].astype(jnp.float32)),
                x_points - 1: 0.5 * (own[1, here, :] + above[here, :].astype(jnp.float32)),
            }
            q = [field[pl.ds(x * rows + at, levels), :] for x in range(x_points)]
            for x in range(1, x_points - 1):
                start = x - x % NODES
                along_x = sum(
                    float(d[x % NODES, a]) * q[start + a]
                    for a in range(NODES)
                    if d[x % NODES, a] != 0
                )
                u = zonal[pl.ds(x * levels, levels), :]
                v = meridional[pl.ds(x * levels, levels), :]
                value = -(u * along_x + v * slopes[pl.ds(x * rows + at, levels), :])
                values[x] = smooth_lines(value, lane)
            for x in range(NODES - 1, x_points - 1, NODES):
                values[x] = values[x + 1] = 0.5 * (values[x] + values[x + 1])
            for x in range(x_points):
                held[x, here, :] = q[x] + STEP_ATMOS * values[x]
            copy = pltpu.make_async_copy(held.at[:, here, :], later.at[:, here, :], sems.at[f])
            copy.start()
            copies.append(copy)
        for copy in copies:
            copy.wait()

    @pl.when(jnp.logical_not(in_air()))
    def _():
        loads = start_all(
            (
                (senders_in, senders),
                (live_in, live),
                (factor_in, factor),
                (offsets_in, offsets),
                (sides_in, sides),
                (mixing_in, mixing),
            ),
            load_sems,
        )
        held[0] = jnp.zeros(held.shape[1:], jnp.float32)
        copies = start_all([(held.at[0], later.at[x]) for x in range(x_points)], sems)
        cells = sides.shape[1]
        x_count = gather.shape[0] // cells
        point = lax.broadcasted_iota(jnp.int32, gather.shape, 0) // x_count
        cell = lax.broadcasted_iota(jnp.int32, gather.shape, 1)
        gather[...] = jnp.where(point == cell, 1.0, 0.0).astype(gather.dtype)
        cell = lax.broadcasted_iota(jnp.int32, spread.shape, 0)
        point = lax.broadcasted_iota(jnp.int32, spread.shape, 1) // x_count
        spread[...] = jnp.where(point == cell, 1.0, 0.0).astype(spread.dtype)
        for load in loads:
            load.wait()

        source = lax.broadcasted_iota(jnp.int32, (cells, cells), 0)
        target = lax.broadcasted_iota(jnp.int32, (cells, cells), 1)
        inside = jnp.zeros((cells, cells), jnp.float32)
        outside = jnp.zeros((cells, cells), jnp.float32)
        total = jnp.zeros((1, cells), jnp.float32)
        for e in range(offsets.shape[0]):
            weight = jnp.where(e < sides[...], mixing[e], 0.0)
            place = target[:1] + offsets[e]
            total = total + weight
            inside = inside + jnp.where(source == place, weight, 0.0)
            hit = (source == place - cells) | (source == place + cells)
            outside = outside + jnp.where(hit, weight, 0.0)
        inside = inside - jnp.where(source == target, total, 0.0)

        value = tracers[...]
        height = value.shape[0]
        cell = lax.broadcasted_iota(jnp.int32, value.shape, 1)
        beside = [
            h[pl.ds(0, height), :].astype(jnp.float32)
            + h[pl.ds(height, height), :].astype(jnp.float32)
            for h in (below, above)
        ]
        outer = jnp.where(cell < cells // 2, beside[1], beside[0])
        change = jnp.dot(
            jnp.concatenate([value, outer], axis=1),
            jnp.concatenate([inside, outside], axis=0),
            precision=HIGHEST,
            preferred_element_type=jnp.float32,
        )
        diffused[...] = value + DIFFUSIVITY * change

        sections = lax.axis_size("sec")
        oceans = sections // 4
        air = sections - oceans
        ocean = jnp.maximum(lax.axis_index("sec") - air, 0)
        width = chosen.shape[1]
        count = live[0, ocean]
        for k in range(senders.shape[2]):
            place = jnp.where(k < count, senders[ocean, 0, k], sections)
            section = lax.broadcasted_iota(jnp.int32, (air, width), 0)
            chosen[pl.ds(k * air, air), :] = jnp.where(section == place, 1.0, 0.0)
            block = section % (air // oceans)
            owner = ((ocean + section // (air // oceans)) % oceans) ^ 1
            returning[pl.ds(k * air, air), :] = jnp.where(
                block * oceans + owner == place, 1.0, 0.0
            )
        tracer_count, flux_count = factor.shape
        depth = forcing.shape[0] // (tracer_count * flux_count)
        level = lax.broadcasted_iota(jnp.int32, (depth, width), 0).astype(jnp.float32)
        profile = STEP_OCEAN * jnp.exp(-0.5 * level)
        for n in range(flux_count):
            for t in range(tracer_count):
                forcing[pl.ds((n * tracer_count + t) * depth, depth), :] = factor[t, n] * profile
        for copy in copies:
            copy.wait()


def remap_kernel(
    regrid, gather, spread, chosen, returning, forcing, diffused, *refs
):
    arrived, renewed, shares = (refs[2], refs[0], refs[1]), refs[3], refs[4:]

    @pl.when(jnp.logical_not(in_air()))
    def _():
        points, cells = gather.shape
        x_count = points // cells
        slots = regrid.shape[0] // points
        air = chosen.shape[0] // slots
        packed = refs[0].shape[1]
        flux_count = packed // x_count
        row = lax.broadcasted_iota(jnp.int32, (x_count, cells), 0)
        column = lax.broadcasted_iota(jnp.int32, (x_count, cells), 1)
        same = jnp.where(row == column % x_count, 1.0, 0.0)

        blocks = [block[s].astype(jnp.float32) for block in arrived for s in range(block.shape[0])]
        matched = None
        for k in range(slots):
            part = chosen[pl.ds(k * air, 1), :] * blocks[0]
            for s in range(1, air):
                part = part + chosen[pl.ds(k * air + s, 1), :] * blocks[s]
            product = lax.dot_general(
                part.astype(jnp.bfloat16),
                regrid[pl.ds(k * points, points), :],
                (((1,), (1,)), ((), ())),
                preferred_element_type=jnp.float32,
            )
            matched = product if matched is None else matched + product
        matched = matched * jnp.tile(same, (flux_count, x_count))
        high = matched.astype(jnp.bfloat16)
        low = (matched - high.astype(jnp.float32)).astype(jnp.bfloat16)
        summed = jnp.dot(
            jnp.concatenate([high, low], axis=0), gather[...], preferred_element_type=jnp.float32
        )
        ocean_flux = (summed[:packed] + summed[packed:]).reshape(flux_count, x_count, cells).sum(axis=1)
        height = diffused.shape[0]
        value = diffused[...]
        for n in range(flux_count):
            value = value + forcing[pl.ds(n * height, height), :] * ocean_flux[n : n + 1]
        renewed[...] = value

        top = jnp.broadcast_to(value[0:1], (x_count, cells)).astype(jnp.bfloat16)
        wide = jnp.dot(top, spread[...], preferred_element_type=jnp.float32)
        wide = (wide * jnp.tile(same, (1, x_count))).astype(jnp.bfloat16)
        back = [
            jnp.dot(wide, regrid[pl.ds(k * points, points), :], preferred_element_type=jnp.float32)
            for k in range(slots)
        ]
        count = shares[0].shape[0]
        for m, share in enumerate(shares):
            for j in range(count):
                at = m * count + j
                total = returning[pl.ds(at, 1), :] * back[0]
                for k in range(1, slots):
                    total = total + returning[pl.ds(k * air + at, 1), :] * back[k]
                share[j] = total


def add_kernel(*refs):
    count = refs[0].shape[0]
    shares, totals = refs[:-count], refs[-count:]

    @pl.when(jnp.logical_not(in_air()))
    def _():
        for j, total in enumerate(totals):
            value = shares[0][j]
            for share in shares[1:]:
                value = value + share[j]
            total[...] = value


def last_kernel(renewed, *refs):
    returned, (tracers_later, warmth) = refs[:-2], refs[-2:]
    sections = lax.axis_size("sec")
    block = lax.axis_index("sec") // (sections // 4)

    @pl.when(in_air())
    def _():
        tracers_later[...] = jnp.zeros(tracers_later.shape, jnp.float32)

    @pl.when(jnp.logical_not(in_air()))
    def _():
        tracers_later[...] = renewed[...]
        warmth[...] = jnp.zeros(warmth.shape, jnp.float32)

    for j, part in enumerate(returned):

        @pl.when(block == j)
        def _(part=part):
            warmth[...] = part[...]


def per_device(
    climate_field_table,
    zonal_wind_speed,
    meridional_wind,
    sea_warmth_field,
    exchange_law_factor,
    regrid_matrix_stack,
    entry_sender_patch,
    holder_live_total,
    marine_salinity_heat,
    adjacent_offset_lists,
    polygon_side_total,
    interface_mixing_factor,
    solute_forcing_factor,
):
    sections = lax.axis_size("sec")
    ranks = lax.axis_size("rank")
    oceans = sections // 4
    air = sections - oceans
    _, x_points, rows, y_points = climate_field_table.shape
    levels = zonal_wind_speed.shape[2]
    flux_count = exchange_law_factor.shape[0]
    _, tracer_count, depth, cells = marine_salinity_heat.shape
    slots = regrid_matrix_stack.shape[2]
    f32, bf16 = jnp.float32, jnp.bfloat16
    shape = jax.ShapeDtypeStruct

    field = climate_field_table.reshape(x_points * rows, y_points)
    zonal = zonal_wind_speed.reshape(x_points * levels, y_points)
    meridional = meridional_wind.reshape(x_points * levels, y_points)
    regrid = regrid_matrix_stack.reshape(slots * cells * x_points, y_points)
    tracers = marine_salinity_heat.reshape(tracer_count * depth, cells)
    offsets = jnp.transpose(adjacent_offset_lists, (1, 0, 2))
    mixing = jnp.transpose(interface_mixing_factor, (1, 0, 2))
    live = jnp.transpose(holder_live_total, (1, 0))

    along = np.kron(np.eye(y_points // NODES, dtype=np.float32), gll_matrix().T)
    along = jnp.asarray(along)

    fields = rows // levels
    tile = min(8, levels)
    in_place = (
        exchange_law_factor,
        climate_field_table.reshape(x_points, fields, levels, y_points),
        zonal_wind_speed[0],
        meridional_wind[0],
        sea_warmth_field,
    )
    swap_rows = max(flux_count * x_points, rows + 16)
    fluxes = pl.pallas_call(
        functools.partial(flux_kernel, levels),
        out_shape=shape((swap_rows, y_points), bf16),
        in_specs=[HBM] * len(in_place),
        out_specs=VMEM,
        scratch_shapes=[
            pltpu.VMEM(exchange_law_factor.shape, f32),
            pltpu.VMEM((x_points, fields, tile, y_points), f32),
            pltpu.VMEM((x_points, tile, y_points), f32),
            pltpu.VMEM((x_points, tile, y_points), f32),
            pltpu.VMEM((1, x_points, y_points), f32),
            pltpu.SemaphoreType.DMA((len(in_place) + x_points - 1,)),
        ],
        compiler_params=PARAMS,
        cost_estimate=cost(1),
        name="flux",
    )(*(pltpu.with_memory_space_constraint(a, pltpu.HBM) for a in in_place))
    first, last, own = pl.pallas_call(
        functools.partial(edge_kernel, levels, rows),
        out_shape=(
            shape((rows, y_points), bf16),
            shape((rows, y_points), bf16),
            shape((2, rows, y_points), f32),
        ),
        in_specs=[VMEM] * 5 + [ANY],
        out_specs=(VMEM,) * 3,
        compiler_params=PARAMS,
        cost_estimate=cost(1),
        name="edges",
    )(field, zonal, meridional, along, tracers, fluxes)
    up = [(i, (i + 1) % ranks) for i in range(ranks)]
    below = lax.ppermute(last, "rank", up)
    above = lax.ppermute(first, "rank", [(j, i) for i, j in up])

    def turned(value, m):
        pairs = [(s, s // oceans * oceans + (s + m) % oceans) for s in range(sections)]
        return lax.ppermute(value, "sec", pairs)

    def paired(value, mask):
        pairs = [
            (s, (s // oceans ^ mask) * oceans + (s % oceans ^ 1)) for s in range(sections)
        ]
        return lax.ppermute(value, "sec", pairs)

    received = [turned(fluxes, m) for m in range(1, oceans)]
    packed = pl.pallas_call(
        pack_kernel,
        out_shape=shape((oceans, flux_count * x_points, y_points), bf16),
        in_specs=[VMEM] * oceans,
        out_specs=VMEM,
        compiler_params=PARAMS,
        cost_estimate=cost(0.2),
        name="pack",
    )(fluxes, *received)
    arrived = [paired(packed, 3 ^ block) for block in range(3)]

    from_memory = (
        entry_sender_patch,
        live,
        solute_forcing_factor,
        offsets,
        polygon_side_total,
        mixing,
    )
    later, diffused, chosen, returning, forcing, gather, spread = pl.pallas_call(
        functools.partial(middle_kernel, levels, rows),
        out_shape=(
            shape((x_points, rows, y_points), f32),
            shape(tracers.shape, f32),
            shape((slots * air, y_points), f32),
            shape((slots * air, y_points), f32),
            shape((flux_count * tracer_count * depth, cells), f32),
            shape((x_points * cells, cells), bf16),
            shape((cells, x_points * cells), bf16),
        ),
        in_specs=[VMEM] * 8 + [HBM] * 6,
        out_specs=(HBM,) + (VMEM,) * 6,
        scratch_shapes=[
            pltpu.VMEM(field.shape, f32),
            pltpu.VMEM((x_points, rows, y_points), f32),
        ]
        + [
            (pltpu.SMEM if i < 3 else pltpu.VMEM)(a.shape, a.dtype)
            for i, a in enumerate(from_memory)
        ]
        + [
            pltpu.SemaphoreType.DMA((max(fields, x_points),)),
            pltpu.SemaphoreType.DMA((len(from_memory),)),
        ],
        compiler_params=PARAMS,
        cost_estimate=cost(1),
        name="middle",
    )(
        field,
        zonal,
        meridional,
        along,
        own,
        below,
        above,
        tracers,
        *(pltpu.with_memory_space_constraint(a, pltpu.HBM) for a in from_memory),
    )

    renewed, *shares = pl.pallas_call(
        remap_kernel,
        out_shape=(shape(tracers.shape, f32),)
        + (shape((air // oceans, x_points, y_points), f32),) * oceans,
        in_specs=[VMEM] * 10,
        out_specs=(VMEM,) * (1 + oceans),
        compiler_params=PARAMS,
        cost_estimate=cost(1),
        name="remap",
    )(regrid, gather, spread, chosen, returning, forcing, diffused, arrived[1], arrived[2], arrived[0])
    shares = shares[:1] + [turned(share, m) for m, share in enumerate(shares[1:], 1)]
    totals = pl.pallas_call(
        add_kernel,
        out_shape=(shape((x_points, y_points), f32),) * (air // oceans),
        in_specs=[VMEM] * oceans,
        out_specs=(VMEM,) * (air // oceans),
        compiler_params=PARAMS,
        cost_estimate=cost(0.3),
        name="add",
    )(*shares)
    returned = [paired(total, 3 ^ block) for block, total in enumerate(totals)]
    tracers_later, warmth = pl.pallas_call(
        last_kernel,
        out_shape=(shape(tracers.shape, f32), shape((x_points, y_points), f32)),
        in_specs=[VMEM] * (1 + len(returned)),
        out_specs=(VMEM,) * 2,
        compiler_params=PARAMS,
        cost_estimate=cost(0.5),
        name="last",
    )(renewed, *returned)
    return (
        later.reshape(climate_field_table.shape),
        tracers_later.reshape(marine_salinity_heat.shape),
        warmth[None],
    )


def solution(mesh):
    return jax.shard_map(
        per_device,
        mesh=mesh,
        in_specs=(
            P("sec", "rank", None, None),
            P("sec", "rank", None, None),
            P("sec", "rank", None, None),
            P("sec", "rank", None),
            P(),
            P("sec", "rank", None, None, None, None),
            P(None, "rank", None),
            P(None, "rank"),
            P("sec", None, None, "rank"),
            P("sec", None, "rank"),
            P("sec", "rank"),
            P("sec", None, "rank"),
            P(),
        ),
        out_specs=(
            P("sec", "rank", None, None),
            P("sec", None, None, "rank"),
            P("sec", "rank", None),
        ),
        check_vma=False,
    )
```

```python
import functools

import jax
import jax.numpy as jnp
import numpy as np
from jax import lax
from jax.experimental import pallas as pl
from jax.experimental.pallas import tpu as pltpu
from jax.sharding import PartitionSpec as P

STEP_ATMOS = 0.05
DIFFUSIVITY = 0.05
STEP_OCEAN = 0.5
NODES = 4

VMEM = pl.BlockSpec(memory_space=pltpu.VMEM)
ANY = pl.BlockSpec(memory_space=pl.ANY)
HBM = pl.BlockSpec(memory_space=pltpu.HBM)
SMEM = pl.BlockSpec(memory_space=pltpu.SMEM)
PARAMS = pltpu.CompilerParams(vmem_limit_bytes=8 * 2**20)
HIGHEST = lax.Precision.HIGHEST


def gll_matrix():
    nodes = np.array([-1.0, -1.0 / np.sqrt(5.0), 1.0 / np.sqrt(5.0), 1.0])
    legendre = (5.0 * nodes**3 - 3.0 * nodes) / 2.0
    matrix = np.zeros((4, 4))
    for i in range(4):
        for j in range(4):
            if i != j:
                matrix[i, j] = legendre[i] / (legendre[j] * (nodes[i] - nodes[j]))
    matrix[0, 0] = -3.0
    matrix[3, 3] = 3.0
    return matrix.astype(np.float32)


def cost(microseconds):
    return pl.CostEstimate(
        flops=0, bytes_accessed=int(microseconds * 3_000_000), transcendentals=0
    )


def in_air():
    sections = lax.axis_size("sec")
    return lax.axis_index("sec") < sections - sections // 4


def smooth_lines(value, lane):
    width = value.shape[-1]
    right = pltpu.roll(value, width - 1, value.ndim - 1)
    left = pltpu.roll(value, 1, value.ndim - 1)
    at_end = (lane % NODES == NODES - 1) & (lane < width - 1)
    at_start = (lane % NODES == 0) & (lane > 0)
    partner = jnp.where(at_end, right, jnp.where(at_start, left, value))
    return 0.5 * (value + partner)


def halves(value):
    high = value.astype(jnp.bfloat16)
    return high, (value - high.astype(jnp.float32)).astype(jnp.bfloat16)


def split_product(left, right):
    (high, low), (right_high, right_low) = halves(left), halves(right)
    return (
        jnp.dot(high, right_high, preferred_element_type=jnp.float32)
        + jnp.dot(low, right_high, preferred_element_type=jnp.float32)
        + jnp.dot(high, right_low, preferred_element_type=jnp.float32)
    )


def start_all(pairs, sems):
    copies = [
        pltpu.make_async_copy(source, target, sems.at[i])
        for i, (source, target) in enumerate(pairs)
    ]
    for copy in copies:
        copy.start()
    return copies


def flux_kernel(
    levels, law_in, field_in, zonal_in, meridional_in, sea_in, sent, law, field, zonal, meridional, sea, sems
):
    @pl.when(in_air())
    def _():
        x_points, fields, tile, y_points = field.shape
        lowest = pl.ds(0, tile)
        copies = start_all(
            [(law_in, law)]
            + [(field_in.at[x, :, lowest, :], field.at[x]) for x in range(x_points)]
            + [
                (zonal_in.at[:, lowest, :], zonal),
                (meridional_in.at[:, lowest, :], meridional),
                (sea_in, sea),
            ],
            sems,
        )
        for copy in copies:
            copy.wait()
        flux_count, columns = law.shape
        flat = field.reshape(x_points * fields * tile, y_points)
        ground = [
            flat[pl.ds(f * tile, x_points, stride=fields * tile), :] for f in range(fields)
        ] + [sea[0]]
        u = zonal.reshape(x_points * tile, y_points)[pl.ds(0, x_points, stride=tile), :]
        v = meridional.reshape(x_points * tile, y_points)[pl.ds(0, x_points, stride=tile), :]
        speed = jnp.sqrt(1.0 + u * u + v * v)
        parts = []
        for n in range(flux_count):
            total = law[n, 0] * ground[0]
            for f in range(1, columns):
                total = total + law[n, f] * ground[f]
            parts.append(speed * total)
        block = jnp.concatenate(parts, axis=0).astype(jnp.bfloat16)
        sent[pl.ds(0, block.shape[0]), :] = block


def edge_kernel(levels, rows, field, zonal, meridional, along, tracers, after, first, last, own):
    x_points = field.shape[0] // rows

    @pl.when(in_air())
    def _():
        d = gll_matrix()
        lane = lax.broadcasted_iota(jnp.int32, (levels, field.shape[1]), 1)
        for side, (x, target) in enumerate(((0, first), (x_points - 1, last))):
            start = x - x % NODES
            along_y = split_product(field[pl.ds(x * rows, rows), :], along[...])
            u = zonal[pl.ds(x * levels, levels), :]
            v = meridional[pl.ds(x * levels, levels), :]
            for f in range(rows // levels):
                at = f * levels
                along_x = sum(
                    float(d[x % NODES, a]) * field[pl.ds((start + a) * rows + at, levels), :]
                    for a in range(NODES)
                    if d[x % NODES, a] != 0
                )
                value = -(u * along_x + v * along_y[at : at + levels])
                value = smooth_lines(value, lane)
                own[side, pl.ds(at, levels), :] = value
                target[pl.ds(at, levels), :] = value.astype(jnp.bfloat16)

    @pl.when(jnp.logical_not(in_air()))
    def _():
        value = tracers[...]
        high = value.astype(jnp.bfloat16)
        low = (value - high.astype(jnp.float32)).astype(jnp.bfloat16)
        both = jnp.concatenate([high, low], axis=0)
        for target in (first, last):
            target[pl.ds(0, both.shape[0]), :] = both


def pack_kernel(own, *refs):
    received, packed = refs[:-1], refs[-1]
    count = len(refs)
    place = lax.axis_index("sec") % count
    here = pl.ds(0, packed.shape[1])
    packed[place] = own[here, :]
    for m, part in enumerate(received, 1):
        packed[(place - m + count) % count] = part[here, :]


def middle_kernel(
    levels,
    rows,
    field,
    zonal,
    meridional,
    along,
    own,
    below,
    above,
    tracers,
    senders_in,
    live_in,
    factor_in,
    offsets_in,
    sides_in,
    mixing_in,
    later,
    diffused,
    chosen,
    returning,
    forcing,
    gather,
    spread,
    slopes,
    held,
    senders,
    live,
    factor,
    offsets,
    sides,
    mixing,
    sems,
    load_sems,
):
    x_points = later.shape[0]

    @pl.when(in_air())
    def _():
        d = gll_matrix()
        lane = lax.broadcasted_iota(jnp.int32, (levels, field.shape[1]), 1)
        inner = pl.ds(rows, (x_points - 2) * rows)
        slopes[inner, :] = jnp.dot(
            field[inner, :], along[...], precision=HIGHEST, preferred_element_type=jnp.float32
        )
        copies = []
        for f in range(rows // levels):
            at = f * levels
            here = pl.ds(at, levels)
            values = {
                0: 0.5 * (own[0, here, :] + below[here, :].astype(jnp.float32)),
                x_points - 1: 0.5 * (own[1, here, :] + above[here, :].astype(jnp.float32)),
            }
            q = [field[pl.ds(x * rows + at, levels), :] for x in range(x_points)]
            for x in range(1, x_points - 1):
                start = x - x % NODES
                along_x = sum(
                    float(d[x % NODES, a]) * q[start + a]
                    for a in range(NODES)
                    if d[x % NODES, a] != 0
                )
                u = zonal[pl.ds(x * levels, levels), :]
                v = meridional[pl.ds(x * levels, levels), :]
                value = -(u * along_x + v * slopes[pl.ds(x * rows + at, levels), :])
                values[x] = smooth_lines(value, lane)
            for x in range(NODES - 1, x_points - 1, NODES):
                values[x] = values[x + 1] = 0.5 * (values[x] + values[x + 1])
            for x in range(x_points):
                held[x, here, :] = q[x] + STEP_ATMOS * values[x]
            copy = pltpu.make_async_copy(held.at[:, here, :], later.at[:, here, :], sems.at[f])
            copy.start()
            copies.append(copy)
        for copy in copies:
            copy.wait()

    @pl.when(jnp.logical_not(in_air()))
    def _():
        loads = start_all(
            (
                (senders_in, senders),
                (live_in, live),
                (factor_in, factor),
                (offsets_in, offsets),
                (sides_in, sides),
                (mixing_in, mixing),
            ),
            load_sems,
        )
        held[0] = jnp.zeros(held.shape[1:], jnp.float32)
        copies = start_all([(held.at[0], later.at[x]) for x in range(x_points)], sems)
        cells = sides.shape[1]
        x_count = gather.shape[0] // cells
        point = lax.broadcasted_iota(jnp.int32, gather.shape, 0) // x_count
        cell = lax.broadcasted_iota(jnp.int32, gather.shape, 1)
        gather[...] = jnp.where(point == cell, 1.0, 0.0).astype(gather.dtype)
        cell = lax.broadcasted_iota(jnp.int32, spread.shape, 0)
        point = lax.broadcasted_iota(jnp.int32, spread.shape, 1) // x_count
        spread[...] = jnp.where(point == cell, 1.0, 0.0).astype(spread.dtype)
        for load in loads:
            load.wait()

        source = lax.broadcasted_iota(jnp.int32, (cells, cells), 0)
        target = lax.broadcasted_iota(jnp.int32, (cells, cells), 1)
        inside = jnp.zeros((cells, cells), jnp.float32)
        outside = jnp.zeros((cells, cells), jnp.float32)
        total = jnp.zeros((1, cells), jnp.float32)
        for e in range(offsets.shape[0]):
            weight = jnp.where(e < sides[...], mixing[e], 0.0)
            place = target[:1] + offsets[e]
            total = total + weight
            inside = inside + jnp.where(source == place, weight, 0.0)
            hit = (source == place - cells) | (source == place + cells)
            outside = outside + jnp.where(hit, weight, 0.0)
        inside = inside - jnp.where(source == target, total, 0.0)

        value = tracers[...]
        height = value.shape[0]
        cell = lax.broadcasted_iota(jnp.int32, value.shape, 1)
        beside = [
            h[pl.ds(0, height), :].astype(jnp.float32)
            + h[pl.ds(height, height), :].astype(jnp.float32)
            for h in (below, above)
        ]
        outer = jnp.where(cell < cells // 2, beside[1], beside[0])
        change = jnp.dot(
            jnp.concatenate([value, outer], axis=1),
            jnp.concatenate([inside, outside], axis=0),
            precision=HIGHEST,
            preferred_element_type=jnp.float32,
        )
        diffused[...] = value + DIFFUSIVITY * change

        sections = lax.axis_size("sec")
        oceans = sections // 4
        air = sections - oceans
        ocean = jnp.maximum(lax.axis_index("sec") - air, 0)
        width = chosen.shape[1]
        count = live[0, ocean]
        for k in range(senders.shape[2]):
            place = jnp.where(k < count, senders[ocean, 0, k], sections)
            section = lax.broadcasted_iota(jnp.int32, (air, width), 0)
            chosen[pl.ds(k * air, air), :] = jnp.where(section == place, 1.0, 0.0)
            block = section % (air // oceans)
            owner = ((ocean + section // (air // oceans)) % oceans) ^ 1
            returning[pl.ds(k * air, air), :] = jnp.where(
                block * oceans + owner == place, 1.0, 0.0
            )
        tracer_count, flux_count = factor.shape
        depth = forcing.shape[0] // (tracer_count * flux_count)
        level = lax.broadcasted_iota(jnp.int32, (depth, width), 0).astype(jnp.float32)
        profile = STEP_OCEAN * jnp.exp(-0.5 * level)
        for n in range(flux_count):
            for t in range(tracer_count):
                forcing[pl.ds((n * tracer_count + t) * depth, depth), :] = factor[t, n] * profile
        for copy in copies:
            copy.wait()


def remap_kernel(
    regrid, gather, spread, chosen, returning, forcing, diffused, *refs
):
    arrived, renewed, shares = (refs[0], refs[1], refs[2]), refs[3], refs[4:]

    @pl.when(jnp.logical_not(in_air()))
    def _():
        points, cells = gather.shape
        x_count = points // cells
        slots = regrid.shape[0] // points
        air = chosen.shape[0] // slots
        packed = refs[0].shape[1]
        flux_count = packed // x_count
        row = lax.broadcasted_iota(jnp.int32, (x_count, cells), 0)
        column = lax.broadcasted_iota(jnp.int32, (x_count, cells), 1)
        same = jnp.where(row == column % x_count, 1.0, 0.0)

        blocks = [block[s].astype(jnp.float32) for block in arrived for s in range(block.shape[0])]
        matched = None
        for k in range(slots):
            part = chosen[pl.ds(k * air, 1), :] * blocks[0]
            for s in range(1, air):
                part = part + chosen[pl.ds(k * air + s, 1), :] * blocks[s]
            product = lax.dot_general(
                part.astype(jnp.bfloat16),
                regrid[pl.ds(k * points, points), :],
                (((1,), (1,)), ((), ())),
                preferred_element_type=jnp.float32,
            )
            matched = product if matched is None else matched + product
        matched = matched * jnp.tile(same, (flux_count, x_count))
        high = matched.astype(jnp.bfloat16)
        low = (matched - high.astype(jnp.float32)).astype(jnp.bfloat16)
        summed = jnp.dot(
            jnp.concatenate([high, low], axis=0), gather[...], preferred_element_type=jnp.float32
        )
        ocean_flux = (summed[:packed] + summed[packed:]).reshape(flux_count, x_count, cells).sum(axis=1)
        height = diffused.shape[0]
        value = diffused[...]
        for n in range(flux_count):
            value = value + forcing[pl.ds(n * height, height), :] * ocean_flux[n : n + 1]
        renewed[...] = value

        top = jnp.broadcast_to(value[0:1], (x_count, cells)).astype(jnp.bfloat16)
        wide = jnp.dot(top, spread[...], preferred_element_type=jnp.float32)
        wide = (wide * jnp.tile(same, (1, x_count))).astype(jnp.bfloat16)
        back = [
            jnp.dot(wide, regrid[pl.ds(k * points, points), :], preferred_element_type=jnp.float32)
            for k in range(slots)
        ]
        count = shares[0].shape[0]
        for m, share in enumerate(shares):
            for j in range(count):
                at = m * count + j
                total = returning[pl.ds(at, 1), :] * back[0]
                for k in range(1, slots):
                    total = total + returning[pl.ds(k * air + at, 1), :] * back[k]
                share[j] = total


def add_kernel(*refs):
    count = refs[0].shape[0]
    shares, totals = refs[:-count], refs[-count:]

    @pl.when(jnp.logical_not(in_air()))
    def _():
        for j, total in enumerate(totals):
            value = shares[0][j]
            for share in shares[1:]:
                value = value + share[j]
            total[...] = value


def last_kernel(renewed, *refs):
    returned, (tracers_later, warmth) = refs[:-2], refs[-2:]
    sections = lax.axis_size("sec")
    block = lax.axis_index("sec") // (sections // 4)

    @pl.when(in_air())
    def _():
        tracers_later[...] = jnp.zeros(tracers_later.shape, jnp.float32)

    @pl.when(jnp.logical_not(in_air()))
    def _():
        tracers_later[...] = renewed[...]
        warmth[...] = jnp.zeros(warmth.shape, jnp.float32)

    for j, part in enumerate(returned):

        @pl.when(block == j)
        def _(part=part):
            warmth[...] = part[...]


def per_device(
    climate_field_table,
    zonal_wind_speed,
    meridional_wind,
    sea_warmth_field,
    exchange_law_factor,
    regrid_matrix_stack,
    entry_sender_patch,
    holder_live_total,
    marine_salinity_heat,
    adjacent_offset_lists,
    polygon_side_total,
    interface_mixing_factor,
    solute_forcing_factor,
):
    sections = lax.axis_size("sec")
    ranks = lax.axis_size("rank")
    oceans = sections // 4
    air = sections - oceans
    _, x_points, rows, y_points = climate_field_table.shape
    levels = zonal_wind_speed.shape[2]
    flux_count = exchange_law_factor.shape[0]
    _, tracer_count, depth, cells = marine_salinity_heat.shape
    slots = regrid_matrix_stack.shape[2]
    f32, bf16 = jnp.float32, jnp.bfloat16
    shape = jax.ShapeDtypeStruct

    field = climate_field_table.reshape(x_points * rows, y_points)
    zonal = zonal_wind_speed.reshape(x_points * levels, y_points)
    meridional = meridional_wind.reshape(x_points * levels, y_points)
    regrid = regrid_matrix_stack.reshape(slots * cells * x_points, y_points)
    tracers = marine_salinity_heat.reshape(tracer_count * depth, cells)
    offsets = jnp.transpose(adjacent_offset_lists, (1, 0, 2))
    mixing = jnp.transpose(interface_mixing_factor, (1, 0, 2))
    live = jnp.transpose(holder_live_total, (1, 0))

    along = np.kron(np.eye(y_points // NODES, dtype=np.float32), gll_matrix().T)
    along = jnp.asarray(along)

    fields = rows // levels
    tile = min(8, levels)
    in_place = (
        exchange_law_factor,
        climate_field_table.reshape(x_points, fields, levels, y_points),
        zonal_wind_speed[0],
        meridional_wind[0],
        sea_warmth_field,
    )
    swap_rows = max(flux_count * x_points, rows + 16)
    fluxes = pl.pallas_call(
        functools.partial(flux_kernel, levels),
        out_shape=shape((swap_rows, y_points), bf16),
        in_specs=[HBM] * len(in_place),
        out_specs=VMEM,
        scratch_shapes=[
            pltpu.SMEM(exchange_law_factor.shape, f32),
            pltpu.VMEM((x_points, fields, tile, y_points), f32),
            pltpu.VMEM((x_points, tile, y_points), f32),
            pltpu.VMEM((x_points, tile, y_points), f32),
            pltpu.VMEM((1, x_points, y_points), f32),
            pltpu.SemaphoreType.DMA((len(in_place) + x_points - 1,)),
        ],
        compiler_params=PARAMS,
        cost_estimate=cost(1),
        name="flux",
    )(*(pltpu.with_memory_space_constraint(a, pltpu.HBM) for a in in_place))
    first, last, own = pl.pallas_call(
        functools.partial(edge_kernel, levels, rows),
        out_shape=(
            shape((rows, y_points), bf16),
            shape((rows, y_points), bf16),
            shape((2, rows, y_points), f32),
        ),
        in_specs=[VMEM] * 5 + [ANY],
        out_specs=(VMEM,) * 3,
        compiler_params=PARAMS,
        cost_estimate=cost(1),
        name="edges",
    )(field, zonal, meridional, along, tracers, fluxes)
    up = [(i, (i + 1) % ranks) for i in range(ranks)]
    below = lax.ppermute(last, "rank", up)
    above = lax.ppermute(first, "rank", [(j, i) for i, j in up])

    def turned(value, m):
        pairs = [(s, s // oceans * oceans + (s + m) % oceans) for s in range(sections)]
        return lax.ppermute(value, "sec", pairs)

    def paired(value, mask):
        pairs = [
            (s, (s // oceans ^ mask) * oceans + (s % oceans ^ 1)) for s in range(sections)
        ]
        return lax.ppermute(value, "sec", pairs)

    received = [turned(fluxes, m) for m in range(1, oceans)]
    packed = pl.pallas_call(
        pack_kernel,
        out_shape=shape((oceans, flux_count * x_points, y_points), bf16),
        in_specs=[VMEM] * oceans,
        out_specs=VMEM,
        compiler_params=PARAMS,
        cost_estimate=cost(0.2),
        name="pack",
    )(fluxes, *received)
    arrived = [paired(packed, 3 ^ block) for block in range(3)]

    from_memory = (
        entry_sender_patch,
        live,
        solute_forcing_factor,
        offsets,
        polygon_side_total,
        mixing,
    )
    later, diffused, chosen, returning, forcing, gather, spread = pl.pallas_call(
        functools.partial(middle_kernel, levels, rows),
        out_shape=(
            shape((x_points, rows, y_points), f32),
            shape(tracers.shape, f32),
            shape((slots * air, y_points), f32),
            shape((slots * air, y_points), f32),
            shape((flux_count * tracer_count * depth, cells), f32),
            shape((x_points * cells, cells), bf16),
            shape((cells, x_points * cells), bf16),
        ),
        in_specs=[VMEM] * 8 + [HBM] * 6,
        out_specs=(HBM,) + (VMEM,) * 6,
        scratch_shapes=[
            pltpu.VMEM(field.shape, f32),
            pltpu.VMEM((x_points, rows, y_points), f32),
        ]
        + [
            (pltpu.SMEM if i < 3 else pltpu.VMEM)(a.shape, a.dtype)
            for i, a in enumerate(from_memory)
        ]
        + [
            pltpu.SemaphoreType.DMA((max(fields, x_points),)),
            pltpu.SemaphoreType.DMA((len(from_memory),)),
        ],
        compiler_params=PARAMS,
        cost_estimate=cost(1),
        name="middle",
    )(
        field,
        zonal,
        meridional,
        along,
        own,
        below,
        above,
        tracers,
        *(pltpu.with_memory_space_constraint(a, pltpu.HBM) for a in from_memory),
    )

    renewed, *shares = pl.pallas_call(
        remap_kernel,
        out_shape=(shape(tracers.shape, f32),)
        + (shape((air // oceans, x_points, y_points), f32),) * oceans,
        in_specs=[VMEM] * 10,
        out_specs=(VMEM,) * (1 + oceans),
        compiler_params=PARAMS,
        cost_estimate=cost(1),
        name="remap",
    )(regrid, gather, spread, chosen, returning, forcing, diffused, arrived[0], arrived[1], arrived[2])
    shares = shares[:1] + [turned(share, m) for m, share in enumerate(shares[1:], 1)]
    totals = pl.pallas_call(
        add_kernel,
        out_shape=(shape((x_points, y_points), f32),) * (air // oceans),
        in_specs=[VMEM] * oceans,
        out_specs=(VMEM,) * (air // oceans),
        compiler_params=PARAMS,
        cost_estimate=cost(0.3),
        name="add",
    )(*shares)
    returned = [paired(total, 3 ^ block) for block, total in enumerate(totals)]
    tracers_later, warmth = pl.pallas_call(
        last_kernel,
        out_shape=(shape(tracers.shape, f32), shape((x_points, y_points), f32)),
        in_specs=[VMEM] * (1 + len(returned)),
        out_specs=(VMEM,) * 2,
        compiler_params=PARAMS,
        cost_estimate=cost(0.5),
        name="last",
    )(renewed, *returned)
    return (
        later.reshape(climate_field_table.shape),
        tracers_later.reshape(marine_salinity_heat.shape),
        warmth[None],
    )


def solution(mesh):
    return jax.shard_map(
        per_device,
        mesh=mesh,
        in_specs=(
            P("sec", "rank", None, None),
            P("sec", "rank", None, None),
            P("sec", "rank", None, None),
            P("sec", "rank", None),
            P(),
            P("sec", "rank", None, None, None, None),
            P(None, "rank", None),
            P(None, "rank"),
            P("sec", None, None, "rank"),
            P("sec", None, "rank"),
            P("sec", "rank"),
            P("sec", None, "rank"),
            P(),
        ),
        out_specs=(
            P("sec", "rank", None, None),
            P("sec", None, None, "rank"),
            P("sec", "rank", None),
        ),
        check_vma=False,
    )
```

```python
import functools

import jax
import jax.numpy as jnp
import numpy as np
from jax import lax
from jax.experimental import pallas as pl
from jax.experimental.pallas import tpu as pltpu
from jax.sharding import PartitionSpec as P

STEP_ATMOS = 0.05
DIFFUSIVITY = 0.05
STEP_OCEAN = 0.5
NODES = 4

VMEM = pl.BlockSpec(memory_space=pltpu.VMEM)
ANY = pl.BlockSpec(memory_space=pl.ANY)
HBM = pl.BlockSpec(memory_space=pltpu.HBM)
SMEM = pl.BlockSpec(memory_space=pltpu.SMEM)
PARAMS = pltpu.CompilerParams(vmem_limit_bytes=8 * 2**20)
HIGHEST = lax.Precision.HIGHEST


def gll_matrix():
    nodes = np.array([-1.0, -1.0 / np.sqrt(5.0), 1.0 / np.sqrt(5.0), 1.0])
    legendre = (5.0 * nodes**3 - 3.0 * nodes) / 2.0
    matrix = np.zeros((4, 4))
    for i in range(4):
        for j in range(4):
            if i != j:
                matrix[i, j] = legendre[i] / (legendre[j] * (nodes[i] - nodes[j]))
    matrix[0, 0] = -3.0
    matrix[3, 3] = 3.0
    return matrix.astype(np.float32)


def cost(microseconds):
    return pl.CostEstimate(
        flops=0, bytes_accessed=int(microseconds * 3_000_000), transcendentals=0
    )


def in_air():
    sections = lax.axis_size("sec")
    return lax.axis_index("sec") < sections - sections // 4


def smooth_lines(value, lane):
    width = value.shape[-1]
    right = pltpu.roll(value, width - 1, value.ndim - 1)
    left = pltpu.roll(value, 1, value.ndim - 1)
    at_end = (lane % NODES == NODES - 1) & (lane < width - 1)
    at_start = (lane % NODES == 0) & (lane > 0)
    partner = jnp.where(at_end, right, jnp.where(at_start, left, value))
    return 0.5 * (value + partner)


def halves(value):
    high = value.astype(jnp.bfloat16)
    return high, (value - high.astype(jnp.float32)).astype(jnp.bfloat16)


def split_product(left, right):
    (high, low), (right_high, right_low) = halves(left), halves(right)
    return (
        jnp.dot(high, right_high, preferred_element_type=jnp.float32)
        + jnp.dot(low, right_high, preferred_element_type=jnp.float32)
        + jnp.dot(high, right_low, preferred_element_type=jnp.float32)
    )


def start_all(pairs, sems):
    copies = [
        pltpu.make_async_copy(source, target, sems.at[i])
        for i, (source, target) in enumerate(pairs)
    ]
    for copy in copies:
        copy.start()
    return copies


def flux_kernel(
    levels, law_in, field_in, zonal_in, meridional_in, sea_in, sent, law, field, zonal, meridional, sea, sems
):
    @pl.when(in_air())
    def _():
        x_points, fields, tile, y_points = field.shape
        lowest = pl.ds(0, tile)
        copies = start_all(
            (
                (law_in, law),
                (field_in.at[:, :, lowest, :], field),
                (zonal_in.at[:, lowest, :], zonal),
                (meridional_in.at[:, lowest, :], meridional),
                (sea_in, sea),
            ),
            sems,
        )
        for copy in copies:
            copy.wait()
        flux_count, columns = law.shape
        flat = field.reshape(x_points * fields * tile, y_points)
        ground = [
            flat[pl.ds(f * tile, x_points, stride=fields * tile), :] for f in range(fields)
        ] + [sea[0]]
        u = zonal.reshape(x_points * tile, y_points)[pl.ds(0, x_points, stride=tile), :]
        v = meridional.reshape(x_points * tile, y_points)[pl.ds(0, x_points, stride=tile), :]
        speed = jnp.sqrt(1.0 + u * u + v * v)
        parts = []
        for n in range(flux_count):
            total = law[n, 0] * ground[0]
            for f in range(1, columns):
                total = total + law[n, f] * ground[f]
            parts.append(speed * total)
        block = jnp.concatenate(parts, axis=0).astype(jnp.bfloat16)
        sent[pl.ds(0, block.shape[0]), :] = block


def edge_kernel(levels, rows, field, zonal, meridional, along, tracers, after, first, last, own):
    x_points = field.shape[0] // rows

    @pl.when(in_air())
    def _():
        d = gll_matrix()
        lane = lax.broadcasted_iota(jnp.int32, (levels, field.shape[1]), 1)
        for side, (x, target) in enumerate(((0, first), (x_points - 1, last))):
            start = x - x % NODES
            along_y = split_product(field[pl.ds(x * rows, rows), :], along[...])
            u = zonal[pl.ds(x * levels, levels), :]
            v = meridional[pl.ds(x * levels, levels), :]
            for f in range(rows // levels):
                at = f * levels
                along_x = sum(
                    float(d[x % NODES, a]) * field[pl.ds((start + a) * rows + at, levels), :]
                    for a in range(NODES)
                    if d[x % NODES, a] != 0
                )
                value = -(u * along_x + v * along_y[at : at + levels])
                value = smooth_lines(value, lane)
                own[side, pl.ds(at, levels), :] = value
                target[pl.ds(at, levels), :] = value.astype(jnp.bfloat16)

    @pl.when(jnp.logical_not(in_air()))
    def _():
        value = tracers[...]
        high = value.astype(jnp.bfloat16)
        low = (value - high.astype(jnp.float32)).astype(jnp.bfloat16)
        both = jnp.concatenate([high, low], axis=0)
        for target in (first, last):
            target[pl.ds(0, both.shape[0]), :] = both


def pack_kernel(own, *refs):
    received, packed = refs[:-1], refs[-1]
    count = len(refs)
    place = lax.axis_index("sec") % count
    here = pl.ds(0, packed.shape[1])
    packed[place] = own[here, :]
    for m, part in enumerate(received, 1):
        packed[(place - m + count) % count] = part[here, :]


def middle_kernel(
    levels,
    rows,
    field,
    zonal,
    meridional,
    along,
    own,
    below,
    above,
    tracers,
    senders_in,
    live_in,
    factor_in,
    offsets_in,
    sides_in,
    mixing_in,
    later,
    diffused,
    chosen,
    returning,
    forcing,
    gather,
    spread,
    slopes,
    held,
    senders,
    live,
    factor,
    offsets,
    sides,
    mixing,
    sems,
    load_sems,
):
    x_points = later.shape[0]

    @pl.when(in_air())
    def _():
        d = gll_matrix()
        lane = lax.broadcasted_iota(jnp.int32, (levels, field.shape[1]), 1)
        inner = pl.ds(rows, (x_points - 2) * rows)
        slopes[inner, :] = jnp.dot(
            field[inner, :], along[...], precision=HIGHEST, preferred_element_type=jnp.float32
        )
        copies = []
        for f in range(rows // levels):
            at = f * levels
            here = pl.ds(at, levels)
            values = {
                0: 0.5 * (own[0, here, :] + below[here, :].astype(jnp.float32)),
                x_points - 1: 0.5 * (own[1, here, :] + above[here, :].astype(jnp.float32)),
            }
            q = [field[pl.ds(x * rows + at, levels), :] for x in range(x_points)]
            for x in range(1, x_points - 1):
                start = x - x % NODES
                along_x = sum(
                    float(d[x % NODES, a]) * q[start + a]
                    for a in range(NODES)
                    if d[x % NODES, a] != 0
                )
                u = zonal[pl.ds(x * levels, levels), :]
                v = meridional[pl.ds(x * levels, levels), :]
                value = -(u * along_x + v * slopes[pl.ds(x * rows + at, levels), :])
                values[x] = smooth_lines(value, lane)
            for x in range(NODES - 1, x_points - 1, NODES):
                values[x] = values[x + 1] = 0.5 * (values[x] + values[x + 1])
            for x in range(x_points):
                held[x, here, :] = q[x] + STEP_ATMOS * values[x]
            copy = pltpu.make_async_copy(held.at[:, here, :], later.at[:, here, :], sems.at[f])
            copy.start()
            copies.append(copy)
        for copy in copies:
            copy.wait()

    @pl.when(jnp.logical_not(in_air()))
    def _():
        loads = start_all(
            (
                (senders_in, senders),
                (live_in, live),
                (factor_in, factor),
                (offsets_in, offsets),
                (sides_in, sides),
                (mixing_in, mixing),
            ),
            load_sems,
        )
        held[0] = jnp.zeros(held.shape[1:], jnp.float32)
        copies = start_all([(held.at[0], later.at[x]) for x in range(x_points)], sems)
        cells = sides.shape[1]
        x_count = gather.shape[0] // cells
        point = lax.broadcasted_iota(jnp.int32, gather.shape, 0) // x_count
        cell = lax.broadcasted_iota(jnp.int32, gather.shape, 1)
        gather[...] = jnp.where(point == cell, 1.0, 0.0).astype(gather.dtype)
        cell = lax.broadcasted_iota(jnp.int32, spread.shape, 0)
        point = lax.broadcasted_iota(jnp.int32, spread.shape, 1) // x_count
        spread[...] = jnp.where(point == cell, 1.0, 0.0).astype(spread.dtype)
        for load in loads:
            load.wait()

        source = lax.broadcasted_iota(jnp.int32, (cells, cells), 0)
        target = lax.broadcasted_iota(jnp.int32, (cells, cells), 1)
        inside = jnp.zeros((cells, cells), jnp.float32)
        outside = jnp.zeros((cells, cells), jnp.float32)
        total = jnp.zeros((1, cells), jnp.float32)
        for e in range(offsets.shape[0]):
            weight = jnp.where(e < sides[...], mixing[e], 0.0)
            place = target[:1] + offsets[e]
            total = total + weight
            inside = inside + jnp.where(source == place, weight, 0.0)
            hit = (source == place - cells) | (source == place + cells)
            outside = outside + jnp.where(hit, weight, 0.0)
        inside = inside - jnp.where(source == target, total, 0.0)

        value = tracers[...]
        height = value.shape[0]
        cell = lax.broadcasted_iota(jnp.int32, value.shape, 1)
        beside = [
            h[pl.ds(0, height), :].astype(jnp.float32)
            + h[pl.ds(height, height), :].astype(jnp.float32)
            for h in (below, above)
        ]
        outer = jnp.where(cell < cells // 2, beside[1], beside[0])
        change = jnp.dot(
            jnp.concatenate([value, outer], axis=1),
            jnp.concatenate([inside, outside], axis=0),
            precision=HIGHEST,
            preferred_element_type=jnp.float32,
        )
        diffused[...] = value + DIFFUSIVITY * change

        sections = lax.axis_size("sec")
        oceans = sections // 4
        air = sections - oceans
        ocean = jnp.maximum(lax.axis_index("sec") - air, 0)
        width = chosen.shape[1]
        count = live[0, ocean]
        for k in range(senders.shape[2]):
            place = jnp.where(k < count, senders[ocean, 0, k], sections)
            section = lax.broadcasted_iota(jnp.int32, (air, width), 0)
            chosen[pl.ds(k * air, air), :] = jnp.where(section == place, 1.0, 0.0)
            block = section % (air // oceans)
            owner = ((ocean + section // (air // oceans)) % oceans) ^ 1
            returning[pl.ds(k * air, air), :] = jnp.where(
                block * oceans + owner == place, 1.0, 0.0
            )
        tracer_count, flux_count = factor.shape
        depth = forcing.shape[0] // (tracer_count * flux_count)
        level = lax.broadcasted_iota(jnp.int32, (depth, width), 0).astype(jnp.float32)
        profile = STEP_OCEAN * jnp.exp(-0.5 * level)
        for n in range(flux_count):
            for t in range(tracer_count):
                forcing[pl.ds((n * tracer_count + t) * depth, depth), :] = factor[t, n] * profile
        for copy in copies:
            copy.wait()


def remap_kernel(
    regrid, gather, spread, chosen, returning, forcing, diffused, *refs
):
    arrived, renewed, shares = (refs[2], refs[0], refs[1]), refs[3], refs[4:]

    @pl.when(jnp.logical_not(in_air()))
    def _():
        points, cells = gather.shape
        x_count = points // cells
        slots = regrid.shape[0] // points
        air = chosen.shape[0] // slots
        packed = refs[0].shape[1]
        flux_count = packed // x_count
        row = lax.broadcasted_iota(jnp.int32, (x_count, cells), 0)
        column = lax.broadcasted_iota(jnp.int32, (x_count, cells), 1)
        same = jnp.where(row == column % x_count, 1.0, 0.0)

        blocks = [block[s].astype(jnp.float32) for block in arrived for s in range(block.shape[0])]
        matched = None
        for k in range(slots):
            part = chosen[pl.ds(k * air, 1), :] * blocks[0]
            for s in range(1, air):
                part = part + chosen[pl.ds(k * air + s, 1), :] * blocks[s]
            product = lax.dot_general(
                part.astype(jnp.bfloat16),
                regrid[pl.ds(k * points, points), :],
                (((1,), (1,)), ((), ())),
                preferred_element_type=jnp.float32,
            )
            matched = product if matched is None else matched + product
        matched = matched * jnp.tile(same, (flux_count, x_count))
        high = matched.astype(jnp.bfloat16)
        low = (matched - high.astype(jnp.float32)).astype(jnp.bfloat16)
        summed = jnp.dot(
            jnp.concatenate([high, low], axis=0), gather[...], preferred_element_type=jnp.float32
        )
        ocean_flux = (summed[:packed] + summed[packed:]).reshape(flux_count, x_count, cells).sum(axis=1)
        height = diffused.shape[0]
        value = diffused[...]
        for n in range(flux_count):
            value = value + forcing[pl.ds(n * height, height), :] * ocean_flux[n : n + 1]
        renewed[...] = value

        top = jnp.broadcast_to(value[0:1], (x_count, cells)).astype(jnp.bfloat16)
        wide = jnp.dot(top, spread[...], preferred_element_type=jnp.float32)
        wide = (wide * jnp.tile(same, (1, x_count))).astype(jnp.bfloat16)
        back = [
            jnp.dot(wide, regrid[pl.ds(k * points, points), :], preferred_element_type=jnp.float32)
            for k in range(slots)
        ]
        count = shares[0].shape[0]
        for m, share in enumerate(shares):
            for j in range(count):
                at = m * count + j
                total = returning[pl.ds(at, 1), :] * back[0]
                for k in range(1, slots):
                    total = total + returning[pl.ds(k * air + at, 1), :] * back[k]
                share[j] = total


def add_kernel(*refs):
    count = refs[0].shape[0]
    shares, totals = refs[:-count], refs[-count:]

    @pl.when(jnp.logical_not(in_air()))
    def _():
        for j, total in enumerate(totals):
            value = shares[0][j]
            for share in shares[1:]:
                value = value + share[j]
            total[...] = value


def last_kernel(renewed, *refs):
    returned, (tracers_later, warmth) = refs[:-2], refs[-2:]
    sections = lax.axis_size("sec")
    block = lax.axis_index("sec") // (sections // 4)

    @pl.when(in_air())
    def _():
        tracers_later[...] = jnp.zeros(tracers_later.shape, jnp.float32)

    @pl.when(jnp.logical_not(in_air()))
    def _():
        tracers_later[...] = renewed[...]
        warmth[...] = jnp.zeros(warmth.shape, jnp.float32)

    for j, part in enumerate(returned):

        @pl.when(block == j)
        def _(part=part):
            warmth[...] = part[...]


def per_device(
    climate_field_table,
    zonal_wind_speed,
    meridional_wind,
    sea_warmth_field,
    exchange_law_factor,
    regrid_matrix_stack,
    entry_sender_patch,
    holder_live_total,
    marine_salinity_heat,
    adjacent_offset_lists,
    polygon_side_total,
    interface_mixing_factor,
    solute_forcing_factor,
):
    sections = lax.axis_size("sec")
    ranks = lax.axis_size("rank")
    oceans = sections // 4
    air = sections - oceans
    _, x_points, rows, y_points = climate_field_table.shape
    levels = zonal_wind_speed.shape[2]
    flux_count = exchange_law_factor.shape[0]
    _, tracer_count, depth, cells = marine_salinity_heat.shape
    slots = regrid_matrix_stack.shape[2]
    f32, bf16 = jnp.float32, jnp.bfloat16
    shape = jax.ShapeDtypeStruct

    field = climate_field_table.reshape(x_points * rows, y_points)
    zonal = zonal_wind_speed.reshape(x_points * levels, y_points)
    meridional = meridional_wind.reshape(x_points * levels, y_points)
    regrid = regrid_matrix_stack.reshape(slots * cells * x_points, y_points)
    tracers = marine_salinity_heat.reshape(tracer_count * depth, cells)
    offsets = jnp.transpose(adjacent_offset_lists, (1, 0, 2))
    mixing = jnp.transpose(interface_mixing_factor, (1, 0, 2))
    live = jnp.transpose(holder_live_total, (1, 0))

    along = np.kron(np.eye(y_points // NODES, dtype=np.float32), gll_matrix().T)
    along = jnp.asarray(along)

    fields = rows // levels
    tile = min(8, levels)
    in_place = (
        exchange_law_factor,
        climate_field_table.reshape(x_points, fields, levels, y_points),
        zonal_wind_speed[0],
        meridional_wind[0],
        sea_warmth_field,
    )
    swap_rows = max(flux_count * x_points, rows + 16)
    fluxes = pl.pallas_call(
        functools.partial(flux_kernel, levels),
        out_shape=shape((swap_rows, y_points), bf16),
        in_specs=[HBM] * len(in_place),
        out_specs=VMEM,
        scratch_shapes=[
            pltpu.SMEM(exchange_law_factor.shape, f32),
            pltpu.VMEM((x_points, fields, tile, y_points), f32),
            pltpu.VMEM((x_points, tile, y_points), f32),
            pltpu.VMEM((x_points, tile, y_points), f32),
            pltpu.VMEM((1, x_points, y_points), f32),
            pltpu.SemaphoreType.DMA((len(in_place),)),
        ],
        compiler_params=PARAMS,
        cost_estimate=cost(1),
        name="flux",
    )(*(pltpu.with_memory_space_constraint(a, pltpu.HBM) for a in in_place))
    first, last, own = pl.pallas_call(
        functools.partial(edge_kernel, levels, rows),
        out_shape=(
            shape((rows, y_points), bf16),
            shape((rows, y_points), bf16),
            shape((2, rows, y_points), f32),
        ),
        in_specs=[VMEM] * 5 + [ANY],
        out_specs=(VMEM,) * 3,
        compiler_params=PARAMS,
        cost_estimate=cost(1),
        name="edges",
    )(field, zonal, meridional, along, tracers, fluxes)
    up = [(i, (i + 1) % ranks) for i in range(ranks)]
    below = lax.ppermute(last, "rank", up)
    above = lax.ppermute(first, "rank", [(j, i) for i, j in up])

    def turned(value, m):
        pairs = [(s, s // oceans * oceans + (s + m) % oceans) for s in range(sections)]
        return lax.ppermute(value, "sec", pairs)

    def paired(value, mask):
        pairs = [
            (s, (s // oceans ^ mask) * oceans + (s % oceans ^ 1)) for s in range(sections)
        ]
        return lax.ppermute(value, "sec", pairs)

    received = [turned(fluxes, m) for m in range(1, oceans)]
    packed = pl.pallas_call(
        pack_kernel,
        out_shape=shape((oceans, flux_count * x_points, y_points), bf16),
        in_specs=[VMEM] * oceans,
        out_specs=VMEM,
        compiler_params=PARAMS,
        cost_estimate=cost(0.2),
        name="pack",
    )(fluxes, *received)
    arrived = [paired(packed, 3 ^ block) for block in range(3)]

    from_memory = (
        entry_sender_patch,
        live,
        solute_forcing_factor,
        offsets,
        polygon_side_total,
        mixing,
    )
    later, diffused, chosen, returning, forcing, gather, spread = pl.pallas_call(
        functools.partial(middle_kernel, levels, rows),
        out_shape=(
            shape((x_points, rows, y_points), f32),
            shape(tracers.shape, f32),
            shape((slots * air, y_points), f32),
            shape((slots * air, y_points), f32),
            shape((flux_count * tracer_count * depth, cells), f32),
            shape((x_points * cells, cells), bf16),
            shape((cells, x_points * cells), bf16),
        ),
        in_specs=[VMEM] * 8 + [HBM] * 6,
        out_specs=(HBM,) + (VMEM,) * 6,
        scratch_shapes=[
            pltpu.VMEM(field.shape, f32),
            pltpu.VMEM((x_points, rows, y_points), f32),
        ]
        + [
            (pltpu.SMEM if i < 3 else pltpu.VMEM)(a.shape, a.dtype)
            for i, a in enumerate(from_memory)
        ]
        + [
            pltpu.SemaphoreType.DMA((max(fields, x_points),)),
            pltpu.SemaphoreType.DMA((len(from_memory),)),
        ],
        compiler_params=PARAMS,
        cost_estimate=cost(1),
        name="middle",
    )(
        field,
        zonal,
        meridional,
        along,
        own,
        below,
        above,
        tracers,
        *(pltpu.with_memory_space_constraint(a, pltpu.HBM) for a in from_memory),
    )

    renewed, *shares = pl.pallas_call(
        remap_kernel,
        out_shape=(shape(tracers.shape, f32),)
        + (shape((air // oceans, x_points, y_points), f32),) * oceans,
        in_specs=[VMEM] * 10,
        out_specs=(VMEM,) * (1 + oceans),
        compiler_params=PARAMS,
        cost_estimate=cost(1),
        name="remap",
    )(regrid, gather, spread, chosen, returning, forcing, diffused, arrived[1], arrived[2], arrived[0])
    shares = shares[:1] + [turned(share, m) for m, share in enumerate(shares[1:], 1)]
    totals = pl.pallas_call(
        add_kernel,
        out_shape=(shape((x_points, y_points), f32),) * (air // oceans),
        in_specs=[VMEM] * oceans,
        out_specs=(VMEM,) * (air // oceans),
        compiler_params=PARAMS,
        cost_estimate=cost(0.3),
        name="add",
    )(*shares)
    returned = [paired(total, 3 ^ block) for block, total in enumerate(totals)]
    tracers_later, warmth = pl.pallas_call(
        last_kernel,
        out_shape=(shape(tracers.shape, f32), shape((x_points, y_points), f32)),
        in_specs=[VMEM] * (1 + len(returned)),
        out_specs=(VMEM,) * 2,
        compiler_params=PARAMS,
        cost_estimate=cost(0.5),
        name="last",
    )(renewed, *returned)
    return (
        later.reshape(climate_field_table.shape),
        tracers_later.reshape(marine_salinity_heat.shape),
        warmth[None],
    )


def solution(mesh):
    return jax.shard_map(
        per_device,
        mesh=mesh,
        in_specs=(
            P("sec", "rank", None, None),
            P("sec", "rank", None, None),
            P("sec", "rank", None, None),
            P("sec", "rank", None),
            P(),
            P("sec", "rank", None, None, None, None),
            P(None, "rank", None),
            P(None, "rank"),
            P("sec", None, None, "rank"),
            P("sec", None, "rank"),
            P("sec", "rank"),
            P("sec", None, "rank"),
            P(),
        ),
        out_specs=(
            P("sec", "rank", None, None),
            P("sec", None, None, "rank"),
            P("sec", "rank", None),
        ),
        check_vma=False,
    )
```

```python
import functools

import jax
import jax.numpy as jnp
import numpy as np
from jax import lax
from jax.experimental import pallas as pl
from jax.experimental.pallas import tpu as pltpu
from jax.sharding import PartitionSpec as P

STEP_ATMOS = 0.05
DIFFUSIVITY = 0.05
STEP_OCEAN = 0.5
NODES = 4

VMEM = pl.BlockSpec(memory_space=pltpu.VMEM)
ANY = pl.BlockSpec(memory_space=pl.ANY)
HBM = pl.BlockSpec(memory_space=pltpu.HBM)
SMEM = pl.BlockSpec(memory_space=pltpu.SMEM)
PARAMS = pltpu.CompilerParams(vmem_limit_bytes=8 * 2**20)
HIGHEST = lax.Precision.HIGHEST


def gll_matrix():
    nodes = np.array([-1.0, -1.0 / np.sqrt(5.0), 1.0 / np.sqrt(5.0), 1.0])
    legendre = (5.0 * nodes**3 - 3.0 * nodes) / 2.0
    matrix = np.zeros((4, 4))
    for i in range(4):
        for j in range(4):
            if i != j:
                matrix[i, j] = legendre[i] / (legendre[j] * (nodes[i] - nodes[j]))
    matrix[0, 0] = -3.0
    matrix[3, 3] = 3.0
    return matrix.astype(np.float32)


def cost(microseconds):
    return pl.CostEstimate(
        flops=0, bytes_accessed=int(microseconds * 3_000_000), transcendentals=0
    )


def in_air():
    sections = lax.axis_size("sec")
    return lax.axis_index("sec") < sections - sections // 4


def smooth_lines(value, lane):
    width = value.shape[-1]
    right = pltpu.roll(value, width - 1, value.ndim - 1)
    left = pltpu.roll(value, 1, value.ndim - 1)
    at_end = (lane % NODES == NODES - 1) & (lane < width - 1)
    at_start = (lane % NODES == 0) & (lane > 0)
    partner = jnp.where(at_end, right, jnp.where(at_start, left, value))
    return 0.5 * (value + partner)


def halves(value):
    high = value.astype(jnp.bfloat16)
    return high, (value - high.astype(jnp.float32)).astype(jnp.bfloat16)


def split_product(left, right):
    (high, low), (right_high, right_low) = halves(left), halves(right)
    return (
        jnp.dot(high, right_high, preferred_element_type=jnp.float32)
        + jnp.dot(low, right_high, preferred_element_type=jnp.float32)
        + jnp.dot(high, right_low, preferred_element_type=jnp.float32)
    )


def start_all(pairs, sems):
    copies = [
        pltpu.make_async_copy(source, target, sems.at[i])
        for i, (source, target) in enumerate(pairs)
    ]
    for copy in copies:
        copy.start()
    return copies


def flux_kernel(
    levels, law_in, field_in, zonal_in, meridional_in, sea_in, sent, law, field, zonal, meridional, sea, sems
):
    @pl.when(in_air())
    def _():
        x_points, fields, tile, y_points = field.shape
        lowest = pl.ds(0, tile)
        copies = start_all(
            (
                (law_in, law),
                (field_in.at[:, :, lowest, :], field),
                (zonal_in.at[:, lowest, :], zonal),
                (meridional_in.at[:, lowest, :], meridional),
                (sea_in, sea),
            ),
            sems,
        )
        for copy in copies:
            copy.wait()
        flux_count, columns = law.shape
        flat = field.reshape(x_points * fields * tile, y_points)
        ground = [
            flat[pl.ds(f * tile, x_points, stride=fields * tile), :] for f in range(fields)
        ] + [sea[0]]
        u = zonal.reshape(x_points * tile, y_points)[pl.ds(0, x_points, stride=tile), :]
        v = meridional.reshape(x_points * tile, y_points)[pl.ds(0, x_points, stride=tile), :]
        speed = jnp.sqrt(1.0 + u * u + v * v)
        parts = []
        for n in range(flux_count):
            total = law[n, 0] * ground[0]
            for f in range(1, columns):
                total = total + law[n, f] * ground[f]
            parts.append(speed * total)
        block = jnp.concatenate(parts, axis=0).astype(jnp.bfloat16)
        sent[pl.ds(0, block.shape[0]), :] = block


def edge_kernel(levels, rows, field, zonal, meridional, along, tracers, after, first, last, own):
    x_points = field.shape[0] // rows

    @pl.when(in_air())
    def _():
        d = gll_matrix()
        lane = lax.broadcasted_iota(jnp.int32, (levels, field.shape[1]), 1)
        for side, (x, target) in enumerate(((0, first), (x_points - 1, last))):
            start = x - x % NODES
            along_y = split_product(field[pl.ds(x * rows, rows), :], along[...])
            u = zonal[pl.ds(x * levels, levels), :]
            v = meridional[pl.ds(x * levels, levels), :]
            for f in range(rows // levels):
                at = f * levels
                along_x = sum(
                    float(d[x % NODES, a]) * field[pl.ds((start + a) * rows + at, levels), :]
                    for a in range(NODES)
                    if d[x % NODES, a] != 0
                )
                value = -(u * along_x + v * along_y[at : at + levels])
                value = smooth_lines(value, lane)
                own[side, pl.ds(at, levels), :] = value
                target[pl.ds(at, levels), :] = value.astype(jnp.bfloat16)

    @pl.when(jnp.logical_not(in_air()))
    def _():
        value = tracers[...]
        high = value.astype(jnp.bfloat16)
        low = (value - high.astype(jnp.float32)).astype(jnp.bfloat16)
        both = jnp.concatenate([high, low], axis=0)
        for target in (first, last):
            target[pl.ds(0, both.shape[0]), :] = both


def pack_kernel(own, *refs):
    received, packed = refs[:-1], refs[-1]
    count = len(refs)
    place = lax.axis_index("sec") % count
    here = pl.ds(0, packed.shape[1])
    packed[place] = own[here, :]
    for m, part in enumerate(received, 1):
        packed[(place - m + count) % count] = part[here, :]


def middle_kernel(
    levels,
    rows,
    field,
    zonal,
    meridional,
    along,
    own,
    below,
    above,
    tracers,
    senders_in,
    live_in,
    factor_in,
    offsets_in,
    sides_in,
    mixing_in,
    later,
    diffused,
    chosen,
    returning,
    forcing,
    gather,
    ring,
    top_wide,
    slopes,
    held,
    senders,
    live,
    factor,
    offsets,
    sides,
    mixing,
    sems,
    load_sems,
):
    x_points = later.shape[0]

    @pl.when(in_air())
    def _():
        d = gll_matrix()
        lane = lax.broadcasted_iota(jnp.int32, (levels, field.shape[1]), 1)
        inner = pl.ds(rows, (x_points - 2) * rows)
        slopes[inner, :] = jnp.dot(
            field[inner, :], along[...], precision=HIGHEST, preferred_element_type=jnp.float32
        )
        copies = []
        for f in range(rows // levels):
            at = f * levels
            here = pl.ds(at, levels)
            values = {
                0: 0.5 * (own[0, here, :] + below[here, :].astype(jnp.float32)),
                x_points - 1: 0.5 * (own[1, here, :] + above[here, :].astype(jnp.float32)),
            }
            q = [field[pl.ds(x * rows + at, levels), :] for x in range(x_points)]
            for x in range(1, x_points - 1):
                start = x - x % NODES
                along_x = sum(
                    float(d[x % NODES, a]) * q[start + a]
                    for a in range(NODES)
                    if d[x % NODES, a] != 0
                )
                u = zonal[pl.ds(x * levels, levels), :]
                v = meridional[pl.ds(x * levels, levels), :]
                value = -(u * along_x + v * slopes[pl.ds(x * rows + at, levels), :])
                values[x] = smooth_lines(value, lane)
            for x in range(NODES - 1, x_points - 1, NODES):
                values[x] = values[x + 1] = 0.5 * (values[x] + values[x + 1])
            for x in range(x_points):
                held[x, here, :] = q[x] + STEP_ATMOS * values[x]
            copy = pltpu.make_async_copy(held.at[:, here, :], later.at[:, here, :], sems.at[f])
            copy.start()
            copies.append(copy)
        for copy in copies:
            copy.wait()

    @pl.when(jnp.logical_not(in_air()))
    def _():
        loads = start_all(
            (
                (senders_in, senders),
                (live_in, live),
                (factor_in, factor),
                (offsets_in, offsets),
                (sides_in, sides),
                (mixing_in, mixing),
            ),
            load_sems,
        )
        held[0] = jnp.zeros(held.shape[1:], jnp.float32)
        copies = start_all([(held.at[0], later.at[x]) for x in range(x_points)], sems)
        cells = sides.shape[1]
        x_count = gather.shape[0] // cells
        point = lax.broadcasted_iota(jnp.int32, gather.shape, 0) // x_count
        cell = lax.broadcasted_iota(jnp.int32, gather.shape, 1)
        gather[...] = jnp.where(point == cell, 1.0, 0.0).astype(gather.dtype)
        row = lax.broadcasted_iota(jnp.int32, ring.shape, 0) // x_count
        column = lax.broadcasted_iota(jnp.int32, ring.shape, 1) // x_count
        ring[...] = jnp.where(row == column, 1.0, 0.0).astype(ring.dtype)
        for load in loads:
            load.wait()

        source = lax.broadcasted_iota(jnp.int32, (cells, cells), 0)
        target = lax.broadcasted_iota(jnp.int32, (cells, cells), 1)
        inside = jnp.zeros((cells, cells), jnp.float32)
        outside = jnp.zeros((cells, cells), jnp.float32)
        total = jnp.zeros((1, cells), jnp.float32)
        for e in range(offsets.shape[0]):
            weight = jnp.where(e < sides[...], mixing[e], 0.0)
            place = target[:1] + offsets[e]
            total = total + weight
            inside = inside + jnp.where(source == place, weight, 0.0)
            hit = (source == place - cells) | (source == place + cells)
            outside = outside + jnp.where(hit, weight, 0.0)
        inside = inside - jnp.where(source == target, total, 0.0)

        value = tracers[...]
        height = value.shape[0]
        cell = lax.broadcasted_iota(jnp.int32, value.shape, 1)
        beside = [
            h[pl.ds(0, height), :].astype(jnp.float32)
            + h[pl.ds(height, height), :].astype(jnp.float32)
            for h in (below, above)
        ]
        outer = jnp.where(cell < cells // 2, beside[1], beside[0])
        change = jnp.dot(
            jnp.concatenate([value, outer], axis=1),
            jnp.concatenate([inside, outside], axis=0),
            precision=HIGHEST,
            preferred_element_type=jnp.float32,
        )
        step = value + DIFFUSIVITY * change
        diffused[...] = step
        cell = lax.broadcasted_iota(jnp.int32, (cells, gather.shape[0]), 0)
        point = lax.broadcasted_iota(jnp.int32, (cells, gather.shape[0]), 1) // x_count
        wide = jnp.dot(
            jnp.broadcast_to(step[0:1], (x_count, cells)),
            jnp.where(point == cell, 1.0, 0.0),
            precision=HIGHEST,
            preferred_element_type=jnp.float32,
        )
        for b in range(x_count):
            top_wide[pl.ds(b, 1), :] = wide[0:1, b * cells : (b + 1) * cells]

        sections = lax.axis_size("sec")
        oceans = sections // 4
        air = sections - oceans
        ocean = jnp.maximum(lax.axis_index("sec") - air, 0)
        width = chosen.shape[1]
        count = live[0, ocean]
        for k in range(senders.shape[2]):
            place = jnp.where(k < count, senders[ocean, 0, k], sections)
            section = lax.broadcasted_iota(jnp.int32, (air, width), 0)
            chosen[pl.ds(k * air, air), :] = jnp.where(section == place, 1.0, 0.0)
            block = section % (air // oceans)
            owner = ((ocean + section // (air // oceans)) % oceans) ^ 1
            returning[pl.ds(k * air, air), :] = jnp.where(
                block * oceans + owner == place, 1.0, 0.0
            )
        tracer_count, flux_count = factor.shape
        depth = forcing.shape[0] // (tracer_count * flux_count)
        level = lax.broadcasted_iota(jnp.int32, (depth, width), 0).astype(jnp.float32)
        profile = STEP_OCEAN * jnp.exp(-0.5 * level)
        for n in range(flux_count):
            for t in range(tracer_count):
                forcing[pl.ds((n * tracer_count + t) * depth, depth), :] = factor[t, n] * profile
        for copy in copies:
            copy.wait()


def remap_kernel(regrid, ring, chosen, returning, forcing, top_wide, *refs):
    arrived, summed, shares = (refs[2], refs[0], refs[1]), refs[3], refs[4:]

    @pl.when(jnp.logical_not(in_air()))
    def _():
        flux_count, points = summed.shape
        x_count, cells = top_wide.shape
        slots = regrid.shape[0] // points
        air = chosen.shape[0] // slots
        row = lax.broadcasted_iota(jnp.int32, (x_count, cells), 0)
        column = lax.broadcasted_iota(jnp.int32, (x_count, cells), 1)
        same = jnp.where(row == column % x_count, 1.0, 0.0)

        blocks = [block[s].astype(jnp.float32) for block in arrived for s in range(block.shape[0])]
        matched = None
        for k in range(slots):
            part = chosen[pl.ds(k * air, 1), :] * blocks[0]
            for s in range(1, air):
                part = part + chosen[pl.ds(k * air + s, 1), :] * blocks[s]
            product = lax.dot_general(
                part.astype(jnp.bfloat16),
                regrid[pl.ds(k * points, points), :],
                (((1,), (1,)), ((), ())),
                preferred_element_type=jnp.float32,
            )
            matched = product if matched is None else matched + product
        matched = matched * jnp.tile(same, (flux_count, x_count))
        sums = matched.reshape(flux_count, x_count, points).sum(axis=1)
        summed[...] = sums
        pieces = jnp.concatenate(
            [sums[:, b * cells : (b + 1) * cells] for b in range(x_count)], axis=0
        )
        both = jnp.dot(
            jnp.concatenate(halves(pieces), axis=0), ring[...], preferred_element_type=jnp.float32
        )
        fluxes = both[: flux_count * x_count] + both[flux_count * x_count :]
        height = forcing.shape[0] // flux_count
        wide = []
        for b in range(x_count):
            top = top_wide[pl.ds(b, 1), :]
            for n in range(flux_count):
                at = b * flux_count + n
                top = top + forcing[pl.ds(n * height, 1), :] * fluxes[at : at + 1]
            top = top.astype(jnp.bfloat16).astype(jnp.float32)
            wide.append((top * same).astype(jnp.bfloat16))
        wide = jnp.concatenate(wide, axis=1)
        back = [
            jnp.dot(wide, regrid[pl.ds(k * points, points), :], preferred_element_type=jnp.float32)
            for k in range(slots)
        ]
        count = shares[0].shape[0]
        for m, share in enumerate(shares):
            for j in range(count):
                at = m * count + j
                total = returning[pl.ds(at, 1), :] * back[0]
                for k in range(1, slots):
                    total = total + returning[pl.ds(k * air + at, 1), :] * back[k]
                share[j] = total


def renew_kernel(summed, gather, forcing, diffused, renewed):
    @pl.when(jnp.logical_not(in_air()))
    def _():
        flux_count = summed.shape[0]
        both = jnp.dot(
            jnp.concatenate(halves(summed[...]), axis=0),
            gather[...],
            preferred_element_type=jnp.float32,
        )
        height = diffused.shape[0]
        value = diffused[...]
        for n in range(flux_count):
            flux = both[n : n + 1] + both[flux_count + n : flux_count + n + 1]
            value = value + forcing[pl.ds(n * height, height), :] * flux
        renewed[...] = value


def add_kernel(*refs):
    count = refs[0].shape[0]
    shares, totals = refs[:-count], refs[-count:]

    @pl.when(jnp.logical_not(in_air()))
    def _():
        for j, total in enumerate(totals):
            value = shares[0][j]
            for share in shares[1:]:
                value = value + share[j]
            total[...] = value


def last_kernel(renewed, *refs):
    returned, (tracers_later, warmth) = refs[:-2], refs[-2:]
    sections = lax.axis_size("sec")
    block = lax.axis_index("sec") // (sections // 4)

    @pl.when(in_air())
    def _():
        tracers_later[...] = jnp.zeros(tracers_later.shape, jnp.float32)

    @pl.when(jnp.logical_not(in_air()))
    def _():
        tracers_later[...] = renewed[...]
        warmth[...] = jnp.zeros(warmth.shape, jnp.float32)

    for j, part in enumerate(returned):

        @pl.when(block == j)
        def _(part=part):
            warmth[...] = part[...]


def per_device(
    climate_field_table,
    zonal_wind_speed,
    meridional_wind,
    sea_warmth_field,
    exchange_law_factor,
    regrid_matrix_stack,
    entry_sender_patch,
    holder_live_total,
    marine_salinity_heat,
    adjacent_offset_lists,
    polygon_side_total,
    interface_mixing_factor,
    solute_forcing_factor,
):
    sections = lax.axis_size("sec")
    ranks = lax.axis_size("rank")
    oceans = sections // 4
    air = sections - oceans
    _, x_points, rows, y_points = climate_field_table.shape
    levels = zonal_wind_speed.shape[2]
    flux_count = exchange_law_factor.shape[0]
    _, tracer_count, depth, cells = marine_salinity_heat.shape
    slots = regrid_matrix_stack.shape[2]
    f32, bf16 = jnp.float32, jnp.bfloat16
    shape = jax.ShapeDtypeStruct

    field = climate_field_table.reshape(x_points * rows, y_points)
    zonal = zonal_wind_speed.reshape(x_points * levels, y_points)
    meridional = meridional_wind.reshape(x_points * levels, y_points)
    regrid = regrid_matrix_stack.reshape(slots * cells * x_points, y_points)
    tracers = marine_salinity_heat.reshape(tracer_count * depth, cells)
    offsets = jnp.transpose(adjacent_offset_lists, (1, 0, 2))
    mixing = jnp.transpose(interface_mixing_factor, (1, 0, 2))
    live = jnp.transpose(holder_live_total, (1, 0))

    along = np.kron(np.eye(y_points // NODES, dtype=np.float32), gll_matrix().T)
    along = jnp.asarray(along)

    fields = rows // levels
    tile = min(8, levels)
    in_place = (
        exchange_law_factor,
        climate_field_table.reshape(x_points, fields, levels, y_points),
        zonal_wind_speed[0],
        meridional_wind[0],
        sea_warmth_field,
    )
    swap_rows = max(flux_count * x_points, rows + 16)
    fluxes = pl.pallas_call(
        functools.partial(flux_kernel, levels),
        out_shape=shape((swap_rows, y_points), bf16),
        in_specs=[HBM] * len(in_place),
        out_specs=VMEM,
        scratch_shapes=[
            pltpu.SMEM(exchange_law_factor.shape, f32),
            pltpu.VMEM((x_points, fields, tile, y_points), f32),
            pltpu.VMEM((x_points, tile, y_points), f32),
            pltpu.VMEM((x_points, tile, y_points), f32),
            pltpu.VMEM((1, x_points, y_points), f32),
            pltpu.SemaphoreType.DMA((len(in_place),)),
        ],
        compiler_params=PARAMS,
        cost_estimate=cost(1),
        name="flux",
    )(*(pltpu.with_memory_space_constraint(a, pltpu.HBM) for a in in_place))
    first, last, own = pl.pallas_call(
        functools.partial(edge_kernel, levels, rows),
        out_shape=(
            shape((rows, y_points), bf16),
            shape((rows, y_points), bf16),
            shape((2, rows, y_points), f32),
        ),
        in_specs=[VMEM] * 5 + [ANY],
        out_specs=(VMEM,) * 3,
        compiler_params=PARAMS,
        cost_estimate=cost(1),
        name="edges",
    )(field, zonal, meridional, along, tracers, fluxes)
    up = [(i, (i + 1) % ranks) for i in range(ranks)]
    below = lax.ppermute(last, "rank", up)
    above = lax.ppermute(first, "rank", [(j, i) for i, j in up])

    def turned(value, m):
        pairs = [(s, s // oceans * oceans + (s + m) % oceans) for s in range(sections)]
        return lax.ppermute(value, "sec", pairs)

    def paired(value, mask):
        pairs = [
            (s, (s // oceans ^ mask) * oceans + (s % oceans ^ 1)) for s in range(sections)
        ]
        return lax.ppermute(value, "sec", pairs)

    received = [turned(fluxes, m) for m in range(1, oceans)]
    packed = pl.pallas_call(
        pack_kernel,
        out_shape=shape((oceans, flux_count * x_points, y_points), bf16),
        in_specs=[VMEM] * oceans,
        out_specs=VMEM,
        compiler_params=PARAMS,
        cost_estimate=cost(0.2),
        name="pack",
    )(fluxes, *received)
    arrived = [paired(packed, 3 ^ block) for block in range(3)]

    from_memory = (
        entry_sender_patch,
        live,
        solute_forcing_factor,
        offsets,
        polygon_side_total,
        mixing,
    )
    later, diffused, chosen, returning, forcing, gather, ring, top_wide = pl.pallas_call(
        functools.partial(middle_kernel, levels, rows),
        out_shape=(
            shape((x_points, rows, y_points), f32),
            shape(tracers.shape, f32),
            shape((slots * air, y_points), f32),
            shape((slots * air, y_points), f32),
            shape((flux_count * tracer_count * depth, cells), f32),
            shape((x_points * cells, cells), bf16),
            shape((cells, cells), bf16),
            shape((x_points, cells), f32),
        ),
        in_specs=[VMEM] * 8 + [HBM] * 6,
        out_specs=(HBM,) + (VMEM,) * 7,
        scratch_shapes=[
            pltpu.VMEM(field.shape, f32),
            pltpu.VMEM((x_points, rows, y_points), f32),
        ]
        + [
            (pltpu.SMEM if i < 3 else pltpu.VMEM)(a.shape, a.dtype)
            for i, a in enumerate(from_memory)
        ]
        + [
            pltpu.SemaphoreType.DMA((max(fields, x_points),)),
            pltpu.SemaphoreType.DMA((len(from_memory),)),
        ],
        compiler_params=PARAMS,
        cost_estimate=cost(1),
        name="middle",
    )(
        field,
        zonal,
        meridional,
        along,
        own,
        below,
        above,
        tracers,
        *(pltpu.with_memory_space_constraint(a, pltpu.HBM) for a in from_memory),
    )

    summed, *shares = pl.pallas_call(
        remap_kernel,
        out_shape=(shape((flux_count, x_points * cells), f32),)
        + (shape((air // oceans, x_points, y_points), f32),) * oceans,
        in_specs=[VMEM] * 9,
        out_specs=(VMEM,) * (1 + oceans),
        compiler_params=PARAMS,
        cost_estimate=cost(1),
        name="remap",
    )(
        regrid,
        ring,
        chosen,
        returning,
        forcing,
        top_wide,
        arrived[1],
        arrived[2],
        arrived[0],
    )
    shares = shares[:1] + [turned(share, m) for m, share in enumerate(shares[1:], 1)]
    totals = pl.pallas_call(
        add_kernel,
        out_shape=(shape((x_points, y_points), f32),) * (air // oceans),
        in_specs=[VMEM] * oceans,
        out_specs=(VMEM,) * (air // oceans),
        compiler_params=PARAMS,
        cost_estimate=cost(0.3),
        name="add",
    )(*shares)
    returned = [paired(total, 3 ^ block) for block, total in enumerate(totals)]
    renewed = pl.pallas_call(
        renew_kernel,
        out_shape=shape(tracers.shape, f32),
        in_specs=[VMEM] * 4,
        out_specs=VMEM,
        compiler_params=PARAMS,
        cost_estimate=cost(0.5),
        name="renew",
    )(summed, gather, forcing, diffused)
    tracers_later, warmth = pl.pallas_call(
        last_kernel,
        out_shape=(shape(tracers.shape, f32), shape((x_points, y_points), f32)),
        in_specs=[VMEM] * (1 + len(returned)),
        out_specs=(VMEM,) * 2,
        compiler_params=PARAMS,
        cost_estimate=cost(0.5),
        name="last",
    )(renewed, *returned)
    return (
        later.reshape(climate_field_table.shape),
        tracers_later.reshape(marine_salinity_heat.shape),
        warmth[None],
    )


def solution(mesh):
    return jax.shard_map(
        per_device,
        mesh=mesh,
        in_specs=(
            P("sec", "rank", None, None),
            P("sec", "rank", None, None),
            P("sec", "rank", None, None),
            P("sec", "rank", None),
            P(),
            P("sec", "rank", None, None, None, None),
            P(None, "rank", None),
            P(None, "rank"),
            P("sec", None, None, "rank"),
            P("sec", None, "rank"),
            P("sec", "rank"),
            P("sec", None, "rank"),
            P(),
        ),
        out_specs=(
            P("sec", "rank", None, None),
            P("sec", None, None, "rank"),
            P("sec", "rank", None),
        ),
        check_vma=False,
    )
```

```python
import functools

import jax
import jax.numpy as jnp
import numpy as np
from jax import lax
from jax.experimental import pallas as pl
from jax.experimental.pallas import tpu as pltpu
from jax.sharding import PartitionSpec as P

STEP_ATMOS = 0.05
DIFFUSIVITY = 0.05
STEP_OCEAN = 0.5
NODES = 4

VMEM = pl.BlockSpec(memory_space=pltpu.VMEM)
ANY = pl.BlockSpec(memory_space=pl.ANY)
HBM = pl.BlockSpec(memory_space=pltpu.HBM)
SMEM = pl.BlockSpec(memory_space=pltpu.SMEM)
PARAMS = pltpu.CompilerParams(vmem_limit_bytes=8 * 2**20)
HIGHEST = lax.Precision.HIGHEST


def gll_matrix():
    nodes = np.array([-1.0, -1.0 / np.sqrt(5.0), 1.0 / np.sqrt(5.0), 1.0])
    legendre = (5.0 * nodes**3 - 3.0 * nodes) / 2.0
    matrix = np.zeros((4, 4))
    for i in range(4):
        for j in range(4):
            if i != j:
                matrix[i, j] = legendre[i] / (legendre[j] * (nodes[i] - nodes[j]))
    matrix[0, 0] = -3.0
    matrix[3, 3] = 3.0
    return matrix.astype(np.float32)


def cost(microseconds):
    return pl.CostEstimate(
        flops=0, bytes_accessed=int(microseconds * 3_000_000), transcendentals=0
    )


def in_air():
    sections = lax.axis_size("sec")
    return lax.axis_index("sec") < sections - sections // 4


def smooth_lines(value, lane):
    width = value.shape[-1]
    right = pltpu.roll(value, width - 1, value.ndim - 1)
    left = pltpu.roll(value, 1, value.ndim - 1)
    at_end = (lane % NODES == NODES - 1) & (lane < width - 1)
    at_start = (lane % NODES == 0) & (lane > 0)
    partner = jnp.where(at_end, right, jnp.where(at_start, left, value))
    return 0.5 * (value + partner)


def halves(value):
    high = value.astype(jnp.bfloat16)
    return high, (value - high.astype(jnp.float32)).astype(jnp.bfloat16)


def split_product(left, right):
    (high, low), (right_high, right_low) = halves(left), halves(right)
    return (
        jnp.dot(high, right_high, preferred_element_type=jnp.float32)
        + jnp.dot(low, right_high, preferred_element_type=jnp.float32)
        + jnp.dot(high, right_low, preferred_element_type=jnp.float32)
    )


def start_all(pairs, sems):
    copies = [
        pltpu.make_async_copy(source, target, sems.at[i])
        for i, (source, target) in enumerate(pairs)
    ]
    for copy in copies:
        copy.start()
    return copies


def flux_kernel(
    levels, law_in, field_in, zonal_in, meridional_in, sea_in, sent, law, field, zonal, meridional, sea, sems
):
    @pl.when(in_air())
    def _():
        x_points, fields, tile, y_points = field.shape
        lowest = pl.ds(0, tile)
        copies = start_all(
            (
                (law_in, law),
                (field_in.at[:, :, lowest, :], field),
                (zonal_in.at[:, lowest, :], zonal),
                (meridional_in.at[:, lowest, :], meridional),
                (sea_in, sea),
            ),
            sems,
        )
        for copy in copies:
            copy.wait()
        flux_count, columns = law.shape
        flat = field.reshape(x_points * fields * tile, y_points)
        ground = [
            flat[pl.ds(f * tile, x_points, stride=fields * tile), :] for f in range(fields)
        ] + [sea[0]]
        u = zonal.reshape(x_points * tile, y_points)[pl.ds(0, x_points, stride=tile), :]
        v = meridional.reshape(x_points * tile, y_points)[pl.ds(0, x_points, stride=tile), :]
        speed = jnp.sqrt(1.0 + u * u + v * v)
        parts = []
        for n in range(flux_count):
            total = law[n, 0] * ground[0]
            for f in range(1, columns):
                total = total + law[n, f] * ground[f]
            parts.append(speed * total)
        block = jnp.concatenate(parts, axis=0).astype(jnp.bfloat16)
        sent[pl.ds(0, block.shape[0]), :] = block


def edge_kernel(levels, rows, field, zonal, meridional, along, tracers, after, first, last, own):
    x_points = field.shape[0] // rows

    @pl.when(in_air())
    def _():
        d = gll_matrix()
        lane = lax.broadcasted_iota(jnp.int32, (levels, field.shape[1]), 1)
        for side, (x, target) in enumerate(((0, first), (x_points - 1, last))):
            start = x - x % NODES
            along_y = split_product(field[pl.ds(x * rows, rows), :], along[...])
            u = zonal[pl.ds(x * levels, levels), :]
            v = meridional[pl.ds(x * levels, levels), :]
            for f in range(rows // levels):
                at = f * levels
                along_x = sum(
                    float(d[x % NODES, a]) * field[pl.ds((start + a) * rows + at, levels), :]
                    for a in range(NODES)
                    if d[x % NODES, a] != 0
                )
                value = -(u * along_x + v * along_y[at : at + levels])
                value = smooth_lines(value, lane)
                own[side, pl.ds(at, levels), :] = value
                target[pl.ds(at, levels), :] = value.astype(jnp.bfloat16)

    @pl.when(jnp.logical_not(in_air()))
    def _():
        value = tracers[...]
        high = value.astype(jnp.bfloat16)
        low = (value - high.astype(jnp.float32)).astype(jnp.bfloat16)
        both = jnp.concatenate([high, low], axis=0)
        for target in (first, last):
            target[pl.ds(0, both.shape[0]), :] = both


def pack_kernel(own, *refs):
    received, packed = refs[:-1], refs[-1]
    count = len(refs)
    place = lax.axis_index("sec") % count
    here = pl.ds(0, packed.shape[1])
    packed[place] = own[here, :]
    for m, part in enumerate(received, 1):
        packed[(place - m + count) % count] = part[here, :]


def middle_kernel(
    levels,
    rows,
    field,
    zonal,
    meridional,
    along,
    own,
    below,
    above,
    tracers,
    senders_in,
    live_in,
    factor_in,
    offsets_in,
    sides_in,
    mixing_in,
    later,
    diffused,
    chosen,
    returning,
    forcing,
    gather,
    spread,
    slopes,
    held,
    senders,
    live,
    factor,
    offsets,
    sides,
    mixing,
    sems,
    load_sems,
):
    x_points = later.shape[0]

    @pl.when(in_air())
    def _():
        d = gll_matrix()
        lane = lax.broadcasted_iota(jnp.int32, (levels, field.shape[1]), 1)
        inner = pl.ds(rows, (x_points - 2) * rows)
        slopes[inner, :] = jnp.dot(
            field[inner, :], along[...], precision=HIGHEST, preferred_element_type=jnp.float32
        )
        copies = []
        for f in range(rows // levels):
            at = f * levels
            here = pl.ds(at, levels)
            values = {
                0: 0.5 * (own[0, here, :] + below[here, :].astype(jnp.float32)),
                x_points - 1: 0.5 * (own[1, here, :] + above[here, :].astype(jnp.float32)),
            }
            q = [field[pl.ds(x * rows + at, levels), :] for x in range(x_points)]
            for x in range(1, x_points - 1):
                start = x - x % NODES
                along_x = sum(
                    float(d[x % NODES, a]) * q[start + a]
                    for a in range(NODES)
                    if d[x % NODES, a] != 0
                )
                u = zonal[pl.ds(x * levels, levels), :]
                v = meridional[pl.ds(x * levels, levels), :]
                value = -(u * along_x + v * slopes[pl.ds(x * rows + at, levels), :])
                values[x] = smooth_lines(value, lane)
            for x in range(NODES - 1, x_points - 1, NODES):
                values[x] = values[x + 1] = 0.5 * (values[x] + values[x + 1])
            for x in range(x_points):
                held[x, here, :] = q[x] + STEP_ATMOS * values[x]
            copy = pltpu.make_async_copy(held.at[:, here, :], later.at[:, here, :], sems.at[f])
            copy.start()
            copies.append(copy)
        for copy in copies:
            copy.wait()

    @pl.when(jnp.logical_not(in_air()))
    def _():
        loads = start_all(
            (
                (senders_in, senders),
                (live_in, live),
                (factor_in, factor),
                (offsets_in, offsets),
                (sides_in, sides),
                (mixing_in, mixing),
            ),
            load_sems,
        )
        held[0] = jnp.zeros(held.shape[1:], jnp.float32)
        copies = start_all([(held.at[0], later.at[x]) for x in range(x_points)], sems)
        cells = sides.shape[1]
        x_count = gather.shape[0] // cells
        point = lax.broadcasted_iota(jnp.int32, gather.shape, 0) // x_count
        cell = lax.broadcasted_iota(jnp.int32, gather.shape, 1)
        gather[...] = jnp.where(point == cell, 1.0, 0.0).astype(gather.dtype)
        cell = lax.broadcasted_iota(jnp.int32, spread.shape, 0)
        point = lax.broadcasted_iota(jnp.int32, spread.shape, 1) // x_count
        spread[...] = jnp.where(point == cell, 1.0, 0.0).astype(spread.dtype)
        for load in loads:
            load.wait()

        source = lax.broadcasted_iota(jnp.int32, (cells, cells), 0)
        target = lax.broadcasted_iota(jnp.int32, (cells, cells), 1)
        inside = jnp.zeros((cells, cells), jnp.float32)
        outside = jnp.zeros((cells, cells), jnp.float32)
        total = jnp.zeros((1, cells), jnp.float32)
        for e in range(offsets.shape[0]):
            weight = jnp.where(e < sides[...], mixing[e], 0.0)
            place = target[:1] + offsets[e]
            total = total + weight
            inside = inside + jnp.where(source == place, weight, 0.0)
            hit = (source == place - cells) | (source == place + cells)
            outside = outside + jnp.where(hit, weight, 0.0)
        inside = inside - jnp.where(source == target, total, 0.0)

        value = tracers[...]
        height = value.shape[0]
        cell = lax.broadcasted_iota(jnp.int32, value.shape, 1)
        beside = [
            h[pl.ds(0, height), :].astype(jnp.float32)
            + h[pl.ds(height, height), :].astype(jnp.float32)
            for h in (below, above)
        ]
        outer = jnp.where(cell < cells // 2, beside[1], beside[0])
        change = jnp.dot(
            jnp.concatenate([value, outer], axis=1),
            jnp.concatenate([inside, outside], axis=0),
            precision=HIGHEST,
            preferred_element_type=jnp.float32,
        )
        diffused[...] = value + DIFFUSIVITY * change

        sections = lax.axis_size("sec")
        oceans = sections // 4
        air = sections - oceans
        ocean = jnp.maximum(lax.axis_index("sec") - air, 0)
        width = chosen.shape[1]
        count = live[0, ocean]
        for k in range(senders.shape[2]):
            place = jnp.where(k < count, senders[ocean, 0, k], sections)
            section = lax.broadcasted_iota(jnp.int32, (air, width), 0)
            chosen[pl.ds(k * air, air), :] = jnp.where(section == place, 1.0, 0.0)
            block = section % (air // oceans)
            owner = ((ocean + section // (air // oceans)) % oceans) ^ 1
            returning[pl.ds(k * air, air), :] = jnp.where(
                block * oceans + owner == place, 1.0, 0.0
            )
        tracer_count, flux_count = factor.shape
        depth = forcing.shape[0] // (tracer_count * flux_count)
        level = lax.broadcasted_iota(jnp.int32, (depth, width), 0).astype(jnp.float32)
        profile = STEP_OCEAN * jnp.exp(-0.5 * level)
        for n in range(flux_count):
            for t in range(tracer_count):
                forcing[pl.ds((n * tracer_count + t) * depth, depth), :] = factor[t, n] * profile
        for copy in copies:
            copy.wait()


def remap_kernel(
    regrid, gather, spread, chosen, returning, forcing, diffused, *refs
):
    arrived, renewed, shares = (refs[2], refs[0], refs[1]), refs[3], refs[4:]

    @pl.when(jnp.logical_not(in_air()))
    def _():
        points, cells = gather.shape
        x_count = points // cells
        slots = regrid.shape[0] // points
        air = chosen.shape[0] // slots
        packed = refs[0].shape[1]
        flux_count = packed // x_count
        row = lax.broadcasted_iota(jnp.int32, (x_count, cells), 0)
        column = lax.broadcasted_iota(jnp.int32, (x_count, cells), 1)
        same = jnp.where(row == column % x_count, 1.0, 0.0)

        blocks = [block[s].astype(jnp.float32) for block in arrived for s in range(block.shape[0])]
        matched = None
        for k in range(slots):
            part = chosen[pl.ds(k * air, 1), :] * blocks[0]
            for s in range(1, air):
                part = part + chosen[pl.ds(k * air + s, 1), :] * blocks[s]
            product = lax.dot_general(
                part.astype(jnp.bfloat16),
                regrid[pl.ds(k * points, points), :],
                (((1,), (1,)), ((), ())),
                preferred_element_type=jnp.float32,
            )
            matched = product if matched is None else matched + product
        matched = matched * jnp.tile(same, (flux_count, x_count))
        high = matched.astype(jnp.bfloat16)
        low = (matched - high.astype(jnp.float32)).astype(jnp.bfloat16)
        summed = jnp.dot(
            jnp.concatenate([high, low], axis=0), gather[...], preferred_element_type=jnp.float32
        )
        ocean_flux = (summed[:packed] + summed[packed:]).reshape(flux_count, x_count, cells).sum(axis=1)
        height = diffused.shape[0]
        value = diffused[...]
        for n in range(flux_count):
            value = value + forcing[pl.ds(n * height, height), :] * ocean_flux[n : n + 1]
        renewed[...] = value

        top = jnp.broadcast_to(value[0:1], (x_count, cells)).astype(jnp.bfloat16)
        wide = jnp.dot(top, spread[...], preferred_element_type=jnp.float32)
        wide = (wide * jnp.tile(same, (1, x_count))).astype(jnp.bfloat16)
        back = [
            jnp.dot(wide, regrid[pl.ds(k * points, points), :], preferred_element_type=jnp.float32)
            for k in range(slots)
        ]
        count = shares[0].shape[0]
        for m, share in enumerate(shares):
            for j in range(count):
                at = m * count + j
                total = returning[pl.ds(at, 1), :] * back[0]
                for k in range(1, slots):
                    total = total + returning[pl.ds(k * air + at, 1), :] * back[k]
                share[j] = total


def add_kernel(*refs):
    count = refs[0].shape[0]
    shares, totals = refs[:-count], refs[-count:]

    @pl.when(jnp.logical_not(in_air()))
    def _():
        for j, total in enumerate(totals):
            value = shares[0][j]
            for share in shares[1:]:
                value = value + share[j]
            total[...] = value


def last_kernel(renewed, *refs):
    returned, (tracers_later, warmth) = refs[:-2], refs[-2:]
    sections = lax.axis_size("sec")
    block = lax.axis_index("sec") // (sections // 4)

    @pl.when(in_air())
    def _():
        tracers_later[...] = jnp.zeros(tracers_later.shape, jnp.float32)

    @pl.when(jnp.logical_not(in_air()))
    def _():
        tracers_later[...] = renewed[...]
        warmth[...] = jnp.zeros(warmth.shape, jnp.float32)

    for j, part in zip((0, 2, 1), returned):

        @pl.when(block == j)
        def _(part=part):
            warmth[...] = part[...]


def per_device(
    climate_field_table,
    zonal_wind_speed,
    meridional_wind,
    sea_warmth_field,
    exchange_law_factor,
    regrid_matrix_stack,
    entry_sender_patch,
    holder_live_total,
    marine_salinity_heat,
    adjacent_offset_lists,
    polygon_side_total,
    interface_mixing_factor,
    solute_forcing_factor,
):
    sections = lax.axis_size("sec")
    ranks = lax.axis_size("rank")
    oceans = sections // 4
    air = sections - oceans
    _, x_points, rows, y_points = climate_field_table.shape
    levels = zonal_wind_speed.shape[2]
    flux_count = exchange_law_factor.shape[0]
    _, tracer_count, depth, cells = marine_salinity_heat.shape
    slots = regrid_matrix_stack.shape[2]
    f32, bf16 = jnp.float32, jnp.bfloat16
    shape = jax.ShapeDtypeStruct

    field = climate_field_table.reshape(x_points * rows, y_points)
    zonal = zonal_wind_speed.reshape(x_points * levels, y_points)
    meridional = meridional_wind.reshape(x_points * levels, y_points)
    regrid = regrid_matrix_stack.reshape(slots * cells * x_points, y_points)
    tracers = marine_salinity_heat.reshape(tracer_count * depth, cells)
    offsets = jnp.transpose(adjacent_offset_lists, (1, 0, 2))
    mixing = jnp.transpose(interface_mixing_factor, (1, 0, 2))
    live = jnp.transpose(holder_live_total, (1, 0))

    along = np.kron(np.eye(y_points // NODES, dtype=np.float32), gll_matrix().T)
    along = jnp.asarray(along)

    fields = rows // levels
    tile = min(8, levels)
    in_place = (
        exchange_law_factor,
        climate_field_table.reshape(x_points, fields, levels, y_points),
        zonal_wind_speed[0],
        meridional_wind[0],
        sea_warmth_field,
    )
    swap_rows = max(flux_count * x_points, rows + 16)
    fluxes = pl.pallas_call(
        functools.partial(flux_kernel, levels),
        out_shape=shape((swap_rows, y_points), bf16),
        in_specs=[HBM] * len(in_place),
        out_specs=VMEM,
        scratch_shapes=[
            pltpu.SMEM(exchange_law_factor.shape, f32),
            pltpu.VMEM((x_points, fields, tile, y_points), f32),
            pltpu.VMEM((x_points, tile, y_points), f32),
            pltpu.VMEM((x_points, tile, y_points), f32),
            pltpu.VMEM((1, x_points, y_points), f32),
            pltpu.SemaphoreType.DMA((len(in_place),)),
        ],
        compiler_params=PARAMS,
        cost_estimate=cost(1),
        name="flux",
    )(*(pltpu.with_memory_space_constraint(a, pltpu.HBM) for a in in_place))
    first, last, own = pl.pallas_call(
        functools.partial(edge_kernel, levels, rows),
        out_shape=(
            shape((rows, y_points), bf16),
            shape((rows, y_points), bf16),
            shape((2, rows, y_points), f32),
        ),
        in_specs=[VMEM] * 5 + [ANY],
        out_specs=(VMEM,) * 3,
        compiler_params=PARAMS,
        cost_estimate=cost(1),
        name="edges",
    )(field, zonal, meridional, along, tracers, fluxes)
    up = [(i, (i + 1) % ranks) for i in range(ranks)]
    below = lax.ppermute(last, "rank", up)
    above = lax.ppermute(first, "rank", [(j, i) for i, j in up])

    def turned(value, m):
        pairs = [(s, s // oceans * oceans + (s + m) % oceans) for s in range(sections)]
        return lax.ppermute(value, "sec", pairs)

    def paired(value, mask):
        pairs = [
            (s, (s // oceans ^ mask) * oceans + (s % oceans ^ 1)) for s in range(sections)
        ]
        return lax.ppermute(value, "sec", pairs)

    received = [turned(fluxes, m) for m in range(1, oceans)]
    packed = pl.pallas_call(
        pack_kernel,
        out_shape=shape((oceans, flux_count * x_points, y_points), bf16),
        in_specs=[VMEM] * oceans,
        out_specs=VMEM,
        compiler_params=PARAMS,
        cost_estimate=cost(0.2),
        name="pack",
    )(fluxes, *received)
    arrived = [paired(packed, 3 ^ block) for block in range(3)]

    from_memory = (
        entry_sender_patch,
        live,
        solute_forcing_factor,
        offsets,
        polygon_side_total,
        mixing,
    )
    later, diffused, chosen, returning, forcing, gather, spread = pl.pallas_call(
        functools.partial(middle_kernel, levels, rows),
        out_shape=(
            shape((x_points, rows, y_points), f32),
            shape(tracers.shape, f32),
            shape((slots * air, y_points), f32),
            shape((slots * air, y_points), f32),
            shape((flux_count * tracer_count * depth, cells), f32),
            shape((x_points * cells, cells), bf16),
            shape((cells, x_points * cells), bf16),
        ),
        in_specs=[VMEM] * 8 + [HBM] * 6,
        out_specs=(HBM,) + (VMEM,) * 6,
        scratch_shapes=[
            pltpu.VMEM(field.shape, f32),
            pltpu.VMEM((x_points, rows, y_points), f32),
        ]
        + [
            (pltpu.SMEM if i < 3 else pltpu.VMEM)(a.shape, a.dtype)
            for i, a in enumerate(from_memory)
        ]
        + [
            pltpu.SemaphoreType.DMA((max(fields, x_points),)),
            pltpu.SemaphoreType.DMA((len(from_memory),)),
        ],
        compiler_params=PARAMS,
        cost_estimate=cost(1),
        name="middle",
    )(
        field,
        zonal,
        meridional,
        along,
        own,
        below,
        above,
        tracers,
        *(pltpu.with_memory_space_constraint(a, pltpu.HBM) for a in from_memory),
    )

    renewed, *shares = pl.pallas_call(
        remap_kernel,
        out_shape=(shape(tracers.shape, f32),)
        + (shape((air // oceans, x_points, y_points), f32),) * oceans,
        in_specs=[VMEM] * 10,
        out_specs=(VMEM,) * (1 + oceans),
        compiler_params=PARAMS,
        cost_estimate=cost(1),
        name="remap",
    )(regrid, gather, spread, chosen, returning, forcing, diffused, arrived[1], arrived[2], arrived[0])
    shares = shares[:1] + [turned(share, m) for m, share in enumerate(shares[1:], 1)]
    totals = pl.pallas_call(
        add_kernel,
        out_shape=(shape((x_points, y_points), f32),) * (air // oceans),
        in_specs=[VMEM] * oceans,
        out_specs=(VMEM,) * (air // oceans),
        compiler_params=PARAMS,
        cost_estimate=cost(0.3),
        name="add",
    )(*shares)
    returned = [paired(total, 3 ^ block) for block, total in enumerate(totals)]
    tracers_later, warmth = pl.pallas_call(
        last_kernel,
        out_shape=(shape(tracers.shape, f32), shape((x_points, y_points), f32)),
        in_specs=[VMEM] * (1 + len(returned)),
        out_specs=(VMEM,) * 2,
        compiler_params=PARAMS,
        cost_estimate=cost(0.5),
        name="last",
    )(renewed, returned[0], returned[2], returned[1])
    return (
        later.reshape(climate_field_table.shape),
        tracers_later.reshape(marine_salinity_heat.shape),
        warmth[None],
    )


def solution(mesh):
    return jax.shard_map(
        per_device,
        mesh=mesh,
        in_specs=(
            P("sec", "rank", None, None),
            P("sec", "rank", None, None),
            P("sec", "rank", None, None),
            P("sec", "rank", None),
            P(),
            P("sec", "rank", None, None, None, None),
            P(None, "rank", None),
            P(None, "rank"),
            P("sec", None, None, "rank"),
            P("sec", None, "rank"),
            P("sec", "rank"),
            P("sec", None, "rank"),
            P(),
        ),
        out_specs=(
            P("sec", "rank", None, None),
            P("sec", None, None, "rank"),
            P("sec", "rank", None),
        ),
        check_vma=False,
    )
```

```python
import functools

import jax
import jax.numpy as jnp
import numpy as np
from jax import lax
from jax.experimental import pallas as pl
from jax.experimental.pallas import tpu as pltpu
from jax.sharding import PartitionSpec as P

STEP_ATMOS = 0.05
DIFFUSIVITY = 0.05
STEP_OCEAN = 0.5
NODES = 4

VMEM = pl.BlockSpec(memory_space=pltpu.VMEM)
ANY = pl.BlockSpec(memory_space=pl.ANY)
HBM = pl.BlockSpec(memory_space=pltpu.HBM)
SMEM = pl.BlockSpec(memory_space=pltpu.SMEM)
PARAMS = pltpu.CompilerParams(vmem_limit_bytes=8 * 2**20)
HIGHEST = lax.Precision.HIGHEST


def gll_matrix():
    nodes = np.array([-1.0, -1.0 / np.sqrt(5.0), 1.0 / np.sqrt(5.0), 1.0])
    legendre = (5.0 * nodes**3 - 3.0 * nodes) / 2.0
    matrix = np.zeros((4, 4))
    for i in range(4):
        for j in range(4):
            if i != j:
                matrix[i, j] = legendre[i] / (legendre[j] * (nodes[i] - nodes[j]))
    matrix[0, 0] = -3.0
    matrix[3, 3] = 3.0
    return matrix.astype(np.float32)


def cost(microseconds):
    return pl.CostEstimate(
        flops=0, bytes_accessed=int(microseconds * 3_000_000), transcendentals=0
    )


def in_air():
    sections = lax.axis_size("sec")
    return lax.axis_index("sec") < sections - sections // 4


def smooth_lines(value, lane):
    width = value.shape[-1]
    right = pltpu.roll(value, width - 1, value.ndim - 1)
    left = pltpu.roll(value, 1, value.ndim - 1)
    at_end = (lane % NODES == NODES - 1) & (lane < width - 1)
    at_start = (lane % NODES == 0) & (lane > 0)
    partner = jnp.where(at_end, right, jnp.where(at_start, left, value))
    return 0.5 * (value + partner)


def halves(value):
    high = value.astype(jnp.bfloat16)
    return high, (value - high.astype(jnp.float32)).astype(jnp.bfloat16)


def split_product(left, right):
    (high, low), (right_high, right_low) = halves(left), halves(right)
    return (
        jnp.dot(high, right_high, preferred_element_type=jnp.float32)
        + jnp.dot(low, right_high, preferred_element_type=jnp.float32)
        + jnp.dot(high, right_low, preferred_element_type=jnp.float32)
    )


def start_all(pairs, sems):
    copies = [
        pltpu.make_async_copy(source, target, sems.at[i])
        for i, (source, target) in enumerate(pairs)
    ]
    for copy in copies:
        copy.start()
    return copies


def flux_kernel(
    levels, law_in, field_in, zonal_in, meridional_in, sea_in, sent, law, field, zonal, meridional, sea, sems
):
    @pl.when(in_air())
    def _():
        x_points, fields, tile, y_points = field.shape
        lowest = pl.ds(0, tile)
        copies = start_all(
            (
                (law_in, law),
                (field_in.at[:, :, lowest, :], field),
                (zonal_in.at[:, lowest, :], zonal),
                (meridional_in.at[:, lowest, :], meridional),
                (sea_in, sea),
            ),
            sems,
        )
        for copy in copies:
            copy.wait()
        flux_count, columns = law.shape
        flat = field.reshape(x_points * fields * tile, y_points)
        ground = [
            flat[pl.ds(f * tile, x_points, stride=fields * tile), :] for f in range(fields)
        ] + [sea[0]]
        u = zonal.reshape(x_points * tile, y_points)[pl.ds(0, x_points, stride=tile), :]
        v = meridional.reshape(x_points * tile, y_points)[pl.ds(0, x_points, stride=tile), :]
        speed = jnp.sqrt(1.0 + u * u + v * v)
        parts = []
        for n in range(flux_count):
            total = law[n, 0] * ground[0]
            for f in range(1, columns):
                total = total + law[n, f] * ground[f]
            parts.append(speed * total)
        block = jnp.concatenate(parts, axis=0).astype(jnp.bfloat16)
        sent[pl.ds(0, block.shape[0]), :] = block


def edge_kernel(levels, rows, field, zonal, meridional, along, tracers, after, first, last, own):
    x_points = field.shape[0] // rows

    @pl.when(in_air())
    def _():
        d = gll_matrix()
        lane = lax.broadcasted_iota(jnp.int32, (levels, field.shape[1]), 1)
        for side, (x, target) in enumerate(((0, first), (x_points - 1, last))):
            start = x - x % NODES
            along_y = split_product(field[pl.ds(x * rows, rows), :], along[...])
            u = zonal[pl.ds(x * levels, levels), :]
            v = meridional[pl.ds(x * levels, levels), :]
            for f in range(rows // levels):
                at = f * levels
                along_x = sum(
                    float(d[x % NODES, a]) * field[pl.ds((start + a) * rows + at, levels), :]
                    for a in range(NODES)
                    if d[x % NODES, a] != 0
                )
                value = -(u * along_x + v * along_y[at : at + levels])
                value = smooth_lines(value, lane)
                own[side, pl.ds(at, levels), :] = value
                target[pl.ds(at, levels), :] = value.astype(jnp.bfloat16)

    @pl.when(jnp.logical_not(in_air()))
    def _():
        value = tracers[...]
        high = value.astype(jnp.bfloat16)
        low = (value - high.astype(jnp.float32)).astype(jnp.bfloat16)
        both = jnp.concatenate([high, low], axis=0)
        for target in (first, last):
            target[pl.ds(0, both.shape[0]), :] = both


def pack_kernel(own, *refs):
    received, packed = refs[:-1], refs[-1]
    count = len(refs)
    place = lax.axis_index("sec") % count
    here = pl.ds(0, packed.shape[1])
    packed[place] = own[here, :]
    for m, part in enumerate(received, 1):
        packed[(place - m + count) % count] = part[here, :]


def middle_kernel(
    levels,
    rows,
    field,
    zonal,
    meridional,
    along,
    own,
    below,
    above,
    tracers,
    senders_in,
    live_in,
    factor_in,
    offsets_in,
    sides_in,
    mixing_in,
    later,
    diffused,
    chosen,
    returning,
    forcing,
    gather,
    spread,
    slopes,
    held,
    senders,
    live,
    factor,
    offsets,
    sides,
    mixing,
    sems,
    load_sems,
):
    x_points = later.shape[0]

    @pl.when(in_air())
    def _():
        d = gll_matrix()
        lane = lax.broadcasted_iota(jnp.int32, (levels, field.shape[1]), 1)
        inner = pl.ds(rows, (x_points - 2) * rows)
        slopes[inner, :] = jnp.dot(
            field[inner, :], along[...], precision=HIGHEST, preferred_element_type=jnp.float32
        )
        copies = []
        for f in range(rows // levels):
            at = f * levels
            here = pl.ds(at, levels)
            values = {
                0: 0.5 * (own[0, here, :] + below[here, :].astype(jnp.float32)),
                x_points - 1: 0.5 * (own[1, here, :] + above[here, :].astype(jnp.float32)),
            }
            q = [field[pl.ds(x * rows + at, levels), :] for x in range(x_points)]
            for x in range(1, x_points - 1):
                start = x - x % NODES
                along_x = sum(
                    float(d[x % NODES, a]) * q[start + a]
                    for a in range(NODES)
                    if d[x % NODES, a] != 0
                )
                u = zonal[pl.ds(x * levels, levels), :]
                v = meridional[pl.ds(x * levels, levels), :]
                value = -(u * along_x + v * slopes[pl.ds(x * rows + at, levels), :])
                values[x] = smooth_lines(value, lane)
            for x in range(NODES - 1, x_points - 1, NODES):
                values[x] = values[x + 1] = 0.5 * (values[x] + values[x + 1])
            for x in range(x_points):
                held[x, here, :] = q[x] + STEP_ATMOS * values[x]
            copy = pltpu.make_async_copy(held.at[:, here, :], later.at[:, here, :], sems.at[f])
            copy.start()
            copies.append(copy)
        for copy in copies:
            copy.wait()

    @pl.when(jnp.logical_not(in_air()))
    def _():
        loads = start_all(
            (
                (senders_in, senders),
                (live_in, live),
                (factor_in, factor),
                (offsets_in, offsets),
                (sides_in, sides),
                (mixing_in, mixing),
            ),
            load_sems,
        )
        held[0] = jnp.zeros(held.shape[1:], jnp.float32)
        copies = start_all([(held.at[0], later.at[x]) for x in range(x_points)], sems)
        cells = sides.shape[1]
        x_count = gather.shape[0] // cells
        point = lax.broadcasted_iota(jnp.int32, gather.shape, 0) // x_count
        cell = lax.broadcasted_iota(jnp.int32, gather.shape, 1)
        gather[...] = jnp.where(point == cell, 1.0, 0.0).astype(gather.dtype)
        cell = lax.broadcasted_iota(jnp.int32, spread.shape, 0)
        point = lax.broadcasted_iota(jnp.int32, spread.shape, 1) // x_count
        spread[...] = jnp.where(point == cell, 1.0, 0.0).astype(spread.dtype)
        for load in loads:
            load.wait()

        source = lax.broadcasted_iota(jnp.int32, (cells, cells), 0)
        target = lax.broadcasted_iota(jnp.int32, (cells, cells), 1)
        inside = jnp.zeros((cells, cells), jnp.float32)
        outside = jnp.zeros((cells, cells), jnp.float32)
        total = jnp.zeros((1, cells), jnp.float32)
        for e in range(offsets.shape[0]):
            weight = jnp.where(e < sides[...], mixing[e], 0.0)
            place = target[:1] + offsets[e]
            total = total + weight
            inside = inside + jnp.where(source == place, weight, 0.0)
            hit = (source == place - cells) | (source == place + cells)
            outside = outside + jnp.where(hit, weight, 0.0)
        inside = inside - jnp.where(source == target, total, 0.0)

        value = tracers[...]
        height = value.shape[0]
        cell = lax.broadcasted_iota(jnp.int32, value.shape, 1)
        beside = [
            h[pl.ds(0, height), :].astype(jnp.float32)
            + h[pl.ds(height, height), :].astype(jnp.float32)
            for h in (below, above)
        ]
        outer = jnp.where(cell < cells // 2, beside[1], beside[0])
        change = jnp.dot(
            jnp.concatenate([value, outer], axis=1),
            jnp.concatenate([inside, outside], axis=0),
            precision=HIGHEST,
            preferred_element_type=jnp.float32,
        )
        diffused[...] = value + DIFFUSIVITY * change

        sections = lax.axis_size("sec")
        oceans = sections // 4
        air = sections - oceans
        ocean = jnp.maximum(lax.axis_index("sec") - air, 0)
        width = chosen.shape[1]
        count = live[0, ocean]
        for k in range(senders.shape[2]):
            place = jnp.where(k < count, senders[ocean, 0, k], sections)
            section = lax.broadcasted_iota(jnp.int32, (air, width), 0)
            chosen[pl.ds(k * air, air), :] = jnp.where(section == place, 1.0, 0.0)
            block = section % (air // oceans)
            owner = ((ocean + section // (air // oceans)) % oceans) ^ 1
            returning[pl.ds(k * air, air), :] = jnp.where(
                block * oceans + owner == place, 1.0, 0.0
            )
        tracer_count, flux_count = factor.shape
        depth = forcing.shape[0] // (tracer_count * flux_count)
        level = lax.broadcasted_iota(jnp.int32, (depth, width), 0).astype(jnp.float32)
        profile = STEP_OCEAN * jnp.exp(-0.5 * level)
        for n in range(flux_count):
            for t in range(tracer_count):
                forcing[pl.ds((n * tracer_count + t) * depth, depth), :] = factor[t, n] * profile
        for copy in copies:
            copy.wait()


def remap_kernel(
    regrid, gather, spread, chosen, returning, forcing, diffused, *refs
):
    arrived, renewed, shares = (refs[1], refs[0], refs[2]), refs[3], refs[4:]

    @pl.when(jnp.logical_not(in_air()))
    def _():
        points, cells = gather.shape
        x_count = points // cells
        slots = regrid.shape[0] // points
        air = chosen.shape[0] // slots
        packed = refs[0].shape[1]
        flux_count = packed // x_count
        row = lax.broadcasted_iota(jnp.int32, (x_count, cells), 0)
        column = lax.broadcasted_iota(jnp.int32, (x_count, cells), 1)
        same = jnp.where(row == column % x_count, 1.0, 0.0)

        blocks = [block[s].astype(jnp.float32) for block in arrived for s in range(block.shape[0])]
        matched = None
        for k in range(slots):
            part = chosen[pl.ds(k * air, 1), :] * blocks[0]
            for s in range(1, air):
                part = part + chosen[pl.ds(k * air + s, 1), :] * blocks[s]
            product = lax.dot_general(
                part.astype(jnp.bfloat16),
                regrid[pl.ds(k * points, points), :],
                (((1,), (1,)), ((), ())),
                preferred_element_type=jnp.float32,
            )
            matched = product if matched is None else matched + product
        matched = matched * jnp.tile(same, (flux_count, x_count))
        high = matched.astype(jnp.bfloat16)
        low = (matched - high.astype(jnp.float32)).astype(jnp.bfloat16)
        summed = jnp.dot(
            jnp.concatenate([high, low], axis=0), gather[...], preferred_element_type=jnp.float32
        )
        ocean_flux = (summed[:packed] + summed[packed:]).reshape(flux_count, x_count, cells).sum(axis=1)
        height = diffused.shape[0]
        value = diffused[...]
        for n in range(flux_count):
            value = value + forcing[pl.ds(n * height, height), :] * ocean_flux[n : n + 1]
        renewed[...] = value

        top = jnp.broadcast_to(value[0:1], (x_count, cells)).astype(jnp.bfloat16)
        wide = jnp.dot(top, spread[...], preferred_element_type=jnp.float32)
        wide = (wide * jnp.tile(same, (1, x_count))).astype(jnp.bfloat16)
        back = [
            jnp.dot(wide, regrid[pl.ds(k * points, points), :], preferred_element_type=jnp.float32)
            for k in range(slots)
        ]
        count = shares[0].shape[0]
        for m, share in enumerate(shares):
            for j in range(count):
                at = m * count + j
                total = returning[pl.ds(at, 1), :] * back[0]
                for k in range(1, slots):
                    total = total + returning[pl.ds(k * air + at, 1), :] * back[k]
                share[j] = total


def add_kernel(*refs):
    count = refs[0].shape[0]
    shares, totals = refs[:-count], refs[-count:]

    @pl.when(jnp.logical_not(in_air()))
    def _():
        for j, total in enumerate(totals):
            value = shares[0][j]
            for share in shares[1:]:
                value = value + share[j]
            total[...] = value


def last_kernel(renewed, *refs):
    returned, (tracers_later, warmth) = refs[:-2], refs[-2:]
    sections = lax.axis_size("sec")
    block = lax.axis_index("sec") // (sections // 4)

    @pl.when(in_air())
    def _():
        tracers_later[...] = jnp.zeros(tracers_later.shape, jnp.float32)

    @pl.when(jnp.logical_not(in_air()))
    def _():
        tracers_later[...] = renewed[...]
        warmth[...] = jnp.zeros(warmth.shape, jnp.float32)

    for j, part in enumerate(returned):

        @pl.when(block == j)
        def _(part=part):
            warmth[...] = part[...]


def per_device(
    climate_field_table,
    zonal_wind_speed,
    meridional_wind,
    sea_warmth_field,
    exchange_law_factor,
    regrid_matrix_stack,
    entry_sender_patch,
    holder_live_total,
    marine_salinity_heat,
    adjacent_offset_lists,
    polygon_side_total,
    interface_mixing_factor,
    solute_forcing_factor,
):
    sections = lax.axis_size("sec")
    ranks = lax.axis_size("rank")
    oceans = sections // 4
    air = sections - oceans
    _, x_points, rows, y_points = climate_field_table.shape
    levels = zonal_wind_speed.shape[2]
    flux_count = exchange_law_factor.shape[0]
    _, tracer_count, depth, cells = marine_salinity_heat.shape
    slots = regrid_matrix_stack.shape[2]
    f32, bf16 = jnp.float32, jnp.bfloat16
    shape = jax.ShapeDtypeStruct

    field = climate_field_table.reshape(x_points * rows, y_points)
    zonal = zonal_wind_speed.reshape(x_points * levels, y_points)
    meridional = meridional_wind.reshape(x_points * levels, y_points)
    regrid = regrid_matrix_stack.reshape(slots * cells * x_points, y_points)
    tracers = marine_salinity_heat.reshape(tracer_count * depth, cells)
    offsets = jnp.transpose(adjacent_offset_lists, (1, 0, 2))
    mixing = jnp.transpose(interface_mixing_factor, (1, 0, 2))
    live = jnp.transpose(holder_live_total, (1, 0))

    along = np.kron(np.eye(y_points // NODES, dtype=np.float32), gll_matrix().T)
    along = jnp.asarray(along)

    fields = rows // levels
    tile = min(8, levels)
    in_place = (
        exchange_law_factor,
        climate_field_table.reshape(x_points, fields, levels, y_points),
        zonal_wind_speed[0],
        meridional_wind[0],
        sea_warmth_field,
    )
    swap_rows = max(flux_count * x_points, rows + 16)
    fluxes = pl.pallas_call(
        functools.partial(flux_kernel, levels),
        out_shape=shape((swap_rows, y_points), bf16),
        in_specs=[HBM] * len(in_place),
        out_specs=VMEM,
        scratch_shapes=[
            pltpu.SMEM(exchange_law_factor.shape, f32),
            pltpu.VMEM((x_points, fields, tile, y_points), f32),
            pltpu.VMEM((x_points, tile, y_points), f32),
            pltpu.VMEM((x_points, tile, y_points), f32),
            pltpu.VMEM((1, x_points, y_points), f32),
            pltpu.SemaphoreType.DMA((len(in_place),)),
        ],
        compiler_params=PARAMS,
        cost_estimate=cost(1),
        name="flux",
    )(*(pltpu.with_memory_space_constraint(a, pltpu.HBM) for a in in_place))
    first, last, own = pl.pallas_call(
        functools.partial(edge_kernel, levels, rows),
        out_shape=(
            shape((rows, y_points), bf16),
            shape((rows, y_points), bf16),
            shape((2, rows, y_points), f32),
        ),
        in_specs=[VMEM] * 5 + [ANY],
        out_specs=(VMEM,) * 3,
        compiler_params=PARAMS,
        cost_estimate=cost(1),
        name="edges",
    )(field, zonal, meridional, along, tracers, fluxes)
    up = [(i, (i + 1) % ranks) for i in range(ranks)]
    below = lax.ppermute(last, "rank", up)
    above = lax.ppermute(first, "rank", [(j, i) for i, j in up])

    def turned(value, m):
        pairs = [(s, s // oceans * oceans + (s + m) % oceans) for s in range(sections)]
        return lax.ppermute(value, "sec", pairs)

    def paired(value, mask):
        pairs = [
            (s, (s // oceans ^ mask) * oceans + (s % oceans ^ 1)) for s in range(sections)
        ]
        return lax.ppermute(value, "sec", pairs)

    received = [turned(fluxes, m) for m in range(1, oceans)]
    packed = pl.pallas_call(
        pack_kernel,
        out_shape=shape((oceans, flux_count * x_points, y_points), bf16),
        in_specs=[VMEM] * oceans,
        out_specs=VMEM,
        compiler_params=PARAMS,
        cost_estimate=cost(0.2),
        name="pack",
    )(fluxes, *received)
    arrived = [paired(packed, 3 ^ block) for block in range(3)]

    from_memory = (
        entry_sender_patch,
        live,
        solute_forcing_factor,
        offsets,
        polygon_side_total,
        mixing,
    )
    later, diffused, chosen, returning, forcing, gather, spread = pl.pallas_call(
        functools.partial(middle_kernel, levels, rows),
        out_shape=(
            shape((x_points, rows, y_points), f32),
            shape(tracers.shape, f32),
            shape((slots * air, y_points), f32),
            shape((slots * air, y_points), f32),
            shape((flux_count * tracer_count * depth, cells), f32),
            shape((x_points * cells, cells), bf16),
            shape((cells, x_points * cells), bf16),
        ),
        in_specs=[VMEM] * 8 + [HBM] * 6,
        out_specs=(HBM,) + (VMEM,) * 6,
        scratch_shapes=[
            pltpu.VMEM(field.shape, f32),
            pltpu.VMEM((x_points, rows, y_points), f32),
        ]
        + [
            (pltpu.SMEM if i < 3 else pltpu.VMEM)(a.shape, a.dtype)
            for i, a in enumerate(from_memory)
        ]
        + [
            pltpu.SemaphoreType.DMA((max(fields, x_points),)),
            pltpu.SemaphoreType.DMA((len(from_memory),)),
        ],
        compiler_params=PARAMS,
        cost_estimate=cost(1),
        name="middle",
    )(
        field,
        zonal,
        meridional,
        along,
        own,
        below,
        above,
        tracers,
        *(pltpu.with_memory_space_constraint(a, pltpu.HBM) for a in from_memory),
    )

    renewed, *shares = pl.pallas_call(
        remap_kernel,
        out_shape=(shape(tracers.shape, f32),)
        + (shape((air // oceans, x_points, y_points), f32),) * oceans,
        in_specs=[VMEM] * 10,
        out_specs=(VMEM,) * (1 + oceans),
        compiler_params=PARAMS,
        cost_estimate=cost(1),
        name="remap",
    )(regrid, gather, spread, chosen, returning, forcing, diffused, arrived[1], arrived[0], arrived[2])
    shares = shares[:1] + [turned(share, m) for m, share in enumerate(shares[1:], 1)]
    totals = pl.pallas_call(
        add_kernel,
        out_shape=(shape((x_points, y_points), f32),) * (air // oceans),
        in_specs=[VMEM] * oceans,
        out_specs=(VMEM,) * (air // oceans),
        compiler_params=PARAMS,
        cost_estimate=cost(0.3),
        name="add",
    )(*shares)
    returned = [paired(total, 3 ^ block) for block, total in enumerate(totals)]
    tracers_later, warmth = pl.pallas_call(
        last_kernel,
        out_shape=(shape(tracers.shape, f32), shape((x_points, y_points), f32)),
        in_specs=[VMEM] * (1 + len(returned)),
        out_specs=(VMEM,) * 2,
        compiler_params=PARAMS,
        cost_estimate=cost(0.5),
        name="last",
    )(renewed, *returned)
    return (
        later.reshape(climate_field_table.shape),
        tracers_later.reshape(marine_salinity_heat.shape),
        warmth[None],
    )


def solution(mesh):
    return jax.shard_map(
        per_device,
        mesh=mesh,
        in_specs=(
            P("sec", "rank", None, None),
            P("sec", "rank", None, None),
            P("sec", "rank", None, None),
            P("sec", "rank", None),
            P(),
            P("sec", "rank", None, None, None, None),
            P(None, "rank", None),
            P(None, "rank"),
            P("sec", None, None, "rank"),
            P("sec", None, "rank"),
            P("sec", "rank"),
            P("sec", None, "rank"),
            P(),
        ),
        out_specs=(
            P("sec", "rank", None, None),
            P("sec", None, None, "rank"),
            P("sec", "rank", None),
        ),
        check_vma=False,
    )
```

```python
import functools

import jax
import jax.numpy as jnp
import numpy as np
from jax import lax
from jax.experimental import pallas as pl
from jax.experimental.pallas import tpu as pltpu
from jax.sharding import PartitionSpec as P

STEP_ATMOS = 0.05
DIFFUSIVITY = 0.05
STEP_OCEAN = 0.5
NODES = 4

VMEM = pl.BlockSpec(memory_space=pltpu.VMEM)
ANY = pl.BlockSpec(memory_space=pl.ANY)
HBM = pl.BlockSpec(memory_space=pltpu.HBM)
SMEM = pl.BlockSpec(memory_space=pltpu.SMEM)
PARAMS = pltpu.CompilerParams(vmem_limit_bytes=8 * 2**20)
HIGHEST = lax.Precision.HIGHEST


def gll_matrix():
    nodes = np.array([-1.0, -1.0 / np.sqrt(5.0), 1.0 / np.sqrt(5.0), 1.0])
    legendre = (5.0 * nodes**3 - 3.0 * nodes) / 2.0
    matrix = np.zeros((4, 4))
    for i in range(4):
        for j in range(4):
            if i != j:
                matrix[i, j] = legendre[i] / (legendre[j] * (nodes[i] - nodes[j]))
    matrix[0, 0] = -3.0
    matrix[3, 3] = 3.0
    return matrix.astype(np.float32)


def cost(microseconds):
    return pl.CostEstimate(
        flops=0, bytes_accessed=int(microseconds * 3_000_000), transcendentals=0
    )


def in_air():
    sections = lax.axis_size("sec")
    return lax.axis_index("sec") < sections - sections // 4


def smooth_lines(value, lane):
    width = value.shape[-1]
    right = pltpu.roll(value, width - 1, value.ndim - 1)
    left = pltpu.roll(value, 1, value.ndim - 1)
    at_end = (lane % NODES == NODES - 1) & (lane < width - 1)
    at_start = (lane % NODES == 0) & (lane > 0)
    partner = jnp.where(at_end, right, jnp.where(at_start, left, value))
    return 0.5 * (value + partner)


def halves(value):
    high = value.astype(jnp.bfloat16)
    return high, (value - high.astype(jnp.float32)).astype(jnp.bfloat16)


def split_product(left, right):
    (high, low), (right_high, right_low) = halves(left), halves(right)
    return (
        jnp.dot(high, right_high, preferred_element_type=jnp.float32)
        + jnp.dot(low, right_high, preferred_element_type=jnp.float32)
        + jnp.dot(high, right_low, preferred_element_type=jnp.float32)
    )


def start_all(pairs, sems):
    copies = [
        pltpu.make_async_copy(source, target, sems.at[i])
        for i, (source, target) in enumerate(pairs)
    ]
    for copy in copies:
        copy.start()
    return copies


def flux_kernel(
    levels, law_in, field_in, zonal_in, meridional_in, sea_in, sent, law, field, zonal, meridional, sea, sems
):
    @pl.when(in_air())
    def _():
        x_points, fields, tile, y_points = field.shape
        lowest = pl.ds(0, tile)
        copies = start_all(
            (
                (law_in, law),
                (field_in.at[:, :, lowest, :], field),
                (zonal_in.at[:, lowest, :], zonal),
                (meridional_in.at[:, lowest, :], meridional),
                (sea_in, sea),
            ),
            sems,
        )
        for copy in copies:
            copy.wait()
        flux_count, columns = law.shape
        flat = field.reshape(x_points * fields * tile, y_points)
        ground = [
            flat[pl.ds(f * tile, x_points, stride=fields * tile), :] for f in range(fields)
        ] + [sea[0]]
        u = zonal.reshape(x_points * tile, y_points)[pl.ds(0, x_points, stride=tile), :]
        v = meridional.reshape(x_points * tile, y_points)[pl.ds(0, x_points, stride=tile), :]
        speed = jnp.sqrt(1.0 + u * u + v * v)
        parts = []
        for n in range(flux_count):
            total = law[n, 0] * ground[0]
            for f in range(1, columns):
                total = total + law[n, f] * ground[f]
            parts.append(speed * total)
        block = jnp.concatenate(parts, axis=0).astype(jnp.bfloat16)
        sent[pl.ds(0, block.shape[0]), :] = block


def edge_kernel(levels, rows, field, zonal, meridional, along, tracers, after, first, last, own):
    x_points = field.shape[0] // rows

    @pl.when(in_air())
    def _():
        d = gll_matrix()
        lane = lax.broadcasted_iota(jnp.int32, (levels, field.shape[1]), 1)
        for side, (x, target) in enumerate(((0, first), (x_points - 1, last))):
            start = x - x % NODES
            along_y = split_product(field[pl.ds(x * rows, rows), :], along[...])
            u = zonal[pl.ds(x * levels, levels), :]
            v = meridional[pl.ds(x * levels, levels), :]
            for f in range(rows // levels):
                at = f * levels
                along_x = sum(
                    float(d[x % NODES, a]) * field[pl.ds((start + a) * rows + at, levels), :]
                    for a in range(NODES)
                    if d[x % NODES, a] != 0
                )
                value = -(u * along_x + v * along_y[at : at + levels])
                value = smooth_lines(value, lane)
                own[side, pl.ds(at, levels), :] = value
                target[pl.ds(at, levels), :] = value.astype(jnp.bfloat16)

    @pl.when(jnp.logical_not(in_air()))
    def _():
        value = tracers[...]
        high = value.astype(jnp.bfloat16)
        low = (value - high.astype(jnp.float32)).astype(jnp.bfloat16)
        both = jnp.concatenate([high, low], axis=0)
        for target in (first, last):
            target[pl.ds(0, both.shape[0]), :] = both


def pack_kernel(own, *refs):
    received, packed = refs[:-1], refs[-1]
    count = len(refs)
    place = lax.axis_index("sec") % count
    here = pl.ds(0, packed.shape[1])
    packed[place] = own[here, :]
    for m, part in enumerate(received, 1):
        packed[(place - m + count) % count] = part[here, :]


def middle_kernel(
    levels,
    rows,
    field,
    zonal,
    meridional,
    along,
    own,
    below,
    above,
    tracers,
    senders_in,
    live_in,
    factor_in,
    offsets_in,
    sides_in,
    mixing_in,
    later,
    diffused,
    chosen,
    returning,
    forcing,
    gather,
    ring,
    top_wide,
    slopes,
    held,
    senders,
    live,
    factor,
    offsets,
    sides,
    mixing,
    sems,
    load_sems,
):
    x_points = later.shape[0]

    @pl.when(in_air())
    def _():
        d = gll_matrix()
        lane = lax.broadcasted_iota(jnp.int32, (levels, field.shape[1]), 1)
        inner = pl.ds(rows, (x_points - 2) * rows)
        slopes[inner, :] = jnp.dot(
            field[inner, :], along[...], precision=HIGHEST, preferred_element_type=jnp.float32
        )
        copies = []
        for f in range(rows // levels):
            at = f * levels
            here = pl.ds(at, levels)
            values = {
                0: 0.5 * (own[0, here, :] + below[here, :].astype(jnp.float32)),
                x_points - 1: 0.5 * (own[1, here, :] + above[here, :].astype(jnp.float32)),
            }
            q = [field[pl.ds(x * rows + at, levels), :] for x in range(x_points)]
            for x in range(1, x_points - 1):
                start = x - x % NODES
                along_x = sum(
                    float(d[x % NODES, a]) * q[start + a]
                    for a in range(NODES)
                    if d[x % NODES, a] != 0
                )
                u = zonal[pl.ds(x * levels, levels), :]
                v = meridional[pl.ds(x * levels, levels), :]
                value = -(u * along_x + v * slopes[pl.ds(x * rows + at, levels), :])
                values[x] = smooth_lines(value, lane)
            for x in range(NODES - 1, x_points - 1, NODES):
                values[x] = values[x + 1] = 0.5 * (values[x] + values[x + 1])
            for x in range(x_points):
                held[x, here, :] = q[x] + STEP_ATMOS * values[x]
            copy = pltpu.make_async_copy(held.at[:, here, :], later.at[:, here, :], sems.at[f])
            copy.start()
            copies.append(copy)
        for copy in copies:
            copy.wait()

    @pl.when(jnp.logical_not(in_air()))
    def _():
        loads = start_all(
            (
                (senders_in, senders),
                (live_in, live),
                (factor_in, factor),
                (offsets_in, offsets),
                (sides_in, sides),
                (mixing_in, mixing),
            ),
            load_sems,
        )
        held[0] = jnp.zeros(held.shape[1:], jnp.float32)
        copies = start_all([(held.at[0], later.at[x]) for x in range(x_points)], sems)
        cells = sides.shape[1]
        x_count = gather.shape[0] // cells
        point = lax.broadcasted_iota(jnp.int32, gather.shape, 0) // x_count
        cell = lax.broadcasted_iota(jnp.int32, gather.shape, 1)
        gather[...] = jnp.where(point == cell, 1.0, 0.0).astype(gather.dtype)
        row = lax.broadcasted_iota(jnp.int32, ring.shape, 0) // x_count
        column = lax.broadcasted_iota(jnp.int32, ring.shape, 1) // x_count
        ring[...] = jnp.where(row == column, 1.0, 0.0).astype(ring.dtype)
        for load in loads:
            load.wait()

        source = lax.broadcasted_iota(jnp.int32, (cells, cells), 0)
        target = lax.broadcasted_iota(jnp.int32, (cells, cells), 1)
        inside = jnp.zeros((cells, cells), jnp.float32)
        outside = jnp.zeros((cells, cells), jnp.float32)
        total = jnp.zeros((1, cells), jnp.float32)
        for e in range(offsets.shape[0]):
            weight = jnp.where(e < sides[...], mixing[e], 0.0)
            place = target[:1] + offsets[e]
            total = total + weight
            inside = inside + jnp.where(source == place, weight, 0.0)
            hit = (source == place - cells) | (source == place + cells)
            outside = outside + jnp.where(hit, weight, 0.0)
        inside = inside - jnp.where(source == target, total, 0.0)

        value = tracers[...]
        height = value.shape[0]
        cell = lax.broadcasted_iota(jnp.int32, value.shape, 1)
        beside = [
            h[pl.ds(0, height), :].astype(jnp.float32)
            + h[pl.ds(height, height), :].astype(jnp.float32)
            for h in (below, above)
        ]
        outer = jnp.where(cell < cells // 2, beside[1], beside[0])
        change = jnp.dot(
            jnp.concatenate([value, outer], axis=1),
            jnp.concatenate([inside, outside], axis=0),
            precision=HIGHEST,
            preferred_element_type=jnp.float32,
        )
        step = value + DIFFUSIVITY * change
        diffused[...] = step
        cell = lax.broadcasted_iota(jnp.int32, (cells, gather.shape[0]), 0)
        point = lax.broadcasted_iota(jnp.int32, (cells, gather.shape[0]), 1) // x_count
        wide = jnp.dot(
            jnp.broadcast_to(step[0:1], (x_count, cells)),
            jnp.where(point == cell, 1.0, 0.0),
            precision=HIGHEST,
            preferred_element_type=jnp.float32,
        )
        for b in range(x_count):
            top_wide[pl.ds(b, 1), :] = wide[0:1, b * cells : (b + 1) * cells]

        sections = lax.axis_size("sec")
        oceans = sections // 4
        air = sections - oceans
        ocean = jnp.maximum(lax.axis_index("sec") - air, 0)
        width = chosen.shape[1]
        count = live[0, ocean]
        for k in range(senders.shape[2]):
            place = jnp.where(k < count, senders[ocean, 0, k], sections)
            section = lax.broadcasted_iota(jnp.int32, (air, width), 0)
            chosen[pl.ds(k * air, air), :] = jnp.where(section == place, 1.0, 0.0)
            block = section % (air // oceans)
            owner = ((ocean + section // (air // oceans)) % oceans) ^ 1
            returning[pl.ds(k * air, air), :] = jnp.where(
                block * oceans + owner == place, 1.0, 0.0
            )
        tracer_count, flux_count = factor.shape
        depth = forcing.shape[0] // (tracer_count * flux_count)
        level = lax.broadcasted_iota(jnp.int32, (depth, width), 0).astype(jnp.float32)
        profile = STEP_OCEAN * jnp.exp(-0.5 * level)
        for n in range(flux_count):
            for t in range(tracer_count):
                forcing[pl.ds((n * tracer_count + t) * depth, depth), :] = factor[t, n] * profile
        for copy in copies:
            copy.wait()


def remap_kernel(regrid, ring, chosen, returning, forcing, top_wide, *refs):
    arrived, summed, shares = (refs[2], refs[0], refs[1]), refs[3], refs[4:]

    @pl.when(jnp.logical_not(in_air()))
    def _():
        flux_count, points = summed.shape
        x_count, cells = top_wide.shape
        slots = regrid.shape[0] // points
        air = chosen.shape[0] // slots
        row = lax.broadcasted_iota(jnp.int32, (x_count, cells), 0)
        column = lax.broadcasted_iota(jnp.int32, (x_count, cells), 1)
        same = jnp.where(row == column % x_count, 1.0, 0.0)

        blocks = [block[s].astype(jnp.float32) for block in arrived for s in range(block.shape[0])]
        matched = None
        for k in range(slots):
            part = chosen[pl.ds(k * air, 1), :] * blocks[0]
            for s in range(1, air):
                part = part + chosen[pl.ds(k * air + s, 1), :] * blocks[s]
            product = lax.dot_general(
                part.astype(jnp.bfloat16),
                regrid[pl.ds(k * points, points), :],
                (((1,), (1,)), ((), ())),
                preferred_element_type=jnp.float32,
            )
            matched = product if matched is None else matched + product
        matched = matched * jnp.tile(same, (flux_count, x_count))
        sums = matched.reshape(flux_count, x_count, points).sum(axis=1)
        summed[...] = sums
        pieces = jnp.concatenate(
            [sums[:, b * cells : (b + 1) * cells] for b in range(x_count)], axis=0
        )
        both = jnp.dot(
            jnp.concatenate(halves(pieces), axis=0), ring[...], preferred_element_type=jnp.float32
        )
        fluxes = both[: flux_count * x_count] + both[flux_count * x_count :]
        height = forcing.shape[0] // flux_count
        wide = []
        for b in range(x_count):
            top = top_wide[pl.ds(b, 1), :]
            for n in range(flux_count):
                at = b * flux_count + n
                top = top + forcing[pl.ds(n * height, 1), :] * fluxes[at : at + 1]
            top = top.astype(jnp.bfloat16).astype(jnp.float32)
            wide.append((top * same).astype(jnp.bfloat16))
        wide = jnp.concatenate(wide, axis=1)
        back = [
            jnp.dot(wide, regrid[pl.ds(k * points, points), :], preferred_element_type=jnp.float32)
            for k in range(slots)
        ]
        count = shares[0].shape[0]
        for m, share in enumerate(shares):
            for j in range(count):
                at = m * count + j
                total = returning[pl.ds(at, 1), :] * back[0]
                for k in range(1, slots):
                    total = total + returning[pl.ds(k * air + at, 1), :] * back[k]
                share[j] = total


def add_kernel(*refs):
    count = refs[0].shape[0]
    shares, totals = refs[:-count], refs[-count:]

    @pl.when(jnp.logical_not(in_air()))
    def _():
        for j, total in enumerate(totals):
            value = shares[0][j]
            for share in shares[1:]:
                value = value + share[j]
            total[...] = value


def last_kernel(summed, gather, forcing, diffused, *refs):
    returned, (tracers_later, warmth) = refs[:-2], refs[-2:]
    sections = lax.axis_size("sec")
    block = lax.axis_index("sec") // (sections // 4)

    @pl.when(in_air())
    def _():
        tracers_later[...] = jnp.zeros(tracers_later.shape, jnp.float32)

    @pl.when(jnp.logical_not(in_air()))
    def _():
        flux_count = summed.shape[0]
        both = jnp.dot(
            jnp.concatenate(halves(summed[...]), axis=0),
            gather[...],
            preferred_element_type=jnp.float32,
        )
        height = diffused.shape[0]
        value = diffused[...]
        for n in range(flux_count):
            flux = both[n : n + 1] + both[flux_count + n : flux_count + n + 1]
            value = value + forcing[pl.ds(n * height, height), :] * flux
        tracers_later[...] = value
        warmth[...] = jnp.zeros(warmth.shape, jnp.float32)

    for j, part in enumerate(returned):

        @pl.when(block == j)
        def _(part=part):
            warmth[...] = part[...]


def per_device(
    climate_field_table,
    zonal_wind_speed,
    meridional_wind,
    sea_warmth_field,
    exchange_law_factor,
    regrid_matrix_stack,
    entry_sender_patch,
    holder_live_total,
    marine_salinity_heat,
    adjacent_offset_lists,
    polygon_side_total,
    interface_mixing_factor,
    solute_forcing_factor,
):
    sections = lax.axis_size("sec")
    ranks = lax.axis_size("rank")
    oceans = sections // 4
    air = sections - oceans
    _, x_points, rows, y_points = climate_field_table.shape
    levels = zonal_wind_speed.shape[2]
    flux_count = exchange_law_factor.shape[0]
    _, tracer_count, depth, cells = marine_salinity_heat.shape
    slots = regrid_matrix_stack.shape[2]
    f32, bf16 = jnp.float32, jnp.bfloat16
    shape = jax.ShapeDtypeStruct

    field = climate_field_table.reshape(x_points * rows, y_points)
    zonal = zonal_wind_speed.reshape(x_points * levels, y_points)
    meridional = meridional_wind.reshape(x_points * levels, y_points)
    regrid = regrid_matrix_stack.reshape(slots * cells * x_points, y_points)
    tracers = marine_salinity_heat.reshape(tracer_count * depth, cells)
    offsets = jnp.transpose(adjacent_offset_lists, (1, 0, 2))
    mixing = jnp.transpose(interface_mixing_factor, (1, 0, 2))
    live = jnp.transpose(holder_live_total, (1, 0))

    along = np.kron(np.eye(y_points // NODES, dtype=np.float32), gll_matrix().T)
    along = jnp.asarray(along)

    fields = rows // levels
    tile = min(8, levels)
    in_place = (
        exchange_law_factor,
        climate_field_table.reshape(x_points, fields, levels, y_points),
        zonal_wind_speed[0],
        meridional_wind[0],
        sea_warmth_field,
    )
    swap_rows = max(flux_count * x_points, rows + 16)
    fluxes = pl.pallas_call(
        functools.partial(flux_kernel, levels),
        out_shape=shape((swap_rows, y_points), bf16),
        in_specs=[HBM] * len(in_place),
        out_specs=VMEM,
        scratch_shapes=[
            pltpu.SMEM(exchange_law_factor.shape, f32),
            pltpu.VMEM((x_points, fields, tile, y_points), f32),
            pltpu.VMEM((x_points, tile, y_points), f32),
            pltpu.VMEM((x_points, tile, y_points), f32),
            pltpu.VMEM((1, x_points, y_points), f32),
            pltpu.SemaphoreType.DMA((len(in_place),)),
        ],
        compiler_params=PARAMS,
        cost_estimate=cost(1),
        name="flux",
    )(*(pltpu.with_memory_space_constraint(a, pltpu.HBM) for a in in_place))
    first, last, own = pl.pallas_call(
        functools.partial(edge_kernel, levels, rows),
        out_shape=(
            shape((rows, y_points), bf16),
            shape((rows, y_points), bf16),
            shape((2, rows, y_points), f32),
        ),
        in_specs=[VMEM] * 5 + [ANY],
        out_specs=(VMEM,) * 3,
        compiler_params=PARAMS,
        cost_estimate=cost(1),
        name="edges",
    )(field, zonal, meridional, along, tracers, fluxes)
    up = [(i, (i + 1) % ranks) for i in range(ranks)]
    below = lax.ppermute(last, "rank", up)
    above = lax.ppermute(first, "rank", [(j, i) for i, j in up])

    def turned(value, m):
        pairs = [(s, s // oceans * oceans + (s + m) % oceans) for s in range(sections)]
        return lax.ppermute(value, "sec", pairs)

    def paired(value, mask):
        pairs = [
            (s, (s // oceans ^ mask) * oceans + (s % oceans ^ 1)) for s in range(sections)
        ]
        return lax.ppermute(value, "sec", pairs)

    received = [turned(fluxes, m) for m in range(1, oceans)]
    packed = pl.pallas_call(
        pack_kernel,
        out_shape=shape((oceans, flux_count * x_points, y_points), bf16),
        in_specs=[VMEM] * oceans,
        out_specs=VMEM,
        compiler_params=PARAMS,
        cost_estimate=cost(0.2),
        name="pack",
    )(fluxes, *received)
    arrived = [paired(packed, 3 ^ block) for block in range(3)]

    from_memory = (
        entry_sender_patch,
        live,
        solute_forcing_factor,
        offsets,
        polygon_side_total,
        mixing,
    )
    later, diffused, chosen, returning, forcing, gather, ring, top_wide = pl.pallas_call(
        functools.partial(middle_kernel, levels, rows),
        out_shape=(
            shape((x_points, rows, y_points), f32),
            shape(tracers.shape, f32),
            shape((slots * air, y_points), f32),
            shape((slots * air, y_points), f32),
            shape((flux_count * tracer_count * depth, cells), f32),
            shape((x_points * cells, cells), bf16),
            shape((cells, cells), bf16),
            shape((x_points, cells), f32),
        ),
        in_specs=[VMEM] * 8 + [HBM] * 6,
        out_specs=(HBM,) + (VMEM,) * 7,
        scratch_shapes=[
            pltpu.VMEM(field.shape, f32),
            pltpu.VMEM((x_points, rows, y_points), f32),
        ]
        + [
            (pltpu.SMEM if i < 3 else pltpu.VMEM)(a.shape, a.dtype)
            for i, a in enumerate(from_memory)
        ]
        + [
            pltpu.SemaphoreType.DMA((max(fields, x_points),)),
            pltpu.SemaphoreType.DMA((len(from_memory),)),
        ],
        compiler_params=PARAMS,
        cost_estimate=cost(1),
        name="middle",
    )(
        field,
        zonal,
        meridional,
        along,
        own,
        below,
        above,
        tracers,
        *(pltpu.with_memory_space_constraint(a, pltpu.HBM) for a in from_memory),
    )

    summed, *shares = pl.pallas_call(
        remap_kernel,
        out_shape=(shape((flux_count, x_points * cells), f32),)
        + (shape((air // oceans, x_points, y_points), f32),) * oceans,
        in_specs=[VMEM] * 9,
        out_specs=(VMEM,) * (1 + oceans),
        compiler_params=PARAMS,
        cost_estimate=cost(1),
        name="remap",
    )(
        regrid,
        ring,
        chosen,
        returning,
        forcing,
        top_wide,
        arrived[1],
        arrived[2],
        arrived[0],
    )
    shares = shares[:1] + [turned(share, m) for m, share in enumerate(shares[1:], 1)]
    totals = pl.pallas_call(
        add_kernel,
        out_shape=(shape((x_points, y_points), f32),) * (air // oceans),
        in_specs=[VMEM] * oceans,
        out_specs=(VMEM,) * (air // oceans),
        compiler_params=PARAMS,
        cost_estimate=cost(0.3),
        name="add",
    )(*shares)
    returned = [paired(total, 3 ^ block) for block, total in enumerate(totals)]
    tracers_later, warmth = pl.pallas_call(
        last_kernel,
        out_shape=(shape(tracers.shape, f32), shape((x_points, y_points), f32)),
        in_specs=[VMEM] * (4 + len(returned)),
        out_specs=(VMEM,) * 2,
        compiler_params=PARAMS,
        cost_estimate=cost(0.5),
        name="last",
    )(summed, gather, forcing, diffused, *returned)
    return (
        later.reshape(climate_field_table.shape),
        tracers_later.reshape(marine_salinity_heat.shape),
        warmth[None],
    )


def solution(mesh):
    return jax.shard_map(
        per_device,
        mesh=mesh,
        in_specs=(
            P("sec", "rank", None, None),
            P("sec", "rank", None, None),
            P("sec", "rank", None, None),
            P("sec", "rank", None),
            P(),
            P("sec", "rank", None, None, None, None),
            P(None, "rank", None),
            P(None, "rank"),
            P("sec", None, None, "rank"),
            P("sec", None, "rank"),
            P("sec", "rank"),
            P("sec", None, "rank"),
            P(),
        ),
        out_specs=(
            P("sec", "rank", None, None),
            P("sec", None, None, "rank"),
            P("sec", "rank", None),
        ),
        check_vma=False,
    )
```

```python
import functools

import jax
import jax.numpy as jnp
import numpy as np
from jax import lax
from jax.experimental import pallas as pl
from jax.experimental.pallas import tpu as pltpu
from jax.sharding import PartitionSpec as P

STEP_ATMOS = 0.05
DIFFUSIVITY = 0.05
STEP_OCEAN = 0.5
NODES = 4

VMEM = pl.BlockSpec(memory_space=pltpu.VMEM)
ANY = pl.BlockSpec(memory_space=pl.ANY)
HBM = pl.BlockSpec(memory_space=pltpu.HBM)
SMEM = pl.BlockSpec(memory_space=pltpu.SMEM)
PARAMS = pltpu.CompilerParams(vmem_limit_bytes=8 * 2**20)
HIGHEST = lax.Precision.HIGHEST


def gll_matrix():
    nodes = np.array([-1.0, -1.0 / np.sqrt(5.0), 1.0 / np.sqrt(5.0), 1.0])
    legendre = (5.0 * nodes**3 - 3.0 * nodes) / 2.0
    matrix = np.zeros((4, 4))
    for i in range(4):
        for j in range(4):
            if i != j:
                matrix[i, j] = legendre[i] / (legendre[j] * (nodes[i] - nodes[j]))
    matrix[0, 0] = -3.0
    matrix[3, 3] = 3.0
    return matrix.astype(np.float32)


def cost(microseconds):
    return pl.CostEstimate(
        flops=0, bytes_accessed=int(microseconds * 3_000_000), transcendentals=0
    )


def in_air():
    sections = lax.axis_size("sec")
    return lax.axis_index("sec") < sections - sections // 4


def smooth_lines(value, lane):
    width = value.shape[-1]
    right = pltpu.roll(value, width - 1, value.ndim - 1)
    left = pltpu.roll(value, 1, value.ndim - 1)
    at_end = (lane % NODES == NODES - 1) & (lane < width - 1)
    at_start = (lane % NODES == 0) & (lane > 0)
    partner = jnp.where(at_end, right, jnp.where(at_start, left, value))
    return 0.5 * (value + partner)


def halves(value):
    high = value.astype(jnp.bfloat16)
    return high, (value - high.astype(jnp.float32)).astype(jnp.bfloat16)


def split_product(left, right):
    (high, low), (right_high, right_low) = halves(left), halves(right)
    return (
        jnp.dot(high, right_high, preferred_element_type=jnp.float32)
        + jnp.dot(low, right_high, preferred_element_type=jnp.float32)
        + jnp.dot(high, right_low, preferred_element_type=jnp.float32)
    )


def start_all(pairs, sems):
    copies = [
        pltpu.make_async_copy(source, target, sems.at[i])
        for i, (source, target) in enumerate(pairs)
    ]
    for copy in copies:
        copy.start()
    return copies


def flux_kernel(
    levels, law_in, field_in, zonal_in, meridional_in, sea_in, sent, law, field, zonal, meridional, sea, sems
):
    @pl.when(in_air())
    def _():
        x_points, fields, tile, y_points = field.shape
        lowest = pl.ds(0, tile)
        copies = start_all(
            (
                (law_in, law),
                (field_in.at[:, :, lowest, :], field),
                (zonal_in.at[:, lowest, :], zonal),
                (meridional_in.at[:, lowest, :], meridional),
                (sea_in, sea),
            ),
            sems,
        )
        for copy in copies:
            copy.wait()
        flux_count, columns = law.shape
        flat = field.reshape(x_points * fields * tile, y_points)
        ground = [
            flat[pl.ds(f * tile, x_points, stride=fields * tile), :] for f in range(fields)
        ] + [sea[0]]
        u = zonal.reshape(x_points * tile, y_points)[pl.ds(0, x_points, stride=tile), :]
        v = meridional.reshape(x_points * tile, y_points)[pl.ds(0, x_points, stride=tile), :]
        speed = jnp.sqrt(1.0 + u * u + v * v)
        parts = []
        for n in range(flux_count):
            total = law[n, 0] * ground[0]
            for f in range(1, columns):
                total = total + law[n, f] * ground[f]
            parts.append(speed * total)
        block = jnp.concatenate(parts, axis=0).astype(jnp.bfloat16)
        sent[pl.ds(0, block.shape[0]), :] = block


def edge_kernel(levels, rows, field, zonal, meridional, along, tracers, after, first, last, own):
    x_points = field.shape[0] // rows

    @pl.when(in_air())
    def _():
        d = gll_matrix()
        lane = lax.broadcasted_iota(jnp.int32, (levels, field.shape[1]), 1)
        for side, (x, target) in enumerate(((0, first), (x_points - 1, last))):
            start = x - x % NODES
            along_y = split_product(field[pl.ds(x * rows, rows), :], along[...])
            u = zonal[pl.ds(x * levels, levels), :]
            v = meridional[pl.ds(x * levels, levels), :]
            for f in range(rows // levels):
                at = f * levels
                along_x = sum(
                    float(d[x % NODES, a]) * field[pl.ds((start + a) * rows + at, levels), :]
                    for a in range(NODES)
                    if d[x % NODES, a] != 0
                )
                value = -(u * along_x + v * along_y[at : at + levels])
                value = smooth_lines(value, lane)
                own[side, pl.ds(at, levels), :] = value
                target[pl.ds(at, levels), :] = value.astype(jnp.bfloat16)

    @pl.when(jnp.logical_not(in_air()))
    def _():
        value = tracers[...]
        high = value.astype(jnp.bfloat16)
        low = (value - high.astype(jnp.float32)).astype(jnp.bfloat16)
        both = jnp.concatenate([high, low], axis=0)
        for target in (first, last):
            target[pl.ds(0, both.shape[0]), :] = both


def pack_kernel(own, *refs):
    received, packed = refs[:-1], refs[-1]
    count = len(refs)
    place = lax.axis_index("sec") % count
    here = pl.ds(0, packed.shape[1])
    packed[place] = own[here, :]
    for m, part in enumerate(received, 1):
        packed[(place - m + count) % count] = part[here, :]


def middle_kernel(
    levels,
    rows,
    field,
    zonal,
    meridional,
    along,
    own,
    below,
    above,
    tracers,
    senders_in,
    live_in,
    factor_in,
    offsets_in,
    sides_in,
    mixing_in,
    later,
    diffused,
    chosen,
    returning,
    forcing,
    gather,
    spread,
    slopes,
    held,
    senders,
    live,
    factor,
    offsets,
    sides,
    mixing,
    sems,
    load_sems,
):
    x_points = later.shape[0]

    @pl.when(in_air())
    def _():
        d = gll_matrix()
        lane = lax.broadcasted_iota(jnp.int32, (levels, field.shape[1]), 1)
        inner = pl.ds(rows, (x_points - 2) * rows)
        slopes[inner, :] = split_product(field[inner, :], along[...])
        copies = []
        for f in range(rows // levels):
            at = f * levels
            here = pl.ds(at, levels)
            values = {
                0: 0.5 * (own[0, here, :] + below[here, :].astype(jnp.float32)),
                x_points - 1: 0.5 * (own[1, here, :] + above[here, :].astype(jnp.float32)),
            }
            q = [field[pl.ds(x * rows + at, levels), :] for x in range(x_points)]
            for x in range(1, x_points - 1):
                start = x - x % NODES
                along_x = sum(
                    float(d[x % NODES, a]) * q[start + a]
                    for a in range(NODES)
                    if d[x % NODES, a] != 0
                )
                u = zonal[pl.ds(x * levels, levels), :]
                v = meridional[pl.ds(x * levels, levels), :]
                value = -(u * along_x + v * slopes[pl.ds(x * rows + at, levels), :])
                values[x] = smooth_lines(value, lane)
            for x in range(NODES - 1, x_points - 1, NODES):
                values[x] = values[x + 1] = 0.5 * (values[x] + values[x + 1])
            for x in range(x_points):
                held[x, here, :] = q[x] + STEP_ATMOS * values[x]
            copy = pltpu.make_async_copy(held.at[:, here, :], later.at[:, here, :], sems.at[f])
            copy.start()
            copies.append(copy)
        for copy in copies:
            copy.wait()

    @pl.when(jnp.logical_not(in_air()))
    def _():
        loads = start_all(
            (
                (senders_in, senders),
                (live_in, live),
                (factor_in, factor),
                (offsets_in, offsets),
                (sides_in, sides),
                (mixing_in, mixing),
            ),
            load_sems,
        )
        held[0] = jnp.zeros(held.shape[1:], jnp.float32)
        copies = start_all([(held.at[0], later.at[x]) for x in range(x_points)], sems)
        cells = sides.shape[1]
        x_count = gather.shape[0] // cells
        point = lax.broadcasted_iota(jnp.int32, gather.shape, 0) // x_count
        cell = lax.broadcasted_iota(jnp.int32, gather.shape, 1)
        gather[...] = jnp.where(point == cell, 1.0, 0.0).astype(gather.dtype)
        cell = lax.broadcasted_iota(jnp.int32, spread.shape, 0)
        point = lax.broadcasted_iota(jnp.int32, spread.shape, 1) // x_count
        spread[...] = jnp.where(point == cell, 1.0, 0.0).astype(spread.dtype)
        for load in loads:
            load.wait()

        source = lax.broadcasted_iota(jnp.int32, (cells, cells), 0)
        target = lax.broadcasted_iota(jnp.int32, (cells, cells), 1)
        inside = jnp.zeros((cells, cells), jnp.float32)
        outside = jnp.zeros((cells, cells), jnp.float32)
        total = jnp.zeros((1, cells), jnp.float32)
        for e in range(offsets.shape[0]):
            weight = jnp.where(e < sides[...], mixing[e], 0.0)
            place = target[:1] + offsets[e]
            total = total + weight
            inside = inside + jnp.where(source == place, weight, 0.0)
            hit = (source == place - cells) | (source == place + cells)
            outside = outside + jnp.where(hit, weight, 0.0)
        inside = inside - jnp.where(source == target, total, 0.0)

        value = tracers[...]
        height = value.shape[0]
        cell = lax.broadcasted_iota(jnp.int32, value.shape, 1)
        beside = [
            h[pl.ds(0, height), :].astype(jnp.float32)
            + h[pl.ds(height, height), :].astype(jnp.float32)
            for h in (below, above)
        ]
        outer = jnp.where(cell < cells // 2, beside[1], beside[0])
        change = jnp.dot(
            jnp.concatenate([value, outer], axis=1),
            jnp.concatenate([inside, outside], axis=0),
            precision=HIGHEST,
            preferred_element_type=jnp.float32,
        )
        diffused[...] = value + DIFFUSIVITY * change

        sections = lax.axis_size("sec")
        oceans = sections // 4
        air = sections - oceans
        ocean = jnp.maximum(lax.axis_index("sec") - air, 0)
        width = chosen.shape[1]
        count = live[0, ocean]
        for k in range(senders.shape[2]):
            place = jnp.where(k < count, senders[ocean, 0, k], sections)
            section = lax.broadcasted_iota(jnp.int32, (air, width), 0)
            chosen[pl.ds(k * air, air), :] = jnp.where(section == place, 1.0, 0.0)
            block = section % (air // oceans)
            owner = ((ocean + section // (air // oceans)) % oceans) ^ 1
            returning[pl.ds(k * air, air), :] = jnp.where(
                block * oceans + owner == place, 1.0, 0.0
            )
        tracer_count, flux_count = factor.shape
        depth = forcing.shape[0] // (tracer_count * flux_count)
        level = lax.broadcasted_iota(jnp.int32, (depth, width), 0).astype(jnp.float32)
        profile = STEP_OCEAN * jnp.exp(-0.5 * level)
        for n in range(flux_count):
            for t in range(tracer_count):
                forcing[pl.ds((n * tracer_count + t) * depth, depth), :] = factor[t, n] * profile
        for copy in copies:
            copy.wait()


def remap_kernel(
    regrid, gather, spread, chosen, returning, forcing, diffused, *refs
):
    arrived, renewed, shares = (refs[2], refs[0], refs[1]), refs[3], refs[4:]

    @pl.when(jnp.logical_not(in_air()))
    def _():
        points, cells = gather.shape
        x_count = points // cells
        slots = regrid.shape[0] // points
        air = chosen.shape[0] // slots
        packed = refs[0].shape[1]
        flux_count = packed // x_count
        row = lax.broadcasted_iota(jnp.int32, (x_count, cells), 0)
        column = lax.broadcasted_iota(jnp.int32, (x_count, cells), 1)
        same = jnp.where(row == column % x_count, 1.0, 0.0)

        blocks = [block[s].astype(jnp.float32) for block in arrived for s in range(block.shape[0])]
        matched = None
        for k in range(slots):
            part = chosen[pl.ds(k * air, 1), :] * blocks[0]
            for s in range(1, air):
                part = part + chosen[pl.ds(k * air + s, 1), :] * blocks[s]
            product = lax.dot_general(
                part.astype(jnp.bfloat16),
                regrid[pl.ds(k * points, points), :],
                (((1,), (1,)), ((), ())),
                preferred_element_type=jnp.float32,
            )
            matched = product if matched is None else matched + product
        matched = matched * jnp.tile(same, (flux_count, x_count))
        high = matched.astype(jnp.bfloat16)
        low = (matched - high.astype(jnp.float32)).astype(jnp.bfloat16)
        summed = jnp.dot(
            jnp.concatenate([high, low], axis=0), gather[...], preferred_element_type=jnp.float32
        )
        ocean_flux = (summed[:packed] + summed[packed:]).reshape(flux_count, x_count, cells).sum(axis=1)
        height = diffused.shape[0]
        value = diffused[...]
        for n in range(flux_count):
            value = value + forcing[pl.ds(n * height, height), :] * ocean_flux[n : n + 1]
        renewed[...] = value

        top = jnp.broadcast_to(value[0:1], (x_count, cells)).astype(jnp.bfloat16)
        wide = jnp.dot(top, spread[...], preferred_element_type=jnp.float32)
        wide = (wide * jnp.tile(same, (1, x_count))).astype(jnp.bfloat16)
        back = [
            jnp.dot(wide, regrid[pl.ds(k * points, points), :], preferred_element_type=jnp.float32)
            for k in range(slots)
        ]
        count = shares[0].shape[0]
        for m, share in enumerate(shares):
            for j in range(count):
                at = m * count + j
                total = returning[pl.ds(at, 1), :] * back[0]
                for k in range(1, slots):
                    total = total + returning[pl.ds(k * air + at, 1), :] * back[k]
                share[j] = total


def add_kernel(*refs):
    count = refs[0].shape[0]
    shares, totals = refs[:-count], refs[-count:]

    @pl.when(jnp.logical_not(in_air()))
    def _():
        for j, total in enumerate(totals):
            value = shares[0][j]
            for share in shares[1:]:
                value = value + share[j]
            total[...] = value


def last_kernel(renewed, *refs):
    returned, (tracers_later, warmth) = refs[:-2], refs[-2:]
    sections = lax.axis_size("sec")
    block = lax.axis_index("sec") // (sections // 4)

    @pl.when(in_air())
    def _():
        tracers_later[...] = jnp.zeros(tracers_later.shape, jnp.float32)

    @pl.when(jnp.logical_not(in_air()))
    def _():
        tracers_later[...] = renewed[...]
        warmth[...] = jnp.zeros(warmth.shape, jnp.float32)

    for j, part in enumerate(returned):

        @pl.when(block == j)
        def _(part=part):
            warmth[...] = part[...]


def per_device(
    climate_field_table,
    zonal_wind_speed,
    meridional_wind,
    sea_warmth_field,
    exchange_law_factor,
    regrid_matrix_stack,
    entry_sender_patch,
    holder_live_total,
    marine_salinity_heat,
    adjacent_offset_lists,
    polygon_side_total,
    interface_mixing_factor,
    solute_forcing_factor,
):
    sections = lax.axis_size("sec")
    ranks = lax.axis_size("rank")
    oceans = sections // 4
    air = sections - oceans
    _, x_points, rows, y_points = climate_field_table.shape
    levels = zonal_wind_speed.shape[2]
    flux_count = exchange_law_factor.shape[0]
    _, tracer_count, depth, cells = marine_salinity_heat.shape
    slots = regrid_matrix_stack.shape[2]
    f32, bf16 = jnp.float32, jnp.bfloat16
    shape = jax.ShapeDtypeStruct

    field = climate_field_table.reshape(x_points * rows, y_points)
    zonal = zonal_wind_speed.reshape(x_points * levels, y_points)
    meridional = meridional_wind.reshape(x_points * levels, y_points)
    regrid = regrid_matrix_stack.reshape(slots * cells * x_points, y_points)
    tracers = marine_salinity_heat.reshape(tracer_count * depth, cells)
    offsets = jnp.transpose(adjacent_offset_lists, (1, 0, 2))
    mixing = jnp.transpose(interface_mixing_factor, (1, 0, 2))
    live = jnp.transpose(holder_live_total, (1, 0))

    along = np.kron(np.eye(y_points // NODES, dtype=np.float32), gll_matrix().T)
    along = jnp.asarray(along)

    fields = rows // levels
    tile = min(8, levels)
    in_place = (
        exchange_law_factor,
        climate_field_table.reshape(x_points, fields, levels, y_points),
        zonal_wind_speed[0],
        meridional_wind[0],
        sea_warmth_field,
    )
    swap_rows = max(flux_count * x_points, rows + 16)
    fluxes = pl.pallas_call(
        functools.partial(flux_kernel, levels),
        out_shape=shape((swap_rows, y_points), bf16),
        in_specs=[HBM] * len(in_place),
        out_specs=VMEM,
        scratch_shapes=[
            pltpu.SMEM(exchange_law_factor.shape, f32),
            pltpu.VMEM((x_points, fields, tile, y_points), f32),
            pltpu.VMEM((x_points, tile, y_points), f32),
            pltpu.VMEM((x_points, tile, y_points), f32),
            pltpu.VMEM((1, x_points, y_points), f32),
            pltpu.SemaphoreType.DMA((len(in_place),)),
        ],
        compiler_params=PARAMS,
        cost_estimate=cost(1),
        name="flux",
    )(*(pltpu.with_memory_space_constraint(a, pltpu.HBM) for a in in_place))
    first, last, own = pl.pallas_call(
        functools.partial(edge_kernel, levels, rows),
        out_shape=(
            shape((rows, y_points), bf16),
            shape((rows, y_points), bf16),
            shape((2, rows, y_points), f32),
        ),
        in_specs=[VMEM] * 5 + [ANY],
        out_specs=(VMEM,) * 3,
        compiler_params=PARAMS,
        cost_estimate=cost(1),
        name="edges",
    )(field, zonal, meridional, along, tracers, fluxes)
    up = [(i, (i + 1) % ranks) for i in range(ranks)]
    below = lax.ppermute(last, "rank", up)
    above = lax.ppermute(first, "rank", [(j, i) for i, j in up])

    def turned(value, m):
        pairs = [(s, s // oceans * oceans + (s + m) % oceans) for s in range(sections)]
        return lax.ppermute(value, "sec", pairs)

    def paired(value, mask):
        pairs = [
            (s, (s // oceans ^ mask) * oceans + (s % oceans ^ 1)) for s in range(sections)
        ]
        return lax.ppermute(value, "sec", pairs)

    received = [turned(fluxes, m) for m in range(1, oceans)]
    packed = pl.pallas_call(
        pack_kernel,
        out_shape=shape((oceans, flux_count * x_points, y_points), bf16),
        in_specs=[VMEM] * oceans,
        out_specs=VMEM,
        compiler_params=PARAMS,
        cost_estimate=cost(0.2),
        name="pack",
    )(fluxes, *received)
    arrived = [paired(packed, 3 ^ block) for block in range(3)]

    from_memory = (
        entry_sender_patch,
        live,
        solute_forcing_factor,
        offsets,
        polygon_side_total,
        mixing,
    )
    later, diffused, chosen, returning, forcing, gather, spread = pl.pallas_call(
        functools.partial(middle_kernel, levels, rows),
        out_shape=(
            shape((x_points, rows, y_points), f32),
            shape(tracers.shape, f32),
            shape((slots * air, y_points), f32),
            shape((slots * air, y_points), f32),
            shape((flux_count * tracer_count * depth, cells), f32),
            shape((x_points * cells, cells), bf16),
            shape((cells, x_points * cells), bf16),
        ),
        in_specs=[VMEM] * 8 + [HBM] * 6,
        out_specs=(HBM,) + (VMEM,) * 6,
        scratch_shapes=[
            pltpu.VMEM(field.shape, f32),
            pltpu.VMEM((x_points, rows, y_points), f32),
        ]
        + [
            (pltpu.SMEM if i < 3 else pltpu.VMEM)(a.shape, a.dtype)
            for i, a in enumerate(from_memory)
        ]
        + [
            pltpu.SemaphoreType.DMA((max(fields, x_points),)),
            pltpu.SemaphoreType.DMA((len(from_memory),)),
        ],
        compiler_params=PARAMS,
        cost_estimate=cost(1),
        name="middle",
    )(
        field,
        zonal,
        meridional,
        along,
        own,
        below,
        above,
        tracers,
        *(pltpu.with_memory_space_constraint(a, pltpu.HBM) for a in from_memory),
    )

    renewed, *shares = pl.pallas_call(
        remap_kernel,
        out_shape=(shape(tracers.shape, f32),)
        + (shape((air // oceans, x_points, y_points), f32),) * oceans,
        in_specs=[VMEM] * 10,
        out_specs=(VMEM,) * (1 + oceans),
        compiler_params=PARAMS,
        cost_estimate=cost(1),
        name="remap",
    )(regrid, gather, spread, chosen, returning, forcing, diffused, arrived[1], arrived[2], arrived[0])
    shares = shares[:1] + [turned(share, m) for m, share in enumerate(shares[1:], 1)]
    totals = pl.pallas_call(
        add_kernel,
        out_shape=(shape((x_points, y_points), f32),) * (air // oceans),
        in_specs=[VMEM] * oceans,
        out_specs=(VMEM,) * (air // oceans),
        compiler_params=PARAMS,
        cost_estimate=cost(0.3),
        name="add",
    )(*shares)
    returned = [paired(total, 3 ^ block) for block, total in enumerate(totals)]
    tracers_later, warmth = pl.pallas_call(
        last_kernel,
        out_shape=(shape(tracers.shape, f32), shape((x_points, y_points), f32)),
        in_specs=[VMEM] * (1 + len(returned)),
        out_specs=(VMEM,) * 2,
        compiler_params=PARAMS,
        cost_estimate=cost(0.5),
        name="last",
    )(renewed, *returned)
    return (
        later.reshape(climate_field_table.shape),
        tracers_later.reshape(marine_salinity_heat.shape),
        warmth[None],
    )


def solution(mesh):
    return jax.shard_map(
        per_device,
        mesh=mesh,
        in_specs=(
            P("sec", "rank", None, None),
            P("sec", "rank", None, None),
            P("sec", "rank", None, None),
            P("sec", "rank", None),
            P(),
            P("sec", "rank", None, None, None, None),
            P(None, "rank", None),
            P(None, "rank"),
            P("sec", None, None, "rank"),
            P("sec", None, "rank"),
            P("sec", "rank"),
            P("sec", None, "rank"),
            P(),
        ),
        out_specs=(
            P("sec", "rank", None, None),
            P("sec", None, None, "rank"),
            P("sec", "rank", None),
        ),
        check_vma=False,
    )
```
